32 devices in a mesh: seq: 8 (over z, core), head: 4 (over y, x).
Axes of the slice: x: 2, y: 2, z: 4, core: 2. Of those that a mesh axis runs over, the one named last changes fastest.
Arguments:
- tokens: bfloat16 [6144, 2048], P('seq'), may hold values from -6 to 6
- lengths: int32 [4], replicated, may hold values from 96 to 5760, as said below
- norm1_gain: float32 [2048], replicated, may hold values from 0.5 to 1.5
- w_query: bfloat16 [2048, 2048], P(None, 'head'), may hold values from -0.125 to 0.125
- key_matrix: bfloat16 [2048, 1024], P(None, 'head'), may hold values from -0.125 to 0.125
- value_matrix: bfloat16 [2048, 1024], P(None, 'head'), may hold values from -0.125 to 0.125
- query_gain: float32 [128], replicated, may hold values from 1 to 2
- key_gain: float32 [128], replicated, may hold values from 0.5 to 1.5
- w_output: bfloat16 [2048, 2048], P('head'), may hold values from -0.5 to 0.5
- norm2_gain: float32 [2048], replicated, may hold values from 0.5 to 1.5
- w_gate: bfloat16 [2048, 6144], P(None, 'head'), may hold values from -0.125 to 0.125
- w_up: bfloat16 [2048, 6144], P(None, 'head'), may hold values from -0.125 to 0.125
- w_down: bfloat16 [6144, 2048], P('head'), may hold values from -0.15625 to 0.15625
- cotangent: bfloat16 [6144, 2048], P('seq'), may hold values from -6 to 6
Outputs:
- mixed: bfloat16 [6144, 2048], P('seq')
- grad_tokens: float32 [6144, 2048], P('seq')
- grad_norm1: float32 [2048], replicated
- grad_query: float32 [2048, 2048], P('seq', 'head')
- grad_key: float32 [2048, 1024], P('seq', 'head')
- grad_value: float32 [2048, 1024], P('seq', 'head')
- grad_qgain: float32 [128], replicated
- grad_kgain: float32 [128], replicated
- grad_output: float32 [2048, 2048], P('head', 'seq')
- grad_norm2: float32 [2048], replicated
- grad_gate: float32 [2048, 6144], P('seq', 'head')
- grad_up: float32 [2048, 6144], P('seq', 'head')
- grad_down: float32 [6144, 2048], P('head', 'seq')
The draws below stay inside these ranges and needn't reach their ends.
Inputs may be any that keep to these rules, and one draw needn't show every extreme that they name: 4 lengths in packing order summing to 6144. One of them, at a place drawn from the seed, holds exactly 5760 tokens; the others together hold 384, each 96 to 192, and one of them exactly 96.
All inputs are finite; a program needn't handle non-finite values.
Results may differ from the reference program's by a relative error of at most 0.025.
Values may be sent and summed in bfloat16 or wider, within the bound.
No kernel may reach another device: no remote copies, remote signals or barrier semaphores. Data moves between devices by JAX's collectives and lax.ppermute only.
A program may use at most 192 MiB of HBM per device.

```python
import math
import jax
import jax.numpy as jnp
from jax import lax

MODEL_WIDTH = 2048
QUERY_HEADS = 16
KEY_VALUE_HEADS = 8
HEAD_WIDTH = 128
FF = 6144
TOKENS_PER_SHARD = 768
NSEQS = 4
TOKEN_COUNT = 6144
N_SEQ = 8


def draw_lengths(key, part):
    key = jax.random.fold_in(key, 11)
    first_key, second_key, third_key = jax.random.split(key, 3)
    middle = jax.random.randint(first_key, (), TOKENS_PER_SHARD // 8, TOKENS_PER_SHARD // 4 + 1).astype(jnp.int32)
    shorts = jnp.stack([jnp.array(TOKENS_PER_SHARD // 8, jnp.int32), middle, (3 * TOKENS_PER_SHARD // 8 - middle).astype(jnp.int32)]).astype(jnp.int32)
    shorts = jax.random.permutation(third_key, shorts)
    long_length = (TOKEN_COUNT - jnp.sum(shorts)).astype(jnp.int32)
    long_place = jax.random.randint(second_key, (), 0, NSEQS).astype(jnp.int32)
    places = jnp.arange(NSEQS, dtype=jnp.int32)
    source = jnp.clip(places - (places > long_place).astype(jnp.int32), 0, NSEQS - 2)
    return jnp.where(places == long_place, long_length, shorts[source]).astype(jnp.int32)


def block_scale(rng, shape, cuts, low, top_value):
    def one(dim, shards_of):
        heights = jax.random.uniform(jax.random.fold_in(jax.random.fold_in(rng, 6), dim), (shards_of,), jnp.float32, low / len(cuts), top_value / len(cuts))
        return jnp.repeat(jnp.exp(heights), shape[dim] // shards_of).reshape((-1,) + (1,) * (len(shape) - dim - 1))

    level = one(*cuts[0])
    for cut in cuts[1:]:
        level = level * one(*cut)
    return level


def scatter_about(own_key, shape, scale, most, shards=(), kind=jnp.bfloat16):
    values = scale * jax.random.normal(own_key, shape, jnp.float32)
    if shards:
        values = values * block_scale(own_key, shape, shards, -0.22, 0.18)
    return jnp.clip(values, -most, most).astype(kind)


def setup_inputs(seed: int = 0) -> dict:
    keys = jax.random.split(jax.random.key(seed), 15)
    tokens = scatter_about(keys[0], (TOKEN_COUNT, MODEL_WIDTH), 1.0, 6.0, ((0, 8),))
    lengths = draw_lengths(jax.random.fold_in(keys[14], 71), 0)
    norm1_gain = jnp.clip(1.0 + 0.1 * jax.random.normal(keys[2], (MODEL_WIDTH,), jnp.float32), 0.5, 1.5)
    w_query = scatter_about(keys[3], (MODEL_WIDTH, QUERY_HEADS * HEAD_WIDTH), MODEL_WIDTH ** -0.5, 0.125, ((1, 4),))
    key_matrix = scatter_about(keys[4], (MODEL_WIDTH, KEY_VALUE_HEADS * HEAD_WIDTH), MODEL_WIDTH ** -0.5, 0.125, ((1, 4),))
    value_matrix = scatter_about(keys[5], (MODEL_WIDTH, KEY_VALUE_HEADS * HEAD_WIDTH), MODEL_WIDTH ** -0.5, 0.125, ((1, 4),))
    query_gain = jnp.clip(jax.random.uniform(keys[6], (HEAD_WIDTH,), jnp.float32, 1.0, 2.0), 1.0, 2.0)
    key_gain = jnp.clip(1.0 + 0.1 * jax.random.normal(keys[7], (HEAD_WIDTH,), jnp.float32), 0.5, 1.5)
    w_output = scatter_about(keys[8], (QUERY_HEADS * HEAD_WIDTH, MODEL_WIDTH), (QUERY_HEADS * HEAD_WIDTH // 16) ** -0.5, 0.5, ((0, 4),))
    norm2_gain = jnp.clip(1.0 + 0.1 * jax.random.normal(keys[9], (MODEL_WIDTH,), jnp.float32), 0.5, 1.5)
    w_gate = scatter_about(keys[10], (MODEL_WIDTH, FF), MODEL_WIDTH ** -0.5, 0.125, ((1, 4),))
    w_up = scatter_about(keys[11], (MODEL_WIDTH, FF), MODEL_WIDTH ** -0.5, 0.125, ((1, 4),))
    w_down = scatter_about(keys[12], (FF, MODEL_WIDTH), (FF // 4) ** -0.5, 0.15625, ((0, 4),))
    cotangent = scatter_about(keys[13], (TOKEN_COUNT, MODEL_WIDTH), 1.0, 6.0, ((0, 8),))
    return {"tokens": tokens, "lengths": lengths, "norm1_gain": norm1_gain, "w_query": w_query, "key_matrix": key_matrix, "value_matrix": value_matrix, "query_gain": query_gain, "key_gain": key_gain, "w_output": w_output, "norm2_gain": norm2_gain, "w_gate": w_gate, "w_up": w_up, "w_down": w_down, "cotangent": cotangent}


EPSILON = 1e-06
ROPE_BASE = 1000000.0
NEGATIVE = -1e+30

@jax.custom_vjp
def low(v):
    return lax.optimization_barrier(v.astype(jnp.bfloat16)).astype(jnp.float32)

@jax.custom_vjp
def low_back(v):
    return v

def low_keep(v):
    return (low(v), None)

def low_pass(kept, grad):
    return (grad,)

def back_keep(v):
    return (v, None)

def back_low(kept, grad):
    return (low(grad),)
low.defvjp(low_keep, low_pass)
low_back.defvjp(back_keep, back_low)

def locate(index, lengths):
    ends = jnp.cumsum(lengths).astype(jnp.int32)
    starts = (ends - lengths).astype(jnp.int32)
    segment = lax.optimization_barrier(jnp.sum((index[:, None] >= ends[None, :]).astype(jnp.int32), axis=1)).astype(jnp.int32)
    chosen = segment[:, None] == jnp.arange(lengths.shape[0], dtype=jnp.int32)[None, :]
    begin = lax.optimization_barrier(jnp.sum(jnp.where(chosen, starts[None, :], 0), axis=1)).astype(jnp.int32)
    return (segment, (index - begin).astype(jnp.int32))

def rotary(position, head_size):
    half_size = head_size // 2
    freq_table = jnp.exp(jnp.arange(half_size, dtype=jnp.float32) * (-2.0 * math.log(ROPE_BASE) / head_size))
    angle = position.astype(jnp.float32)[:, None] * freq_table[None, :]
    cosine = jnp.concatenate([jnp.cos(angle), jnp.cos(angle)], axis=1)
    sine_table = jnp.concatenate([jnp.sin(angle), jnp.sin(angle)], axis=1)
    return (cosine, sine_table)

def rotate(values, cosine, sine_table):
    half_size = values.shape[-1] // 2
    turned = jnp.concatenate([-values[..., half_size:], values[..., :half_size]], axis=-1)
    return values * cosine[:, None, :] + turned * sine_table[:, None, :]

def rms_scale(values, gain):
    inverse = lax.rsqrt(lax.optimization_barrier(jnp.mean(values * values, axis=-1, keepdims=True)) + EPSILON)
    return values * inverse * gain

def prepare(query_in, key_in, query_gain, key_gain, cosine, sine_table):
    row_count = query_in.shape[0]
    head_size = query_gain.shape[0]
    query_heads = query_in.reshape(row_count, -1, head_size)
    key_head_rows = key_in.reshape(row_count, -1, head_size)
    query_rot = rotate(rms_scale(query_heads, query_gain), cosine, sine_table)
    key_rot = rotate(rms_scale(key_head_rows, key_gain), cosine, sine_table)
    return (query_rot.reshape(row_count, -1), key_rot.reshape(row_count, -1))

def exact_dot(left, right):
    return jnp.dot(left, right, precision=lax.Precision.HIGHEST, preferred_element_type=jnp.float32)

def reference(tokens, lengths, norm1_gain, w_query, key_matrix, value_matrix, query_gain, key_gain, w_output, norm2_gain, w_gate, w_up, w_down, cotangent):
    index = jnp.arange(TOKEN_COUNT, dtype=jnp.int32)
    segment, position = locate(index, lengths)
    cosine, sine_table = rotary(position, HEAD_WIDTH)
    score_scale = 1.0 / math.sqrt(HEAD_WIDTH)
    query_group_width = QUERY_HEADS // KEY_VALUE_HEADS

    def attention(query_reduced, key_reduced, value_reduced):
        query_block_list = query_reduced.reshape(N_SEQ, TOKENS_PER_SHARD, KEY_VALUE_HEADS, query_group_width, HEAD_WIDTH)
        key_head_rows = key_reduced.reshape(TOKEN_COUNT, KEY_VALUE_HEADS, HEAD_WIDTH)
        value_head_rows = value_reduced.reshape(TOKEN_COUNT, KEY_VALUE_HEADS, HEAD_WIDTH)
        index_blocks = index.reshape(N_SEQ, TOKENS_PER_SHARD)
        segment_blocks = segment.reshape(N_SEQ, TOKENS_PER_SHARD)

        def one_block(block_items):
            query_block, row_index, row_segment = block_items
            score = score_scale * jnp.einsum('qkgd,rkd->kgqr', query_block, key_head_rows, precision=lax.Precision.HIGHEST)
            score = low_back(score)
            allowed = (index[None, :] <= row_index[:, None]) & (segment[None, :] == row_segment[:, None])
            masked = jnp.where(allowed, score, NEGATIVE)
            row_max = lax.optimization_barrier(jnp.max(masked, axis=-1, keepdims=True))
            weights = jnp.where(allowed, jnp.exp(masked - row_max), 0.0)
            probs = low(weights / lax.optimization_barrier(jnp.sum(weights, axis=-1, keepdims=True)))
            return jnp.einsum('kgqr,rkd->qkgd', probs, value_head_rows, precision=lax.Precision.HIGHEST)
        blocks_out = lax.map(jax.checkpoint(one_block), (query_block_list, index_blocks, segment_blocks))
        return blocks_out.reshape(TOKEN_COUNT, QUERY_HEADS * HEAD_WIDTH)

    def layer(token_f, gain_one, query_w, key_w, value_w, qgain_f, kgain_f, output_w, gain_two, gate_w, up_w, down_w):
        first_in = low(rms_scale(token_f, gain_one))
        query_raw = low_back(exact_dot(first_in, query_w))
        key_raw = low_back(exact_dot(first_in, key_w))
        value_raw = low_back(exact_dot(first_in, value_w))
        query_rot, key_rot = prepare(query_raw, key_raw, qgain_f, kgain_f, cosine, sine_table)
        outcome = attention(low(query_rot), low(key_rot), low(value_raw))
        attn_out = low_back(exact_dot(low(low_back(outcome)), output_w))
        hidden = token_f + attn_out
        second_in = low(rms_scale(hidden, gain_two))
        gate_raw = low_back(exact_dot(second_in, gate_w))
        up_raw = low_back(exact_dot(second_in, up_w))
        down_out = low_back(exact_dot(low(jax.nn.silu(gate_raw) * up_raw), down_w))
        return hidden + down_out
    floats = tuple((array.astype(jnp.float32) for array in (tokens, norm1_gain, w_query, key_matrix, value_matrix, query_gain, key_gain, w_output, norm2_gain, w_gate, w_up, w_down)))
    result, pullback = jax.vjp(layer, *floats)
    grads = pullback(cotangent.astype(jnp.float32))
    return (result.astype(jnp.bfloat16), grads[0], grads[1], grads[2], grads[3], grads[4], grads[5], grads[6], grads[7], grads[8], grads[9], grads[10], grads[11])
```

```python
import functools
import math

import jax
import jax.numpy as jnp
from jax import lax
from jax.experimental import pallas as pl
from jax.experimental.pallas import tpu as pltpu
from jax.sharding import PartitionSpec as P

HEAD_WIDTH = 128
EPSILON = 1e-06
ROPE_BASE = 1000000.0
LOG2E = math.log2(math.e)
SCORE_SCALE = 1.0 / math.sqrt(HEAD_WIDTH)
SCORE_SCALE_2 = LOG2E / math.sqrt(HEAD_WIDTH)
KEY_CHUNK = 256
MIB = 2**20

f32 = jnp.float32
bf16 = jnp.bfloat16
NT = (((1,), (1,)), ((), ()))
TN = (((0,), (0,)), ((), ()))


def dot(left, right):
    return jnp.dot(left, right, preferred_element_type=f32)


def dot_nt(left, right):
    return lax.dot_general(left, right, NT, preferred_element_type=f32)


def dot_tn(left, right):
    return lax.dot_general(left, right, TN, preferred_element_type=f32)


def locate(index, lengths):
    ends = jnp.cumsum(lengths)
    starts = ends - lengths
    segment = jnp.sum((index[:, None] >= ends[None, :]).astype(jnp.int32), axis=1)
    chosen = segment[:, None] == jnp.arange(lengths.shape[0], dtype=jnp.int32)[None, :]
    return jnp.sum(jnp.where(chosen, starts[None, :], 0), axis=1)


def rotary(position):
    half = HEAD_WIDTH // 2
    freq = jnp.exp(jnp.arange(half, dtype=f32) * (-2.0 * math.log(ROPE_BASE) / HEAD_WIDTH))
    angle = position.astype(f32)[:, None] * freq[None, :]
    cosine = jnp.cos(angle)
    sine = jnp.sin(angle)
    return (
        jnp.concatenate([cosine, cosine], axis=1),
        jnp.concatenate([-sine, sine], axis=1),
    )


def head_prep_kernel(raw_ref, gain_ref, cos_ref, sin_ref, out_ref):
    raw = raw_ref[...]
    inverse = lax.rsqrt(jnp.mean(raw * raw, axis=-1, keepdims=True) + EPSILON)
    scaled = raw * inverse * gain_ref[...]
    turned = pltpu.roll(scaled, HEAD_WIDTH // 2, 1)
    out_ref[...] = (scaled * cos_ref[...] + turned * sin_ref[...]).astype(bf16)


def head_prep(raw, gain, cosine, sine):
    rows, width = raw.shape
    block = pl.BlockSpec((rows, HEAD_WIDTH), lambda j: (0, j))
    table = pl.BlockSpec((rows, HEAD_WIDTH), lambda j: (0, 0))
    return pl.pallas_call(
        head_prep_kernel,
        grid=(width // HEAD_WIDTH,),
        in_specs=[block, pl.BlockSpec((1, HEAD_WIDTH), lambda j: (0, 0)), table, table],
        out_specs=block,
        out_shape=jax.ShapeDtypeStruct((rows, width), bf16),
        name="head_prep",
    )(raw, gain[None, :], cosine, sine)


def head_back_kernel(raw_ref, grad_ref, gain_ref, cos_ref, sin_ref, out_ref, gain_grad_ref):
    @pl.when(pl.program_id(0) == 0)
    def _():
        gain_grad_ref[...] = jnp.zeros_like(gain_grad_ref)

    raw = raw_ref[...]
    inverse = lax.rsqrt(jnp.mean(raw * raw, axis=-1, keepdims=True) + EPSILON)
    hat = raw * inverse
    grad = grad_ref[...] * SCORE_SCALE
    back = grad * cos_ref[...] - pltpu.roll(grad, HEAD_WIDTH // 2, 1) * sin_ref[...]
    gain_grad_ref[...] += jnp.sum(back * hat, axis=0, keepdims=True)
    back = back * gain_ref[...]
    out_ref[...] = (inverse * (back - hat * jnp.mean(back * hat, axis=-1, keepdims=True))).astype(
        bf16
    )


def head_back(raw, grad, gain, cosine, sine):
    rows, width = raw.shape
    block = pl.BlockSpec((rows, HEAD_WIDTH), lambda j: (0, j))
    table = pl.BlockSpec((rows, HEAD_WIDTH), lambda j: (0, 0))
    one = pl.BlockSpec((1, HEAD_WIDTH), lambda j: (0, 0))
    return pl.pallas_call(
        head_back_kernel,
        grid=(width // HEAD_WIDTH,),
        in_specs=[block, block, one, table, table],
        out_specs=[block, one],
        out_shape=[
            jax.ShapeDtypeStruct((rows, width), bf16),
            jax.ShapeDtypeStruct((1, HEAD_WIDTH), f32),
        ],
        name="head_back",
    )(raw, grad, gain[None, :], cosine, sine)


def block_cases(meta, key_start, key_rows, rows):
    whole = (key_start + key_rows - 1 <= meta[0]) & (key_start >= meta[2]) & (key_start >= 0)
    none = (
        (key_start > meta[0] + rows - 1) | (key_start + key_rows - 1 < meta[1]) | (key_start < 0)
    )
    return whole, jnp.logical_not(whole | none)


def attend_kernel(
    meta,
    q_ref,
    ka_ref,
    va_ref,
    kb_ref,
    vb_ref,
    begin_ref,
    acc_in,
    sum_in,
    acc_ref,
    sum_ref,
    *,
    first,
):
    rows = q_ref.shape[0]
    if first:
        acc_ref[...] = jnp.zeros_like(acc_ref)
        sum_ref[...] = jnp.zeros_like(sum_ref)
    else:
        acc_ref[...] = acc_in[...]
        sum_ref[...] = sum_in[...]
    ones = jnp.ones((KEY_CHUNK, HEAD_WIDTH), bf16)
    for k_ref, v_ref, key_start in ((ka_ref, va_ref, meta[3]), (kb_ref, vb_ref, meta[4])):
        key_rows = k_ref.shape[0]
        whole, part = block_cases(meta, key_start, key_rows, rows)

        def work(keys, queries, mask):
            score = dot_nt(q_ref[queries, :], k_ref[keys, :])
            weight = jnp.exp2(score * SCORE_SCALE_2)
            if mask is not None:
                weight = jnp.where(mask, weight, 0.0)
            out = dot(weight.astype(bf16), jnp.concatenate([v_ref[keys, :], ones], axis=1))
            acc_ref[queries, :] += out[:, :HEAD_WIDTH]
            sum_ref[queries, :] += out[:, HEAD_WIDTH:]

        @pl.when(whole)
        def _():
            for c in range(key_rows // KEY_CHUNK):
                work(slice(c * KEY_CHUNK, (c + 1) * KEY_CHUNK), slice(0, rows), None)

        @pl.when(part)
        def _():
            for c in range(key_rows // KEY_CHUNK):
                for r in range(rows // KEY_CHUNK):
                    key0 = key_start + c * KEY_CHUNK
                    row0 = meta[0] + r * KEY_CHUNK

                    @pl.when(key0 <= row0 + KEY_CHUNK - 1)
                    def _():
                        queries = slice(r * KEY_CHUNK, (r + 1) * KEY_CHUNK)
                        shape = (KEY_CHUNK, KEY_CHUNK)
                        query_index = row0 + lax.broadcasted_iota(jnp.int32, shape, 0)
                        key_index = key0 + lax.broadcasted_iota(jnp.int32, shape, 1)
                        mask = (key_index <= query_index) & (
                            key_index >= begin_ref[queries, :][:, :1]
                        )
                        work(slice(c * KEY_CHUNK, (c + 1) * KEY_CHUNK), queries, mask)


def attend_stage(q, kv_a, kv_b, begin, meta, acc, total):
    rows, width = q.shape
    key_rows = kv_a.shape[0]
    q_heads = width // HEAD_WIDTH
    kv_heads = kv_a.shape[1] // (2 * HEAD_WIDTH)
    group = q_heads // kv_heads
    first = acc is None
    if first:
        acc = total = jnp.zeros((8, HEAD_WIDTH), f32)
    per_q = pl.BlockSpec((rows, HEAD_WIDTH), lambda j, m: (0, j))
    per_k = pl.BlockSpec((key_rows, HEAD_WIDTH), lambda j, m: (0, j // group))
    per_v = pl.BlockSpec((key_rows, HEAD_WIDTH), lambda j, m: (0, kv_heads + j // group))
    carried = pl.BlockSpec((8, HEAD_WIDTH), lambda j, m: (0, 0)) if first else per_q
    return pl.pallas_call(
        functools.partial(attend_kernel, first=first),
        grid_spec=pltpu.PrefetchScalarGridSpec(
            num_scalar_prefetch=1,
            grid=(q_heads,),
            in_specs=[
                per_q,
                per_k,
                per_v,
                per_k,
                per_v,
                pl.BlockSpec(begin.shape, lambda j, m: (0, 0)),
                carried,
                carried,
            ],
            out_specs=[per_q, per_q],
        ),
        out_shape=[jax.ShapeDtypeStruct(q.shape, f32)] * 2,
        compiler_params=pltpu.CompilerParams(vmem_limit_bytes=40 * MIB),
        cost_estimate=pl.CostEstimate(
            flops=8 * rows * key_rows * width,
            bytes_accessed=10 * MIB,
            transcendentals=2 * rows * key_rows * q_heads,
        ),
        name="attend_stage",
    )(meta, q, kv_a, kv_a, kv_b, kv_b, begin, acc, total)


def attend_back_kernel(
    meta,
    q_ref,
    do_ref,
    ka_ref,
    va_ref,
    kb_ref,
    vb_ref,
    begin_ref,
    lse_ref,
    delta_ref,
    dq_in,
    dq_ref,
    dka_ref,
    dva_ref,
    dkb_ref,
    dvb_ref,
    *,
    first,
    group,
):
    rows = q_ref.shape[0]
    if first:
        dq_ref[...] = jnp.zeros_like(dq_ref)
    else:
        dq_ref[...] = dq_in[...]

    @pl.when(lax.rem(pl.program_id(0), group) == 0)
    def _():
        for ref in (dka_ref, dva_ref, dkb_ref, dvb_ref):
            ref[...] = jnp.zeros_like(ref)

    for k_ref, v_ref, dk_ref, dv_ref, key_start in (
        (ka_ref, va_ref, dka_ref, dva_ref, meta[3]),
        (kb_ref, vb_ref, dkb_ref, dvb_ref, meta[4]),
    ):
        key_rows = k_ref.shape[0]
        whole, part = block_cases(meta, key_start, key_rows, rows)

        def work(keys, queries, mask):
            k = k_ref[keys, :]
            q = q_ref[queries, :]
            do = do_ref[queries, :]
            score = dot_nt(k, q)
            weight = jnp.exp2(score * SCORE_SCALE_2 - lse_ref[0, :, queries])
            if mask is not None:
                weight = jnp.where(mask, weight, 0.0)
            d_weight = dot_nt(v_ref[keys, :], do)
            d_score = (weight * (d_weight - delta_ref[0, :, queries])).astype(bf16)
            dv_ref[keys, :] += dot(weight.astype(bf16), do)
            dk_ref[keys, :] += dot(d_score, q)
            dq_ref[queries, :] += dot_tn(k, d_score).T

        @pl.when(whole)
        def _():
            for c in range(key_rows // KEY_CHUNK):
                work(slice(c * KEY_CHUNK, (c + 1) * KEY_CHUNK), slice(0, rows), None)

        @pl.when(part)
        def _():
            for c in range(key_rows // KEY_CHUNK):
                for r in range(rows // KEY_CHUNK):
                    key0 = key_start + c * KEY_CHUNK
                    row0 = meta[0] + r * KEY_CHUNK

                    @pl.when(key0 <= row0 + KEY_CHUNK - 1)
                    def _():
                        queries = slice(r * KEY_CHUNK, (r + 1) * KEY_CHUNK)
                        shape = (KEY_CHUNK, KEY_CHUNK)
                        key_index = key0 + lax.broadcasted_iota(jnp.int32, shape, 0)
                        query_index = row0 + lax.broadcasted_iota(jnp.int32, shape, 1)
                        mask = (key_index <= query_index) & (key_index >= begin_ref[:, queries])
                        work(slice(c * KEY_CHUNK, (c + 1) * KEY_CHUNK), queries, mask)


def attend_back_stage(q, do, kv_a, kv_b, begin, lse, delta, meta, dq):
    rows, width = q.shape
    key_rows = kv_a.shape[0]
    q_heads = width // HEAD_WIDTH
    kv_heads = kv_a.shape[1] // (2 * HEAD_WIDTH)
    group = q_heads // kv_heads
    first = dq is None
    if first:
        dq = jnp.zeros((8, HEAD_WIDTH), f32)
    per_q = pl.BlockSpec((rows, HEAD_WIDTH), lambda j, m: (0, j))
    per_k = pl.BlockSpec((key_rows, HEAD_WIDTH), lambda j, m: (0, j // group))
    per_v = pl.BlockSpec((key_rows, HEAD_WIDTH), lambda j, m: (0, kv_heads + j // group))
    per_row = pl.BlockSpec((1, 1, rows), lambda j, m: (j, 0, 0))
    carried = pl.BlockSpec((8, HEAD_WIDTH), lambda j, m: (0, 0)) if first else per_q
    grad_shape = jax.ShapeDtypeStruct((key_rows, kv_heads * HEAD_WIDTH), f32)
    return pl.pallas_call(
        functools.partial(attend_back_kernel, first=first, group=group),
        grid_spec=pltpu.PrefetchScalarGridSpec(
            num_scalar_prefetch=1,
            grid=(q_heads,),
            in_specs=[
                per_q,
                per_q,
                per_k,
                per_v,
                per_k,
                per_v,
                pl.BlockSpec(begin.shape, lambda j, m: (0, 0)),
                per_row,
                per_row,
                carried,
            ],
            out_specs=[per_q, per_k, per_k, per_k, per_k],
        ),
        out_shape=[jax.ShapeDtypeStruct(q.shape, f32)] + [grad_shape] * 4,
        compiler_params=pltpu.CompilerParams(vmem_limit_bytes=40 * MIB),
        cost_estimate=pl.CostEstimate(
            flops=20 * rows * key_rows * width,
            bytes_accessed=16 * MIB,
            transcendentals=2 * rows * key_rows * q_heads,
        ),
        name="attend_back_stage",
    )(meta, q, do, kv_a, kv_a, kv_b, kv_b, begin, lse, delta, dq)


def pick(array, index):
    return lax.dynamic_index_in_dim(array, index, 0, keepdims=False)


def solution(mesh):
    n_seq = mesh.shape["seq"]
    n_head = mesh.shape["head"]
    n_chip = n_seq // 2

    def swap_core(value):
        return lax.ppermute(value, "seq", [(i, i ^ 1) for i in range(n_seq)])

    def to_next(value):
        return lax.ppermute(value, "seq", [(i, i + 2) for i in range(n_seq - 2)])

    def to_previous(value):
        return lax.ppermute(value, "seq", [(i + 2, i) for i in range(n_seq - 2)])

    def across(value, bits):
        return lax.ppermute(value, "head", [(i, i ^ bits) for i in range(n_head)])

    def gather_head(value):
        me = lax.axis_index("head")
        if n_head != 4:
            every = lax.all_gather(value, "head", axis=0)
            return [(every[i], i) for i in range(n_head)]
        half = value.shape[0] // 2
        by_x = across(value, 1)
        by_y = across(value, 2)
        low = across(by_x[:half], 2)
        high = across(by_y[half:], 1)
        far = jnp.concatenate([low, high], axis=0)
        return [(value, me), (by_x, me ^ 1), (by_y, me ^ 2), (far, me ^ 3)]

    def scatter_head(value):
        rows, width = value.shape
        if n_head != 4:
            return lax.psum_scatter(value, "head", scatter_dimension=0, tiled=True).astype(f32)
        me = lax.axis_index("head")
        x, y = me & 1, me >> 1
        part = value.reshape(2, 2, 2, rows // 8, width)
        first, second = part[:, :, 0], part[:, :, 1]
        first_x = jnp.swapaxes(first, 0, 1)
        got_first = across(pick(first_x, 1 - x), 1)
        got_second = across(pick(second, 1 - y), 2)
        sum_first = pick(first_x, x).astype(f32) + got_first.astype(f32)
        sum_second = pick(second, y).astype(f32) + got_second.astype(f32)
        last_first = across(pick(sum_first, 1 - y).astype(bf16), 2)
        last_second = across(pick(sum_second, 1 - x).astype(bf16), 1)
        return jnp.concatenate(
            [
                pick(sum_first, y) + last_first.astype(f32),
                pick(sum_second, x) + last_second.astype(f32),
            ],
            axis=0,
        )

    def in_order(pieces):
        rows = pieces[0][0].shape[0]
        out = jnp.zeros((rows * len(pieces),) + pieces[0][0].shape[1:], pieces[0][0].dtype)
        for piece, owner in pieces:
            out = lax.dynamic_update_slice_in_dim(out, piece, owner * rows, 0)
        return out

    def exchange_head(value):
        me = lax.axis_index("head")
        if n_head != 4:
            got = lax.all_to_all(value, "head", 0, 0)
            return got.reshape(-1, value.shape[-1])
        pieces = [(pick(value, me), me)]
        for bits in (3, 1, 2):
            pieces.append((across(pick(value, me ^ bits), bits), me ^ bits))
        return in_order(pieces)

    def body(
        tokens,
        lengths,
        norm1_gain,
        w_query,
        key_matrix,
        value_matrix,
        query_gain,
        key_gain,
        w_output,
        norm2_gain,
        w_gate,
        w_up,
        w_down,
        cotangent,
    ):
        rows = tokens.shape[0]
        share = rows // n_head
        seq_index = lax.axis_index("seq")
        head_index = lax.axis_index("head")
        chip, core = seq_index // 2, seq_index % 2

        half_rows = w_output.shape[0] // 2
        w_half = lax.dynamic_slice_in_dim(w_output, core * half_rows, half_rows, 0)
        w_mine = lax.all_gather(w_half, "head", axis=0)

        index = seq_index * rows + jnp.arange(rows, dtype=jnp.int32)
        begin = locate(index, lengths)
        cosine, sine = rotary(index - begin)
        begin_column = jnp.broadcast_to(begin[:, None], (rows, HEAD_WIDTH))
        begin_row = begin[None, :]

        xf = tokens.astype(f32)
        inverse1 = lax.rsqrt(jnp.mean(xf * xf, axis=-1, keepdims=True) + EPSILON)
        first_in = (xf * inverse1 * norm1_gain).astype(bf16)
        key_raw = dot(first_in, key_matrix)
        v_low = dot(first_in, value_matrix).astype(bf16)
        k_low = head_prep(key_raw, key_gain, cosine, sine)
        current = jnp.concatenate([k_low, v_low], axis=1)
        query_raw = dot(first_in, w_query)
        q_low = head_prep(query_raw, query_gain, cosine, sine)

        stages = []
        acc = total = None
        for stage in range(n_chip):
            sibling = swap_core(current)
            following = to_next(current) if stage + 1 < n_chip else None
            source = chip - stage
            meta = jnp.stack(
                [
                    seq_index * rows,
                    begin[0],
                    begin[rows - 1],
                    (2 * source + core) * rows,
                    (2 * source + 1 - core) * rows,
                ]
            ).astype(jnp.int32)
            stages.append((current, sibling, meta))
            acc, total = attend_stage(q_low, current, sibling, begin_column, meta, acc, total)
            current = following
        outcome = acc / total
        o_low = outcome.astype(bf16)
        q_heads = o_low.shape[1] // HEAD_WIDTH
        lse = jnp.log2(total[:, ::HEAD_WIDTH]).T[:, None, :]

        w_other = swap_core(w_mine)
        w_full = jnp.where(
            core == 0,
            jnp.concatenate([w_mine, w_other], axis=1),
            jnp.concatenate([w_other, w_mine], axis=1),
        )
        hidden = xf
        for piece, owner in gather_head(o_low):
            hidden = hidden + dot(piece, pick(w_full, owner))

        inverse2 = lax.rsqrt(jnp.mean(hidden * hidden, axis=-1, keepdims=True) + EPSILON)
        second_in = (hidden * inverse2 * norm2_gain).astype(bf16)
        gate_raw = dot(second_in, w_gate)
        up_raw = dot(second_in, w_up)
        d_mixed = dot_nt(cotangent, w_down)
        sigmoid = jax.nn.sigmoid(gate_raw)
        silu = gate_raw * sigmoid
        mixed_low = (silu * up_raw).astype(bf16)
        gate_low = (d_mixed * up_raw * (sigmoid * (1.0 + gate_raw * (1.0 - sigmoid)))).astype(bf16)
        up_low = (d_mixed * silu).astype(bf16)
        second_part = (dot_nt(gate_low, w_gate) + dot_nt(up_low, w_up)).astype(bf16)

        def scatter_seq(value, dimension):
            return lax.psum_scatter(
                value.astype(bf16), "seq", scatter_dimension=dimension, tiled=True
            ).astype(f32)

        grad_down = scatter_seq(dot_tn(mixed_low, cotangent), 1)
        grad_gate = scatter_seq(dot_tn(second_in, gate_low), 0)
        grad_up = scatter_seq(dot_tn(second_in, up_low), 0)

        second_grad = scatter_head(second_part)
        my_hidden = lax.dynamic_slice_in_dim(hidden, head_index * share, share, 0)
        my_inverse = lax.rsqrt(jnp.mean(my_hidden * my_hidden, axis=-1, keepdims=True) + EPSILON)
        my_hat = my_hidden * my_inverse
        grad_norm2 = jnp.sum(second_grad * my_hat, axis=0)
        scaled = second_grad * norm2_gain
        my_dy = lax.dynamic_slice_in_dim(cotangent, head_index * share, share, 0).astype(f32)
        hidden_grad = my_dy + my_inverse * (
            scaled - my_hat * jnp.mean(scaled * my_hat, axis=-1, keepdims=True)
        )
        my_branch = hidden_grad.astype(bf16)
        do_rows = dot_nt(my_branch, w_full.reshape(-1, w_full.shape[-1])).astype(bf16)
        do_pieces = jnp.stack(jnp.split(do_rows, n_head, axis=1))
        do_low = exchange_head(do_pieces)

        branch, down_part, do_low = lax.optimization_barrier(
            (my_branch, dot(mixed_low, w_down).astype(bf16), do_low)
        )
        branch = lax.all_gather(branch, "head", axis=0, tiled=True)
        mixed = (hidden + lax.psum(down_part, "head").astype(f32)).astype(bf16)
        grad_output = scatter_seq(dot_tn(o_low, branch), 1)

        product = do_low.astype(f32) * outcome
        delta = jnp.stack(
            [
                jnp.sum(product[:, j * HEAD_WIDTH : (j + 1) * HEAD_WIDTH], axis=-1)
                for j in range(q_heads)
            ]
        )[:, None, :]

        dq = None
        arrived = None
        for stage in reversed(range(n_chip)):
            kv_a, kv_b, meta = stages[stage]
            dq, dk_a, dv_a, dk_b, dv_b = attend_back_stage(
                q_low, do_low, kv_a, kv_b, begin_row, lse, delta, meta, dq
            )
            theirs = swap_core(jnp.concatenate([dk_b, dv_b], axis=1).astype(bf16))
            mine = jnp.concatenate([dk_a, dv_a], axis=1) + theirs.astype(f32)
            if arrived is not None:
                mine = mine + arrived.astype(f32)
            if stage > 0:
                arrived = to_previous(mine.astype(bf16))
        key_width = key_raw.shape[1]
        query_grad, grad_qgain = head_back(query_raw, dq, query_gain, cosine, sine)
        key_grad, grad_kgain = head_back(key_raw, mine[:, :key_width], key_gain, cosine, sine)
        value_grad = mine[:, key_width:].astype(bf16)

        first_part = (
            dot_nt(query_grad, w_query)
            + dot_nt(key_grad, key_matrix)
            + dot_nt(value_grad, value_matrix)
        ).astype(bf16)
        grad_query = scatter_seq(dot_tn(first_in, query_grad), 0)
        grad_key = scatter_seq(dot_tn(first_in, key_grad), 0)
        grad_value = scatter_seq(dot_tn(first_in, value_grad), 0)

        first_grad = scatter_head(first_part)
        my_x = lax.dynamic_slice_in_dim(tokens, head_index * share, share, 0).astype(f32)
        my_inverse1 = lax.rsqrt(jnp.mean(my_x * my_x, axis=-1, keepdims=True) + EPSILON)
        my_hat1 = my_x * my_inverse1
        grad_norm1 = jnp.sum(first_grad * my_hat1, axis=0)
        scaled1 = first_grad * norm1_gain
        my_tokens_grad = hidden_grad + my_inverse1 * (
            scaled1 - my_hat1 * jnp.mean(scaled1 * my_hat1, axis=-1, keepdims=True)
        )
        grad_tokens = in_order(gather_head(my_tokens_grad.astype(bf16))).astype(f32)

        grad_norm1, grad_qgain, grad_kgain, grad_norm2 = lax.psum(
            (grad_norm1, grad_qgain[0], grad_kgain[0], grad_norm2), ("seq", "head")
        )
        return (
            mixed,
            grad_tokens,
            grad_norm1,
            grad_query,
            grad_key,
            grad_value,
            grad_qgain,
            grad_kgain,
            grad_output,
            grad_norm2,
            grad_gate,
            grad_up,
            grad_down,
        )

    in_specs = (
        P("seq", None),
        P(),
        P(),
        P(None, "head"),
        P(None, "head"),
        P(None, "head"),
        P(),
        P(),
        P("head", None),
        P(),
        P(None, "head"),
        P(None, "head"),
        P("head", None),
        P("seq", None),
    )
    out_specs = (
        P("seq", None),
        P("seq", None),
        P(),
        P("seq", "head"),
        P("seq", "head"),
        P("seq", "head"),
        P(),
        P(),
        P("head", "seq"),
        P(),
        P("seq", "head"),
        P("seq", "head"),
        P("head", "seq"),
    )
    return jax.shard_map(body, mesh=mesh, in_specs=in_specs, out_specs=out_specs, check_vma=False)
```

```python
import functools
import math

import jax
import jax.numpy as jnp
from jax import lax
from jax.experimental import pallas as pl
from jax.experimental.pallas import tpu as pltpu
from jax.sharding import PartitionSpec as P

HEAD_WIDTH = 128
EPSILON = 1e-06
ROPE_BASE = 1000000.0
LOG2E = math.log2(math.e)
SCORE_SCALE = 1.0 / math.sqrt(HEAD_WIDTH)
SCORE_SCALE_2 = LOG2E / math.sqrt(HEAD_WIDTH)
KEY_CHUNK = 256
FAR = 512.0
LOG_LANE = 64
MIB = 2**20
SMALL = pl.CostEstimate(flops=1, bytes_accessed=1, transcendentals=0)

f32 = jnp.float32
bf16 = jnp.bfloat16
NT = (((1,), (1,)), ((), ()))
TN = (((0,), (0,)), ((), ()))


def dot(left, right):
    return jnp.dot(left, right, preferred_element_type=f32)


def dot_nt(left, right):
    return lax.dot_general(left, right, NT, preferred_element_type=f32)


def dot_tn(left, right):
    return lax.dot_general(left, right, TN, preferred_element_type=f32)


def locate(index, lengths):
    ends = jnp.cumsum(lengths)
    starts = ends - lengths
    segment = jnp.sum((index[:, None] >= ends[None, :]).astype(jnp.int32), axis=1)
    chosen = segment[:, None] == jnp.arange(lengths.shape[0], dtype=jnp.int32)[None, :]
    return jnp.sum(jnp.where(chosen, starts[None, :], 0), axis=1)


def rotary(position):
    half = HEAD_WIDTH // 2
    freq = jnp.exp(jnp.arange(half, dtype=f32) * (-2.0 * math.log(ROPE_BASE) / HEAD_WIDTH))
    angle = position.astype(f32)[:, None] * freq[None, :]
    cosine = jnp.cos(angle)
    sine = jnp.sin(angle)
    return (
        jnp.concatenate([cosine, cosine], axis=1),
        jnp.concatenate([-sine, sine], axis=1),
    )


def lane_index(rows):
    return lax.broadcasted_iota(jnp.int32, (rows, HEAD_WIDTH), 1)


def row_index(rows):
    return lax.broadcasted_iota(jnp.int32, (rows, HEAD_WIDTH), 0)


def in_segment(index, bounds_ref):
    return (index >= bounds_ref[0:1, :]) & (index < bounds_ref[1:2, :])


def split_parts(value):
    high = value.astype(bf16)
    rest = value - high.astype(f32)
    middle = rest.astype(bf16)
    return high, middle, (rest - middle.astype(f32)).astype(bf16)


def normed(raw, gain, cosine, sine):
    inverse = lax.rsqrt(jnp.mean(raw * raw, axis=-1, keepdims=True) + EPSILON)
    scaled = raw * inverse * gain
    return scaled * cosine + pltpu.roll(scaled, HEAD_WIDTH // 2, 1) * sine


def key_prep_kernel(raw_ref, value_ref, gain_ref, cos_ref, sin_ref, out_ref):
    key = normed(raw_ref[...], gain_ref[...], cos_ref[...], sin_ref[...])
    out_ref[:, :HEAD_WIDTH] = key.astype(bf16)
    out_ref[:, HEAD_WIDTH:] = value_ref[...].astype(bf16)


def key_prep(raw, value, gain, cosine, sine):
    rows, width = raw.shape
    block = pl.BlockSpec((rows, HEAD_WIDTH), lambda j: (0, j))
    table = pl.BlockSpec((rows, HEAD_WIDTH), lambda j: (0, 0))
    return pl.pallas_call(
        key_prep_kernel,
        grid=(width // HEAD_WIDTH,),
        in_specs=[block, block, pl.BlockSpec((1, HEAD_WIDTH), lambda j: (0, 0)), table, table],
        out_specs=pl.BlockSpec((rows, 2 * HEAD_WIDTH), lambda j: (0, j)),
        out_shape=jax.ShapeDtypeStruct((rows, 2 * width), bf16),
        name="key_prep",
    )(raw, value, gain[None, :], cosine, sine)


def query_prep_kernel(meta, raw_ref, gain_ref, cos_ref, sin_ref, bounds_ref, out_ref):
    rows = raw_ref.shape[0]
    query = normed(raw_ref[...], gain_ref[...], cos_ref[...], sin_ref[...])
    out_ref[:, :HEAD_WIDTH] = (query * SCORE_SCALE_2).astype(bf16)
    inside = in_segment(meta[0] + row_index(rows), bounds_ref)
    free = inside | (lane_index(rows) >= LOG_LANE)
    out_ref[:, HEAD_WIDTH:] = jnp.where(free, 0.0, -FAR).astype(bf16)


def query_prep(meta, raw, gain, cosine, sine, bounds):
    rows, width = raw.shape
    table = pl.BlockSpec((rows, HEAD_WIDTH), lambda j, m: (0, 0))
    return pl.pallas_call(
        query_prep_kernel,
        grid_spec=pltpu.PrefetchScalarGridSpec(
            num_scalar_prefetch=1,
            grid=(width // HEAD_WIDTH,),
            in_specs=[
                pl.BlockSpec((rows, HEAD_WIDTH), lambda j, m: (0, j)),
                pl.BlockSpec((1, HEAD_WIDTH), lambda j, m: (0, 0)),
                table,
                table,
                pl.BlockSpec((8, HEAD_WIDTH), lambda j, m: (0, 0)),
            ],
            out_specs=pl.BlockSpec((rows, 2 * HEAD_WIDTH), lambda j, m: (0, j)),
        ),
        out_shape=jax.ShapeDtypeStruct((rows, 2 * width), bf16),
        name="query_prep",
    )(meta, raw, gain[None, :], cosine, sine, bounds)


def head_back_kernel(raw_ref, grad_ref, gain_ref, cos_ref, sin_ref, out_ref, gain_grad_ref, *, scale):
    @pl.when(pl.program_id(0) == 0)
    def _():
        gain_grad_ref[...] = jnp.zeros_like(gain_grad_ref)

    raw = raw_ref[...]
    inverse = lax.rsqrt(jnp.mean(raw * raw, axis=-1, keepdims=True) + EPSILON)
    hat = raw * inverse
    grad = grad_ref[...] * scale
    back = grad * cos_ref[...] - pltpu.roll(grad, HEAD_WIDTH // 2, 1) * sin_ref[...]
    gain_grad_ref[...] += jnp.sum(back * hat, axis=0, keepdims=True)
    back = back * gain_ref[...]
    out_ref[...] = (inverse * (back - hat * jnp.mean(back * hat, axis=-1, keepdims=True))).astype(
        bf16
    )


def head_back(raw, grad, gain, cosine, sine, scale, stride):
    rows, width = raw.shape
    block = pl.BlockSpec((rows, HEAD_WIDTH), lambda j: (0, j))
    spaced = pl.BlockSpec((rows, HEAD_WIDTH), lambda j: (0, j * stride))
    table = pl.BlockSpec((rows, HEAD_WIDTH), lambda j: (0, 0))
    one = pl.BlockSpec((1, HEAD_WIDTH), lambda j: (0, 0))
    return pl.pallas_call(
        functools.partial(head_back_kernel, scale=scale),
        grid=(width // HEAD_WIDTH,),
        in_specs=[block, spaced, one, table, table],
        out_specs=[block, one],
        out_shape=[
            jax.ShapeDtypeStruct((rows, width), bf16),
            jax.ShapeDtypeStruct((1, HEAD_WIDTH), f32),
        ],
        name="head_back",
    )(raw, grad, gain[None, :], cosine, sine)


def key_lanes(meta, key_start, rows, bounds_ref):
    inside = in_segment(key_start + row_index(rows), bounds_ref)
    lanes = lane_index(rows)
    log_lanes = (lanes >= LOG_LANE) & (lanes < LOG_LANE + 3)
    return jnp.where(inside | log_lanes, 1.0, 0.0).astype(bf16)


def block_used(meta, key_start, key_rows, rows):
    return (
        (key_start >= 0) & (key_start <= meta[0] + rows - 1) & (key_start + key_rows - 1 >= meta[1])
    )


def lower_mask(transposed):
    shape = (KEY_CHUNK, KEY_CHUNK)
    first = lax.broadcasted_iota(jnp.int32, shape, 0)
    second = lax.broadcasted_iota(jnp.int32, shape, 1)
    return first <= second if transposed else second <= first


def chunk(i, n=1):
    return slice(i * KEY_CHUNK, (i + n) * KEY_CHUNK)


def attend_kernel(
    meta, q_ref, kva_ref, kvb_ref, bounds_ref, acc_in, sum_in, acc_ref, sum_ref, *, first
):
    rows = q_ref.shape[0]
    key_rows = kva_ref.shape[0]
    if first:
        acc_ref[...] = jnp.zeros_like(acc_ref)
        sum_ref[...] = jnp.zeros_like(sum_ref)
    else:
        acc_ref[...] = acc_in[...]
        sum_ref[...] = sum_in[...]
    ones = jnp.ones((KEY_CHUNK, HEAD_WIDTH), bf16)

    def work(kv_ref, lanes, keys, queries, mask):
        key = jnp.concatenate([kv_ref[keys, :HEAD_WIDTH], lanes[keys, :]], axis=1)
        weight = jnp.exp2(dot_nt(q_ref[queries, :], key))
        if mask:
            weight = jnp.where(lower_mask(False), weight, 0.0)
        value = jnp.concatenate([kv_ref[keys, HEAD_WIDTH:], ones], axis=1)
        out = dot(weight.astype(bf16), value)
        acc_ref[queries, :] += out[:, :HEAD_WIDTH]
        sum_ref[queries, :] += out[:, HEAD_WIDTH:]

    for place, kv_ref in enumerate((kva_ref, kvb_ref)):
        key_start = meta[2 + place]
        diagonal = first and place == 0

        @pl.when(block_used(meta, key_start, key_rows, rows))
        def _():
            lanes = key_lanes(meta, key_start, key_rows, bounds_ref)
            for c in range(key_rows // KEY_CHUNK):
                if diagonal:
                    work(kv_ref, lanes, chunk(c), chunk(c), True)
                    if c + 1 < rows // KEY_CHUNK:
                        work(kv_ref, lanes, chunk(c), slice((c + 1) * KEY_CHUNK, rows), False)
                else:
                    work(kv_ref, lanes, chunk(c), slice(0, rows), False)


def attend_stage(q, kv_a, kv_b, bounds, meta, acc, total):
    rows = q.shape[0]
    key_rows = kv_a.shape[0]
    q_heads = q.shape[1] // (2 * HEAD_WIDTH)
    group = q.shape[1] // kv_a.shape[1]
    width = q_heads * HEAD_WIDTH
    first = acc is None
    if first:
        acc = total = jnp.zeros((8, HEAD_WIDTH), f32)
    wide = 2 * HEAD_WIDTH
    per_q = pl.BlockSpec((rows, wide), lambda j, m: (0, j))
    per_kv = pl.BlockSpec((key_rows, wide), lambda j, m: (0, j // group))
    per_out = pl.BlockSpec((rows, HEAD_WIDTH), lambda j, m: (0, j))
    carried = pl.BlockSpec((8, HEAD_WIDTH), lambda j, m: (0, 0)) if first else per_out
    return pl.pallas_call(
        functools.partial(attend_kernel, first=first),
        grid_spec=pltpu.PrefetchScalarGridSpec(
            num_scalar_prefetch=1,
            grid=(q_heads,),
            in_specs=[
                per_q,
                per_kv,
                per_kv,
                pl.BlockSpec((8, HEAD_WIDTH), lambda j, m: (0, 0)),
                carried,
                carried,
            ],
            out_specs=[per_out, per_out],
        ),
        out_shape=[jax.ShapeDtypeStruct((rows, width), f32)] * 2,
        input_output_aliases={} if first else {5: 0, 6: 1},
        compiler_params=pltpu.CompilerParams(vmem_limit_bytes=40 * MIB),
        cost_estimate=SMALL,
        name="attend_stage",
    )(meta, q, kv_a, kv_b, bounds, acc, total)


def finish_kernel(q_ref, acc_ref, sum_ref, o_ref, q_out_ref):
    total = sum_ref[...]
    o_ref[...] = (acc_ref[...] / total).astype(bf16)
    rows = total.shape[0]
    lanes = lane_index(rows)
    extra = q_ref[:, HEAD_WIDTH:].astype(f32)
    for i, part in enumerate(split_parts(jnp.log2(total))):
        extra = jnp.where(lanes == LOG_LANE + i, -part.astype(f32), extra)
    q_out_ref[:, :HEAD_WIDTH] = q_ref[:, :HEAD_WIDTH]
    q_out_ref[:, HEAD_WIDTH:] = extra.astype(bf16)


def finish(q, acc, total):
    rows, width = acc.shape
    narrow = pl.BlockSpec((rows, HEAD_WIDTH), lambda j: (0, j))
    wide = pl.BlockSpec((rows, 2 * HEAD_WIDTH), lambda j: (0, j))
    return pl.pallas_call(
        finish_kernel,
        grid=(width // HEAD_WIDTH,),
        in_specs=[wide, narrow, narrow],
        out_specs=[narrow, wide],
        out_shape=[
            jax.ShapeDtypeStruct((rows, width), bf16),
            jax.ShapeDtypeStruct((rows, 2 * width), bf16),
        ],
        name="finish",
    )(q, acc, total)


def delta_kernel(do_ref, acc_ref, sum_ref, out_ref):
    do = do_ref[...]
    outcome = acc_ref[...] / sum_ref[...]
    delta = jnp.sum(do.astype(f32) * outcome, axis=-1, keepdims=True)
    rows = do.shape[0]
    lanes = lane_index(rows)
    extra = jnp.zeros((rows, HEAD_WIDTH), f32)
    for i, part in enumerate(split_parts(delta)):
        extra = jnp.where(lanes == i, -part.astype(f32), extra)
    out_ref[:, :HEAD_WIDTH] = do
    out_ref[:, HEAD_WIDTH:] = extra.astype(bf16)


def with_delta(do, acc, total):
    rows, width = acc.shape
    narrow = pl.BlockSpec((rows, HEAD_WIDTH), lambda j: (0, j))
    return pl.pallas_call(
        delta_kernel,
        grid=(width // HEAD_WIDTH,),
        in_specs=[narrow, narrow, narrow],
        out_specs=pl.BlockSpec((rows, 2 * HEAD_WIDTH), lambda j: (0, j)),
        out_shape=jax.ShapeDtypeStruct((rows, 2 * width), bf16),
        name="with_delta",
    )(do, acc, total)


def attend_back_kernel(
    meta,
    q_ref,
    do_ref,
    kv_ref,
    bounds_ref,
    dq_in,
    dq_ref,
    dkv_ref,
    dq_turned,
    dkv_sum,
    *,
    first,
    group,
    diagonal,
    place,
):
    rows = q_ref.shape[0]
    key_rows = kv_ref.shape[0]
    key_start = meta[2 + place]
    step = lax.rem(pl.program_id(0), group)

    @pl.when(step == 0)
    def _():
        dkv_sum[...] = jnp.zeros_like(dkv_sum)

    def work(lanes, ones, keys, queries, mask):
        key = kv_ref[keys, :HEAD_WIDTH]
        q = q_ref[queries, :]
        do = do_ref[queries, :]
        weight = jnp.exp2(dot_nt(jnp.concatenate([key, lanes[keys, :]], axis=1), q))
        if mask:
            weight = jnp.where(lower_mask(True), weight, 0.0)
        value = jnp.concatenate([kv_ref[keys, HEAD_WIDTH:], ones], axis=1)
        d_score = (weight * dot_nt(value, do)).astype(bf16)
        dkv_sum[keys, HEAD_WIDTH:] += dot(weight.astype(bf16), do[:, :HEAD_WIDTH])
        dkv_sum[keys, :HEAD_WIDTH] += dot(d_score, q[:, :HEAD_WIDTH])
        dq_turned[:, queries] += dot_tn(key, d_score)

    used = block_used(meta, key_start, key_rows, rows)

    @pl.when(used)
    def _():
        dq_turned[...] = jnp.zeros_like(dq_turned)
        lanes = key_lanes(meta, key_start, key_rows, bounds_ref)
        ones = jnp.where(lane_index(KEY_CHUNK) < 3, 1.0, 0.0).astype(bf16)
        for c in range(key_rows // KEY_CHUNK):
            if diagonal:
                work(lanes, ones, chunk(c), chunk(c), True)
                if c + 1 < rows // KEY_CHUNK:
                    work(lanes, ones, chunk(c), slice((c + 1) * KEY_CHUNK, rows), False)
            else:
                work(lanes, ones, chunk(c), slice(0, rows), False)
        turned = dq_turned[...].T
        dq_ref[...] = turned if first else dq_in[...] + turned

    @pl.when(jnp.logical_not(used))
    def _():
        dq_ref[...] = jnp.zeros_like(dq_ref) if first else dq_in[...]

    @pl.when(step == group - 1)
    def _():
        dkv_ref[...] = dkv_sum[...].astype(dkv_ref.dtype)


def attend_back(q, do, kv, bounds, meta, dq, place, diagonal, kind):
    rows = q.shape[0]
    key_rows = kv.shape[0]
    q_heads = q.shape[1] // (2 * HEAD_WIDTH)
    group = q.shape[1] // kv.shape[1]
    width = q_heads * HEAD_WIDTH
    first = dq is None
    if first:
        dq = jnp.zeros((8, HEAD_WIDTH), f32)
    wide = 2 * HEAD_WIDTH
    per_q = pl.BlockSpec((rows, wide), lambda j, m: (0, j))
    per_kv = pl.BlockSpec((key_rows, wide), lambda j, m: (0, j // group))
    per_out = pl.BlockSpec((rows, HEAD_WIDTH), lambda j, m: (0, j))
    carried = pl.BlockSpec((8, HEAD_WIDTH), lambda j, m: (0, 0)) if first else per_out
    return pl.pallas_call(
        functools.partial(
            attend_back_kernel, first=first, group=group, diagonal=diagonal, place=place
        ),
        grid_spec=pltpu.PrefetchScalarGridSpec(
            num_scalar_prefetch=1,
            grid=(q_heads,),
            in_specs=[
                per_q,
                per_q,
                per_kv,
                pl.BlockSpec((8, HEAD_WIDTH), lambda j, m: (0, 0)),
                carried,
            ],
            out_specs=[per_out, per_kv],
            scratch_shapes=[
                pltpu.VMEM((HEAD_WIDTH, rows), f32),
                pltpu.VMEM((key_rows, wide), f32),
            ],
        ),
        out_shape=[
            jax.ShapeDtypeStruct((rows, width), f32),
            jax.ShapeDtypeStruct(kv.shape, kind),
        ],
        input_output_aliases={} if first else {5: 0},
        compiler_params=pltpu.CompilerParams(vmem_limit_bytes=40 * MIB),
        cost_estimate=SMALL,
        name="attend_back",
    )(meta, q, do, kv, bounds, dq)


def after(values):
    return lax.optimization_barrier(values)


def pick(array, index):
    return lax.dynamic_index_in_dim(array, index, 0, keepdims=False)


def solution(mesh):
    n_seq = mesh.shape["seq"]
    n_head = mesh.shape["head"]
    n_chip = n_seq // 2

    def swap_core(value):
        return lax.ppermute(value, "seq", [(i, i ^ 1) for i in range(n_seq)])

    def to_next(value):
        return lax.ppermute(value, "seq", [(i, i + 2) for i in range(n_seq - 2)])

    def to_previous(value):
        return lax.ppermute(value, "seq", [(i + 2, i) for i in range(n_seq - 2)])

    def across(value, bits):
        return lax.ppermute(value, "head", [(i, i ^ bits) for i in range(n_head)])

    def gather_head(value):
        me = lax.axis_index("head")
        if n_head != 4:
            every = lax.all_gather(value, "head", axis=0)
            return [(every[i], i) for i in range(n_head)]
        half = value.shape[0] // 2
        by_x = across(value, 1)
        by_y = across(value, 2)
        low = across(by_x[:half], 2)
        high = across(by_y[half:], 1)
        far = jnp.concatenate([low, high], axis=0)
        return [(value, me), (by_x, me ^ 1), (by_y, me ^ 2), (far, me ^ 3)]

    def scatter_head(value, *beside):
        rows, width = value.shape
        if n_head != 4:
            total = lax.psum_scatter(value, "head", scatter_dimension=0, tiled=True).astype(f32)
            return total, [work() for work in beside]
        me = lax.axis_index("head")
        x, y = me & 1, me >> 1
        part = value.reshape(2, 2, 2, rows // 8, width)
        first, second = part[:, :, 0], part[:, :, 1]
        first_x = jnp.swapaxes(first, 0, 1)
        got_first = across(pick(first_x, 1 - x), 1)
        got_second = across(pick(second, 1 - y), 2)
        made = []
        if beside:
            got_first, got_second, made_first = after((got_first, got_second, beside[0]()))
            made.append(made_first)
        sum_first = pick(first_x, x).astype(f32) + got_first.astype(f32)
        sum_second = pick(second, y).astype(f32) + got_second.astype(f32)
        last_first = across(pick(sum_first, 1 - y).astype(bf16), 2)
        last_second = across(pick(sum_second, 1 - x).astype(bf16), 1)
        if beside:
            last_first, last_second, made_second = after((last_first, last_second, beside[1]()))
            made.append(made_second)
        total = jnp.concatenate(
            [
                pick(sum_first, y) + last_first.astype(f32),
                pick(sum_second, x) + last_second.astype(f32),
            ],
            axis=0,
        )
        return total, made

    def in_order(pieces):
        rows = pieces[0][0].shape[0]
        out = jnp.zeros((rows * len(pieces),) + pieces[0][0].shape[1:], pieces[0][0].dtype)
        for piece, owner in pieces:
            out = lax.dynamic_update_slice_in_dim(out, piece, owner * rows, 0)
        return out

    def exchange_head(value):
        me = lax.axis_index("head")
        if n_head != 4:
            got = lax.all_to_all(value, "head", 0, 0)
            return got.reshape(-1, value.shape[-1])
        pieces = [(pick(value, me), me)]
        for bits in (3, 1, 2):
            pieces.append((across(pick(value, me ^ bits), bits), me ^ bits))
        return in_order(pieces)

    def body(
        tokens,
        lengths,
        norm1_gain,
        w_query,
        key_matrix,
        value_matrix,
        query_gain,
        key_gain,
        w_output,
        norm2_gain,
        w_gate,
        w_up,
        w_down,
        cotangent,
    ):
        rows = tokens.shape[0]
        share = rows // n_head
        seq_index = lax.axis_index("seq")
        head_index = lax.axis_index("head")
        chip, core = seq_index // 2, seq_index % 2

        half_rows = w_output.shape[0] // 2
        w_half = lax.dynamic_slice_in_dim(w_output, core * half_rows, half_rows, 0)
        w_mine = lax.all_gather(w_half, "head", axis=0)

        index = seq_index * rows + jnp.arange(rows, dtype=jnp.int32)
        begin = locate(index, lengths)
        cosine, sine = rotary(index - begin)
        ends = jnp.cumsum(lengths)
        n_lengths = lengths.shape[0]
        bounds = jnp.zeros((8, HEAD_WIDTH), jnp.int32).at[0].set(2**30)
        bounds = bounds.at[0, :n_lengths].set(ends - lengths).at[1, :n_lengths].set(ends)

        def stage_meta(stage):
            source = 2 * (chip - stage)
            return jnp.stack(
                [seq_index * rows, begin[0], (source + core) * rows, (source + 1 - core) * rows]
            ).astype(jnp.int32)

        metas = [stage_meta(stage) for stage in range(n_chip)]

        xf = tokens.astype(f32)
        inverse1 = lax.rsqrt(jnp.mean(xf * xf, axis=-1, keepdims=True) + EPSILON)
        first_in = (xf * inverse1 * norm1_gain).astype(bf16)
        key_raw = dot(first_in, key_matrix)
        value_raw = dot(first_in, value_matrix)
        current = key_prep(key_raw, value_raw, key_gain, cosine, sine)
        sibling = swap_core(current)
        following = to_next(current)
        query_raw = dot(first_in, w_query)
        q_wide = query_prep(metas[0], query_raw, query_gain, cosine, sine, bounds)
        d_mixed = dot_nt(cotangent, w_down)
        following, q_wide, d_mixed = after((following, q_wide, d_mixed))

        blocks = []
        acc = total = None
        for stage in range(n_chip):
            blocks.append((current, sibling))
            if stage + 1 < n_chip:
                current = following
                sibling = swap_core(current)
                following = to_next(current) if stage + 2 < n_chip else None
            acc, total = attend_stage(q_wide, *blocks[stage], bounds, metas[stage], acc, total)
            if following is not None:
                following, acc, total = after((following, acc, total))
            if stage == 1:
                w_mine, acc = after((w_mine, acc))
                w_other = swap_core(w_mine)
                w_full = jnp.where(
                    core == 0,
                    jnp.concatenate([w_mine, w_other], axis=1),
                    jnp.concatenate([w_other, w_mine], axis=1),
                )
            if stage == n_chip - 2:
                w_full, acc = after((w_full, acc))
        o_low, q_back = finish(q_wide, acc, total)

        hidden = xf
        for piece, owner in gather_head(o_low):
            hidden = hidden + dot(piece, pick(w_full, owner))

        inverse2 = lax.rsqrt(jnp.mean(hidden * hidden, axis=-1, keepdims=True) + EPSILON)
        second_in = (hidden * inverse2 * norm2_gain).astype(bf16)
        gate_raw = dot(second_in, w_gate)
        up_raw = dot(second_in, w_up)
        sigmoid = jax.nn.sigmoid(gate_raw)
        silu = gate_raw * sigmoid
        mixed_low = (silu * up_raw).astype(bf16)
        gate_low = (d_mixed * up_raw * (sigmoid * (1.0 + gate_raw * (1.0 - sigmoid)))).astype(bf16)
        up_low = (d_mixed * silu).astype(bf16)

        def scatter_seq(value, dimension):
            return lax.psum_scatter(value, "seq", scatter_dimension=dimension, tiled=True)

        down_sum = dot_tn(mixed_low, cotangent).astype(bf16)
        down_sum, gate_low, up_low = after((down_sum, gate_low, up_low))
        grad_down = scatter_seq(down_sum, 1)
        second_part = (dot_nt(gate_low, w_gate) + dot_nt(up_low, w_up)).astype(bf16)

        second_grad, (gate_sum, up_sum) = scatter_head(
            second_part,
            lambda: dot_tn(second_in, gate_low).astype(bf16),
            lambda: dot_tn(second_in, up_low).astype(bf16),
        )
        gate_up_sum = jnp.concatenate([gate_sum, up_sum], axis=1)
        my_hidden = lax.dynamic_slice_in_dim(hidden, head_index * share, share, 0)
        my_inverse = lax.rsqrt(jnp.mean(my_hidden * my_hidden, axis=-1, keepdims=True) + EPSILON)
        my_hat = my_hidden * my_inverse
        grad_norm2 = jnp.sum(second_grad * my_hat, axis=0)
        scaled = second_grad * norm2_gain
        my_dy = lax.dynamic_slice_in_dim(cotangent, head_index * share, share, 0).astype(f32)
        hidden_grad = my_dy + my_inverse * (
            scaled - my_hat * jnp.mean(scaled * my_hat, axis=-1, keepdims=True)
        )
        my_branch = hidden_grad.astype(bf16)
        do_rows = dot_nt(my_branch, w_full.reshape(-1, w_full.shape[-1])).astype(bf16)
        do_pieces = jnp.stack(jnp.split(do_rows, n_head, axis=1))
        do_low = exchange_head(do_pieces)

        do_wide = with_delta(do_low, acc, total)
        grad_down, gate_up_sum, do_wide = after((grad_down, gate_up_sum, do_wide))
        grad_gate_up = scatter_seq(gate_up_sum, 0)

        mixed_late, my_branch, do_wide = after((mixed_low, my_branch, do_wide))
        mixed_sum, unused = scatter_head(dot(mixed_late, w_down).astype(bf16))
        mixed = in_order(gather_head((my_hidden + mixed_sum).astype(bf16)))
        branch = in_order(gather_head(my_branch))

        dq = None
        arrived = None
        for stage in reversed(range(n_chip)):
            kv_a, kv_b = blocks[stage]
            meta = metas[stage]
            dq, dkv_b = attend_back(q_back, do_wide, kv_b, bounds, meta, dq, 1, False, bf16)
            theirs = swap_core(dkv_b)
            dq, dkv_a = attend_back(q_back, do_wide, kv_a, bounds, meta, dq, 0, stage == 0, f32)
            dkv = dkv_a + theirs.astype(f32)
            if arrived is not None:
                dkv = dkv + arrived.astype(f32)
            if stage > 0:
                sent, dq = after((dkv.astype(bf16), dq))
                arrived = to_previous(sent)
        query_grad, grad_qgain = head_back(
            query_raw, dq, query_gain, cosine, sine, SCORE_SCALE, 1
        )
        key_grad, grad_kgain = head_back(
            key_raw, dkv, key_gain, cosine, sine, 1.0 / LOG2E, 2
        )
        value_grad = jnp.concatenate(
            [
                dkv[:, (2 * j + 1) * HEAD_WIDTH : (2 * j + 2) * HEAD_WIDTH]
                for j in range(dkv.shape[1] // (2 * HEAD_WIDTH))
            ],
            axis=1,
        ).astype(bf16)

        first_part = (
            dot_nt(query_grad, w_query)
            + dot_nt(key_grad, key_matrix)
            + dot_nt(value_grad, value_matrix)
        ).astype(bf16)
        first_grad, (attn_sum, output_sum) = scatter_head(
            first_part,
            lambda: jnp.concatenate(
                [
                    dot_tn(first_in, query_grad).astype(bf16),
                    dot_tn(first_in, key_grad).astype(bf16),
                    dot_tn(first_in, value_grad).astype(bf16),
                ],
                axis=1,
            ),
            lambda: dot_tn(o_low, branch).astype(bf16),
        )
        grad_gate_up, attn_sum, output_sum = after((grad_gate_up, attn_sum, output_sum))
        grad_attn = scatter_seq(attn_sum, 0)
        grad_output = scatter_seq(output_sum, 1)
        widths = (query_grad.shape[1], query_grad.shape[1] + key_grad.shape[1])
        grad_query, grad_key, grad_value = jnp.split(grad_attn, widths, axis=1)

        my_x = lax.dynamic_slice_in_dim(tokens, head_index * share, share, 0).astype(f32)
        my_inverse1 = lax.rsqrt(jnp.mean(my_x * my_x, axis=-1, keepdims=True) + EPSILON)
        my_hat1 = my_x * my_inverse1
        grad_norm1 = jnp.sum(first_grad * my_hat1, axis=0)
        scaled1 = first_grad * norm1_gain
        my_tokens_grad = hidden_grad + my_inverse1 * (
            scaled1 - my_hat1 * jnp.mean(scaled1 * my_hat1, axis=-1, keepdims=True)
        )
        grad_tokens = in_order(gather_head(my_tokens_grad.astype(bf16))).astype(f32)

        gains = jnp.concatenate([grad_norm1, grad_norm2, grad_qgain[0], grad_kgain[0]])
        gains = gains.reshape(-1, HEAD_WIDTH)
        for axis, size in (("head", n_head), ("seq", n_seq)):
            bit = 1
            while bit < size:
                gains = gains + lax.ppermute(gains, axis, [(i, i ^ bit) for i in range(size)])
                bit *= 2
        gains = gains.reshape(-1)
        width = tokens.shape[1]
        grad_norm1, grad_norm2 = gains[:width], gains[width : 2 * width]
        grad_qgain = gains[2 * width : 2 * width + HEAD_WIDTH]
        grad_kgain = gains[2 * width + HEAD_WIDTH :]
        return (
            mixed,
            grad_tokens,
            grad_norm1,
            grad_query.astype(f32),
            grad_key.astype(f32),
            grad_value.astype(f32),
            grad_qgain,
            grad_kgain,
            grad_output.astype(f32),
            grad_norm2,
            grad_gate_up[:, : w_gate.shape[1]].astype(f32),
            grad_gate_up[:, w_gate.shape[1] :].astype(f32),
            grad_down.astype(f32),
        )

    in_specs = (
        P("seq", None),
        P(),
        P(),
        P(None, "head"),
        P(None, "head"),
        P(None, "head"),
        P(),
        P(),
        P("head", None),
        P(),
        P(None, "head"),
        P(None, "head"),
        P("head", None),
        P("seq", None),
    )
    out_specs = (
        P("seq", None),
        P("seq", None),
        P(),
        P("seq", "head"),
        P("seq", "head"),
        P("seq", "head"),
        P(),
        P(),
        P("head", "seq"),
        P(),
        P("seq", "head"),
        P("seq", "head"),
        P("head", "seq"),
    )
    return jax.shard_map(body, mesh=mesh, in_specs=in_specs, out_specs=out_specs, check_vma=False)
```

```python
import functools
import math

import jax
import jax.numpy as jnp
from jax import lax
from jax.experimental import pallas as pl
from jax.experimental.pallas import tpu as pltpu
from jax.sharding import PartitionSpec as P

HEAD_WIDTH = 128
EPSILON = 1e-06
ROPE_BASE = 1000000.0
LOG2E = math.log2(math.e)
SCORE_SCALE = 1.0 / math.sqrt(HEAD_WIDTH)
SCORE_SCALE_2 = LOG2E / math.sqrt(HEAD_WIDTH)
KEY_CHUNK = 256
FAR = 512.0
LOG_LANE = 64
MIB = 2**20
SMALL = pl.CostEstimate(flops=1, bytes_accessed=1, transcendentals=0)

f32 = jnp.float32
bf16 = jnp.bfloat16
NT = (((1,), (1,)), ((), ()))
TN = (((0,), (0,)), ((), ()))


def dot(left, right):
    return jnp.dot(left, right, preferred_element_type=f32)


def dot_nt(left, right):
    return lax.dot_general(left, right, NT, preferred_element_type=f32)


def dot_tn(left, right):
    return lax.dot_general(left, right, TN, preferred_element_type=f32)


def locate(index, lengths):
    ends = jnp.cumsum(lengths)
    starts = ends - lengths
    segment = jnp.sum((index[:, None] >= ends[None, :]).astype(jnp.int32), axis=1)
    chosen = segment[:, None] == jnp.arange(lengths.shape[0], dtype=jnp.int32)[None, :]
    return jnp.sum(jnp.where(chosen, starts[None, :], 0), axis=1)


def rotary(position):
    half = HEAD_WIDTH // 2
    freq = jnp.exp(jnp.arange(half, dtype=f32) * (-2.0 * math.log(ROPE_BASE) / HEAD_WIDTH))
    angle = position.astype(f32)[:, None] * freq[None, :]
    cosine = jnp.cos(angle)
    sine = jnp.sin(angle)
    return (
        jnp.concatenate([cosine, cosine], axis=1),
        jnp.concatenate([-sine, sine], axis=1),
    )


def lane_index(rows):
    return lax.broadcasted_iota(jnp.int32, (rows, HEAD_WIDTH), 1)


def row_index(rows):
    return lax.broadcasted_iota(jnp.int32, (rows, HEAD_WIDTH), 0)


def in_segment(index, bounds_ref):
    return (index >= bounds_ref[0:1, :]) & (index < bounds_ref[1:2, :])


def split_parts(value):
    high = value.astype(bf16)
    rest = value - high.astype(f32)
    middle = rest.astype(bf16)
    return high, middle, (rest - middle.astype(f32)).astype(bf16)


def normed(raw, gain, cosine, sine):
    inverse = lax.rsqrt(jnp.mean(raw * raw, axis=-1, keepdims=True) + EPSILON)
    scaled = raw * inverse * gain
    return scaled * cosine + pltpu.roll(scaled, HEAD_WIDTH // 2, 1) * sine


def key_prep_kernel(raw_ref, value_ref, gain_ref, cos_ref, sin_ref, out_ref):
    key = normed(raw_ref[...], gain_ref[...], cos_ref[...], sin_ref[...])
    out_ref[:, :HEAD_WIDTH] = key.astype(bf16)
    out_ref[:, HEAD_WIDTH:] = value_ref[...].astype(bf16)


def key_prep(raw, value, gain, cosine, sine):
    rows, width = raw.shape
    block = pl.BlockSpec((rows, HEAD_WIDTH), lambda j: (0, j))
    table = pl.BlockSpec((rows, HEAD_WIDTH), lambda j: (0, 0))
    return pl.pallas_call(
        key_prep_kernel,
        grid=(width // HEAD_WIDTH,),
        in_specs=[block, block, pl.BlockSpec((1, HEAD_WIDTH), lambda j: (0, 0)), table, table],
        out_specs=pl.BlockSpec((rows, 2 * HEAD_WIDTH), lambda j: (0, j)),
        out_shape=jax.ShapeDtypeStruct((rows, 2 * width), bf16),
        name="key_prep",
    )(raw, value, gain[None, :], cosine, sine)


def query_prep_kernel(meta, raw_ref, gain_ref, cos_ref, sin_ref, bounds_ref, out_ref):
    rows = raw_ref.shape[0]
    query = normed(raw_ref[...], gain_ref[...], cos_ref[...], sin_ref[...])
    out_ref[:, :HEAD_WIDTH] = (query * SCORE_SCALE_2).astype(bf16)
    inside = in_segment(meta[0] + row_index(rows), bounds_ref)
    free = inside | (lane_index(rows) >= LOG_LANE)
    out_ref[:, HEAD_WIDTH:] = jnp.where(free, 0.0, -FAR).astype(bf16)


def query_prep(meta, raw, gain, cosine, sine, bounds):
    rows, width = raw.shape
    table = pl.BlockSpec((rows, HEAD_WIDTH), lambda j, m: (0, 0))
    return pl.pallas_call(
        query_prep_kernel,
        grid_spec=pltpu.PrefetchScalarGridSpec(
            num_scalar_prefetch=1,
            grid=(width // HEAD_WIDTH,),
            in_specs=[
                pl.BlockSpec((rows, HEAD_WIDTH), lambda j, m: (0, j)),
                pl.BlockSpec((1, HEAD_WIDTH), lambda j, m: (0, 0)),
                table,
                table,
                pl.BlockSpec((8, HEAD_WIDTH), lambda j, m: (0, 0)),
            ],
            out_specs=pl.BlockSpec((rows, 2 * HEAD_WIDTH), lambda j, m: (0, j)),
        ),
        out_shape=jax.ShapeDtypeStruct((rows, 2 * width), bf16),
        name="query_prep",
    )(meta, raw, gain[None, :], cosine, sine, bounds)


def head_back_kernel(raw_ref, grad_ref, gain_ref, cos_ref, sin_ref, out_ref, gain_grad_ref, *, scale):
    @pl.when(pl.program_id(0) == 0)
    def _():
        gain_grad_ref[...] = jnp.zeros_like(gain_grad_ref)

    raw = raw_ref[...]
    inverse = lax.rsqrt(jnp.mean(raw * raw, axis=-1, keepdims=True) + EPSILON)
    hat = raw * inverse
    grad = grad_ref[...] * scale
    back = grad * cos_ref[...] - pltpu.roll(grad, HEAD_WIDTH // 2, 1) * sin_ref[...]
    gain_grad_ref[...] += jnp.sum(back * hat, axis=0, keepdims=True)
    back = back * gain_ref[...]
    out_ref[...] = (inverse * (back - hat * jnp.mean(back * hat, axis=-1, keepdims=True))).astype(
        bf16
    )


def head_back(raw, grad, gain, cosine, sine, scale, stride):
    rows, width = raw.shape
    block = pl.BlockSpec((rows, HEAD_WIDTH), lambda j: (0, j))
    spaced = pl.BlockSpec((rows, HEAD_WIDTH), lambda j: (0, j * stride))
    table = pl.BlockSpec((rows, HEAD_WIDTH), lambda j: (0, 0))
    one = pl.BlockSpec((1, HEAD_WIDTH), lambda j: (0, 0))
    return pl.pallas_call(
        functools.partial(head_back_kernel, scale=scale),
        grid=(width // HEAD_WIDTH,),
        in_specs=[block, spaced, one, table, table],
        out_specs=[block, one],
        out_shape=[
            jax.ShapeDtypeStruct((rows, width), bf16),
            jax.ShapeDtypeStruct((1, HEAD_WIDTH), f32),
        ],
        name="head_back",
    )(raw, grad, gain[None, :], cosine, sine)


def key_lanes(meta, key_start, rows, bounds_ref):
    inside = in_segment(key_start + row_index(rows), bounds_ref)
    lanes = lane_index(rows)
    log_lanes = (lanes >= LOG_LANE) & (lanes < LOG_LANE + 3)
    return jnp.where(inside | log_lanes, 1.0, 0.0).astype(bf16)


def block_used(meta, key_start, key_rows, rows):
    return (
        (key_start >= 0) & (key_start <= meta[0] + rows - 1) & (key_start + key_rows - 1 >= meta[1])
    )


def lower_mask(transposed):
    shape = (KEY_CHUNK, KEY_CHUNK)
    first = lax.broadcasted_iota(jnp.int32, shape, 0)
    second = lax.broadcasted_iota(jnp.int32, shape, 1)
    return first <= second if transposed else second <= first


def chunk(i, n=1):
    return slice(i * KEY_CHUNK, (i + n) * KEY_CHUNK)


def attend_kernel(meta, q_ref, kva_ref, kvb_ref, bounds_ref, *refs, first, last):
    rows = q_ref.shape[0]
    key_rows = kva_ref.shape[0]
    if last:
        acc_in, sum_in, o_ref, q_out_ref, acc_ref, sum_ref = refs
    elif first:
        acc_ref, sum_ref = refs
    else:
        acc_in, sum_in, acc_ref, sum_ref = refs
    if first:
        acc_ref[...] = jnp.zeros_like(acc_ref)
        sum_ref[...] = jnp.zeros_like(sum_ref)
    else:
        acc_ref[...] = acc_in[...]
        sum_ref[...] = sum_in[...]
    ones = jnp.ones((KEY_CHUNK, HEAD_WIDTH), bf16)

    def work(kv_ref, lanes, keys, queries, mask):
        key = jnp.concatenate([kv_ref[keys, :HEAD_WIDTH], lanes[keys, :]], axis=1)
        weight = jnp.exp2(dot_nt(q_ref[queries, :], key))
        if mask:
            weight = jnp.where(lower_mask(False), weight, 0.0)
        value = jnp.concatenate([kv_ref[keys, HEAD_WIDTH:], ones], axis=1)
        out = dot(weight.astype(bf16), value)
        acc_ref[queries, :] += out[:, :HEAD_WIDTH]
        sum_ref[queries, :] += out[:, HEAD_WIDTH:]

    for place, kv_ref in enumerate((kva_ref, kvb_ref)):
        key_start = meta[2 + place]
        diagonal = first and place == 0

        @pl.when(block_used(meta, key_start, key_rows, rows))
        def _():
            lanes = key_lanes(meta, key_start, key_rows, bounds_ref)
            for c in range(key_rows // KEY_CHUNK):
                if diagonal:
                    work(kv_ref, lanes, chunk(c), chunk(c), True)
                    if c + 1 < rows // KEY_CHUNK:
                        work(kv_ref, lanes, chunk(c), slice((c + 1) * KEY_CHUNK, rows), False)
                else:
                    work(kv_ref, lanes, chunk(c), slice(0, rows), False)

    if last:
        total = sum_ref[...]
        outcome = acc_ref[...] / total
        acc_ref[...] = outcome
        o_ref[...] = outcome.astype(bf16)
        lanes = lane_index(rows)
        extra = q_ref[:, HEAD_WIDTH:].astype(f32)
        for i, part in enumerate(split_parts(jnp.log2(total))):
            extra = jnp.where(lanes == LOG_LANE + i, -part.astype(f32), extra)
        q_out_ref[:, :HEAD_WIDTH] = q_ref[:, :HEAD_WIDTH]
        q_out_ref[:, HEAD_WIDTH:] = extra.astype(bf16)


def attend_stage(q, kv_a, kv_b, bounds, meta, carried, last):
    rows = q.shape[0]
    key_rows = kv_a.shape[0]
    q_heads = q.shape[1] // (2 * HEAD_WIDTH)
    group = q.shape[1] // kv_a.shape[1]
    width = q_heads * HEAD_WIDTH
    first = not carried
    wide = 2 * HEAD_WIDTH
    per_q = pl.BlockSpec((rows, wide), lambda j, m: (0, j))
    per_kv = pl.BlockSpec((key_rows, wide), lambda j, m: (0, j // group))
    per_out = pl.BlockSpec((rows, HEAD_WIDTH), lambda j, m: (0, j))
    table = pl.BlockSpec((8, HEAD_WIDTH), lambda j, m: (0, 0))
    running = jax.ShapeDtypeStruct((rows, width), f32)
    if last:
        out_specs = [per_out, per_q, per_out]
        out_shape = [jax.ShapeDtypeStruct((rows, width), bf16), jax.ShapeDtypeStruct(q.shape, bf16), running]
        scratch = [pltpu.VMEM((rows, HEAD_WIDTH), f32)]
        aliases = {5: 2}
    else:
        out_specs = [per_out, per_out]
        out_shape = [running, running]
        scratch = []
        aliases = {} if first else {5: 0, 6: 1}
    return pl.pallas_call(
        functools.partial(attend_kernel, first=first, last=last),
        grid_spec=pltpu.PrefetchScalarGridSpec(
            num_scalar_prefetch=1,
            grid=(q_heads,),
            in_specs=[per_q, per_kv, per_kv, table] + [per_out] * len(carried),
            out_specs=out_specs,
            scratch_shapes=scratch,
        ),
        out_shape=out_shape,
        input_output_aliases=aliases,
        compiler_params=pltpu.CompilerParams(vmem_limit_bytes=40 * MIB),
        cost_estimate=SMALL,
        name="attend_stage",
    )(meta, q, kv_a, kv_b, bounds, *carried)


def delta_kernel(owners, *refs):
    *pieces, outcome_ref, out_ref = refs
    for i, piece in enumerate(pieces):

        @pl.when(pl.program_id(0) == i)
        def _():
            rows, width = piece.shape
            lanes = lane_index(rows)
            for j in range(width // HEAD_WIDTH):
                head = slice(j * HEAD_WIDTH, (j + 1) * HEAD_WIDTH)
                do = piece[:, head]
                delta = jnp.sum(do.astype(f32) * outcome_ref[:, head], axis=-1, keepdims=True)
                extra = jnp.zeros((rows, HEAD_WIDTH), f32)
                for k, part in enumerate(split_parts(delta)):
                    extra = jnp.where(lanes == k, -part.astype(f32), extra)
                start = 2 * j * HEAD_WIDTH
                out_ref[:, start : start + HEAD_WIDTH] = do
                out_ref[:, start + HEAD_WIDTH : start + 2 * HEAD_WIDTH] = extra.astype(bf16)


def with_delta(pieces, outcome):
    owners = jnp.stack([jnp.asarray(owner, jnp.int32) for unused, owner in pieces])
    rows, width = outcome.shape
    share = rows // len(pieces)
    whole = pl.BlockSpec((share, width), lambda i, m: (0, 0))
    return pl.pallas_call(
        delta_kernel,
        grid_spec=pltpu.PrefetchScalarGridSpec(
            num_scalar_prefetch=1,
            grid=(len(pieces),),
            in_specs=[whole] * len(pieces) + [pl.BlockSpec((share, width), lambda i, m: (m[i], 0))],
            out_specs=pl.BlockSpec((share, 2 * width), lambda i, m: (m[i], 0)),
        ),
        out_shape=jax.ShapeDtypeStruct((rows, 2 * width), bf16),
        cost_estimate=SMALL,
        name="with_delta",
    )(owners, *[piece for piece, unused in pieces], outcome)


def assemble_kernel(owners, *refs):
    *pieces, out_ref = refs
    for i, piece in enumerate(pieces):

        @pl.when(pl.program_id(0) == i)
        def _():
            out_ref[...] = piece[...].astype(out_ref.dtype)


def assemble(pieces, kind):
    owners = jnp.stack([jnp.asarray(owner, jnp.int32) for unused, owner in pieces])
    share, width = pieces[0][0].shape
    return pl.pallas_call(
        assemble_kernel,
        grid_spec=pltpu.PrefetchScalarGridSpec(
            num_scalar_prefetch=1,
            grid=(len(pieces),),
            in_specs=[pl.BlockSpec((share, width), lambda i, m: (0, 0))] * len(pieces),
            out_specs=pl.BlockSpec((share, width), lambda i, m: (m[i], 0)),
        ),
        out_shape=jax.ShapeDtypeStruct((share * len(pieces), width), kind),
        compiler_params=pltpu.CompilerParams(vmem_limit_bytes=40 * MIB),
        cost_estimate=SMALL,
        name="assemble",
    )(owners, *[piece for piece, unused in pieces])


def attend_back_kernel(
    meta,
    q_ref,
    do_ref,
    kv_ref,
    bounds_ref,
    dq_in,
    dq_ref,
    dkv_ref,
    dq_turned,
    dkv_sum,
    *,
    first,
    group,
    diagonal,
    place,
):
    rows = q_ref.shape[0]
    key_rows = kv_ref.shape[0]
    key_start = meta[2 + place]
    step = lax.rem(pl.program_id(0), group)

    @pl.when(step == 0)
    def _():
        dkv_sum[...] = jnp.zeros_like(dkv_sum)

    def work(lanes, ones, keys, queries, mask):
        key = kv_ref[keys, :HEAD_WIDTH]
        q = q_ref[queries, :]
        do = do_ref[queries, :]
        weight = jnp.exp2(dot_nt(jnp.concatenate([key, lanes[keys, :]], axis=1), q))
        if mask:
            weight = jnp.where(lower_mask(True), weight, 0.0)
        value = jnp.concatenate([kv_ref[keys, HEAD_WIDTH:], ones], axis=1)
        d_score = (weight * dot_nt(value, do)).astype(bf16)
        dkv_sum[keys, HEAD_WIDTH:] += dot(weight.astype(bf16), do[:, :HEAD_WIDTH])
        dkv_sum[keys, :HEAD_WIDTH] += dot(d_score, q[:, :HEAD_WIDTH])
        dq_turned[:, queries] += dot_tn(key, d_score)

    used = block_used(meta, key_start, key_rows, rows)

    @pl.when(used)
    def _():
        dq_turned[...] = jnp.zeros_like(dq_turned)
        lanes = key_lanes(meta, key_start, key_rows, bounds_ref)
        ones = jnp.where(lane_index(KEY_CHUNK) < 3, 1.0, 0.0).astype(bf16)
        for c in range(key_rows // KEY_CHUNK):
            if diagonal:
                work(lanes, ones, chunk(c), chunk(c), True)
                if c + 1 < rows // KEY_CHUNK:
                    work(lanes, ones, chunk(c), slice((c + 1) * KEY_CHUNK, rows), False)
            else:
                work(lanes, ones, chunk(c), slice(0, rows), False)
        turned = dq_turned[...].T
        dq_ref[...] = turned if first else dq_in[...] + turned

    @pl.when(jnp.logical_not(used))
    def _():
        dq_ref[...] = jnp.zeros_like(dq_ref) if first else dq_in[...]

    @pl.when(step == group - 1)
    def _():
        dkv_ref[...] = dkv_sum[...].astype(dkv_ref.dtype)


def attend_back(q, do, kv, bounds, meta, dq, place, diagonal, kind):
    rows = q.shape[0]
    key_rows = kv.shape[0]
    q_heads = q.shape[1] // (2 * HEAD_WIDTH)
    group = q.shape[1] // kv.shape[1]
    width = q_heads * HEAD_WIDTH
    first = dq is None
    if first:
        dq = jnp.zeros((8, HEAD_WIDTH), f32)
    wide = 2 * HEAD_WIDTH
    per_q = pl.BlockSpec((rows, wide), lambda j, m: (0, j))
    per_kv = pl.BlockSpec((key_rows, wide), lambda j, m: (0, j // group))
    per_out = pl.BlockSpec((rows, HEAD_WIDTH), lambda j, m: (0, j))
    carried = pl.BlockSpec((8, HEAD_WIDTH), lambda j, m: (0, 0)) if first else per_out
    return pl.pallas_call(
        functools.partial(
            attend_back_kernel, first=first, group=group, diagonal=diagonal, place=place
        ),
        grid_spec=pltpu.PrefetchScalarGridSpec(
            num_scalar_prefetch=1,
            grid=(q_heads,),
            in_specs=[
                per_q,
                per_q,
                per_kv,
                pl.BlockSpec((8, HEAD_WIDTH), lambda j, m: (0, 0)),
                carried,
            ],
            out_specs=[per_out, per_kv],
            scratch_shapes=[
                pltpu.VMEM((HEAD_WIDTH, rows), f32),
                pltpu.VMEM((key_rows, wide), f32),
            ],
        ),
        out_shape=[
            jax.ShapeDtypeStruct((rows, width), f32),
            jax.ShapeDtypeStruct(kv.shape, kind),
        ],
        input_output_aliases={} if first else {5: 0},
        compiler_params=pltpu.CompilerParams(vmem_limit_bytes=40 * MIB),
        cost_estimate=SMALL,
        name="attend_back",
    )(meta, q, do, kv, bounds, dq)


def project_kernel(meta, base_ref, *refs, count, final):
    pieces, mine, other = refs[:count], refs[count : 2 * count], refs[2 * count : 3 * count]
    if final:
        gain_ref, out_ref, normed_ref = refs[3 * count :]
    else:
        (out_ref,) = refs[3 * count :]
    first_core = meta[0] == 0
    total = base_ref[...].astype(f32)
    for piece, mine_ref, other_ref in zip(pieces, mine, other):
        half = piece.shape[1] // 2
        low, high = piece[:, :half], piece[:, half:]
        total += dot(jnp.where(first_core, low, high), mine_ref[0])
        total += dot(jnp.where(first_core, high, low), other_ref[0])
    out_ref[...] = total
    if final:
        inverse = lax.rsqrt(jnp.mean(total * total, axis=-1, keepdims=True) + EPSILON)
        normed_ref[...] = (total * inverse * gain_ref[...]).astype(bf16)


def project(base, pieces, w_mine, w_other, core, gain=None):
    meta = jnp.stack([jnp.asarray(v, jnp.int32) for v in [core] + [owner for unused, owner in pieces]])
    rows, width = base.shape
    count = len(pieces)
    final = gain is not None
    step = rows // 3 if rows % 768 == 0 else rows
    half = w_mine.shape[1]
    per_row = pl.BlockSpec((step, width), lambda i, m: (i, 0))
    per_piece = pl.BlockSpec((step, 2 * half), lambda i, m: (i, 0))
    weights = [
        pl.BlockSpec((1, half, width), lambda i, m, k=k: (m[1 + k], 0, 0)) for k in range(count)
    ]
    in_specs = [per_row] + [per_piece] * count + weights + weights
    args = [base] + [piece for piece, unused in pieces] + [w_mine] * count + [w_other] * count
    out_shape = [jax.ShapeDtypeStruct((rows, width), f32)]
    if final:
        in_specs.append(pl.BlockSpec((1, width), lambda i, m: (0, 0)))
        args.append(gain[None, :])
        out_shape.append(jax.ShapeDtypeStruct((rows, width), bf16))
    return pl.pallas_call(
        functools.partial(project_kernel, count=count, final=final),
        grid_spec=pltpu.PrefetchScalarGridSpec(
            num_scalar_prefetch=1,
            grid=(rows // step,),
            in_specs=in_specs,
            out_specs=[per_row] * len(out_shape),
        ),
        out_shape=out_shape,
        compiler_params=pltpu.CompilerParams(vmem_limit_bytes=48 * MIB),
        cost_estimate=SMALL,
        name="project",
    )(meta, *args)


def project_back_kernel(meta, branch_ref, mine_ref, other_ref, out_ref):
    half = mine_ref.shape[1]
    mine = dot_nt(branch_ref[...], mine_ref[0])
    other = dot_nt(branch_ref[...], other_ref[0])
    first_core = meta[0] == 0
    out_ref[0, :, :half] = jnp.where(first_core, mine, other).astype(bf16)
    out_ref[0, :, half:] = jnp.where(first_core, other, mine).astype(bf16)


def project_back(branch, w_mine, w_other, core):
    meta = jnp.asarray(core, jnp.int32)[None]
    rows, width = branch.shape
    n_head, half, unused = w_mine.shape
    weight = pl.BlockSpec((1, half, width), lambda i, m: (i, 0, 0))
    return pl.pallas_call(
        project_back_kernel,
        grid_spec=pltpu.PrefetchScalarGridSpec(
            num_scalar_prefetch=1,
            grid=(n_head,),
            in_specs=[pl.BlockSpec((rows, width), lambda i, m: (0, 0)), weight, weight],
            out_specs=pl.BlockSpec((1, rows, 2 * half), lambda i, m: (i, 0, 0)),
        ),
        out_shape=jax.ShapeDtypeStruct((n_head, rows, 2 * half), bf16),
        compiler_params=pltpu.CompilerParams(vmem_limit_bytes=40 * MIB),
        cost_estimate=SMALL,
        name="project_back",
    )(meta, branch, w_mine, w_other)


def after(values):
    return lax.optimization_barrier(values)


def pick(array, index):
    return lax.dynamic_index_in_dim(array, index, 0, keepdims=False)


def solution(mesh):
    n_seq = mesh.shape["seq"]
    n_head = mesh.shape["head"]
    n_chip = n_seq // 2

    def swap_core(value):
        return lax.ppermute(value, "seq", [(i, i ^ 1) for i in range(n_seq)])

    def to_next(value):
        return lax.ppermute(value, "seq", [(i, i + 2) for i in range(n_seq - 2)])

    def to_previous(value):
        return lax.ppermute(value, "seq", [(i + 2, i) for i in range(n_seq - 2)])

    def across(value, bits):
        return lax.ppermute(value, "head", [(i, i ^ bits) for i in range(n_head)])

    def gather_steps(value):
        me = lax.axis_index("head")
        if n_head != 4:
            every = yield lax.all_gather(value, "head", axis=0)
            return [(every[i], i) for i in range(n_head)]
        half = value.shape[0] // 2
        by_x, by_y = yield across(value, 1), across(value, 2)
        low, high = yield across(by_x[:half], 2), across(by_y[half:], 1)
        far = jnp.concatenate([low, high], axis=0)
        return [(value, me), (by_x, me ^ 1), (by_y, me ^ 2), (far, me ^ 3)]

    def scatter_steps(value):
        rows, width = value.shape
        if n_head != 4:
            total = yield lax.psum_scatter(value, "head", scatter_dimension=0, tiled=True)
            return total.astype(f32)
        me = lax.axis_index("head")
        x, y = me & 1, me >> 1
        part = value.reshape(2, 2, 2, rows // 8, width)
        first, second = part[:, :, 0], part[:, :, 1]
        first_x = jnp.swapaxes(first, 0, 1)
        got_first, got_second = yield (
            across(pick(first_x, 1 - x), 1),
            across(pick(second, 1 - y), 2),
        )
        sum_first = pick(first_x, x).astype(f32) + got_first.astype(f32)
        sum_second = pick(second, y).astype(f32) + got_second.astype(f32)
        last_first, last_second = yield (
            across(pick(sum_first, 1 - y).astype(bf16), 2),
            across(pick(sum_second, 1 - x).astype(bf16), 1),
        )
        return jnp.concatenate(
            [
                pick(sum_first, y) + last_first.astype(f32),
                pick(sum_second, x) + last_second.astype(f32),
            ],
            axis=0,
        )

    def run_steps(steps, works=()):
        works = list(works)
        made = []
        arrived = next(steps)
        while True:
            if works:
                arrived, done = after((arrived, works.pop(0)()))
                made.append(done)
            try:
                arrived = steps.send(arrived)
            except StopIteration as stop:
                return stop.value, made + [work() for work in works]

    def exchange_head(value):
        me = lax.axis_index("head")
        if n_head != 4:
            got = lax.all_to_all(value, "head", 0, 0)
            return [(got[i], i) for i in range(n_head)]
        pieces = [(pick(value, me), me)]
        for bits in (3, 1, 2):
            pieces.append((across(pick(value, me ^ bits), bits), me ^ bits))
        return pieces

    def body(
        tokens,
        lengths,
        norm1_gain,
        w_query,
        key_matrix,
        value_matrix,
        query_gain,
        key_gain,
        w_output,
        norm2_gain,
        w_gate,
        w_up,
        w_down,
        cotangent,
    ):
        rows = tokens.shape[0]
        share = rows // n_head
        seq_index = lax.axis_index("seq")
        head_index = lax.axis_index("head")
        chip, core = seq_index // 2, seq_index % 2

        index = seq_index * rows + jnp.arange(rows, dtype=jnp.int32)
        begin = locate(index, lengths)
        cosine, sine = rotary(index - begin)
        ends = jnp.cumsum(lengths)
        n_lengths = lengths.shape[0]
        bounds = jnp.zeros((8, HEAD_WIDTH), jnp.int32).at[0].set(2**30)
        bounds = bounds.at[0, :n_lengths].set(ends - lengths).at[1, :n_lengths].set(ends)

        def stage_meta(stage):
            source = 2 * (chip - stage)
            return jnp.stack(
                [seq_index * rows, begin[0], (source + core) * rows, (source + 1 - core) * rows]
            ).astype(jnp.int32)

        metas = [stage_meta(stage) for stage in range(n_chip)]

        xf = tokens.astype(f32)
        inverse1 = lax.rsqrt(jnp.mean(xf * xf, axis=-1, keepdims=True) + EPSILON)
        first_in = (xf * inverse1 * norm1_gain).astype(bf16)
        key_raw = dot(first_in, key_matrix)
        value_raw = dot(first_in, value_matrix)
        current = key_prep(key_raw, value_raw, key_gain, cosine, sine)
        sibling = swap_core(current)
        following = to_next(current)

        half_rows = w_output.shape[0] // 2
        w_half = lax.dynamic_slice_in_dim(w_output, core * half_rows, half_rows, 0)
        w_half, current = after((w_half, current))
        w_mine = lax.all_gather(w_half, "head", axis=0)

        query_raw = dot(first_in, w_query)
        q_wide = query_prep(metas[0], query_raw, query_gain, cosine, sine, bounds)
        d_mixed = dot_nt(cotangent, w_down)
        following, q_wide, d_mixed = after((following, q_wide, d_mixed))

        blocks = []
        carried = ()
        for stage in range(n_chip):
            blocks.append((current, sibling))
            if stage + 1 < n_chip:
                current = following
                sibling = swap_core(current)
                following = to_next(current) if stage + 2 < n_chip else None
            if stage == n_chip - 1:
                w_mine, carried = after((w_mine, carried))
                w_other = swap_core(w_mine)
            carried = attend_stage(
                q_wide, *blocks[stage], bounds, metas[stage], carried, stage == n_chip - 1
            )
            if following is not None:
                following, carried = after((following, carried))
        o_low, q_back, outcome = carried

        steps = gather_steps(o_low)
        arrived = next(steps)
        if n_head == 4:
            me = lax.axis_index("head")
            (hidden,) = project(tokens, [(o_low, me)], w_mine, w_other, core)
            arrived, hidden = after((arrived, hidden))
            far = steps.send(arrived)
            (hidden,) = project(
                hidden, [(arrived[0], me ^ 1), (arrived[1], me ^ 2)], w_mine, w_other, core
            )
            far, hidden = after((far, hidden))
            try:
                steps.send(far)
            except StopIteration as stop:
                last_pieces = stop.value[3:]
        else:
            hidden = tokens
            try:
                steps.send(arrived)
            except StopIteration as stop:
                last_pieces = stop.value
        hidden, second_in = project(hidden, last_pieces, w_mine, w_other, core, norm2_gain)
        gate_raw = dot(second_in, w_gate)
        up_raw = dot(second_in, w_up)
        sigmoid = jax.nn.sigmoid(gate_raw)
        silu = gate_raw * sigmoid
        mixed_low = (silu * up_raw).astype(bf16)
        gate_low = (d_mixed * up_raw * (sigmoid * (1.0 + gate_raw * (1.0 - sigmoid)))).astype(bf16)
        up_low = (d_mixed * silu).astype(bf16)

        def scatter_seq(value, dimension):
            return lax.psum_scatter(value, "seq", scatter_dimension=dimension, tiled=True)

        down_sum = dot_tn(mixed_low, cotangent).astype(bf16)
        down_sum, gate_low, up_low = after((down_sum, gate_low, up_low))
        grad_down = scatter_seq(down_sum, 1)
        second_part = (dot_nt(gate_low, w_gate) + dot_nt(up_low, w_up)).astype(bf16)

        second_grad, (gate_sum, up_sum) = run_steps(
            scatter_steps(second_part),
            (
                lambda: dot_tn(second_in, gate_low).astype(bf16),
                lambda: dot_tn(second_in, up_low).astype(bf16),
            ),
        )
        gate_up_sum = jnp.concatenate([gate_sum, up_sum], axis=1)
        my_hidden = lax.dynamic_slice_in_dim(hidden, head_index * share, share, 0)
        my_inverse = lax.rsqrt(jnp.mean(my_hidden * my_hidden, axis=-1, keepdims=True) + EPSILON)
        my_hat = my_hidden * my_inverse
        grad_norm2 = jnp.sum(second_grad * my_hat, axis=0)
        scaled = second_grad * norm2_gain
        my_dy = lax.dynamic_slice_in_dim(cotangent, head_index * share, share, 0).astype(f32)
        hidden_grad = my_dy + my_inverse * (
            scaled - my_hat * jnp.mean(scaled * my_hat, axis=-1, keepdims=True)
        )
        my_branch = hidden_grad.astype(bf16)
        do_pieces = exchange_head(project_back(my_branch, w_mine, w_other, core))
        do_wide = with_delta(do_pieces, outcome)
        grad_down, gate_up_sum, do_wide = after((grad_down, gate_up_sum, do_wide))
        grad_gate_up = scatter_seq(gate_up_sum, 0)

        def side_work(mixed_low, my_branch):
            branch_steps = gather_steps(my_branch)
            got = yield next(branch_steps)
            mixed_steps = scatter_steps(dot(mixed_low, w_down).astype(bf16))
            got_branch, got = yield branch_steps.send(got) if n_head == 4 else got, next(mixed_steps)
            try:
                branch_steps.send(got_branch)
            except StopIteration as stop:
                branch = assemble(stop.value, bf16)
            output_sum = dot_tn(o_low, branch).astype(bf16)
            if n_head == 4:
                got = yield mixed_steps.send(got)
            try:
                mixed_steps.send(got)
            except StopIteration as stop:
                my_mixed = (my_hidden + stop.value).astype(bf16)
            mixed_steps = gather_steps(my_mixed)
            got = yield next(mixed_steps)
            if n_head == 4:
                got = yield mixed_steps.send(got)
            try:
                mixed_steps.send(got)
            except StopIteration as stop:
                mixed = assemble(stop.value, bf16)
            return mixed, output_sum

        mixed_late, my_branch, do_wide = after((mixed_low, my_branch, do_wide))
        side = side_work(mixed_late, my_branch)
        waiting = next(side)
        side_made = None

        dq = None
        arrived = None
        kernels = 0
        for stage in reversed(range(n_chip)):
            kv_a, kv_b = blocks[stage]
            meta = metas[stage]
            dq, dkv_b = attend_back(q_back, do_wide, kv_b, bounds, meta, dq, 1, False, bf16)
            theirs = swap_core(dkv_b)
            if stage != n_chip - 1 and side_made is None:
                try:
                    waiting, dq = after((waiting, dq))
                    waiting = side.send(waiting)
                except StopIteration as stop:
                    side_made = stop.value
            dq, dkv_a = attend_back(q_back, do_wide, kv_a, bounds, meta, dq, 0, stage == 0, f32)
            dkv = dkv_a + theirs.astype(f32)
            if arrived is not None:
                dkv = dkv + arrived.astype(f32)
            if stage > 0:
                sent, dq = after((dkv.astype(bf16), dq))
                arrived = to_previous(sent)
            if side_made is None:
                try:
                    waiting, dq = after((waiting, dq))
                    waiting = side.send(waiting)
                except StopIteration as stop:
                    side_made = stop.value
        mixed, output_sum = side_made
        grad_gate_up, output_sum, dkv = after((grad_gate_up, output_sum, dkv))
        grad_output = scatter_seq(output_sum, 1)
        query_grad, grad_qgain = head_back(
            query_raw, dq, query_gain, cosine, sine, SCORE_SCALE, 1
        )
        key_grad, grad_kgain = head_back(
            key_raw, dkv, key_gain, cosine, sine, 1.0 / LOG2E, 2
        )
        value_grad = jnp.concatenate(
            [
                dkv[:, (2 * j + 1) * HEAD_WIDTH : (2 * j + 2) * HEAD_WIDTH]
                for j in range(dkv.shape[1] // (2 * HEAD_WIDTH))
            ],
            axis=1,
        ).astype(bf16)

        first_part = (
            dot_nt(query_grad, w_query)
            + dot_nt(key_grad, key_matrix)
            + dot_nt(value_grad, value_matrix)
        ).astype(bf16)
        hat1 = xf * inverse1
        grad_norm1 = jnp.sum(first_part.astype(f32) * hat1, axis=0)
        gains = jnp.concatenate([grad_norm1, grad_norm2, grad_qgain[0], grad_kgain[0]])
        gains = gains.reshape(-1, HEAD_WIDTH)
        first_grad, (attn_sum,) = run_steps(
            scatter_steps(first_part),
            (
                lambda: jnp.concatenate(
                    [
                        dot_tn(first_in, query_grad).astype(bf16),
                        dot_tn(first_in, key_grad).astype(bf16),
                        dot_tn(first_in, value_grad).astype(bf16),
                    ],
                    axis=1,
                ),
            ),
        )
        grad_attn = scatter_seq(attn_sum, 0)
        widths = (query_grad.shape[1], query_grad.shape[1] + key_grad.shape[1])
        grad_query, grad_key, grad_value = jnp.split(grad_attn, widths, axis=1)

        my_x = lax.dynamic_slice_in_dim(tokens, head_index * share, share, 0).astype(f32)
        my_inverse1 = lax.rsqrt(jnp.mean(my_x * my_x, axis=-1, keepdims=True) + EPSILON)
        my_hat1 = my_x * my_inverse1
        scaled1 = first_grad * norm1_gain
        my_tokens_grad = hidden_grad + my_inverse1 * (
            scaled1 - my_hat1 * jnp.mean(scaled1 * my_hat1, axis=-1, keepdims=True)
        )
        tokens_pieces, unused = run_steps(gather_steps(my_tokens_grad.astype(bf16)))
        grad_tokens = assemble(tokens_pieces, f32)

        for axis, size in (("head", n_head), ("seq", n_seq)):
            bit = 1
            while bit < size:
                gains = gains + lax.ppermute(gains, axis, [(i, i ^ bit) for i in range(size)])
                bit *= 2
        gains = gains.reshape(-1)
        width = tokens.shape[1]
        grad_norm1, grad_norm2 = gains[:width], gains[width : 2 * width]
        grad_qgain = gains[2 * width : 2 * width + HEAD_WIDTH]
        grad_kgain = gains[2 * width + HEAD_WIDTH :]
        return (
            mixed,
            grad_tokens,
            grad_norm1,
            grad_query.astype(f32),
            grad_key.astype(f32),
            grad_value.astype(f32),
            grad_qgain,
            grad_kgain,
            grad_output.astype(f32),
            grad_norm2,
            grad_gate_up[:, : w_gate.shape[1]].astype(f32),
            grad_gate_up[:, w_gate.shape[1] :].astype(f32),
            grad_down.astype(f32),
        )

    in_specs = (
        P("seq", None),
        P(),
        P(),
        P(None, "head"),
        P(None, "head"),
        P(None, "head"),
        P(),
        P(),
        P("head", None),
        P(),
        P(None, "head"),
        P(None, "head"),
        P("head", None),
        P("seq", None),
    )
    out_specs = (
        P("seq", None),
        P("seq", None),
        P(),
        P("seq", "head"),
        P("seq", "head"),
        P("seq", "head"),
        P(),
        P(),
        P("head", "seq"),
        P(),
        P("seq", "head"),
        P("seq", "head"),
        P("head", "seq"),
    )
    return jax.shard_map(body, mesh=mesh, in_specs=in_specs, out_specs=out_specs, check_vma=False)
```

```python
import functools
import math

import jax
import jax.numpy as jnp
from jax import lax
from jax.experimental import pallas as pl
from jax.experimental.pallas import tpu as pltpu
from jax.sharding import PartitionSpec as P

HEAD_WIDTH = 128
EPSILON = 1e-06
ROPE_BASE = 1000000.0
LOG2E = math.log2(math.e)
SCORE_SCALE = 1.0 / math.sqrt(HEAD_WIDTH)
SCORE_SCALE_2 = LOG2E / math.sqrt(HEAD_WIDTH)
KEY_CHUNK = 256
HIDDEN_STEP = 256
FAR = 512.0
LOG_LANE = 64
MIB = 2**20
SMALL = pl.CostEstimate(flops=1, bytes_accessed=1, transcendentals=0)

f32 = jnp.float32
bf16 = jnp.bfloat16
NT = (((1,), (1,)), ((), ()))
TN = (((0,), (0,)), ((), ()))


def dot(left, right):
    return jnp.dot(left, right, preferred_element_type=f32)


def dot_nt(left, right):
    return lax.dot_general(left, right, NT, preferred_element_type=f32)


def dot_tn(left, right):
    return lax.dot_general(left, right, TN, preferred_element_type=f32)


def locate(index, lengths):
    ends = jnp.cumsum(lengths)
    starts = ends - lengths
    segment = jnp.sum((index[:, None] >= ends[None, :]).astype(jnp.int32), axis=1)
    chosen = segment[:, None] == jnp.arange(lengths.shape[0], dtype=jnp.int32)[None, :]
    return jnp.sum(jnp.where(chosen, starts[None, :], 0), axis=1)


def rotary(position):
    half = HEAD_WIDTH // 2
    freq = jnp.exp(jnp.arange(half, dtype=f32) * (-2.0 * math.log(ROPE_BASE) / HEAD_WIDTH))
    angle = position.astype(f32)[:, None] * freq[None, :]
    cosine = jnp.cos(angle)
    sine = jnp.sin(angle)
    return (
        jnp.concatenate([cosine, cosine], axis=1),
        jnp.concatenate([-sine, sine], axis=1),
    )


def lane_index(rows):
    return lax.broadcasted_iota(jnp.int32, (rows, HEAD_WIDTH), 1)


def row_index(rows):
    return lax.broadcasted_iota(jnp.int32, (rows, HEAD_WIDTH), 0)


def in_segment(index, bounds_ref):
    return (index >= bounds_ref[0:1, :]) & (index < bounds_ref[1:2, :])


def split_parts(value):
    high = value.astype(bf16)
    rest = value - high.astype(f32)
    middle = rest.astype(bf16)
    return high, middle, (rest - middle.astype(f32)).astype(bf16)


def normed(raw, gain, cosine, sine):
    inverse = lax.rsqrt(jnp.mean(raw * raw, axis=-1, keepdims=True) + EPSILON)
    scaled = raw * inverse * gain
    return scaled * cosine + pltpu.roll(scaled, HEAD_WIDTH // 2, 1) * sine


def enter_kernel(
    x_ref, gain_ref, key_w_ref, value_w_ref, key_gain_ref, cos_ref, sin_ref, in_ref, raw_ref, kv_ref
):
    x = x_ref[...].astype(f32)
    inverse = lax.rsqrt(jnp.mean(x * x, axis=-1, keepdims=True) + EPSILON)
    first_in = (x * inverse * gain_ref[...]).astype(bf16)
    in_ref[...] = first_in
    raw = dot(first_in, key_w_ref[...])
    raw_ref[...] = raw
    value = dot(first_in, value_w_ref[...]).astype(bf16)
    for j in range(raw.shape[1] // HEAD_WIDTH):
        head = slice(j * HEAD_WIDTH, (j + 1) * HEAD_WIDTH)
        key = normed(raw[:, head], key_gain_ref[...], cos_ref[...], sin_ref[...])
        start = 2 * j * HEAD_WIDTH
        kv_ref[:, start : start + HEAD_WIDTH] = key.astype(bf16)
        kv_ref[:, start + HEAD_WIDTH : start + 2 * HEAD_WIDTH] = value[:, head]


def enter(tokens, gain, key_w, value_w, key_gain, cosine, sine):
    rows, width = tokens.shape
    kv_width = key_w.shape[1]
    step = rows // 3 if rows % 768 == 0 else rows
    table = pl.BlockSpec((step, HEAD_WIDTH), lambda i: (i, 0))
    weight = pl.BlockSpec((width, kv_width), lambda i: (0, 0))
    return pl.pallas_call(
        enter_kernel,
        grid=(rows // step,),
        in_specs=[
            pl.BlockSpec((step, width), lambda i: (i, 0)),
            pl.BlockSpec((1, width), lambda i: (0, 0)),
            weight,
            weight,
            pl.BlockSpec((1, HEAD_WIDTH), lambda i: (0, 0)),
            table,
            table,
        ],
        out_specs=[
            pl.BlockSpec((step, width), lambda i: (i, 0)),
            pl.BlockSpec((step, kv_width), lambda i: (i, 0)),
            pl.BlockSpec((step, 2 * kv_width), lambda i: (i, 0)),
        ],
        out_shape=[
            jax.ShapeDtypeStruct((rows, width), bf16),
            jax.ShapeDtypeStruct((rows, kv_width), f32),
            jax.ShapeDtypeStruct((rows, 2 * kv_width), bf16),
        ],
        compiler_params=pltpu.CompilerParams(vmem_limit_bytes=32 * MIB),
        cost_estimate=SMALL,
        name="enter",
    )(tokens, gain[None, :], key_w, value_w, key_gain[None, :], cosine, sine)


def query_prep_kernel(meta, raw_ref, gain_ref, cos_ref, sin_ref, bounds_ref, out_ref):
    rows = raw_ref.shape[0]
    query = normed(raw_ref[...], gain_ref[...], cos_ref[...], sin_ref[...])
    out_ref[:, :HEAD_WIDTH] = (query * SCORE_SCALE_2).astype(bf16)
    inside = in_segment(meta[0] + row_index(rows), bounds_ref)
    free = inside | (lane_index(rows) >= LOG_LANE)
    out_ref[:, HEAD_WIDTH:] = jnp.where(free, 0.0, -FAR).astype(bf16)


def query_prep(meta, raw, gain, cosine, sine, bounds):
    rows, width = raw.shape
    table = pl.BlockSpec((rows, HEAD_WIDTH), lambda j, m: (0, 0))
    return pl.pallas_call(
        query_prep_kernel,
        grid_spec=pltpu.PrefetchScalarGridSpec(
            num_scalar_prefetch=1,
            grid=(width // HEAD_WIDTH,),
            in_specs=[
                pl.BlockSpec((rows, HEAD_WIDTH), lambda j, m: (0, j)),
                pl.BlockSpec((1, HEAD_WIDTH), lambda j, m: (0, 0)),
                table,
                table,
                pl.BlockSpec((8, HEAD_WIDTH), lambda j, m: (0, 0)),
            ],
            out_specs=pl.BlockSpec((rows, 2 * HEAD_WIDTH), lambda j, m: (0, j)),
        ),
        out_shape=jax.ShapeDtypeStruct((rows, 2 * width), bf16),
        name="query_prep",
    )(meta, raw, gain[None, :], cosine, sine, bounds)


def head_back_kernel(raw_ref, grad_ref, gain_ref, cos_ref, sin_ref, out_ref, gain_grad_ref, *, scale):
    @pl.when(pl.program_id(0) == 0)
    def _():
        gain_grad_ref[...] = jnp.zeros_like(gain_grad_ref)

    raw = raw_ref[...]
    inverse = lax.rsqrt(jnp.mean(raw * raw, axis=-1, keepdims=True) + EPSILON)
    hat = raw * inverse
    grad = grad_ref[...] * scale
    back = grad * cos_ref[...] - pltpu.roll(grad, HEAD_WIDTH // 2, 1) * sin_ref[...]
    gain_grad_ref[...] += jnp.sum(back * hat, axis=0, keepdims=True)
    back = back * gain_ref[...]
    out_ref[...] = (inverse * (back - hat * jnp.mean(back * hat, axis=-1, keepdims=True))).astype(
        bf16
    )


def head_back(raw, grad, gain, cosine, sine, scale, stride):
    rows, width = raw.shape
    block = pl.BlockSpec((rows, HEAD_WIDTH), lambda j: (0, j))
    spaced = pl.BlockSpec((rows, HEAD_WIDTH), lambda j: (0, j * stride))
    table = pl.BlockSpec((rows, HEAD_WIDTH), lambda j: (0, 0))
    one = pl.BlockSpec((1, HEAD_WIDTH), lambda j: (0, 0))
    return pl.pallas_call(
        functools.partial(head_back_kernel, scale=scale),
        grid=(width // HEAD_WIDTH,),
        in_specs=[block, spaced, one, table, table],
        out_specs=[block, one],
        out_shape=[
            jax.ShapeDtypeStruct((rows, width), bf16),
            jax.ShapeDtypeStruct((1, HEAD_WIDTH), f32),
        ],
        name="head_back",
    )(raw, grad, gain[None, :], cosine, sine)


def key_lanes(meta, key_start, rows, bounds_ref):
    inside = in_segment(key_start + row_index(rows), bounds_ref)
    lanes = lane_index(rows)
    log_lanes = (lanes >= LOG_LANE) & (lanes < LOG_LANE + 3)
    return jnp.where(inside | log_lanes, 1.0, 0.0).astype(bf16)


def block_used(meta, key_start, key_rows, rows):
    return (
        (key_start >= 0) & (key_start <= meta[0] + rows - 1) & (key_start + key_rows - 1 >= meta[1])
    )


def lower_mask(transposed):
    shape = (KEY_CHUNK, KEY_CHUNK)
    first = lax.broadcasted_iota(jnp.int32, shape, 0)
    second = lax.broadcasted_iota(jnp.int32, shape, 1)
    return first <= second if transposed else second <= first


def chunk(i, n=1):
    return slice(i * KEY_CHUNK, (i + n) * KEY_CHUNK)


def attend_kernel(meta, q_ref, kva_ref, kvb_ref, bounds_ref, *refs, first, last):
    rows = q_ref.shape[0]
    key_rows = kva_ref.shape[0]
    if last:
        acc_in, sum_in, o_ref, q_out_ref, acc_ref, sum_ref = refs
    elif first:
        acc_ref, sum_ref = refs
    else:
        acc_in, sum_in, acc_ref, sum_ref = refs
    if first:
        acc_ref[...] = jnp.zeros_like(acc_ref)
        sum_ref[...] = jnp.zeros_like(sum_ref)
    else:
        acc_ref[...] = acc_in[...]
        sum_ref[...] = sum_in[...]
    ones = jnp.ones((KEY_CHUNK, HEAD_WIDTH), bf16)

    def work(kv_ref, lanes, keys, queries, mask):
        key = jnp.concatenate([kv_ref[keys, :HEAD_WIDTH], lanes[keys, :]], axis=1)
        weight = jnp.exp2(dot_nt(q_ref[queries, :], key))
        if mask:
            weight = jnp.where(lower_mask(False), weight, 0.0)
        value = jnp.concatenate([kv_ref[keys, HEAD_WIDTH:], ones], axis=1)
        out = dot(weight.astype(bf16), value)
        acc_ref[queries, :] += out[:, :HEAD_WIDTH]
        sum_ref[queries, :] += out[:, HEAD_WIDTH:]

    for place, kv_ref in enumerate((kva_ref, kvb_ref)):
        key_start = meta[2 + place]
        diagonal = first and place == 0

        @pl.when(block_used(meta, key_start, key_rows, rows))
        def _():
            lanes = key_lanes(meta, key_start, key_rows, bounds_ref)
            for c in range(key_rows // KEY_CHUNK):
                if diagonal:
                    work(kv_ref, lanes, chunk(c), chunk(c), True)
                    if c + 1 < rows // KEY_CHUNK:
                        work(kv_ref, lanes, chunk(c), slice((c + 1) * KEY_CHUNK, rows), False)
                else:
                    work(kv_ref, lanes, chunk(c), slice(0, rows), False)

    if last:
        total = sum_ref[...]
        outcome = acc_ref[...] / total
        acc_ref[...] = outcome
        o_ref[...] = outcome.astype(bf16)
        lanes = lane_index(rows)
        extra = q_ref[:, HEAD_WIDTH:].astype(f32)
        for i, part in enumerate(split_parts(jnp.log2(total))):
            extra = jnp.where(lanes == LOG_LANE + i, -part.astype(f32), extra)
        q_out_ref[:, :HEAD_WIDTH] = q_ref[:, :HEAD_WIDTH]
        q_out_ref[:, HEAD_WIDTH:] = extra.astype(bf16)


def attend_stage(q, kv_a, kv_b, bounds, meta, carried, last):
    rows = q.shape[0]
    key_rows = kv_a.shape[0]
    q_heads = q.shape[1] // (2 * HEAD_WIDTH)
    group = q.shape[1] // kv_a.shape[1]
    width = q_heads * HEAD_WIDTH
    first = not carried
    wide = 2 * HEAD_WIDTH
    per_q = pl.BlockSpec((rows, wide), lambda j, m: (0, j))
    per_kv = pl.BlockSpec((key_rows, wide), lambda j, m: (0, j // group))
    per_out = pl.BlockSpec((rows, HEAD_WIDTH), lambda j, m: (0, j))
    table = pl.BlockSpec((8, HEAD_WIDTH), lambda j, m: (0, 0))
    running = jax.ShapeDtypeStruct((rows, width), f32)
    if last:
        out_specs = [per_out, per_q, per_out]
        out_shape = [jax.ShapeDtypeStruct((rows, width), bf16), jax.ShapeDtypeStruct(q.shape, bf16), running]
        scratch = [pltpu.VMEM((rows, HEAD_WIDTH), f32)]
        aliases = {5: 2}
    else:
        out_specs = [per_out, per_out]
        out_shape = [running, running]
        scratch = []
        aliases = {} if first else {5: 0, 6: 1}
    return pl.pallas_call(
        functools.partial(attend_kernel, first=first, last=last),
        grid_spec=pltpu.PrefetchScalarGridSpec(
            num_scalar_prefetch=1,
            grid=(q_heads,),
            in_specs=[per_q, per_kv, per_kv, table] + [per_out] * len(carried),
            out_specs=out_specs,
            scratch_shapes=scratch,
        ),
        out_shape=out_shape,
        input_output_aliases=aliases,
        compiler_params=pltpu.CompilerParams(vmem_limit_bytes=40 * MIB),
        cost_estimate=SMALL,
        name="attend_stage",
    )(meta, q, kv_a, kv_b, bounds, *carried)


def delta_kernel(owners, *refs):
    *pieces, outcome_ref, out_ref = refs
    for i, piece in enumerate(pieces):

        @pl.when(pl.program_id(0) == i)
        def _():
            rows, width = piece.shape
            lanes = lane_index(rows)
            for j in range(width // HEAD_WIDTH):
                head = slice(j * HEAD_WIDTH, (j + 1) * HEAD_WIDTH)
                do = piece[:, head]
                delta = jnp.sum(do.astype(f32) * outcome_ref[:, head], axis=-1, keepdims=True)
                extra = jnp.zeros((rows, HEAD_WIDTH), f32)
                for k, part in enumerate(split_parts(delta)):
                    extra = jnp.where(lanes == k, -part.astype(f32), extra)
                start = 2 * j * HEAD_WIDTH
                out_ref[:, start : start + HEAD_WIDTH] = do
                out_ref[:, start + HEAD_WIDTH : start + 2 * HEAD_WIDTH] = extra.astype(bf16)


def with_delta(pieces, outcome):
    owners = jnp.stack([jnp.asarray(owner, jnp.int32) for unused, owner in pieces])
    rows, width = outcome.shape
    share = rows // len(pieces)
    whole = pl.BlockSpec((share, width), lambda i, m: (0, 0))
    return pl.pallas_call(
        delta_kernel,
        grid_spec=pltpu.PrefetchScalarGridSpec(
            num_scalar_prefetch=1,
            grid=(len(pieces),),
            in_specs=[whole] * len(pieces) + [pl.BlockSpec((share, width), lambda i, m: (m[i], 0))],
            out_specs=pl.BlockSpec((share, 2 * width), lambda i, m: (m[i], 0)),
        ),
        out_shape=jax.ShapeDtypeStruct((rows, 2 * width), bf16),
        cost_estimate=SMALL,
        name="with_delta",
    )(owners, *[piece for piece, unused in pieces], outcome)


def assemble_kernel(owners, *refs):
    *pieces, out_ref = refs
    for i, piece in enumerate(pieces):

        @pl.when(pl.program_id(0) == i)
        def _():
            out_ref[...] = piece[...].astype(out_ref.dtype)


def assemble(pieces, kind):
    owners = jnp.stack([jnp.asarray(owner, jnp.int32) for unused, owner in pieces])
    share, width = pieces[0][0].shape
    return pl.pallas_call(
        assemble_kernel,
        grid_spec=pltpu.PrefetchScalarGridSpec(
            num_scalar_prefetch=1,
            grid=(len(pieces),),
            in_specs=[pl.BlockSpec((share, width), lambda i, m: (0, 0))] * len(pieces),
            out_specs=pl.BlockSpec((share, width), lambda i, m: (m[i], 0)),
        ),
        out_shape=jax.ShapeDtypeStruct((share * len(pieces), width), kind),
        compiler_params=pltpu.CompilerParams(vmem_limit_bytes=40 * MIB),
        cost_estimate=SMALL,
        name="assemble",
    )(owners, *[piece for piece, unused in pieces])


def attend_back_kernel(
    meta,
    q_ref,
    do_ref,
    kv_ref,
    bounds_ref,
    dq_in,
    dq_ref,
    dkv_ref,
    dq_turned,
    dkv_sum,
    *,
    first,
    group,
    diagonal,
    place,
):
    rows = q_ref.shape[0]
    key_rows = kv_ref.shape[0]
    key_start = meta[2 + place]
    step = lax.rem(pl.program_id(0), group)

    @pl.when(step == 0)
    def _():
        dkv_sum[...] = jnp.zeros_like(dkv_sum)

    def work(lanes, ones, keys, queries, mask):
        key = kv_ref[keys, :HEAD_WIDTH]
        q = q_ref[queries, :]
        do = do_ref[queries, :]
        weight = jnp.exp2(dot_nt(jnp.concatenate([key, lanes[keys, :]], axis=1), q))
        if mask:
            weight = jnp.where(lower_mask(True), weight, 0.0)
        value = jnp.concatenate([kv_ref[keys, HEAD_WIDTH:], ones], axis=1)
        d_score = (weight * dot_nt(value, do)).astype(bf16)
        dkv_sum[keys, HEAD_WIDTH:] += dot(weight.astype(bf16), do[:, :HEAD_WIDTH])
        dkv_sum[keys, :HEAD_WIDTH] += dot(d_score, q[:, :HEAD_WIDTH])
        dq_turned[:, queries] += dot_tn(key, d_score)

    used = block_used(meta, key_start, key_rows, rows)

    @pl.when(used)
    def _():
        dq_turned[...] = jnp.zeros_like(dq_turned)
        lanes = key_lanes(meta, key_start, key_rows, bounds_ref)
        ones = jnp.where(lane_index(KEY_CHUNK) < 3, 1.0, 0.0).astype(bf16)
        for c in range(key_rows // KEY_CHUNK):
            if diagonal:
                work(lanes, ones, chunk(c), chunk(c), True)
                if c + 1 < rows // KEY_CHUNK:
                    work(lanes, ones, chunk(c), slice((c + 1) * KEY_CHUNK, rows), False)
            else:
                work(lanes, ones, chunk(c), slice(0, rows), False)
        turned = dq_turned[...].T
        dq_ref[...] = turned if first else dq_in[...] + turned

    @pl.when(jnp.logical_not(used))
    def _():
        dq_ref[...] = jnp.zeros_like(dq_ref) if first else dq_in[...]

    @pl.when(step == group - 1)
    def _():
        dkv_ref[...] = dkv_sum[...].astype(dkv_ref.dtype)


def attend_back(q, do, kv, bounds, meta, dq, place, diagonal, kind):
    rows = q.shape[0]
    key_rows = kv.shape[0]
    q_heads = q.shape[1] // (2 * HEAD_WIDTH)
    group = q.shape[1] // kv.shape[1]
    width = q_heads * HEAD_WIDTH
    first = dq is None
    if first:
        dq = jnp.zeros((8, HEAD_WIDTH), f32)
    wide = 2 * HEAD_WIDTH
    per_q = pl.BlockSpec((rows, wide), lambda j, m: (0, j))
    per_kv = pl.BlockSpec((key_rows, wide), lambda j, m: (0, j // group))
    per_out = pl.BlockSpec((rows, HEAD_WIDTH), lambda j, m: (0, j))
    carried = pl.BlockSpec((8, HEAD_WIDTH), lambda j, m: (0, 0)) if first else per_out
    return pl.pallas_call(
        functools.partial(
            attend_back_kernel, first=first, group=group, diagonal=diagonal, place=place
        ),
        grid_spec=pltpu.PrefetchScalarGridSpec(
            num_scalar_prefetch=1,
            grid=(q_heads,),
            in_specs=[
                per_q,
                per_q,
                per_kv,
                pl.BlockSpec((8, HEAD_WIDTH), lambda j, m: (0, 0)),
                carried,
            ],
            out_specs=[per_out, per_kv],
            scratch_shapes=[
                pltpu.VMEM((HEAD_WIDTH, rows), f32),
                pltpu.VMEM((key_rows, wide), f32),
            ],
        ),
        out_shape=[
            jax.ShapeDtypeStruct((rows, width), f32),
            jax.ShapeDtypeStruct(kv.shape, kind),
        ],
        input_output_aliases={} if first else {5: 0},
        compiler_params=pltpu.CompilerParams(vmem_limit_bytes=40 * MIB),
        cost_estimate=SMALL,
        name="attend_back",
    )(meta, q, do, kv, bounds, dq)


def project_kernel(meta, base_ref, *refs, count, final):
    pieces, mine, other = refs[:count], refs[count : 2 * count], refs[2 * count : 3 * count]
    if final:
        gain_ref, share_ref, normed_ref = refs[3 * count :]
    else:
        (out_ref,) = refs[3 * count :]
    first_core = meta[0] == 0
    total = base_ref[...].astype(f32)
    for piece, mine_ref, other_ref in zip(pieces, mine, other):
        half = piece.shape[1] // 2
        low, high = piece[:, :half], piece[:, half:]
        total += dot(jnp.where(first_core, low, high), mine_ref[0])
        total += dot(jnp.where(first_core, high, low), other_ref[0])
    if final:
        inverse = lax.rsqrt(jnp.mean(total * total, axis=-1, keepdims=True) + EPSILON)
        normed_ref[...] = (total * inverse * gain_ref[...]).astype(bf16)

        @pl.when(pl.program_id(0) == meta[1])
        def _():
            share_ref[...] = total

    else:
        out_ref[...] = total


def project(base, pieces, w_mine, w_other, core, me, gain=None):
    meta = jnp.stack(
        [jnp.asarray(v, jnp.int32) for v in [core, me] + [owner for unused, owner in pieces]]
    )
    rows, width = base.shape
    n_head, half, unused = w_mine.shape
    count = len(pieces)
    final = gain is not None
    step = rows // n_head
    per_row = pl.BlockSpec((step, width), lambda i, m: (i, 0))
    per_piece = pl.BlockSpec((step, 2 * half), lambda i, m: (i, 0))
    weights = [
        pl.BlockSpec((1, half, width), lambda i, m, k=k: (m[2 + k], 0, 0)) for k in range(count)
    ]
    in_specs = [per_row] + [per_piece] * count + weights + weights
    args = [base] + [piece for piece, unused in pieces] + [w_mine] * count + [w_other] * count
    if final:
        in_specs.append(pl.BlockSpec((1, width), lambda i, m: (0, 0)))
        args.append(gain[None, :])
        out_specs = [pl.BlockSpec((step, width), lambda i, m: (0, 0)), per_row]
        out_shape = [
            jax.ShapeDtypeStruct((step, width), f32),
            jax.ShapeDtypeStruct((rows, width), bf16),
        ]
    else:
        out_specs = per_row
        out_shape = jax.ShapeDtypeStruct((rows, width), f32)
    return pl.pallas_call(
        functools.partial(project_kernel, count=count, final=final),
        grid_spec=pltpu.PrefetchScalarGridSpec(
            num_scalar_prefetch=1,
            grid=(rows // step,),
            in_specs=in_specs,
            out_specs=out_specs,
        ),
        out_shape=out_shape,
        compiler_params=pltpu.CompilerParams(vmem_limit_bytes=(24 + 8 * count) * MIB),
        cost_estimate=SMALL,
        name="project",
    )(meta, *args)


def project_back_kernel(meta, branch_ref, mine_ref, other_ref, out_ref):
    half = mine_ref.shape[1]
    mine = dot_nt(branch_ref[...], mine_ref[0])
    other = dot_nt(branch_ref[...], other_ref[0])
    first_core = meta[0] == 0
    out_ref[0, :, :half] = jnp.where(first_core, mine, other).astype(bf16)
    out_ref[0, :, half:] = jnp.where(first_core, other, mine).astype(bf16)


def project_back(branch, w_mine, w_other, core):
    meta = jnp.asarray(core, jnp.int32)[None]
    rows, width = branch.shape
    n_head, half, unused = w_mine.shape
    weight = pl.BlockSpec((1, half, width), lambda i, m: (i, 0, 0))
    return pl.pallas_call(
        project_back_kernel,
        grid_spec=pltpu.PrefetchScalarGridSpec(
            num_scalar_prefetch=1,
            grid=(n_head,),
            in_specs=[pl.BlockSpec((rows, width), lambda i, m: (0, 0)), weight, weight],
            out_specs=pl.BlockSpec((1, rows, 2 * half), lambda i, m: (i, 0, 0)),
        ),
        out_shape=jax.ShapeDtypeStruct((n_head, rows, 2 * half), bf16),
        compiler_params=pltpu.CompilerParams(vmem_limit_bytes=40 * MIB),
        cost_estimate=SMALL,
        name="project_back",
    )(meta, branch, w_mine, w_other)


def feed_kernel(
    x_ref, gate_w_ref, up_w_ref, d_mixed_ref, dy_ref, mixed_ref, gate_ref, up_ref, down_ref
):
    x = x_ref[...]
    gate = dot(x, gate_w_ref[...])
    up = dot(x, up_w_ref[...])
    d_mixed = d_mixed_ref[...]
    sigmoid = 0.5 * jnp.tanh(0.5 * gate) + 0.5
    silu = gate * sigmoid
    mixed = (silu * up).astype(bf16)
    mixed_ref[...] = mixed
    gate_ref[...] = (d_mixed * up * (sigmoid * (1.0 + gate * (1.0 - sigmoid)))).astype(bf16)
    up_ref[...] = (d_mixed * silu).astype(bf16)
    shares, unused, width = down_ref.shape
    for i in range(shares):
        down_ref[i] = dot_tn(mixed, dy_ref[:, i * width : (i + 1) * width]).astype(bf16)


def feed(x, w_gate, w_up, d_mixed, dy, shares):
    rows, width = x.shape
    hidden = w_gate.shape[1]
    whole = pl.BlockSpec((rows, width), lambda i: (0, 0))
    weight = pl.BlockSpec((width, HIDDEN_STEP), lambda i: (0, i))
    act = pl.BlockSpec((rows, HIDDEN_STEP), lambda i: (0, i))
    return pl.pallas_call(
        feed_kernel,
        grid=(hidden // HIDDEN_STEP,),
        in_specs=[whole, weight, weight, act, whole],
        out_specs=[
            act,
            act,
            act,
            pl.BlockSpec((shares, HIDDEN_STEP, width // shares), lambda i: (0, i, 0)),
        ],
        out_shape=[jax.ShapeDtypeStruct((rows, hidden), bf16)] * 3
        + [jax.ShapeDtypeStruct((shares, hidden, width // shares), bf16)],
        compiler_params=pltpu.CompilerParams(vmem_limit_bytes=40 * MIB),
        cost_estimate=SMALL,
        name="feed",
    )(x, w_gate, w_up, d_mixed, dy)


def feed_back_kernel(gate_ref, up_ref, gate_w_ref, up_w_ref, out_ref):
    out_ref[...] = (
        dot_nt(gate_ref[...], gate_w_ref[...]) + dot_nt(up_ref[...], up_w_ref[...])
    ).astype(bf16)


def feed_back(gate, up, w_gate, w_up):
    rows, hidden = gate.shape
    width = w_gate.shape[0]
    step = width // 4
    whole = pl.BlockSpec((rows, hidden), lambda i: (0, 0))
    weight = pl.BlockSpec((step, hidden), lambda i: (i, 0))
    return pl.pallas_call(
        feed_back_kernel,
        grid=(width // step,),
        in_specs=[whole, whole, weight, weight],
        out_specs=pl.BlockSpec((rows, step), lambda i: (0, i)),
        out_shape=jax.ShapeDtypeStruct((rows, width), bf16),
        compiler_params=pltpu.CompilerParams(vmem_limit_bytes=36 * MIB),
        cost_estimate=SMALL,
        name="feed_back",
    )(gate, up, w_gate, w_up)


def feed_sums_kernel(x_ref, gate_ref, up_ref, out_ref):
    hidden = gate_ref.shape[1]
    x = x_ref[...]
    out_ref[:, :hidden] = dot_tn(x, gate_ref[...]).astype(bf16)
    out_ref[:, hidden:] = dot_tn(x, up_ref[...]).astype(bf16)


def feed_sums(x, gate, up):
    rows, width = x.shape
    hidden = gate.shape[1]
    step = width // 8
    act = pl.BlockSpec((rows, hidden), lambda i: (0, 0))
    return pl.pallas_call(
        feed_sums_kernel,
        grid=(width // step,),
        in_specs=[pl.BlockSpec((rows, step), lambda i: (0, i)), act, act],
        out_specs=pl.BlockSpec((step, 2 * hidden), lambda i: (i, 0)),
        out_shape=jax.ShapeDtypeStruct((width, 2 * hidden), bf16),
        compiler_params=pltpu.CompilerParams(vmem_limit_bytes=32 * MIB),
        cost_estimate=SMALL,
        name="feed_sums",
    )(x, gate, up)


def attn_sums_kernel(x_ref, q_ref, k_ref, v_ref, o_ref, branch_ref, out_ref):
    x = x_ref[...]
    share = x.shape[1]
    width = out_ref.shape[2]
    start = 0
    for ref in (q_ref, k_ref, v_ref):
        out_ref[0, :share, start : start + ref.shape[1]] = dot_tn(x, ref[...]).astype(bf16)
        start += ref.shape[1]
    branch = branch_ref[...]
    heads = o_ref.shape[1] // HEAD_WIDTH
    if heads * share % width:
        out_ref[0, share:, :] = jnp.zeros((out_ref.shape[1] - share, width), bf16)
    for j in range(heads):
        row, lane = output_place(j, share, width)
        out_ref[0, row : row + HEAD_WIDTH, lane : lane + share] = dot_tn(
            o_ref[:, j * HEAD_WIDTH : (j + 1) * HEAD_WIDTH], branch
        ).astype(bf16)


def output_place(head, share, width):
    return share + HEAD_WIDTH * (head * share // width), head * share % width


def attn_sums(x, query, key, value, o_low, branch, shares):
    rows, width = x.shape
    share = width // shares
    out_width = query.shape[1] + key.shape[1] + value.shape[1]
    heads = o_low.shape[1] // HEAD_WIDTH
    out_rows = output_place(heads - 1, share, out_width)[0] + HEAD_WIDTH

    def full(array):
        return pl.BlockSpec(array.shape, lambda i: (0, 0))

    part = pl.BlockSpec((rows, share), lambda i: (0, i))
    return pl.pallas_call(
        attn_sums_kernel,
        grid=(shares,),
        in_specs=[part, full(query), full(key), full(value), full(o_low), part],
        out_specs=pl.BlockSpec((1, out_rows, out_width), lambda i: (i, 0, 0)),
        out_shape=jax.ShapeDtypeStruct((shares, out_rows, out_width), bf16),
        compiler_params=pltpu.CompilerParams(vmem_limit_bytes=24 * MIB),
        cost_estimate=SMALL,
        name="attn_sums",
    )(x, query, key, value, o_low, branch)


def after(values):
    return lax.optimization_barrier(values)


def pick(array, index):
    return lax.dynamic_index_in_dim(array, index, 0, keepdims=False)


def solution(mesh):
    n_seq = mesh.shape["seq"]
    n_head = mesh.shape["head"]
    n_chip = n_seq // 2

    def swap_core(value):
        return lax.ppermute(value, "seq", [(i, i ^ 1) for i in range(n_seq)])

    def to_next(value):
        return lax.ppermute(value, "seq", [(i, i + 2) for i in range(n_seq - 2)])

    def to_previous(value):
        return lax.ppermute(value, "seq", [(i + 2, i) for i in range(n_seq - 2)])

    def across(value, bits):
        return lax.ppermute(value, "head", [(i, i ^ bits) for i in range(n_head)])

    def gather_steps(value):
        me = lax.axis_index("head")
        if n_head != 4:
            every = yield lax.all_gather(value, "head", axis=0)
            return [(every[i], i) for i in range(n_head)]
        half = value.shape[0] // 2
        by_x, by_y = yield across(value, 1), across(value, 2)
        low, high = yield across(by_x[:half], 2), across(by_y[half:], 1)
        far = jnp.concatenate([low, high], axis=0)
        return [(value, me), (by_x, me ^ 1), (by_y, me ^ 2), (far, me ^ 3)]

    def scatter_steps(value):
        rows, width = value.shape
        if n_head != 4:
            total = yield lax.psum_scatter(value, "head", scatter_dimension=0, tiled=True)
            return total.astype(f32)
        me = lax.axis_index("head")
        x, y = me & 1, me >> 1
        part = value.reshape(2, 2, 2, rows // 8, width)
        first, second = part[:, :, 0], part[:, :, 1]
        first_x = jnp.swapaxes(first, 0, 1)
        got_first, got_second = yield (
            across(pick(first_x, 1 - x), 1),
            across(pick(second, 1 - y), 2),
        )
        sum_first = pick(first_x, x).astype(f32) + got_first.astype(f32)
        sum_second = pick(second, y).astype(f32) + got_second.astype(f32)
        last_first, last_second = yield (
            across(pick(sum_first, 1 - y).astype(bf16), 2),
            across(pick(sum_second, 1 - x).astype(bf16), 1),
        )
        return jnp.concatenate(
            [
                pick(sum_first, y) + last_first.astype(f32),
                pick(sum_second, x) + last_second.astype(f32),
            ],
            axis=0,
        )

    def run_steps(steps, works=()):
        works = list(works)
        made = []
        arrived = next(steps)
        while True:
            if works:
                arrived, done = after((arrived, works.pop(0)()))
                made.append(done)
            try:
                arrived = steps.send(arrived)
            except StopIteration as stop:
                return stop.value, made + [work() for work in works]

    def exchange_head(value):
        me = lax.axis_index("head")
        if n_head != 4:
            got = lax.all_to_all(value, "head", 0, 0)
            return [(got[i], i) for i in range(n_head)]
        pieces = [(pick(value, me), me)]
        for bits in (3, 1, 2):
            pieces.append((across(pick(value, me ^ bits), bits), me ^ bits))
        return pieces

    def body(
        tokens,
        lengths,
        norm1_gain,
        w_query,
        key_matrix,
        value_matrix,
        query_gain,
        key_gain,
        w_output,
        norm2_gain,
        w_gate,
        w_up,
        w_down,
        cotangent,
    ):
        rows = tokens.shape[0]
        share = rows // n_head
        seq_index = lax.axis_index("seq")
        head_index = lax.axis_index("head")
        chip, core = seq_index // 2, seq_index % 2

        index = seq_index * rows + jnp.arange(rows, dtype=jnp.int32)
        begin = locate(index, lengths)
        cosine, sine = rotary(index - begin)
        ends = jnp.cumsum(lengths)
        n_lengths = lengths.shape[0]
        bounds = jnp.zeros((8, HEAD_WIDTH), jnp.int32).at[0].set(2**30)
        bounds = bounds.at[0, :n_lengths].set(ends - lengths).at[1, :n_lengths].set(ends)

        def stage_meta(stage):
            source = 2 * (chip - stage)
            return jnp.stack(
                [seq_index * rows, begin[0], (source + core) * rows, (source + 1 - core) * rows]
            ).astype(jnp.int32)

        metas = [stage_meta(stage) for stage in range(n_chip)]

        first_in, key_raw, current = enter(
            tokens, norm1_gain, key_matrix, value_matrix, key_gain, cosine, sine
        )
        sibling = swap_core(current)
        following = to_next(current)

        half_rows = w_output.shape[0] // 2
        w_late, unused = after((w_output, current))
        w_half = lax.dynamic_slice_in_dim(w_late, core * half_rows, half_rows, 0)
        w_mine = lax.all_gather(w_half, "head", axis=0)

        query_raw = dot(first_in, w_query)
        q_wide = query_prep(metas[0], query_raw, query_gain, cosine, sine, bounds)
        following, q_wide = after((following, q_wide))
        d_mixed = dot_nt(cotangent, w_down)

        blocks = []
        carried = ()
        for stage in range(n_chip):
            blocks.append((current, sibling))
            if stage + 2 < n_chip:
                current = following
                sibling = swap_core(current)
                following = to_next(current)
            carried = attend_stage(
                q_wide, *blocks[stage], bounds, metas[stage], carried, stage == n_chip - 1
            )
            if stage == 0:
                carried, d_mixed = after((carried, d_mixed))
            if stage + 3 < n_chip:
                following, carried = after((following, carried))
            if stage + 2 == n_chip:
                current, carried = after((following, carried))
                sibling = swap_core(current)
                w_mine, sibling, carried = after((w_mine, sibling, carried))
                w_other = swap_core(w_mine)
        o_low, q_back, outcome = carried

        steps = gather_steps(o_low)
        arrived = next(steps)
        base = tokens
        if n_head == 4:
            far = steps.send(arrived)
            pieces = [(o_low, head_index), (arrived[0], head_index ^ 1), (arrived[1], head_index ^ 2)]
            base = project(tokens, pieces, w_mine, w_other, core, head_index)
            arrived, base = after((far, base))
        try:
            steps.send(arrived)
        except StopIteration as stop:
            pieces = stop.value[3:] if n_head == 4 else stop.value
        my_hidden, second_in = project(
            base, pieces, w_mine, w_other, core, head_index, norm2_gain
        )
        mixed_low, gate_low, up_low, down_sum = feed(
            second_in, w_gate, w_up, d_mixed, cotangent, n_seq
        )

        def scatter_seq(value, tiled):
            return lax.psum_scatter(value, "seq", scatter_dimension=0, tiled=tiled)

        grad_down = scatter_seq(down_sum, False)

        second_grad, (gate_up_sum,) = run_steps(
            scatter_steps(feed_back(gate_low, up_low, w_gate, w_up)),
            (lambda: feed_sums(second_in, gate_low, up_low),),
        )
        my_inverse = lax.rsqrt(jnp.mean(my_hidden * my_hidden, axis=-1, keepdims=True) + EPSILON)
        my_hat = my_hidden * my_inverse
        grad_norm2 = jnp.sum(second_grad * my_hat, axis=0)
        scaled = second_grad * norm2_gain
        my_dy = lax.dynamic_slice_in_dim(cotangent, head_index * share, share, 0).astype(f32)
        hidden_grad = my_dy + my_inverse * (
            scaled - my_hat * jnp.mean(scaled * my_hat, axis=-1, keepdims=True)
        )
        my_branch = hidden_grad.astype(bf16)
        do_pieces = exchange_head(project_back(my_branch, w_mine, w_other, core))
        do_wide = with_delta(do_pieces, outcome)
        grad_down, gate_up_sum, do_wide = after((grad_down, gate_up_sum, do_wide))
        grad_gate_up = scatter_seq(gate_up_sum, True)

        def side_work(mixed_low, my_branch):
            branch_steps = gather_steps(my_branch)
            got = yield next(branch_steps)
            mixed_steps = scatter_steps(dot(mixed_low, w_down).astype(bf16))
            got_branch, got = yield branch_steps.send(got) if n_head == 4 else got, next(mixed_steps)
            try:
                branch_steps.send(got_branch)
            except StopIteration as stop:
                branch = assemble(stop.value, bf16)
            if n_head == 4:
                got = yield mixed_steps.send(got)
            try:
                mixed_steps.send(got)
            except StopIteration as stop:
                my_mixed = (my_hidden + stop.value).astype(bf16)
            mixed_steps = gather_steps(my_mixed)
            got = yield next(mixed_steps)
            if n_head == 4:
                got = yield mixed_steps.send(got)
            try:
                mixed_steps.send(got)
            except StopIteration as stop:
                mixed = assemble(stop.value, bf16)
            return mixed, branch

        mixed_late, my_branch, do_wide = after((mixed_low, my_branch, do_wide))
        side = side_work(mixed_late, my_branch)
        waiting = next(side)
        side_made = None

        def side_step():
            nonlocal waiting, side_made, dq
            if side_made is None:
                waiting, dq = after((waiting, dq))
                try:
                    waiting = side.send(waiting)
                except StopIteration as stop:
                    side_made = stop.value

        dq = None
        arrived = None
        pending = None
        for stage in reversed(range(n_chip)):
            kv_a, kv_b = blocks[stage]
            meta = metas[stage]
            dq, dkv_b = attend_back(q_back, do_wide, kv_b, bounds, meta, dq, 1, False, bf16)
            theirs = swap_core(dkv_b)
            if stage < n_chip - 2:
                side_step()
            dq, dkv_a = attend_back(q_back, do_wide, kv_a, bounds, meta, dq, 0, stage == 0, f32)
            part = dkv_a + theirs.astype(f32)
            if pending is not None:
                arrived, unused = after((arrived, dq))
                arrived = to_previous((pending + arrived.astype(f32)).astype(bf16))
            if stage == n_chip - 1:
                arrived = to_previous(part.astype(bf16))
            else:
                pending = part
            if stage >= n_chip - 2 or stage == 0:
                side_step()
        while side_made is None:
            side_step()
        dkv = pending + arrived.astype(f32)
        mixed, branch = side_made
        query_grad, grad_qgain = head_back(
            query_raw, dq, query_gain, cosine, sine, SCORE_SCALE, 1
        )
        key_grad, grad_kgain = head_back(
            key_raw, dkv, key_gain, cosine, sine, 1.0 / LOG2E, 2
        )
        value_grad = jnp.concatenate(
            [
                dkv[:, (2 * j + 1) * HEAD_WIDTH : (2 * j + 2) * HEAD_WIDTH]
                for j in range(dkv.shape[1] // (2 * HEAD_WIDTH))
            ],
            axis=1,
        ).astype(bf16)

        first_part = (
            dot_nt(query_grad, w_query)
            + dot_nt(key_grad, key_matrix)
            + dot_nt(value_grad, value_matrix)
        ).astype(bf16)
        xf = tokens.astype(f32)
        hat1 = xf * lax.rsqrt(jnp.mean(xf * xf, axis=-1, keepdims=True) + EPSILON)
        grad_norm1 = jnp.sum(first_part.astype(f32) * hat1, axis=0)
        gains = jnp.concatenate([grad_norm1, grad_norm2, grad_qgain[0], grad_kgain[0]])
        gains = gains.reshape(-1, HEAD_WIDTH)
        first_grad, (attn_sum,) = run_steps(
            scatter_steps(first_part),
            (
                lambda: attn_sums(
                    first_in, query_grad, key_grad, value_grad, o_low, branch, n_seq
                ),
            ),
        )
        grad_gate_up, attn_sum = after((grad_gate_up, attn_sum))
        grad_attn = scatter_seq(attn_sum, False).astype(f32)
        share_width = tokens.shape[1] // n_seq
        widths = (query_grad.shape[1], query_grad.shape[1] + key_grad.shape[1])
        grad_query, grad_key, grad_value = jnp.split(grad_attn[:share_width], widths, axis=1)
        output_heads = []
        for j in range(o_low.shape[1] // HEAD_WIDTH):
            row, lane = output_place(j, share_width, grad_attn.shape[1])
            output_heads.append(grad_attn[row : row + HEAD_WIDTH, lane : lane + share_width])
        grad_output = jnp.concatenate(output_heads, axis=0)

        my_x = lax.dynamic_slice_in_dim(tokens, head_index * share, share, 0).astype(f32)
        my_inverse1 = lax.rsqrt(jnp.mean(my_x * my_x, axis=-1, keepdims=True) + EPSILON)
        my_hat1 = my_x * my_inverse1
        scaled1 = first_grad * norm1_gain
        my_tokens_grad = hidden_grad + my_inverse1 * (
            scaled1 - my_hat1 * jnp.mean(scaled1 * my_hat1, axis=-1, keepdims=True)
        )
        tokens_pieces, unused = run_steps(gather_steps(my_tokens_grad.astype(bf16)))
        grad_tokens = assemble(tokens_pieces, f32)

        for axis, size in (("head", n_head), ("seq", n_seq)):
            bit = 1
            while bit < size:
                gains = gains + lax.ppermute(gains, axis, [(i, i ^ bit) for i in range(size)])
                bit *= 2
        gains = gains.reshape(-1)
        width = tokens.shape[1]
        grad_norm1, grad_norm2 = gains[:width], gains[width : 2 * width]
        grad_qgain = gains[2 * width : 2 * width + HEAD_WIDTH]
        grad_kgain = gains[2 * width + HEAD_WIDTH :]
        return (
            mixed,
            grad_tokens,
            grad_norm1,
            grad_query,
            grad_key,
            grad_value,
            grad_qgain,
            grad_kgain,
            grad_output,
            grad_norm2,
            grad_gate_up[:, : w_gate.shape[1]].astype(f32),
            grad_gate_up[:, w_gate.shape[1] :].astype(f32),
            grad_down.astype(f32),
        )

    in_specs = (
        P("seq", None),
        P(),
        P(),
        P(None, "head"),
        P(None, "head"),
        P(None, "head"),
        P(),
        P(),
        P("head", None),
        P(),
        P(None, "head"),
        P(None, "head"),
        P("head", None),
        P("seq", None),
    )
    out_specs = (
        P("seq", None),
        P("seq", None),
        P(),
        P("seq", "head"),
        P("seq", "head"),
        P("seq", "head"),
        P(),
        P(),
        P("head", "seq"),
        P(),
        P("seq", "head"),
        P("seq", "head"),
        P("head", "seq"),
    )
    return jax.shard_map(body, mesh=mesh, in_specs=in_specs, out_specs=out_specs, check_vma=False)
```

```python
import functools
import math

import jax
import jax.numpy as jnp
from jax import lax
from jax.experimental import pallas as pl
from jax.experimental.pallas import tpu as pltpu
from jax.sharding import PartitionSpec as P

HEAD_WIDTH = 128
EPSILON = 1e-06
ROPE_BASE = 1000000.0
LOG2E = math.log2(math.e)
SCORE_SCALE = 1.0 / math.sqrt(HEAD_WIDTH)
SCORE_SCALE_2 = LOG2E / math.sqrt(HEAD_WIDTH)
KEY_CHUNK = 256
HIDDEN_STEP = 256
FAR = 512.0
LOG_LANE = 64
MIB = 2**20
SMALL = pl.CostEstimate(flops=1, bytes_accessed=1, transcendentals=0)
WHOLE_VMEM = pltpu.CompilerParams(vmem_limit_bytes=60 * MIB)

f32 = jnp.float32
bf16 = jnp.bfloat16
NT = (((1,), (1,)), ((), ()))
TN = (((0,), (0,)), ((), ()))


def dot(left, right):
    return jnp.dot(left, right, preferred_element_type=f32)


def dot_nt(left, right):
    return lax.dot_general(left, right, NT, preferred_element_type=f32)


def dot_tn(left, right):
    return lax.dot_general(left, right, TN, preferred_element_type=f32)


def locate(index, lengths):
    ends = jnp.cumsum(lengths)
    starts = ends - lengths
    segment = jnp.sum((index[:, None] >= ends[None, :]).astype(jnp.int32), axis=1)
    chosen = segment[:, None] == jnp.arange(lengths.shape[0], dtype=jnp.int32)[None, :]
    return jnp.sum(jnp.where(chosen, starts[None, :], 0), axis=1)


def rotary(position):
    half = HEAD_WIDTH // 2
    freq = jnp.exp(jnp.arange(half, dtype=f32) * (-2.0 * math.log(ROPE_BASE) / HEAD_WIDTH))
    angle = position.astype(f32)[:, None] * freq[None, :]
    cosine = jnp.cos(angle)
    sine = jnp.sin(angle)
    return (
        jnp.concatenate([cosine, cosine], axis=1),
        jnp.concatenate([-sine, sine], axis=1),
    )


def lane_index(rows):
    return lax.broadcasted_iota(jnp.int32, (rows, HEAD_WIDTH), 1)


def row_index(rows):
    return lax.broadcasted_iota(jnp.int32, (rows, HEAD_WIDTH), 0)


def in_segment(index, bounds_ref):
    return (index >= bounds_ref[0:1, :]) & (index < bounds_ref[1:2, :])


def split_parts(value):
    high = value.astype(bf16)
    rest = value - high.astype(f32)
    middle = rest.astype(bf16)
    return high, middle, (rest - middle.astype(f32)).astype(bf16)


def normed(raw, gain, cosine, sine):
    inverse = lax.rsqrt(jnp.mean(raw * raw, axis=-1, keepdims=True) + EPSILON)
    scaled = raw * inverse * gain
    return scaled * cosine + pltpu.roll(scaled, HEAD_WIDTH // 2, 1) * sine


def enter_kernel(
    x_ref, gain_ref, key_w_ref, value_w_ref, key_gain_ref, cos_ref, sin_ref, in_ref, raw_ref, kv_ref
):
    x = x_ref[...].astype(f32)
    inverse = lax.rsqrt(jnp.mean(x * x, axis=-1, keepdims=True) + EPSILON)
    first_in = (x * inverse * gain_ref[...]).astype(bf16)
    in_ref[...] = first_in
    raw = dot(first_in, key_w_ref[...])
    raw_ref[...] = raw
    value = dot(first_in, value_w_ref[...]).astype(bf16)
    for j in range(raw.shape[1] // HEAD_WIDTH):
        head = slice(j * HEAD_WIDTH, (j + 1) * HEAD_WIDTH)
        key = normed(raw[:, head], key_gain_ref[...], cos_ref[...], sin_ref[...])
        start = 2 * j * HEAD_WIDTH
        kv_ref[:, start : start + HEAD_WIDTH] = key.astype(bf16)
        kv_ref[:, start + HEAD_WIDTH : start + 2 * HEAD_WIDTH] = value[:, head]


def enter(tokens, gain, key_w, value_w, key_gain, cosine, sine):
    rows, width = tokens.shape
    kv_width = key_w.shape[1]
    step = rows // 3 if rows % 768 == 0 else rows
    table = pl.BlockSpec((step, HEAD_WIDTH), lambda i: (i, 0))
    weight = pl.BlockSpec((width, kv_width), lambda i: (0, 0))
    return pl.pallas_call(
        enter_kernel,
        grid=(rows // step,),
        in_specs=[
            pl.BlockSpec((step, width), lambda i: (i, 0)),
            pl.BlockSpec((1, width), lambda i: (0, 0)),
            weight,
            weight,
            pl.BlockSpec((1, HEAD_WIDTH), lambda i: (0, 0)),
            table,
            table,
        ],
        out_specs=[
            pl.BlockSpec((step, width), lambda i: (i, 0)),
            pl.BlockSpec((step, kv_width), lambda i: (i, 0)),
            pl.BlockSpec((step, 2 * kv_width), lambda i: (i, 0)),
        ],
        out_shape=[
            jax.ShapeDtypeStruct((rows, width), bf16),
            jax.ShapeDtypeStruct((rows, kv_width), f32),
            jax.ShapeDtypeStruct((rows, 2 * kv_width), bf16),
        ],
        compiler_params=WHOLE_VMEM,
        cost_estimate=SMALL,
        name="enter",
    )(tokens, gain[None, :], key_w, value_w, key_gain[None, :], cosine, sine)


def query_prep_kernel(meta, raw_ref, gain_ref, cos_ref, sin_ref, bounds_ref, out_ref):
    rows = raw_ref.shape[0]
    query = normed(raw_ref[...], gain_ref[...], cos_ref[...], sin_ref[...])
    out_ref[:, :HEAD_WIDTH] = (query * SCORE_SCALE_2).astype(bf16)
    inside = in_segment(meta[0] + row_index(rows), bounds_ref)
    free = inside | (lane_index(rows) >= LOG_LANE)
    out_ref[:, HEAD_WIDTH:] = jnp.where(free, 0.0, -FAR).astype(bf16)


def query_prep(meta, raw, gain, cosine, sine, bounds):
    rows, width = raw.shape
    table = pl.BlockSpec((rows, HEAD_WIDTH), lambda j, m: (0, 0))
    return pl.pallas_call(
        query_prep_kernel,
        grid_spec=pltpu.PrefetchScalarGridSpec(
            num_scalar_prefetch=1,
            grid=(width // HEAD_WIDTH,),
            in_specs=[
                pl.BlockSpec((rows, HEAD_WIDTH), lambda j, m: (0, j)),
                pl.BlockSpec((1, HEAD_WIDTH), lambda j, m: (0, 0)),
                table,
                table,
                pl.BlockSpec((8, HEAD_WIDTH), lambda j, m: (0, 0)),
            ],
            out_specs=pl.BlockSpec((rows, 2 * HEAD_WIDTH), lambda j, m: (0, j)),
        ),
        out_shape=jax.ShapeDtypeStruct((rows, 2 * width), bf16),
        compiler_params=WHOLE_VMEM,
        cost_estimate=SMALL,
        name="query_prep",
    )(meta, raw, gain[None, :], cosine, sine, bounds)


def head_backward(raw, grad, gain, cosine, sine):
    inverse = lax.rsqrt(jnp.mean(raw * raw, axis=-1, keepdims=True) + EPSILON)
    hat = raw * inverse
    back = grad * cosine - pltpu.roll(grad, HEAD_WIDTH // 2, 1) * sine
    gain_grad = jnp.sum(back * hat, axis=0, keepdims=True)
    back = back * gain
    back = inverse * (back - hat * jnp.mean(back * hat, axis=-1, keepdims=True))
    return back.astype(bf16), gain_grad


def head_back_kernel(raw_ref, grad_ref, gain_ref, cos_ref, sin_ref, out_ref, gain_grad_ref, *, scale):
    @pl.when(pl.program_id(0) == 0)
    def _():
        gain_grad_ref[...] = jnp.zeros_like(gain_grad_ref)

    out_ref[...], gain_grad = head_backward(
        raw_ref[...], grad_ref[...] * scale, gain_ref[...], cos_ref[...], sin_ref[...]
    )
    gain_grad_ref[...] += gain_grad


def head_back(raw, grad, gain, cosine, sine, scale, stride):
    rows, width = raw.shape
    block = pl.BlockSpec((rows, HEAD_WIDTH), lambda j: (0, j))
    spaced = pl.BlockSpec((rows, HEAD_WIDTH), lambda j: (0, j * stride))
    table = pl.BlockSpec((rows, HEAD_WIDTH), lambda j: (0, 0))
    one = pl.BlockSpec((1, HEAD_WIDTH), lambda j: (0, 0))
    return pl.pallas_call(
        functools.partial(head_back_kernel, scale=scale),
        grid=(width // HEAD_WIDTH,),
        in_specs=[block, spaced, one, table, table],
        out_specs=[block, one],
        out_shape=[
            jax.ShapeDtypeStruct((rows, width), bf16),
            jax.ShapeDtypeStruct((1, HEAD_WIDTH), f32),
        ],
        compiler_params=WHOLE_VMEM,
        cost_estimate=SMALL,
        name="head_back",
    )(raw, grad, gain[None, :], cosine, sine)


def key_lanes(meta, key_start, rows, bounds_ref):
    inside = in_segment(key_start + row_index(rows), bounds_ref)
    lanes = lane_index(rows)
    log_lanes = (lanes >= LOG_LANE) & (lanes < LOG_LANE + 3)
    return jnp.where(inside | log_lanes, 1.0, 0.0).astype(bf16)


def block_used(meta, key_start, key_rows, rows):
    return (
        (key_start >= 0) & (key_start <= meta[0] + rows - 1) & (key_start + key_rows - 1 >= meta[1])
    )


def lower_mask(transposed):
    shape = (KEY_CHUNK, KEY_CHUNK)
    first = lax.broadcasted_iota(jnp.int32, shape, 0)
    second = lax.broadcasted_iota(jnp.int32, shape, 1)
    return first <= second if transposed else second <= first


def chunk(i, n=1):
    return slice(i * KEY_CHUNK, (i + n) * KEY_CHUNK)


def attend_kernel(meta, q_ref, kva_ref, kvb_ref, bounds_ref, *refs, first, last):
    rows = q_ref.shape[0]
    key_rows = kva_ref.shape[0]
    if last:
        acc_in, sum_in, o_ref, q_out_ref, acc_ref, sum_ref = refs
    elif first:
        acc_ref, sum_ref = refs
    else:
        acc_in, sum_in, acc_ref, sum_ref = refs
    if first:
        acc_ref[...] = jnp.zeros_like(acc_ref)
        sum_ref[...] = jnp.zeros_like(sum_ref)
    else:
        acc_ref[...] = acc_in[...]
        sum_ref[...] = sum_in[...]
    ones = jnp.ones((KEY_CHUNK, HEAD_WIDTH), bf16)

    def work(kv_ref, lanes, keys, queries, mask):
        key = jnp.concatenate([kv_ref[keys, :HEAD_WIDTH], lanes[keys, :]], axis=1)
        weight = jnp.exp2(dot_nt(q_ref[queries, :], key))
        if mask:
            weight = jnp.where(lower_mask(False), weight, 0.0)
        value = jnp.concatenate([kv_ref[keys, HEAD_WIDTH:], ones], axis=1)
        out = dot(weight.astype(bf16), value)
        acc_ref[queries, :] += out[:, :HEAD_WIDTH]
        sum_ref[queries, :] += out[:, HEAD_WIDTH:]

    for place, kv_ref in enumerate((kva_ref, kvb_ref)):
        key_start = meta[2 + place]
        diagonal = first and place == 0

        @pl.when(block_used(meta, key_start, key_rows, rows))
        def _():
            lanes = key_lanes(meta, key_start, key_rows, bounds_ref)
            for c in range(key_rows // KEY_CHUNK):
                if diagonal:
                    work(kv_ref, lanes, chunk(c), chunk(c), True)
                    if c + 1 < rows // KEY_CHUNK:
                        work(kv_ref, lanes, chunk(c), slice((c + 1) * KEY_CHUNK, rows), False)
                else:
                    work(kv_ref, lanes, chunk(c), slice(0, rows), False)

    if last:
        total = sum_ref[...]
        outcome = acc_ref[...] / total
        acc_ref[...] = outcome
        o_ref[...] = outcome.astype(bf16)
        lanes = lane_index(rows)
        extra = q_ref[:, HEAD_WIDTH:].astype(f32)
        for i, part in enumerate(split_parts(jnp.log2(total))):
            extra = jnp.where(lanes == LOG_LANE + i, -part.astype(f32), extra)
        q_out_ref[:, :HEAD_WIDTH] = q_ref[:, :HEAD_WIDTH]
        q_out_ref[:, HEAD_WIDTH:] = extra.astype(bf16)


def attend_stage(q, kv_a, kv_b, bounds, meta, carried, last):
    rows = q.shape[0]
    key_rows = kv_a.shape[0]
    q_heads = q.shape[1] // (2 * HEAD_WIDTH)
    group = q.shape[1] // kv_a.shape[1]
    width = q_heads * HEAD_WIDTH
    first = not carried
    wide = 2 * HEAD_WIDTH
    per_q = pl.BlockSpec((rows, wide), lambda j, m: (0, j))
    per_kv = pl.BlockSpec((key_rows, wide), lambda j, m: (0, j // group))
    per_out = pl.BlockSpec((rows, HEAD_WIDTH), lambda j, m: (0, j))
    table = pl.BlockSpec((8, HEAD_WIDTH), lambda j, m: (0, 0))
    running = jax.ShapeDtypeStruct((rows, width), f32)
    if last:
        out_specs = [per_out, per_q, per_out]
        out_shape = [jax.ShapeDtypeStruct((rows, width), bf16), jax.ShapeDtypeStruct(q.shape, bf16), running]
        scratch = [pltpu.VMEM((rows, HEAD_WIDTH), f32)]
        aliases = {5: 2}
    else:
        out_specs = [per_out, per_out]
        out_shape = [running, running]
        scratch = []
        aliases = {} if first else {5: 0, 6: 1}
    return pl.pallas_call(
        functools.partial(attend_kernel, first=first, last=last),
        grid_spec=pltpu.PrefetchScalarGridSpec(
            num_scalar_prefetch=1,
            grid=(q_heads,),
            in_specs=[per_q, per_kv, per_kv, table] + [per_out] * len(carried),
            out_specs=out_specs,
            scratch_shapes=scratch,
        ),
        out_shape=out_shape,
        input_output_aliases=aliases,
        compiler_params=WHOLE_VMEM,
        cost_estimate=SMALL,
        name="attend_stage",
    )(meta, q, kv_a, kv_b, bounds, *carried)


def delta_kernel(owners, *refs):
    *pieces, outcome_ref, out_ref = refs
    for i, piece in enumerate(pieces):

        @pl.when(pl.program_id(0) == i)
        def _():
            rows, width = piece.shape
            lanes = lane_index(rows)
            for j in range(width // HEAD_WIDTH):
                head = slice(j * HEAD_WIDTH, (j + 1) * HEAD_WIDTH)
                do = piece[:, head]
                delta = jnp.sum(do.astype(f32) * outcome_ref[:, head], axis=-1, keepdims=True)
                extra = jnp.zeros((rows, HEAD_WIDTH), f32)
                for k, part in enumerate(split_parts(delta)):
                    extra = jnp.where(lanes == k, -part.astype(f32), extra)
                start = 2 * j * HEAD_WIDTH
                out_ref[:, start : start + HEAD_WIDTH] = do
                out_ref[:, start + HEAD_WIDTH : start + 2 * HEAD_WIDTH] = extra.astype(bf16)


def with_delta(pieces, outcome):
    owners = jnp.stack([jnp.asarray(owner, jnp.int32) for unused, owner in pieces])
    rows, width = outcome.shape
    share = rows // len(pieces)
    whole = pl.BlockSpec((share, width), lambda i, m: (0, 0))
    return pl.pallas_call(
        delta_kernel,
        grid_spec=pltpu.PrefetchScalarGridSpec(
            num_scalar_prefetch=1,
            grid=(len(pieces),),
            in_specs=[whole] * len(pieces) + [pl.BlockSpec((share, width), lambda i, m: (m[i], 0))],
            out_specs=pl.BlockSpec((share, 2 * width), lambda i, m: (m[i], 0)),
        ),
        out_shape=jax.ShapeDtypeStruct((rows, 2 * width), bf16),
        compiler_params=WHOLE_VMEM,
        cost_estimate=SMALL,
        name="with_delta",
    )(owners, *[piece for piece, unused in pieces], outcome)


def assemble_kernel(places, *refs, count):
    blocks, out_ref = refs[:count], refs[-1]
    for i, block in enumerate(blocks):

        @pl.when(pl.program_id(0) == i)
        def _():
            out_ref[...] = block[...].astype(out_ref.dtype)


def assemble(entries, rows, kind, total=None, base=None):
    places = jnp.stack([jnp.asarray(place, jnp.int32) for unused, also, place in entries])
    width = entries[0][0].shape[1]
    count = len(entries)
    in_specs = [
        pl.BlockSpec((rows, width), lambda i, m, k=block: (k, 0)) for unused, block, also in entries
    ]
    args = [array for array, unused, also in entries]
    if base is not None:
        in_specs.append(pl.BlockSpec(memory_space=pl.ANY))
        args.append(base)
    return pl.pallas_call(
        functools.partial(assemble_kernel, count=count),
        grid_spec=pltpu.PrefetchScalarGridSpec(
            num_scalar_prefetch=1,
            grid=(count,),
            in_specs=in_specs,
            out_specs=pl.BlockSpec((rows, width), lambda i, m: (m[i], 0)),
        ),
        out_shape=jax.ShapeDtypeStruct((rows * (total or count), width), kind),
        input_output_aliases={} if base is None else {1 + count: 0},
        compiler_params=WHOLE_VMEM,
        cost_estimate=SMALL,
        name="assemble",
    )(places, *args)


def cut_kernel(in_ref, *outs, axis):
    start = 0
    for out_ref in outs:
        size = out_ref.shape[axis]
        part = in_ref[start : start + size, :] if axis == 0 else in_ref[:, start : start + size]
        out_ref[...] = part.astype(f32)
        start += size


def cut_up(array, shapes, axis):
    return pl.pallas_call(
        functools.partial(cut_kernel, axis=axis),
        out_shape=[jax.ShapeDtypeStruct(shape, f32) for shape in shapes],
        compiler_params=WHOLE_VMEM,
        cost_estimate=SMALL,
        name="cut_up",
    )(array)


def cut_columns(array, widths):
    return cut_up(array, [(array.shape[0], width) for width in widths], 1)


def cut_rows(array, heights):
    return cut_up(array, [(height, array.shape[1]) for height in heights], 0)


def attend_back_kernel(
    meta, q_ref, do_ref, kva_ref, kvb_ref, bounds_ref, *refs, first, group, diagonal
):
    if first:
        dq_ref, dkva_ref, dkvb_ref, dq_turned, sum_a, sum_b = refs
    else:
        dq_in, dq_ref, dkva_ref, dkvb_ref, dq_turned, sum_a, sum_b = refs
    rows = q_ref.shape[0]
    key_rows = kva_ref.shape[0]
    step = lax.rem(pl.program_id(0), group)
    dq_turned[...] = jnp.zeros_like(dq_turned)

    @pl.when(step == 0)
    def _():
        sum_a[...] = jnp.zeros_like(sum_a)
        sum_b[...] = jnp.zeros_like(sum_b)

    def work(kv_ref, total, lanes, ones, keys, queries, mask):
        key = kv_ref[keys, :HEAD_WIDTH]
        q = q_ref[queries, :]
        do = do_ref[queries, :]
        weight = jnp.exp2(dot_nt(jnp.concatenate([key, lanes[keys, :]], axis=1), q))
        if mask:
            weight = jnp.where(lower_mask(True), weight, 0.0)
        value = jnp.concatenate([kv_ref[keys, HEAD_WIDTH:], ones], axis=1)
        d_score = (weight * dot_nt(value, do)).astype(bf16)
        total[keys, HEAD_WIDTH:] += dot(weight.astype(bf16), do[:, :HEAD_WIDTH])
        total[keys, :HEAD_WIDTH] += dot(d_score, q[:, :HEAD_WIDTH])
        dq_turned[:, queries] += dot_tn(key, d_score)

    for place, (kv_ref, total) in enumerate(((kva_ref, sum_a), (kvb_ref, sum_b))):
        key_start = meta[2 + place]

        @pl.when(block_used(meta, key_start, key_rows, rows))
        def _():
            lanes = key_lanes(meta, key_start, key_rows, bounds_ref)
            ones = jnp.where(lane_index(KEY_CHUNK) < 3, 1.0, 0.0).astype(bf16)
            for c in range(key_rows // KEY_CHUNK):
                if diagonal and place == 0:
                    work(kv_ref, total, lanes, ones, chunk(c), chunk(c), True)
                    if c + 1 < rows // KEY_CHUNK:
                        later = slice((c + 1) * KEY_CHUNK, rows)
                        work(kv_ref, total, lanes, ones, chunk(c), later, False)
                else:
                    work(kv_ref, total, lanes, ones, chunk(c), slice(0, rows), False)

    turned = dq_turned[...].T
    dq_ref[...] = turned if first else dq_in[...] + turned

    @pl.when(step == group - 1)
    def _():
        dkva_ref[...] = sum_a[...]
        dkvb_ref[...] = sum_b[...].astype(bf16)


def attend_back(q, do, kv_a, kv_b, bounds, meta, dq, diagonal):
    rows = q.shape[0]
    key_rows = kv_a.shape[0]
    q_heads = q.shape[1] // (2 * HEAD_WIDTH)
    group = q.shape[1] // kv_a.shape[1]
    width = q_heads * HEAD_WIDTH
    first = dq is None
    wide = 2 * HEAD_WIDTH
    per_q = pl.BlockSpec((rows, wide), lambda j, m: (0, j))
    per_kv = pl.BlockSpec((key_rows, wide), lambda j, m: (0, j // group))
    per_out = pl.BlockSpec((rows, HEAD_WIDTH), lambda j, m: (0, j))
    table = pl.BlockSpec((8, HEAD_WIDTH), lambda j, m: (0, 0))
    return pl.pallas_call(
        functools.partial(attend_back_kernel, first=first, group=group, diagonal=diagonal),
        grid_spec=pltpu.PrefetchScalarGridSpec(
            num_scalar_prefetch=1,
            grid=(q_heads,),
            in_specs=[per_q, per_q, per_kv, per_kv, table] + ([] if first else [per_out]),
            out_specs=[per_out, per_kv, per_kv],
            scratch_shapes=[
                pltpu.VMEM((HEAD_WIDTH, rows), f32),
                pltpu.VMEM((key_rows, wide), f32),
                pltpu.VMEM((key_rows, wide), f32),
            ],
        ),
        out_shape=[
            jax.ShapeDtypeStruct((rows, width), f32),
            jax.ShapeDtypeStruct(kv_a.shape, f32),
            jax.ShapeDtypeStruct(kv_b.shape, bf16),
        ],
        input_output_aliases={} if first else {6: 0},
        compiler_params=WHOLE_VMEM,
        cost_estimate=SMALL,
        name="attend_back",
    )(meta, q, do, kv_a, kv_b, bounds, *(() if first else (dq,)))


def project_kernel(meta, base_ref, *refs, count, final):
    pieces, mine, other = refs[:count], refs[count : 2 * count], refs[2 * count : 3 * count]
    if final:
        gain_ref, share_ref, normed_ref = refs[3 * count :]
    else:
        (out_ref,) = refs[3 * count :]
    first_core = meta[0] == 0
    total = base_ref[...].astype(f32)
    for piece, mine_ref, other_ref in zip(pieces, mine, other):
        half = piece.shape[1] // 2
        low, high = piece[:, :half], piece[:, half:]
        total += dot(jnp.where(first_core, low, high), mine_ref[0])
        total += dot(jnp.where(first_core, high, low), other_ref[0])
    if final:
        inverse = lax.rsqrt(jnp.mean(total * total, axis=-1, keepdims=True) + EPSILON)
        normed_ref[...] = (total * inverse * gain_ref[...]).astype(bf16)

        @pl.when(pl.program_id(0) == meta[1])
        def _():
            share_ref[...] = total

    else:
        out_ref[...] = total


def project(base, pieces, w_mine, w_other, core, me, gain=None):
    meta = jnp.stack(
        [jnp.asarray(v, jnp.int32) for v in [core, me] + [owner for unused, owner in pieces]]
    )
    rows, width = base.shape
    n_head, half, unused = w_mine.shape
    count = len(pieces)
    final = gain is not None
    step = rows // n_head
    per_row = pl.BlockSpec((step, width), lambda i, m: (i, 0))
    per_piece = pl.BlockSpec((step, 2 * half), lambda i, m: (i, 0))
    weights = [
        pl.BlockSpec((1, half, width), lambda i, m, k=k: (m[2 + k], 0, 0)) for k in range(count)
    ]
    in_specs = [per_row] + [per_piece] * count + weights + weights
    args = [base] + [piece for piece, unused in pieces] + [w_mine] * count + [w_other] * count
    if final:
        in_specs.append(pl.BlockSpec((1, width), lambda i, m: (0, 0)))
        args.append(gain[None, :])
        out_specs = [pl.BlockSpec((step, width), lambda i, m: (0, 0)), per_row]
        out_shape = [
            jax.ShapeDtypeStruct((step, width), f32),
            jax.ShapeDtypeStruct((rows, width), bf16),
        ]
    else:
        out_specs = per_row
        out_shape = jax.ShapeDtypeStruct((rows, width), f32)
    return pl.pallas_call(
        functools.partial(project_kernel, count=count, final=final),
        grid_spec=pltpu.PrefetchScalarGridSpec(
            num_scalar_prefetch=1,
            grid=(rows // step,),
            in_specs=in_specs,
            out_specs=out_specs,
        ),
        out_shape=out_shape,
        compiler_params=WHOLE_VMEM,
        cost_estimate=SMALL,
        name="project",
    )(meta, *args)


def arranged_shapes(rows, width):
    return [
        jax.ShapeDtypeStruct((rows // 4, width), bf16),
        jax.ShapeDtypeStruct((rows // 4, width), bf16),
        jax.ShapeDtypeStruct((rows // 2, width), bf16),
    ]


def store_arranged(me, outs, share_y, share_x, half, value):
    along_x, along_y, stays = outs
    rows = value.shape[0]
    other_x = share_x ^ (me & 1)
    other_y = share_y ^ (me >> 1)

    def store(ref, place):
        ref[pl.ds(pl.multiple_of(place * rows, rows), rows), :] = value

    if half == 0:
        pl.when(other_x == 1)(lambda: store(along_x, other_y))
        pl.when(other_x == 0)(lambda: store(stays, other_y))
    else:
        pl.when(other_y == 1)(lambda: store(along_y, other_x))
        pl.when(other_y == 0)(lambda: store(stays, 2 + other_x))


def store_all_arranged(me, outs, value):
    rows = value.shape[0] // 8
    for i in range(8):
        block = value[i * rows : (i + 1) * rows, :]
        store_arranged(me, outs, i // 4, i // 2 % 2, i % 2, block)


def meet_kernel(stays_ref, x_ref, y_ref, mine_ref, to_y_ref, to_x_ref):
    rows = mine_ref.shape[0] // 2
    for start, got_ref, sent_ref in ((0, x_ref, to_y_ref), (2, y_ref, to_x_ref)):
        total = stays_ref[start * rows : (start + 2) * rows, :].astype(f32) + got_ref[...].astype(f32)
        mine_ref[start // 2 * rows : (start // 2 + 1) * rows, :] = total[:rows]
        sent_ref[...] = total[rows:].astype(bf16)


def meet(stays, from_x, from_y):
    rows, width = stays.shape
    return pl.pallas_call(
        meet_kernel,
        out_shape=[
            jax.ShapeDtypeStruct((rows // 2, width), f32),
            jax.ShapeDtypeStruct((rows // 4, width), bf16),
            jax.ShapeDtypeStruct((rows // 4, width), bf16),
        ],
        compiler_params=WHOLE_VMEM,
        cost_estimate=SMALL,
        name="meet",
    )(stays, from_x, from_y)


def share_sum(terms):
    first, *rest = terms
    total = first[...].astype(f32)
    if len(rest) == 2:
        return total + jnp.concatenate([part[...].astype(f32) for part in rest], axis=0)
    return total


def add_rows_kernel(base_ref, *refs):
    *terms, out_ref = refs
    out_ref[...] = (base_ref[...] + share_sum(terms)).astype(bf16)


def add_rows(base, terms):
    return pl.pallas_call(
        add_rows_kernel,
        out_shape=jax.ShapeDtypeStruct(base.shape, bf16),
        compiler_params=WHOLE_VMEM,
        cost_estimate=SMALL,
        name="add_rows",
    )(base, *terms)


def norm_backward(grad, x, gain):
    inverse = lax.rsqrt(jnp.mean(x * x, axis=-1, keepdims=True) + EPSILON)
    hat = x * inverse
    scaled = grad * gain
    back = inverse * (scaled - hat * jnp.mean(scaled * hat, axis=-1, keepdims=True))
    return back, jnp.sum(grad * hat, axis=0, keepdims=True)


def turn_kernel(meta, *refs, count):
    terms = refs[:count]
    hidden_ref, dy_ref, gain_ref, mine_ref, other_ref = refs[count : count + 5]
    out_ref, grad_ref, branch_ref, gain_grad_ref = refs[count + 5 :]

    @pl.when(pl.program_id(0) == 0)
    def _():
        back, gain_grad_ref[...] = norm_backward(
            share_sum(terms), hidden_ref[...], gain_ref[...]
        )
        total = dy_ref[...].astype(f32) + back
        grad_ref[...] = total
        branch_ref[...] = total.astype(bf16)

    half = mine_ref.shape[1]
    branch = branch_ref[...]
    mine = dot_nt(branch, mine_ref[0])
    other = dot_nt(branch, other_ref[0])
    first_core = meta[0] == 0
    out_ref[0, :, :half] = jnp.where(first_core, mine, other).astype(bf16)
    out_ref[0, :, half:] = jnp.where(first_core, other, mine).astype(bf16)


def turn(terms, hidden, dy, gain, w_mine, w_other, core, me):
    rows, width = hidden.shape
    n_head, half, unused = w_mine.shape
    meta = jnp.stack([jnp.asarray(v, jnp.int32) for v in (core, me)])

    def full(array):
        return pl.BlockSpec(array.shape, lambda i, m: (0, 0))

    weight = pl.BlockSpec((1, half, width), lambda i, m: (i ^ m[1], 0, 0))
    share = pl.BlockSpec((rows, width), lambda i, m: (0, 0))
    return pl.pallas_call(
        functools.partial(turn_kernel, count=len(terms)),
        grid_spec=pltpu.PrefetchScalarGridSpec(
            num_scalar_prefetch=1,
            grid=(n_head,),
            in_specs=[full(term) for term in terms]
            + [
                share,
                pl.BlockSpec((rows, width), lambda i, m: (m[1], 0)),
                pl.BlockSpec((1, width), lambda i, m: (0, 0)),
                weight,
                weight,
            ],
            out_specs=[
                pl.BlockSpec((1, rows, 2 * half), lambda i, m: (i, 0, 0)),
                share,
                share,
                pl.BlockSpec((1, width), lambda i, m: (0, 0)),
            ],
        ),
        out_shape=[
            jax.ShapeDtypeStruct((n_head, rows, 2 * half), bf16),
            jax.ShapeDtypeStruct((rows, width), f32),
            jax.ShapeDtypeStruct((rows, width), bf16),
            jax.ShapeDtypeStruct((1, width), f32),
        ],
        compiler_params=WHOLE_VMEM,
        cost_estimate=SMALL,
        name="turn",
    )(meta, *terms, hidden, dy, gain[None, :], w_mine, w_other)


def last_kernel(meta, *refs, count):
    terms = refs[:count]
    x_ref, grad_ref, gain_ref, rider_ref, out_ref = refs[count:]
    rows = x_ref.shape[0]
    back, unused = norm_backward(share_sum(terms), x_ref[...].astype(f32), gain_ref[...])
    out_ref[:rows, :] = (grad_ref[...] + back).astype(bf16)
    out_ref[rows:, :] = rider_ref[...]


def last(terms, tokens, hidden_grad, gain, rider, me):
    rows, width = hidden_grad.shape
    meta = jnp.asarray(me, jnp.int32)[None]

    def full(array):
        return pl.BlockSpec(array.shape, lambda i, m: (0, 0))

    out_rows = rows + rider.shape[0]
    return pl.pallas_call(
        functools.partial(last_kernel, count=len(terms)),
        grid_spec=pltpu.PrefetchScalarGridSpec(
            num_scalar_prefetch=1,
            grid=(1,),
            in_specs=[full(term) for term in terms]
            + [
                pl.BlockSpec((rows, width), lambda i, m: (m[0], 0)),
                full(hidden_grad),
                pl.BlockSpec((1, width), lambda i, m: (0, 0)),
                full(rider),
            ],
            out_specs=pl.BlockSpec((out_rows, width), lambda i, m: (0, 0)),
        ),
        out_shape=jax.ShapeDtypeStruct((out_rows, width), bf16),
        compiler_params=WHOLE_VMEM,
        cost_estimate=SMALL,
        name="last",
    )(meta, *terms, tokens, hidden_grad, gain[None, :], rider)


def feed_kernel(x_ref, gate_w_ref, up_w_ref, d_mixed_ref, mixed_ref, gate_ref, up_ref, sum_ref):
    x = x_ref[...]
    gate = dot(x, gate_w_ref[...])
    up = dot(x, up_w_ref[...])
    d_mixed = d_mixed_ref[...]
    sigmoid = 0.5 * jnp.tanh(0.5 * gate) + 0.5
    silu = gate * sigmoid
    mixed_ref[...] = (silu * up).astype(bf16)
    gate_low = (d_mixed * up * (sigmoid * (1.0 + gate * (1.0 - sigmoid)))).astype(bf16)
    up_low = (d_mixed * silu).astype(bf16)
    gate_ref[...] = gate_low
    up_ref[...] = up_low
    step = gate_low.shape[1]
    sum_ref[:, :step] = dot_tn(x, gate_low).astype(bf16)
    sum_ref[:, step:] = dot_tn(x, up_low).astype(bf16)


def feed(x, w_gate, w_up, d_mixed):
    rows, width = x.shape
    hidden = w_gate.shape[1]
    whole = pl.BlockSpec((rows, width), lambda i: (0, 0))
    weight = pl.BlockSpec((width, HIDDEN_STEP), lambda i: (0, i))
    act = pl.BlockSpec((rows, HIDDEN_STEP), lambda i: (0, i))
    return pl.pallas_call(
        feed_kernel,
        grid=(hidden // HIDDEN_STEP,),
        in_specs=[whole, weight, weight, act],
        out_specs=[act, act, act, pl.BlockSpec((width, 2 * HIDDEN_STEP), lambda i: (0, i))],
        out_shape=[jax.ShapeDtypeStruct((rows, hidden), bf16)] * 3
        + [jax.ShapeDtypeStruct((width, 2 * hidden), bf16)],
        compiler_params=WHOLE_VMEM,
        cost_estimate=SMALL,
        name="feed",
    )(x, w_gate, w_up, d_mixed)


def split_kernel(sum_ref, gate_ref, up_ref):
    step = gate_ref.shape[1]
    gate_ref[...] = sum_ref[:, :step].astype(f32)
    up_ref[...] = sum_ref[:, step:].astype(f32)


def split_gate_up(sums):
    rows, width = sums.shape
    out = pl.BlockSpec((rows, HIDDEN_STEP), lambda i: (0, i))
    return pl.pallas_call(
        split_kernel,
        grid=(width // (2 * HIDDEN_STEP),),
        in_specs=[pl.BlockSpec((rows, 2 * HIDDEN_STEP), lambda i: (0, i))],
        out_specs=[out, out],
        out_shape=[jax.ShapeDtypeStruct((rows, width // 2), f32)] * 2,
        compiler_params=WHOLE_VMEM,
        cost_estimate=SMALL,
        name="split_gate_up",
    )(sums)


def products_kernel(meta, *refs, count, turned, arranged):
    lefts, rights, outs = refs[:count], refs[count : 2 * count], refs[2 * count :]
    total = 0.0
    for left, right in zip(lefts, rights):
        total += (dot_nt if turned else dot)(left[...], right[...])
    if arranged:
        store_all_arranged(meta[0], outs, total.astype(bf16))
    else:
        outs[0][...] = total.astype(bf16)


def products(lefts, rights, turned, me, arranged):
    meta = jnp.asarray(me, jnp.int32)[None]
    rows, depth = lefts[0].shape
    width = rights[0].shape[0 if turned else 1]
    step = width // 4
    whole = pl.BlockSpec((rows, depth), lambda i, m: (0, 0))
    if turned:
        right = pl.BlockSpec((step, depth), lambda i, m: (i, 0))
    else:
        right = pl.BlockSpec((depth, step), lambda i, m: (0, i))
    shapes = arranged_shapes(rows, width) if arranged else [jax.ShapeDtypeStruct((rows, width), bf16)]
    return pl.pallas_call(
        functools.partial(products_kernel, count=len(lefts), turned=turned, arranged=arranged),
        grid_spec=pltpu.PrefetchScalarGridSpec(
            num_scalar_prefetch=1,
            grid=(width // step,),
            in_specs=[whole] * len(lefts) + [right] * len(lefts),
            out_specs=[pl.BlockSpec((v.shape[0], step), lambda i, m: (0, i)) for v in shapes],
        ),
        out_shape=shapes,
        compiler_params=WHOLE_VMEM,
        cost_estimate=SMALL,
        name="products",
    )(meta, *lefts, *rights)


def column_sums_kernel(owners, mixed_ref, o_ref, dy_ref, *refs):
    *pieces, out_ref, branch = refs
    hidden = mixed_ref.shape[1]
    for i, piece in enumerate(pieces):
        rows = piece.shape[0]
        branch[pl.ds(pl.multiple_of(owners[i] * rows, rows), rows), :] = piece[...]
    out_ref[0, :hidden, :] = dot_tn(mixed_ref[...], dy_ref[...]).astype(bf16)
    out_ref[0, hidden:, :] = dot_tn(o_ref[...], branch[...]).astype(bf16)


def column_sums(mixed, o_low, dy, pieces, shares):
    owners = jnp.stack([jnp.asarray(owner, jnp.int32) for unused, owner in pieces])
    rows, width = dy.shape
    share = width // shares
    out_rows = mixed.shape[1] + o_low.shape[1]
    return pl.pallas_call(
        column_sums_kernel,
        grid_spec=pltpu.PrefetchScalarGridSpec(
            num_scalar_prefetch=1,
            grid=(shares,),
            in_specs=[
                pl.BlockSpec(mixed.shape, lambda i, m: (0, 0)),
                pl.BlockSpec(o_low.shape, lambda i, m: (0, 0)),
                pl.BlockSpec((rows, share), lambda i, m: (0, i)),
            ]
            + [
                pl.BlockSpec((piece.shape[0], share), lambda i, m: (0, i))
                for piece, unused in pieces
            ],
            out_specs=pl.BlockSpec((1, out_rows, share), lambda i, m: (i, 0, 0)),
            scratch_shapes=[pltpu.VMEM((rows, share), bf16)],
        ),
        out_shape=jax.ShapeDtypeStruct((shares, out_rows, share), bf16),
        compiler_params=WHOLE_VMEM,
        cost_estimate=SMALL,
        name="column_sums",
    )(owners, mixed, o_low, dy, *[piece for piece, unused in pieces])


def pass_on_kernel(part_ref, theirs_ref, *refs):
    *arrived, low_ref, high_ref = refs
    half = low_ref.shape[0]
    for i, out_ref in enumerate((low_ref, high_ref)):
        rows = slice(i * half, (i + 1) * half)
        total = part_ref[rows, :] + theirs_ref[rows, :].astype(f32)
        if arrived:
            total += arrived[i][...].astype(f32)
        out_ref[...] = total.astype(bf16)


def pass_on(part, theirs, *arrived):
    rows, width = part.shape
    return pl.pallas_call(
        pass_on_kernel,
        out_shape=[jax.ShapeDtypeStruct((rows // 2, width), bf16)] * 2,
        compiler_params=WHOLE_VMEM,
        cost_estimate=SMALL,
        name="pass_on",
    )(part, theirs, *arrived)


def leave_kernel(
    meta,
    x_ref,
    q_ref,
    dkv_ref,
    theirs_ref,
    first_ref,
    second_ref,
    raw_ref,
    key_gain_ref,
    cos_ref,
    sin_ref,
    q_w_ref,
    key_w_ref,
    value_w_ref,
    key_ref,
    value_ref,
    gain_grad_ref,
    norm_grad_ref,
    *outs,
    arranged,
):
    @pl.when(pl.program_id(0) == 0)
    def _():
        gain_grad_ref[...] = jnp.zeros_like(gain_grad_ref)
        norm_grad_ref[...] = jnp.zeros_like(norm_grad_ref)

    arrived = jnp.where(pl.program_id(0) == 0, first_ref[...], second_ref[...])
    dkv = dkv_ref[...] + theirs_ref[...].astype(f32) + arrived.astype(f32)
    for j in range(key_ref.shape[1] // HEAD_WIDTH):
        head = slice(j * HEAD_WIDTH, (j + 1) * HEAD_WIDTH)
        start = 2 * j * HEAD_WIDTH
        grad, gain_grad = head_backward(
            raw_ref[:, head],
            dkv[:, start : start + HEAD_WIDTH] * (1.0 / LOG2E),
            key_gain_ref[...],
            cos_ref[...],
            sin_ref[...],
        )
        key_ref[:, head] = grad
        value_ref[:, head] = dkv[:, start + HEAD_WIDTH : start + 2 * HEAD_WIDTH].astype(bf16)
        gain_grad_ref[...] += gain_grad
    total = dot_nt(q_ref[...], q_w_ref[...])
    total += dot_nt(key_ref[...], key_w_ref[...])
    total += dot_nt(value_ref[...], value_w_ref[...])
    result = total.astype(bf16)
    if arranged:
        block = result.shape[0] // 4
        for i in range(4):
            store_arranged(
                meta[0],
                outs,
                pl.program_id(0),
                i // 2,
                i % 2,
                result[i * block : (i + 1) * block, :],
            )
    else:
        outs[0][...] = result
    x = x_ref[...].astype(f32)
    hat = x * lax.rsqrt(jnp.mean(x * x, axis=-1, keepdims=True) + EPSILON)
    norm_grad_ref[...] += jnp.sum(total * hat, axis=0, keepdims=True)


def leave(tokens, q_grad, dkv, theirs, arrived, key_raw, key_gain, cosine, sine, weights, me, arranged):
    meta = jnp.asarray(me, jnp.int32)[None]
    rows, width = tokens.shape
    kv_width = key_raw.shape[1]
    step = rows // 2

    def per_row(array):
        return pl.BlockSpec((step, array.shape[1]), lambda i, m: (i, 0))

    def full(array):
        return pl.BlockSpec(array.shape, lambda i, m: (0, 0))

    key_gain = key_gain[None, :]
    if arranged:
        shapes = arranged_shapes(rows, width)
        out_specs = [full(v) for v in shapes]
    else:
        shapes = [jax.ShapeDtypeStruct((rows, width), bf16)]
        out_specs = [per_row(shapes[0])]
    return pl.pallas_call(
        functools.partial(leave_kernel, arranged=arranged),
        grid_spec=pltpu.PrefetchScalarGridSpec(
            num_scalar_prefetch=1,
            grid=(2,),
            in_specs=[per_row(v) for v in (tokens, q_grad, dkv, theirs)]
            + [full(v) for v in arrived]
            + [per_row(key_raw), full(key_gain), per_row(cosine), per_row(sine)]
            + [full(v) for v in weights],
            out_specs=[
                per_row(key_raw),
                per_row(key_raw),
                pl.BlockSpec((1, HEAD_WIDTH), lambda i, m: (0, 0)),
                pl.BlockSpec((1, width), lambda i, m: (0, 0)),
            ]
            + out_specs,
        ),
        out_shape=[
            jax.ShapeDtypeStruct((rows, kv_width), bf16),
            jax.ShapeDtypeStruct((rows, kv_width), bf16),
            jax.ShapeDtypeStruct((1, HEAD_WIDTH), f32),
            jax.ShapeDtypeStruct((1, width), f32),
        ]
        + shapes,
        compiler_params=WHOLE_VMEM,
        cost_estimate=SMALL,
        name="leave",
    )(meta, tokens, q_grad, dkv, theirs, *arrived, key_raw, key_gain, cosine, sine, *weights)


def attn_sums_kernel(x_ref, q_ref, k_ref, v_ref, out_ref):
    x = x_ref[...]
    start = 0
    for ref in (q_ref, k_ref, v_ref):
        out_ref[:, start : start + ref.shape[1]] = dot_tn(x, ref[...]).astype(bf16)
        start += ref.shape[1]


def attn_sums(x, query, key, value):
    rows, width = x.shape
    step = width // 8
    out_width = query.shape[1] + key.shape[1] + value.shape[1]

    def full(array):
        return pl.BlockSpec(array.shape, lambda i: (0, 0))

    return pl.pallas_call(
        attn_sums_kernel,
        grid=(width // step,),
        in_specs=[pl.BlockSpec((rows, step), lambda i: (0, i)), full(query), full(key), full(value)],
        out_specs=pl.BlockSpec((step, out_width), lambda i: (i, 0)),
        out_shape=jax.ShapeDtypeStruct((width, out_width), bf16),
        compiler_params=WHOLE_VMEM,
        cost_estimate=SMALL,
        name="attn_sums",
    )(x, query, key, value)


def after(values):
    return lax.optimization_barrier(values)


def pick(array, index):
    return lax.dynamic_index_in_dim(array, index, 0, keepdims=False)


def solution(mesh):
    n_seq = mesh.shape["seq"]
    n_head = mesh.shape["head"]
    n_chip = n_seq // 2

    def swap_core(value):
        return lax.ppermute(value, "seq", [(i, i ^ 1) for i in range(n_seq)])

    def to_next(value):
        return lax.ppermute(value, "seq", [(i, i + 2) for i in range(n_seq - 2)])

    def to_previous(value):
        return lax.ppermute(value, "seq", [(i + 2, i) for i in range(n_seq - 2)])

    def across(value, bits):
        return lax.ppermute(value, "head", [(i, i ^ bits) for i in range(n_head)])

    def gather_steps(value):
        me = lax.axis_index("head")
        if n_head != 4:
            every = yield lax.all_gather(value, "head", axis=0)
            return [(every[i], i) for i in range(n_head)]
        half = value.shape[0] // 2
        by_x, by_y = yield across(value, 1), across(value, 2)
        low, high = yield across(by_x[:half], 2), across(by_y[half:], 1)
        far = jnp.concatenate([low, high], axis=0)
        return [(value, me), (by_x, me ^ 1), (by_y, me ^ 2), (far, me ^ 3)]

    def rider_entries(value, count):
        me = lax.axis_index("head")
        half = count // 2
        if n_head != 4:
            every = yield lax.all_gather(value, "head", axis=0)
            entries = [(every[i], k, 2 * i + k) for i in range(n_head) for k in range(2)]
            return entries, [every[i, count:] for i in range(n_head)]
        by_x, by_y = yield across(value, 1), across(value, 2)
        low, high = yield across(by_x[:half], 2), across(by_y[half:], 1)
        owners = ((value, me), (by_x, me ^ 1), (by_y, me ^ 2))
        entries = [(array, k, 2 * owner + k) for array, owner in owners for k in range(2)]
        entries += [(low, 0, 2 * (me ^ 3)), (high, 0, 2 * (me ^ 3) + 1)]
        return entries, [value[count:], by_x[count:], by_y[count:], high[half:]]

    def scatter_steps(value):
        if n_head != 4:
            total = yield lax.psum_scatter(value[0], "head", scatter_dimension=0, tiled=True)
            return (total,)
        along_x, along_y, stays = value
        from_x, from_y = yield across(along_x, 1), across(along_y, 2)
        mine, to_y, to_x = meet(stays, from_x, from_y)
        first, second = yield across(to_y, 2), across(to_x, 1)
        return mine, first, second

    def run_steps(steps, works=()):
        works = list(works)
        made = []
        arrived = next(steps)
        while True:
            if works:
                arrived, done = after((arrived, works.pop(0)()))
                made.append(done)
            try:
                arrived = steps.send(arrived)
            except StopIteration as stop:
                return stop.value, made + [work() for work in works]

    def end_steps(steps, arrived):
        try:
            steps.send(arrived)
        except StopIteration as stop:
            return stop.value

    def exchange_head(value):
        me = lax.axis_index("head")
        if n_head == 4:
            return [(value[0], me)] + [(across(value[i], i), me ^ i) for i in (3, 1, 2)]
        ordered = jnp.stack([pick(value, i ^ me) for i in range(n_head)])
        got = lax.all_to_all(ordered, "head", 0, 0)
        return [(got[i], i) for i in range(n_head)]

    def body(
        tokens,
        lengths,
        norm1_gain,
        w_query,
        key_matrix,
        value_matrix,
        query_gain,
        key_gain,
        w_output,
        norm2_gain,
        w_gate,
        w_up,
        w_down,
        cotangent,
    ):
        rows = tokens.shape[0]
        share = rows // n_head
        seq_index = lax.axis_index("seq")
        head_index = lax.axis_index("head")
        chip, core = seq_index // 2, seq_index % 2
        cut = n_head == 4

        index = seq_index * rows + jnp.arange(rows, dtype=jnp.int32)
        begin = locate(index, lengths)
        cosine, sine = rotary(index - begin)
        ends = jnp.cumsum(lengths)
        n_lengths = lengths.shape[0]
        bounds = jnp.zeros((8, HEAD_WIDTH), jnp.int32).at[0].set(2**30)
        bounds = bounds.at[0, :n_lengths].set(ends - lengths).at[1, :n_lengths].set(ends)

        def stage_meta(stage):
            source = 2 * (chip - stage)
            return jnp.stack(
                [seq_index * rows, begin[0], (source + core) * rows, (source + 1 - core) * rows]
            ).astype(jnp.int32)

        metas = [stage_meta(stage) for stage in range(n_chip)]

        first_in, key_raw, current = enter(
            tokens, norm1_gain, key_matrix, value_matrix, key_gain, cosine, sine
        )
        sibling = swap_core(current)
        following = to_next(current)

        half_rows = w_output.shape[0] // 2
        w_late, unused = after((w_output, current))
        w_half = lax.dynamic_slice_in_dim(w_late, core * half_rows, half_rows, 0)
        w_mine = lax.all_gather(w_half, "head", axis=0)

        query_raw = dot(first_in, w_query)
        q_wide = query_prep(metas[0], query_raw, query_gain, cosine, sine, bounds)
        following, q_wide = after((following, q_wide))

        blocks = []
        carried = ()
        for stage in range(n_chip):
            blocks.append((current, sibling))
            if stage + 2 < n_chip:
                current = following
                sibling = swap_core(current)
                following = to_next(current)
            carried = attend_stage(
                q_wide, *blocks[stage], bounds, metas[stage], carried, stage == n_chip - 1
            )
            if stage == 0:
                dy, carried = after((cotangent, carried))
                d_mixed = dot_nt(dy, w_down)
                carried, d_mixed = after((carried, d_mixed))
            if stage + 3 < n_chip:
                following, carried = after((following, carried))
            if stage + 2 == n_chip:
                current, carried = after((following, carried))
                sibling = swap_core(current)
                w_mine, sibling, carried = after((w_mine, sibling, carried))
                w_other = swap_core(w_mine)
        o_low, q_back, outcome = carried

        steps = gather_steps(o_low)
        arrived = next(steps)
        base = tokens
        if n_head == 4:
            base = project(base, [(o_low, head_index)], w_mine, w_other, core, head_index)
            arrived, base = after((arrived, base))
            far = steps.send(arrived)
            pieces = [(arrived[0], head_index ^ 1), (arrived[1], head_index ^ 2)]
            base = project(base, pieces, w_mine, w_other, core, head_index)
            arrived, base = after((far, base))
        try:
            steps.send(arrived)
        except StopIteration as stop:
            pieces = stop.value[3:] if n_head == 4 else stop.value
        my_hidden, second_in = project(
            base, pieces, w_mine, w_other, core, head_index, norm2_gain
        )
        mixed_low, gate_low, up_low, gate_up_sum = feed(second_in, w_gate, w_up, d_mixed)

        def scatter_seq(value, tiled):
            return lax.psum_scatter(value, "seq", scatter_dimension=0, tiled=tiled)

        grad_gate_up = scatter_seq(gate_up_sum, True)

        terms, (down_part,) = run_steps(
            scatter_steps(products((gate_low, up_low), (w_gate, w_up), True, head_index, cut)),
            (lambda: products((mixed_low,), (w_down,), False, head_index, cut),),
        )
        do_pieces, hidden_grad, my_branch, grad_norm2 = turn(
            terms, my_hidden, cotangent, norm2_gain, w_mine, w_other, core, head_index
        )
        do_wide = with_delta(exchange_head(do_pieces), outcome)
        down_part, my_branch, do_wide = after((down_part, my_branch, do_wide))

        dq = None
        parts = []
        moving = []
        landed = []
        hops = 0

        def hop_piece():
            if not moving:
                return None
            value = moving.pop(0)
            return lambda: to_previous(value)

        def stage_work(stage):
            return lambda: attend_back(
                q_back, do_wide, *blocks[stage], bounds, metas[stage], dq, stage == 0
            )

        def next_hop():
            nonlocal dq, hops
            if hops < n_chip - 1 and len(parts) > hops and len(landed) == (2 if hops else 0):
                sent, dq = after((pass_on(*parts[hops], *landed), dq))
                landed.clear()
                moving.extend(sent)
                hops += 1

        branch_steps = gather_steps(my_branch)
        (dq, dkv_a, dkv_b), got_branch = after(
            (stage_work(n_chip - 1)(), next(branch_steps))
        )
        theirs, dq = after((swap_core(dkv_b), dq))
        parts.append((dkv_a, theirs))
        next_hop()
        flying = hop_piece()()
        if cut:
            got_branch = branch_steps.send(got_branch)
        (dq, dkv_a, dkv_b), got_branch, flying = after(
            (stage_work(n_chip - 2)(), got_branch, flying)
        )
        branch_pieces = end_steps(branch_steps, got_branch)
        landed.append(flying)
        parts.append((dkv_a, swap_core(dkv_b)))
        flying = hop_piece()()
        column_sum = column_sums(mixed_low, o_low, cotangent, branch_pieces, n_seq)
        dkv_a, theirs = parts[1]
        column_sum, flying, theirs, dq = after((column_sum, flying, theirs, dq))
        parts[1] = (dkv_a, theirs)
        landed.append(flying)
        grad_gate_up, column_sum, dq, landed[:] = after(
            (grad_gate_up, column_sum, dq, list(landed))
        )
        grad_columns = scatter_seq(column_sum, False)
        next_hop()
        down_part, dq = after((down_part, dq))
        mixed_steps = scatter_steps(down_part)
        got_mixed = next(mixed_steps)
        for stage in reversed(range(n_chip - 2)):
            if cut and stage == n_chip - 4:
                got_mixed = mixed_steps.send(got_mixed)
            hop = hop_piece()
            flying = None if hop is None else hop()
            (dq, dkv_a, dkv_b), got_mixed, flying = after((stage_work(stage)(), got_mixed, flying))
            if hop is not None:
                landed.append(flying)
            parts.append((dkv_a, swap_core(dkv_b)))
            next_hop()
        my_mixed = add_rows(my_hidden, end_steps(mixed_steps, got_mixed))
        mixed_steps = gather_steps(my_mixed)
        got_mixed = next(mixed_steps)
        query_grad, grad_qgain = head_back(query_raw, dq, query_gain, cosine, sine, SCORE_SCALE, 1)
        grad_gate_up = split_gate_up(grad_gate_up)
        query_grad, grad_gate_up = after((query_grad, grad_gate_up))
        while hops < n_chip - 1:
            while len(landed) < 2:
                landed.append(hop_piece()())
            next_hop()
        flying = [hop_piece()() for unused in range(2 - len(landed))]
        if cut:
            flying[0], got_mixed, query_grad = after((flying[0], got_mixed, query_grad))
            got_mixed = mixed_steps.send(got_mixed)
        flying, got_mixed, query_grad = after((flying, got_mixed, query_grad))
        landed = (*landed, *flying)
        mixed_pieces = end_steps(mixed_steps, got_mixed)
        key_grad, value_grad, grad_kgain, grad_norm1, *first_part = leave(
            tokens,
            query_grad,
            *parts[-1],
            landed,
            key_raw,
            key_gain,
            cosine,
            sine,
            (w_query, key_matrix, value_matrix),
            head_index,
            cut,
        )
        gains = jnp.concatenate([grad_norm1[0], grad_norm2[0], grad_qgain[0], grad_kgain[0]])
        gains = gains.reshape(-1, HEAD_WIDTH)

        def sum_seq(total, bits):
            for bit in bits:
                total = total + lax.ppermute(total, "seq", [(i, i ^ bit) for i in range(n_seq)])
            return total

        bits = [1 << k for k in range(n_seq.bit_length() - 1)]
        steps = scatter_steps(first_part)
        got = next(steps)
        attn_sum = attn_sums(first_in, query_grad, key_grad, value_grad)
        gains = sum_seq(gains, bits[:1])
        gains, attn_sum = after((gains, attn_sum))
        got, gains, attn_sum = after((got, gains, attn_sum))
        if cut:
            got = steps.send(got)
        grad_columns, attn_sum = after((grad_columns, attn_sum))
        grad_attn = scatter_seq(attn_sum, True)
        grad_query, grad_key, grad_value = cut_columns(
            grad_attn, (query_grad.shape[1], key_grad.shape[1], value_grad.shape[1])
        )
        got, gains = after((got, sum_seq(gains, bits[1:])))
        terms = end_steps(steps, got)

        width = tokens.shape[1]
        n_gains = gains.size
        gain_rows = -(-n_gains // width)
        flat = jnp.pad(gains.reshape(-1), (0, gain_rows * width - n_gains))
        high = lax.reduce_precision(flat, 8, 7)
        middle = lax.reduce_precision(flat - high, 8, 7)
        rider = jnp.concatenate([high, middle, flat - high - middle]).astype(bf16)
        rider = rider.reshape(3 * gain_rows, width)
        rider = jnp.pad(rider, ((0, 32 - rider.shape[0]), (0, 0)))
        my_tokens_grad = last(terms, tokens, hidden_grad, norm1_gain, rider, head_index)
        steps = rider_entries(my_tokens_grad, share)
        got = next(steps)
        mixed = assemble([(piece, 0, owner) for piece, owner in mixed_pieces], share, bf16)
        grad_down, grad_output = cut_rows(grad_columns, (w_gate.shape[1], o_low.shape[1]))
        got, mixed, grad_down, grad_output = after((got, mixed, grad_down, grad_output))
        if cut:
            got = steps.send(got)
        entries, gain_pieces = end_steps(steps, got)
        near = len(entries) - 2
        grad_tokens = assemble(entries[:near], share // 2, f32, len(entries))
        grad_tokens = assemble(entries[near:], share // 2, f32, len(entries), grad_tokens)
        gains = sum(part[: 3 * gain_rows].astype(f32) for part in gain_pieces)
        gains = jnp.sum(gains.reshape(3, -1), axis=0)
        grad_norm1, grad_norm2 = gains[:width], gains[width : 2 * width]
        grad_qgain = gains[2 * width : 2 * width + HEAD_WIDTH]
        grad_kgain = gains[2 * width + HEAD_WIDTH : n_gains]
        grad_gate, grad_up = grad_gate_up
        return (
            mixed,
            grad_tokens,
            grad_norm1,
            grad_query,
            grad_key,
            grad_value,
            grad_qgain,
            grad_kgain,
            grad_output,
            grad_norm2,
            grad_gate,
            grad_up,
            grad_down,
        )

    in_specs = (
        P("seq", None),
        P(),
        P(),
        P(None, "head"),
        P(None, "head"),
        P(None, "head"),
        P(),
        P(),
        P("head", None),
        P(),
        P(None, "head"),
        P(None, "head"),
        P("head", None),
        P("seq", None),
    )
    out_specs = (
        P("seq", None),
        P("seq", None),
        P(),
        P("seq", "head"),
        P("seq", "head"),
        P("seq", "head"),
        P(),
        P(),
        P("head", "seq"),
        P(),
        P("seq", "head"),
        P("seq", "head"),
        P("head", "seq"),
    )
    return jax.shard_map(body, mesh=mesh, in_specs=in_specs, out_specs=out_specs, check_vma=False)
```

```python
import functools
import math

import jax
import jax.numpy as jnp
from jax import lax
from jax.experimental import pallas as pl
from jax.experimental.pallas import tpu as pltpu
from jax.sharding import PartitionSpec as P

HEAD_WIDTH = 128
EPSILON = 1e-06
ROPE_BASE = 1000000.0
LOG2E = math.log2(math.e)
SCORE_SCALE = 1.0 / math.sqrt(HEAD_WIDTH)
SCORE_SCALE_2 = LOG2E / math.sqrt(HEAD_WIDTH)
KEY_CHUNK = 256
HIDDEN_STEP = 256
FAR = 512.0
LOG_LANE = 64
MIB = 2**20
SMALL = pl.CostEstimate(flops=1, bytes_accessed=1, transcendentals=0)
WHOLE_VMEM = pltpu.CompilerParams(vmem_limit_bytes=60 * MIB)

f32 = jnp.float32
bf16 = jnp.bfloat16
NT = (((1,), (1,)), ((), ()))
TN = (((0,), (0,)), ((), ()))


def dot(left, right):
    return jnp.dot(left, right, preferred_element_type=f32)


def dot_nt(left, right):
    return lax.dot_general(left, right, NT, preferred_element_type=f32)


def dot_tn(left, right):
    return lax.dot_general(left, right, TN, preferred_element_type=f32)


def locate(index, lengths):
    ends = jnp.cumsum(lengths)
    starts = ends - lengths
    segment = jnp.sum((index[:, None] >= ends[None, :]).astype(jnp.int32), axis=1)
    chosen = segment[:, None] == jnp.arange(lengths.shape[0], dtype=jnp.int32)[None, :]
    return jnp.sum(jnp.where(chosen, starts[None, :], 0), axis=1)


def rotary(position):
    half = HEAD_WIDTH // 2
    freq = jnp.exp(jnp.arange(half, dtype=f32) * (-2.0 * math.log(ROPE_BASE) / HEAD_WIDTH))
    angle = position.astype(f32)[:, None] * freq[None, :]
    cosine = jnp.cos(angle)
    sine = jnp.sin(angle)
    return (
        jnp.concatenate([cosine, cosine], axis=1),
        jnp.concatenate([-sine, sine], axis=1),
    )


def lane_index(rows):
    return lax.broadcasted_iota(jnp.int32, (rows, HEAD_WIDTH), 1)


def row_index(rows):
    return lax.broadcasted_iota(jnp.int32, (rows, HEAD_WIDTH), 0)


def in_segment(index, bounds_ref):
    return (index >= bounds_ref[0:1, :]) & (index < bounds_ref[1:2, :])


def split_parts(value):
    high = value.astype(bf16)
    rest = value - high.astype(f32)
    middle = rest.astype(bf16)
    return high, middle, (rest - middle.astype(f32)).astype(bf16)


def normed(raw, gain, cosine, sine):
    inverse = lax.rsqrt(jnp.mean(raw * raw, axis=-1, keepdims=True) + EPSILON)
    scaled = raw * inverse * gain
    return scaled * cosine + pltpu.roll(scaled, HEAD_WIDTH // 2, 1) * sine


def enter_kernel(
    x_ref, gain_ref, key_w_ref, value_w_ref, key_gain_ref, cos_ref, sin_ref, in_ref, raw_ref, kv_ref
):
    x = x_ref[...].astype(f32)
    inverse = lax.rsqrt(jnp.mean(x * x, axis=-1, keepdims=True) + EPSILON)
    first_in = (x * inverse * gain_ref[...]).astype(bf16)
    in_ref[...] = first_in
    raw = dot(first_in, key_w_ref[...])
    raw_ref[...] = raw
    value = dot(first_in, value_w_ref[...]).astype(bf16)
    for j in range(raw.shape[1] // HEAD_WIDTH):
        head = slice(j * HEAD_WIDTH, (j + 1) * HEAD_WIDTH)
        key = normed(raw[:, head], key_gain_ref[...], cos_ref[...], sin_ref[...])
        start = 2 * j * HEAD_WIDTH
        kv_ref[:, start : start + HEAD_WIDTH] = key.astype(bf16)
        kv_ref[:, start + HEAD_WIDTH : start + 2 * HEAD_WIDTH] = value[:, head]


def enter(tokens, gain, key_w, value_w, key_gain, cosine, sine):
    rows, width = tokens.shape
    kv_width = key_w.shape[1]
    step = rows // 3 if rows % 768 == 0 else rows
    table = pl.BlockSpec((step, HEAD_WIDTH), lambda i: (i, 0))
    weight = pl.BlockSpec((width, kv_width), lambda i: (0, 0))
    return pl.pallas_call(
        enter_kernel,
        grid=(rows // step,),
        in_specs=[
            pl.BlockSpec((step, width), lambda i: (i, 0)),
            pl.BlockSpec((1, width), lambda i: (0, 0)),
            weight,
            weight,
            pl.BlockSpec((1, HEAD_WIDTH), lambda i: (0, 0)),
            table,
            table,
        ],
        out_specs=[
            pl.BlockSpec((step, width), lambda i: (i, 0)),
            pl.BlockSpec((step, kv_width), lambda i: (i, 0)),
            pl.BlockSpec((step, 2 * kv_width), lambda i: (i, 0)),
        ],
        out_shape=[
            jax.ShapeDtypeStruct((rows, width), bf16),
            jax.ShapeDtypeStruct((rows, kv_width), f32),
            jax.ShapeDtypeStruct((rows, 2 * kv_width), bf16),
        ],
        compiler_params=WHOLE_VMEM,
        cost_estimate=SMALL,
        name="enter",
    )(tokens, gain[None, :], key_w, value_w, key_gain[None, :], cosine, sine)


def query_prep_kernel(meta, raw_ref, gain_ref, cos_ref, sin_ref, bounds_ref, out_ref):
    rows = raw_ref.shape[0]
    query = normed(raw_ref[...], gain_ref[...], cos_ref[...], sin_ref[...])
    out_ref[:, :HEAD_WIDTH] = (query * SCORE_SCALE_2).astype(bf16)
    inside = in_segment(meta[0] + row_index(rows), bounds_ref)
    free = inside | (lane_index(rows) >= LOG_LANE)
    out_ref[:, HEAD_WIDTH:] = jnp.where(free, 0.0, -FAR).astype(bf16)


def query_prep(meta, raw, gain, cosine, sine, bounds):
    rows, width = raw.shape
    table = pl.BlockSpec((rows, HEAD_WIDTH), lambda j, m: (0, 0))
    return pl.pallas_call(
        query_prep_kernel,
        grid_spec=pltpu.PrefetchScalarGridSpec(
            num_scalar_prefetch=1,
            grid=(width // HEAD_WIDTH,),
            in_specs=[
                pl.BlockSpec((rows, HEAD_WIDTH), lambda j, m: (0, j)),
                pl.BlockSpec((1, HEAD_WIDTH), lambda j, m: (0, 0)),
                table,
                table,
                pl.BlockSpec((8, HEAD_WIDTH), lambda j, m: (0, 0)),
            ],
            out_specs=pl.BlockSpec((rows, 2 * HEAD_WIDTH), lambda j, m: (0, j)),
        ),
        out_shape=jax.ShapeDtypeStruct((rows, 2 * width), bf16),
        compiler_params=WHOLE_VMEM,
        cost_estimate=SMALL,
        name="query_prep",
    )(meta, raw, gain[None, :], cosine, sine, bounds)


def head_backward(raw, grad, gain, cosine, sine):
    inverse = lax.rsqrt(jnp.mean(raw * raw, axis=-1, keepdims=True) + EPSILON)
    hat = raw * inverse
    back = grad * cosine - pltpu.roll(grad, HEAD_WIDTH // 2, 1) * sine
    gain_grad = jnp.sum(back * hat, axis=0, keepdims=True)
    back = back * gain
    back = inverse * (back - hat * jnp.mean(back * hat, axis=-1, keepdims=True))
    return back.astype(bf16), gain_grad


def head_back_kernel(raw_ref, grad_ref, gain_ref, cos_ref, sin_ref, out_ref, gain_grad_ref, *, scale):
    @pl.when(pl.program_id(0) == 0)
    def _():
        gain_grad_ref[...] = jnp.zeros_like(gain_grad_ref)

    out_ref[...], gain_grad = head_backward(
        raw_ref[...], grad_ref[...] * scale, gain_ref[...], cos_ref[...], sin_ref[...]
    )
    gain_grad_ref[...] += gain_grad


def head_back(raw, grad, gain, cosine, sine, scale, stride):
    rows, width = raw.shape
    block = pl.BlockSpec((rows, HEAD_WIDTH), lambda j: (0, j))
    spaced = pl.BlockSpec((rows, HEAD_WIDTH), lambda j: (0, j * stride))
    table = pl.BlockSpec((rows, HEAD_WIDTH), lambda j: (0, 0))
    one = pl.BlockSpec((1, HEAD_WIDTH), lambda j: (0, 0))
    return pl.pallas_call(
        functools.partial(head_back_kernel, scale=scale),
        grid=(width // HEAD_WIDTH,),
        in_specs=[block, spaced, one, table, table],
        out_specs=[block, one],
        out_shape=[
            jax.ShapeDtypeStruct((rows, width), bf16),
            jax.ShapeDtypeStruct((1, HEAD_WIDTH), f32),
        ],
        compiler_params=WHOLE_VMEM,
        cost_estimate=SMALL,
        name="head_back",
    )(raw, grad, gain[None, :], cosine, sine)


def key_lanes(meta, key_start, rows, bounds_ref):
    inside = in_segment(key_start + row_index(rows), bounds_ref)
    lanes = lane_index(rows)
    log_lanes = (lanes >= LOG_LANE) & (lanes < LOG_LANE + 3)
    return jnp.where(inside | log_lanes, 1.0, 0.0).astype(bf16)


def block_used(meta, key_start, key_rows, rows):
    return (
        (key_start >= 0) & (key_start <= meta[0] + rows - 1) & (key_start + key_rows - 1 >= meta[1])
    )


def lower_mask(transposed):
    shape = (KEY_CHUNK, KEY_CHUNK)
    first = lax.broadcasted_iota(jnp.int32, shape, 0)
    second = lax.broadcasted_iota(jnp.int32, shape, 1)
    return first <= second if transposed else second <= first


def chunk(i, n=1):
    return slice(i * KEY_CHUNK, (i + n) * KEY_CHUNK)


def attend_kernel(meta, q_ref, *refs, places, first, last):
    kv_refs, bounds_ref, refs = refs[: len(places)], refs[len(places)], refs[len(places) + 1 :]
    rows = q_ref.shape[0]
    if last:
        acc_in, sum_in, o_ref, q_out_ref, acc_ref, sum_ref = refs
    elif first:
        acc_ref, sum_ref = refs
    else:
        acc_in, sum_in, acc_ref, sum_ref = refs
    if first:
        acc_ref[...] = jnp.zeros_like(acc_ref)
        sum_ref[...] = jnp.zeros_like(sum_ref)
    else:
        acc_ref[...] = acc_in[...]
        sum_ref[...] = sum_in[...]
    ones = jnp.ones((KEY_CHUNK, HEAD_WIDTH), bf16)

    def work(kv_ref, lanes, keys, queries, mask):
        key = jnp.concatenate([kv_ref[keys, :HEAD_WIDTH], lanes[keys, :]], axis=1)
        weight = jnp.exp2(dot_nt(q_ref[queries, :], key))
        if mask:
            weight = jnp.where(lower_mask(False), weight, 0.0)
        value = jnp.concatenate([kv_ref[keys, HEAD_WIDTH:], ones], axis=1)
        out = dot(weight.astype(bf16), value)
        acc_ref[queries, :] += out[:, :HEAD_WIDTH]
        sum_ref[queries, :] += out[:, HEAD_WIDTH:]

    for place, kv_ref in zip(places, kv_refs):
        key_start = meta[2 + place]
        key_rows = kv_ref.shape[0]
        diagonal = first and place == 0

        @pl.when(block_used(meta, key_start, key_rows, rows))
        def _():
            lanes = key_lanes(meta, key_start, key_rows, bounds_ref)
            for c in range(key_rows // KEY_CHUNK):
                if diagonal:
                    work(kv_ref, lanes, chunk(c), chunk(c), True)
                    if c + 1 < rows // KEY_CHUNK:
                        work(kv_ref, lanes, chunk(c), slice((c + 1) * KEY_CHUNK, rows), False)
                else:
                    work(kv_ref, lanes, chunk(c), slice(0, rows), False)

    if last:
        total = sum_ref[...]
        outcome = acc_ref[...] / total
        acc_ref[...] = outcome
        o_ref[...] = outcome.astype(bf16)
        lanes = lane_index(rows)
        extra = q_ref[:, HEAD_WIDTH:].astype(f32)
        for i, part in enumerate(split_parts(jnp.log2(total))):
            extra = jnp.where(lanes == LOG_LANE + i, -part.astype(f32), extra)
        q_out_ref[:, :HEAD_WIDTH] = q_ref[:, :HEAD_WIDTH]
        q_out_ref[:, HEAD_WIDTH:] = extra.astype(bf16)


def attend_stage(q, blocks, places, bounds, meta, carried, last=None):
    rows = q.shape[0]
    kv = blocks[0]
    q_heads = q.shape[1] // (2 * HEAD_WIDTH)
    group = q.shape[1] // kv.shape[1]
    width = q_heads * HEAD_WIDTH
    first = not carried
    wide = 2 * HEAD_WIDTH
    count = len(blocks)
    grid = q_heads if last is None else q_heads // last[1]
    start = 0 if last is None else last[0] * grid
    per_q = pl.BlockSpec((rows, wide), lambda j, m: (0, j + start))
    per_kv = pl.BlockSpec((kv.shape[0], wide), lambda j, m: (0, (j + start) // group))
    per_out = pl.BlockSpec((rows, HEAD_WIDTH), lambda j, m: (0, j + start))
    table = pl.BlockSpec((8, HEAD_WIDTH), lambda j, m: (0, 0))
    running = jax.ShapeDtypeStruct((rows, width), f32)
    if last is not None:
        out_specs = [pl.BlockSpec((rows, HEAD_WIDTH), lambda j, m: (0, j)), per_q, per_out]
        out_shape = [
            jax.ShapeDtypeStruct((rows, grid * HEAD_WIDTH), bf16),
            jax.ShapeDtypeStruct(q.shape, bf16),
            running,
        ]
        scratch = [pltpu.VMEM((rows, HEAD_WIDTH), f32)]
        aliases = {1: 1, 3 + count: 2}
    else:
        out_specs = [per_out, per_out]
        out_shape = [running, running]
        scratch = []
        aliases = {} if first else {3 + count: 0, 4 + count: 1}
    return pl.pallas_call(
        functools.partial(attend_kernel, places=places, first=first, last=last is not None),
        grid_spec=pltpu.PrefetchScalarGridSpec(
            num_scalar_prefetch=1,
            grid=(grid,),
            in_specs=[per_q] + [per_kv] * count + [table] + [per_out] * len(carried),
            out_specs=out_specs,
            scratch_shapes=scratch,
        ),
        out_shape=out_shape,
        input_output_aliases=aliases,
        compiler_params=WHOLE_VMEM,
        cost_estimate=SMALL,
        name="attend_stage",
    )(meta, q, *blocks, bounds, *carried)


def delta_kernel(owners, *refs):
    *pieces, outcome_ref, out_ref = refs
    for i, piece in enumerate(pieces):

        @pl.when(pl.program_id(0) == i)
        def _():
            rows, width = piece.shape
            lanes = lane_index(rows)
            for j in range(width // HEAD_WIDTH):
                head = slice(j * HEAD_WIDTH, (j + 1) * HEAD_WIDTH)
                do = piece[:, head]
                delta = jnp.sum(do.astype(f32) * outcome_ref[:, head], axis=-1, keepdims=True)
                extra = jnp.zeros((rows, HEAD_WIDTH), f32)
                for k, part in enumerate(split_parts(delta)):
                    extra = jnp.where(lanes == k, -part.astype(f32), extra)
                start = 2 * j * HEAD_WIDTH
                out_ref[:, start : start + HEAD_WIDTH] = do
                out_ref[:, start + HEAD_WIDTH : start + 2 * HEAD_WIDTH] = extra.astype(bf16)


def with_delta(pieces, outcome):
    owners = jnp.stack([jnp.asarray(owner, jnp.int32) for unused, owner in pieces])
    rows, width = outcome.shape
    share = rows // len(pieces)
    whole = pl.BlockSpec((share, width), lambda i, m: (0, 0))
    return pl.pallas_call(
        delta_kernel,
        grid_spec=pltpu.PrefetchScalarGridSpec(
            num_scalar_prefetch=1,
            grid=(len(pieces),),
            in_specs=[whole] * len(pieces) + [pl.BlockSpec((share, width), lambda i, m: (m[i], 0))],
            out_specs=pl.BlockSpec((share, 2 * width), lambda i, m: (m[i], 0)),
        ),
        out_shape=jax.ShapeDtypeStruct((rows, 2 * width), bf16),
        compiler_params=WHOLE_VMEM,
        cost_estimate=SMALL,
        name="with_delta",
    )(owners, *[piece for piece, unused in pieces], outcome)


def assemble_kernel(places, *refs, count):
    blocks, out_ref = refs[:count], refs[-1]
    for i, block in enumerate(blocks):

        @pl.when(pl.program_id(0) == i)
        def _():
            out_ref[...] = block[...].astype(out_ref.dtype)


def assemble(entries, rows, kind, total=None, base=None):
    places = jnp.stack([jnp.asarray(place, jnp.int32) for unused, also, place in entries])
    width = entries[0][0].shape[1]
    count = len(entries)
    in_specs = [
        pl.BlockSpec((rows, width), lambda i, m, k=block: (k, 0)) for unused, block, also in entries
    ]
    args = [array for array, unused, also in entries]
    if base is not None:
        in_specs.append(pl.BlockSpec(memory_space=pl.ANY))
        args.append(base)
    return pl.pallas_call(
        functools.partial(assemble_kernel, count=count),
        grid_spec=pltpu.PrefetchScalarGridSpec(
            num_scalar_prefetch=1,
            grid=(count,),
            in_specs=in_specs,
            out_specs=pl.BlockSpec((rows, width), lambda i, m: (m[i], 0)),
        ),
        out_shape=jax.ShapeDtypeStruct((rows * (total or count), width), kind),
        input_output_aliases={} if base is None else {1 + count: 0},
        compiler_params=WHOLE_VMEM,
        cost_estimate=SMALL,
        name="assemble",
    )(places, *args)


def cut_kernel(in_ref, *outs, axis):
    start = 0
    for out_ref in outs:
        size = out_ref.shape[axis]
        part = in_ref[start : start + size, :] if axis == 0 else in_ref[:, start : start + size]
        out_ref[...] = part.astype(f32)
        start += size


def cut_up(array, shapes, axis):
    return pl.pallas_call(
        functools.partial(cut_kernel, axis=axis),
        out_shape=[jax.ShapeDtypeStruct(shape, f32) for shape in shapes],
        compiler_params=WHOLE_VMEM,
        cost_estimate=SMALL,
        name="cut_up",
    )(array)


def cut_columns(array, widths):
    return cut_up(array, [(array.shape[0], width) for width in widths], 1)


def cut_rows(array, heights):
    return cut_up(array, [(height, array.shape[1]) for height in heights], 0)


def attend_back_kernel(meta, q_ref, do_ref, *refs, places, first, group, diagonal):
    count = len(places)
    kv_refs, bounds_ref, refs = refs[:count], refs[count], refs[count + 1 :]
    if not first:
        dq_in, *refs = refs
    dq_ref, dkv_refs, dq_turned, sums = refs[0], refs[1 : 1 + count], refs[1 + count], refs[2 + count :]
    rows = q_ref.shape[0]
    step = lax.rem(pl.program_id(0), group)
    dq_turned[...] = jnp.zeros_like(dq_turned)

    @pl.when(step == 0)
    def _():
        for total in sums:
            total[...] = jnp.zeros_like(total)

    def work(kv_ref, total, lanes, ones, keys, queries, mask):
        key = kv_ref[keys, :HEAD_WIDTH]
        q = q_ref[queries, :]
        do = do_ref[queries, :]
        weight = jnp.exp2(dot_nt(jnp.concatenate([key, lanes[keys, :]], axis=1), q))
        if mask:
            weight = jnp.where(lower_mask(True), weight, 0.0)
        value = jnp.concatenate([kv_ref[keys, HEAD_WIDTH:], ones], axis=1)
        d_score = (weight * dot_nt(value, do)).astype(bf16)
        total[keys, HEAD_WIDTH:] += dot(weight.astype(bf16), do[:, :HEAD_WIDTH])
        total[keys, :HEAD_WIDTH] += dot(d_score, q[:, :HEAD_WIDTH])
        dq_turned[:, queries] += dot_tn(key, d_score)

    for place, kv_ref, total in zip(places, kv_refs, sums):
        key_start = meta[2 + place]
        key_rows = kv_ref.shape[0]

        @pl.when(block_used(meta, key_start, key_rows, rows))
        def _():
            lanes = key_lanes(meta, key_start, key_rows, bounds_ref)
            ones = jnp.where(lane_index(KEY_CHUNK) < 3, 1.0, 0.0).astype(bf16)
            for c in range(key_rows // KEY_CHUNK):
                if diagonal and place == 0:
                    work(kv_ref, total, lanes, ones, chunk(c), chunk(c), True)
                    if c + 1 < rows // KEY_CHUNK:
                        later = slice((c + 1) * KEY_CHUNK, rows)
                        work(kv_ref, total, lanes, ones, chunk(c), later, False)
                else:
                    work(kv_ref, total, lanes, ones, chunk(c), slice(0, rows), False)

    turned = dq_turned[...].T
    dq_ref[...] = turned if first else dq_in[...] + turned

    @pl.when(step == group - 1)
    def _():
        for ref, total in zip(dkv_refs, sums):
            ref[...] = total[...].astype(ref.dtype)


def attend_back(q, do, blocks, places, bounds, meta, dq, diagonal):
    rows = q.shape[0]
    kv = blocks[0]
    q_heads = q.shape[1] // (2 * HEAD_WIDTH)
    group = q.shape[1] // kv.shape[1]
    width = q_heads * HEAD_WIDTH
    first = dq is None
    count = len(places)
    wide = 2 * HEAD_WIDTH
    per_q = pl.BlockSpec((rows, wide), lambda j, m: (0, j))
    per_kv = pl.BlockSpec((kv.shape[0], wide), lambda j, m: (0, j // group))
    per_out = pl.BlockSpec((rows, HEAD_WIDTH), lambda j, m: (0, j))
    table = pl.BlockSpec((8, HEAD_WIDTH), lambda j, m: (0, 0))
    return pl.pallas_call(
        functools.partial(
            attend_back_kernel, places=places, first=first, group=group, diagonal=diagonal
        ),
        grid_spec=pltpu.PrefetchScalarGridSpec(
            num_scalar_prefetch=1,
            grid=(q_heads,),
            in_specs=[per_q, per_q] + [per_kv] * count + [table] + ([] if first else [per_out]),
            out_specs=[per_out] + [per_kv] * count,
            scratch_shapes=[pltpu.VMEM((HEAD_WIDTH, rows), f32)]
            + [pltpu.VMEM((kv.shape[0], wide), f32)] * count,
        ),
        out_shape=[jax.ShapeDtypeStruct((rows, width), f32)]
        + [jax.ShapeDtypeStruct(kv.shape, bf16 if place else f32) for place in places],
        input_output_aliases={} if first else {4 + count: 0},
        compiler_params=WHOLE_VMEM,
        cost_estimate=SMALL,
        name="attend_back",
    )(meta, q, do, *blocks, bounds, *(() if first else (dq,)))


def project_kernel(meta, base_ref, *refs, count):
    lows, highs = refs[:count], refs[count : 2 * count]
    mine, other = refs[2 * count : 3 * count], refs[3 * count : 4 * count]
    gain_ref, share_ref, normed_ref = refs[4 * count :]
    first_core = meta[0] == 0
    total = base_ref[...].astype(f32)
    for low_ref, high_ref, mine_ref, other_ref in zip(lows, highs, mine, other):
        low, high = low_ref[...], high_ref[...]
        total += dot(jnp.where(first_core, low, high), mine_ref[0])
        total += dot(jnp.where(first_core, high, low), other_ref[0])
    inverse = lax.rsqrt(jnp.mean(total * total, axis=-1, keepdims=True) + EPSILON)
    normed_ref[...] = (total * inverse * gain_ref[...]).astype(bf16)

    @pl.when(pl.program_id(0) == meta[1])
    def _():
        share_ref[...] = total


def project(base, pieces, w_mine, w_other, core, me, gain):
    meta = jnp.stack(
        [jnp.asarray(v, jnp.int32) for v in [core, me] + [piece[2] for piece in pieces]]
    )
    rows, width = base.shape
    n_head, half, unused = w_mine.shape
    count = len(pieces)
    step = rows // n_head
    per_row = pl.BlockSpec((step, width), lambda i, m: (i, 0))
    per_piece = pl.BlockSpec((step, half), lambda i, m: (i, 0))
    weights = [
        pl.BlockSpec((1, half, width), lambda i, m, k=k: (m[2 + k], 0, 0)) for k in range(count)
    ]
    return pl.pallas_call(
        functools.partial(project_kernel, count=count),
        grid_spec=pltpu.PrefetchScalarGridSpec(
            num_scalar_prefetch=1,
            grid=(n_head,),
            in_specs=[per_row]
            + [per_piece] * (2 * count)
            + weights
            + weights
            + [pl.BlockSpec((1, width), lambda i, m: (0, 0))],
            out_specs=[pl.BlockSpec((step, width), lambda i, m: (0, 0)), per_row],
        ),
        out_shape=[
            jax.ShapeDtypeStruct((step, width), f32),
            jax.ShapeDtypeStruct((rows, width), bf16),
        ],
        compiler_params=WHOLE_VMEM,
        cost_estimate=SMALL,
        name="project",
    )(
        meta,
        base,
        *[piece[0] for piece in pieces],
        *[piece[1] for piece in pieces],
        *[w_mine] * count,
        *[w_other] * count,
        gain[None, :],
    )


def arranged_shapes(rows, width):
    return [
        jax.ShapeDtypeStruct((rows // 4, width), bf16),
        jax.ShapeDtypeStruct((rows // 4, width), bf16),
        jax.ShapeDtypeStruct((rows // 2, width), bf16),
    ]


def store_arranged(me, outs, share_y, share_x, half, value):
    along_x, along_y, stays = outs
    rows = value.shape[0]
    other_x = share_x ^ (me & 1)
    other_y = share_y ^ (me >> 1)

    def store(ref, place):
        ref[pl.ds(pl.multiple_of(place * rows, rows), rows), :] = value

    if half == 0:
        pl.when(other_x == 1)(lambda: store(along_x, other_y))
        pl.when(other_x == 0)(lambda: store(stays, other_y))
    else:
        pl.when(other_y == 1)(lambda: store(along_y, other_x))
        pl.when(other_y == 0)(lambda: store(stays, 2 + other_x))


def store_all_arranged(me, outs, value):
    rows = value.shape[0] // 8
    for i in range(8):
        block = value[i * rows : (i + 1) * rows, :]
        store_arranged(me, outs, i // 4, i // 2 % 2, i % 2, block)


def meet_kernel(stays_ref, x_ref, y_ref, mine_ref, to_y_ref, to_x_ref):
    rows = mine_ref.shape[0] // 2
    for start, got_ref, sent_ref in ((0, x_ref, to_y_ref), (2, y_ref, to_x_ref)):
        total = stays_ref[start * rows : (start + 2) * rows, :].astype(f32) + got_ref[...].astype(f32)
        mine_ref[start // 2 * rows : (start // 2 + 1) * rows, :] = total[:rows]
        sent_ref[...] = total[rows:].astype(bf16)


def meet(stays, from_x, from_y):
    rows, width = stays.shape
    return pl.pallas_call(
        meet_kernel,
        out_shape=[
            jax.ShapeDtypeStruct((rows // 2, width), f32),
            jax.ShapeDtypeStruct((rows // 4, width), bf16),
            jax.ShapeDtypeStruct((rows // 4, width), bf16),
        ],
        compiler_params=WHOLE_VMEM,
        cost_estimate=SMALL,
        name="meet",
    )(stays, from_x, from_y)


def share_sum(terms):
    first, *rest = terms
    total = first[...].astype(f32)
    if len(rest) == 2:
        return total + jnp.concatenate([part[...].astype(f32) for part in rest], axis=0)
    return total


def add_rows_kernel(base_ref, *refs):
    *terms, out_ref = refs
    out_ref[...] = (base_ref[...] + share_sum(terms)).astype(bf16)


def add_rows(base, terms):
    return pl.pallas_call(
        add_rows_kernel,
        out_shape=jax.ShapeDtypeStruct(base.shape, bf16),
        compiler_params=WHOLE_VMEM,
        cost_estimate=SMALL,
        name="add_rows",
    )(base, *terms)


def norm_backward(grad, x, gain):
    inverse = lax.rsqrt(jnp.mean(x * x, axis=-1, keepdims=True) + EPSILON)
    hat = x * inverse
    scaled = grad * gain
    back = inverse * (scaled - hat * jnp.mean(scaled * hat, axis=-1, keepdims=True))
    return back, jnp.sum(grad * hat, axis=0, keepdims=True)


def turn_kernel(meta, *refs, count):
    terms = refs[:count]
    hidden_ref, dy_ref, gain_ref, mine_ref, other_ref = refs[count : count + 5]
    *outs, grad_ref, branch_ref, gain_grad_ref = refs[count + 5 :]

    @pl.when(pl.program_id(0) == 0)
    def _():
        back, gain_grad_ref[...] = norm_backward(
            share_sum(terms), hidden_ref[...], gain_ref[...]
        )
        total = dy_ref[...].astype(f32) + back
        grad_ref[...] = total
        branch_ref[...] = total.astype(bf16)

    half = mine_ref.shape[1]
    branch = branch_ref[...]
    mine = dot_nt(branch, mine_ref[0])
    other = dot_nt(branch, other_ref[0])
    first_core = meta[0] == 0
    low = jnp.where(first_core, mine, other).astype(bf16)
    high = jnp.where(first_core, other, mine).astype(bf16)
    for i, out_ref in enumerate(outs):

        @pl.when(pl.program_id(0) == i)
        def _():
            out_ref[:, :half] = low
            out_ref[:, half:] = high


def turn(terms, hidden, dy, gain, w_mine, w_other, core, me):
    rows, width = hidden.shape
    n_head, half, unused = w_mine.shape
    meta = jnp.stack([jnp.asarray(v, jnp.int32) for v in (core, me)])

    def full(array):
        return pl.BlockSpec(array.shape, lambda i, m: (0, 0))

    weight = pl.BlockSpec((1, half, width), lambda i, m: (i ^ m[1], 0, 0))
    share = pl.BlockSpec((rows, width), lambda i, m: (0, 0))
    return pl.pallas_call(
        functools.partial(turn_kernel, count=len(terms)),
        grid_spec=pltpu.PrefetchScalarGridSpec(
            num_scalar_prefetch=1,
            grid=(n_head,),
            in_specs=[full(term) for term in terms]
            + [
                share,
                pl.BlockSpec((rows, width), lambda i, m: (m[1], 0)),
                pl.BlockSpec((1, width), lambda i, m: (0, 0)),
                weight,
                weight,
            ],
            out_specs=[
                *[pl.BlockSpec((rows, 2 * half), lambda i, m: (0, 0))] * n_head,
                share,
                share,
                pl.BlockSpec((1, width), lambda i, m: (0, 0)),
            ],
        ),
        out_shape=[
            *[jax.ShapeDtypeStruct((rows, 2 * half), bf16)] * n_head,
            jax.ShapeDtypeStruct((rows, width), f32),
            jax.ShapeDtypeStruct((rows, width), bf16),
            jax.ShapeDtypeStruct((1, width), f32),
        ],
        compiler_params=WHOLE_VMEM,
        cost_estimate=SMALL,
        name="turn",
    )(meta, *terms, hidden, dy, gain[None, :], w_mine, w_other)


def last_kernel(meta, *refs, count):
    terms = refs[:count]
    x_ref, grad_ref, gain_ref, rider_ref, out_ref = refs[count:]
    rows = x_ref.shape[0]
    back, unused = norm_backward(share_sum(terms), x_ref[...].astype(f32), gain_ref[...])
    out_ref[:rows, :] = (grad_ref[...] + back).astype(bf16)
    out_ref[rows:, :] = rider_ref[...]


def last(terms, tokens, hidden_grad, gain, rider, me):
    rows, width = hidden_grad.shape
    meta = jnp.asarray(me, jnp.int32)[None]

    def full(array):
        return pl.BlockSpec(array.shape, lambda i, m: (0, 0))

    out_rows = rows + rider.shape[0]
    return pl.pallas_call(
        functools.partial(last_kernel, count=len(terms)),
        grid_spec=pltpu.PrefetchScalarGridSpec(
            num_scalar_prefetch=1,
            grid=(1,),
            in_specs=[full(term) for term in terms]
            + [
                pl.BlockSpec((rows, width), lambda i, m: (m[0], 0)),
                full(hidden_grad),
                pl.BlockSpec((1, width), lambda i, m: (0, 0)),
                full(rider),
            ],
            out_specs=pl.BlockSpec((out_rows, width), lambda i, m: (0, 0)),
        ),
        out_shape=jax.ShapeDtypeStruct((out_rows, width), bf16),
        compiler_params=WHOLE_VMEM,
        cost_estimate=SMALL,
        name="last",
    )(meta, *terms, tokens, hidden_grad, gain[None, :], rider)


def feed_kernel(x_ref, gate_w_ref, up_w_ref, d_mixed_ref, mixed_ref, gate_ref, up_ref, sum_ref):
    x = x_ref[...]
    gate = dot(x, gate_w_ref[...])
    up = dot(x, up_w_ref[...])
    d_mixed = d_mixed_ref[...]
    sigmoid = 0.5 * jnp.tanh(0.5 * gate) + 0.5
    silu = gate * sigmoid
    mixed_ref[...] = (silu * up).astype(bf16)
    gate_low = (d_mixed * up * (sigmoid * (1.0 + gate * (1.0 - sigmoid)))).astype(bf16)
    up_low = (d_mixed * silu).astype(bf16)
    gate_ref[...] = gate_low
    up_ref[...] = up_low
    step = gate_low.shape[1]
    sum_ref[:, :step] = dot_tn(x, gate_low).astype(bf16)
    sum_ref[:, step:] = dot_tn(x, up_low).astype(bf16)


def feed(x, w_gate, w_up, d_mixed):
    rows, width = x.shape
    hidden = w_gate.shape[1]
    whole = pl.BlockSpec((rows, width), lambda i: (0, 0))
    weight = pl.BlockSpec((width, HIDDEN_STEP), lambda i: (0, i))
    act = pl.BlockSpec((rows, HIDDEN_STEP), lambda i: (0, i))
    return pl.pallas_call(
        feed_kernel,
        grid=(hidden // HIDDEN_STEP,),
        in_specs=[whole, weight, weight, act],
        out_specs=[act, act, act, pl.BlockSpec((width, 2 * HIDDEN_STEP), lambda i: (0, i))],
        out_shape=[jax.ShapeDtypeStruct((rows, hidden), bf16)] * 3
        + [jax.ShapeDtypeStruct((width, 2 * hidden), bf16)],
        compiler_params=WHOLE_VMEM,
        cost_estimate=SMALL,
        name="feed",
    )(x, w_gate, w_up, d_mixed)


def split_kernel(sum_ref, gate_ref, up_ref):
    step = gate_ref.shape[1]
    gate_ref[...] = sum_ref[:, :step].astype(f32)
    up_ref[...] = sum_ref[:, step:].astype(f32)


def split_gate_up(sums):
    rows, width = sums.shape
    out = pl.BlockSpec((rows, HIDDEN_STEP), lambda i: (0, i))
    return pl.pallas_call(
        split_kernel,
        grid=(width // (2 * HIDDEN_STEP),),
        in_specs=[pl.BlockSpec((rows, 2 * HIDDEN_STEP), lambda i: (0, i))],
        out_specs=[out, out],
        out_shape=[jax.ShapeDtypeStruct((rows, width // 2), f32)] * 2,
        compiler_params=WHOLE_VMEM,
        cost_estimate=SMALL,
        name="split_gate_up",
    )(sums)


def products_kernel(meta, *refs, count, turned, arranged):
    lefts, rights, outs = refs[:count], refs[count : 2 * count], refs[2 * count :]
    total = 0.0
    for left, right in zip(lefts, rights):
        total += (dot_nt if turned else dot)(left[...], right[...])
    if arranged:
        store_all_arranged(meta[0], outs, total.astype(bf16))
    else:
        outs[0][...] = total.astype(bf16)


def products(lefts, rights, turned, me, arranged):
    meta = jnp.asarray(me, jnp.int32)[None]
    rows, depth = lefts[0].shape
    width = rights[0].shape[0 if turned else 1]
    step = width // 4
    whole = pl.BlockSpec((rows, depth), lambda i, m: (0, 0))
    if turned:
        right = pl.BlockSpec((step, depth), lambda i, m: (i, 0))
    else:
        right = pl.BlockSpec((depth, step), lambda i, m: (0, i))
    shapes = arranged_shapes(rows, width) if arranged else [jax.ShapeDtypeStruct((rows, width), bf16)]
    return pl.pallas_call(
        functools.partial(products_kernel, count=len(lefts), turned=turned, arranged=arranged),
        grid_spec=pltpu.PrefetchScalarGridSpec(
            num_scalar_prefetch=1,
            grid=(width // step,),
            in_specs=[whole] * len(lefts) + [right] * len(lefts),
            out_specs=[pl.BlockSpec((v.shape[0], step), lambda i, m: (0, i)) for v in shapes],
        ),
        out_shape=shapes,
        compiler_params=WHOLE_VMEM,
        cost_estimate=SMALL,
        name="products",
    )(meta, *lefts, *rights)


def down_sums_kernel(mixed_ref, dy_ref, out_ref):
    count, unused, share = out_ref.shape
    for i in range(count):
        out_ref[i] = dot_tn(mixed_ref[...], dy_ref[:, i * share : (i + 1) * share]).astype(bf16)


def down_sums(mixed, dy, shares, more):
    rows, width = dy.shape
    share = width // shares
    hidden = mixed.shape[1]
    return pl.pallas_call(
        down_sums_kernel,
        grid=(shares // 2,),
        in_specs=[
            pl.BlockSpec(mixed.shape, lambda i: (0, 0)),
            pl.BlockSpec((rows, 2 * share), lambda i: (0, i)),
        ],
        out_specs=pl.BlockSpec((2, hidden, share), lambda i: (i, 0, 0)),
        out_shape=jax.ShapeDtypeStruct((shares, hidden + more, share), bf16),
        compiler_params=WHOLE_VMEM,
        cost_estimate=SMALL,
        name="down_sums",
    )(mixed, dy)


def output_sums_kernel(owners, *refs, groups):
    o_refs, pieces, (out_ref, branch) = refs[:groups], refs[groups:-3], refs[-2:]
    for i, piece in enumerate(pieces):
        rows = piece.shape[0]
        branch[pl.ds(pl.multiple_of(owners[i] * rows, rows), rows), :] = piece[...]
    count, unused, share = out_ref.shape
    start = 0
    for o_ref in o_refs:
        end = start + o_ref.shape[1]
        for i in range(count):
            part = branch[:, i * share : (i + 1) * share]
            out_ref[i, start:end, :] = dot_tn(o_ref[...], part).astype(bf16)
        start = end


def output_sums(o_groups, pieces, base):
    owners = jnp.stack([jnp.asarray(owner, jnp.int32) for unused, owner in pieces])
    shares, all_rows, share = base.shape
    size = sum(o.shape[1] for o in o_groups)
    place = all_rows // size - 1
    return pl.pallas_call(
        functools.partial(output_sums_kernel, groups=len(o_groups)),
        grid_spec=pltpu.PrefetchScalarGridSpec(
            num_scalar_prefetch=1,
            grid=(shares // 2,),
            in_specs=[pl.BlockSpec(o.shape, lambda i, m: (0, 0)) for o in o_groups]
            + [
                pl.BlockSpec((piece.shape[0], 2 * share), lambda i, m: (0, i))
                for piece, unused in pieces
            ]
            + [pl.BlockSpec(memory_space=pl.ANY)],
            out_specs=pl.BlockSpec((2, size, share), lambda i, m: (i, place, 0)),
            scratch_shapes=[pltpu.VMEM((o_groups[0].shape[0], 2 * share), bf16)],
        ),
        out_shape=jax.ShapeDtypeStruct(base.shape, bf16),
        input_output_aliases={1 + len(o_groups) + len(pieces): 0},
        compiler_params=WHOLE_VMEM,
        cost_estimate=SMALL,
        name="output_sums",
    )(owners, *o_groups, *[piece for piece, unused in pieces], base)


def pass_on_kernel(part_ref, theirs_ref, *refs, count):
    arrived, outs = refs[:-count], refs[-count:]
    size = outs[0].shape[0]
    for i, out_ref in enumerate(outs):
        rows = slice(i * size, (i + 1) * size)
        out_ref[...] = (part_ref[rows, :] + theirs_ref[rows, :].astype(f32)).astype(bf16)
    if arrived:
        whole = jnp.concatenate([ref[...] for ref in arrived], axis=0).astype(f32)
        for i, out_ref in enumerate(outs):
            rows = slice(i * size, (i + 1) * size)
            total = part_ref[rows, :] + theirs_ref[rows, :].astype(f32) + whole[rows]
            out_ref[...] = total.astype(bf16)


def pass_on(part, theirs, arrived, count):
    rows, width = part.shape
    return pl.pallas_call(
        functools.partial(pass_on_kernel, count=count),
        out_shape=[jax.ShapeDtypeStruct((rows // count, width), bf16)] * count,
        compiler_params=WHOLE_VMEM,
        cost_estimate=SMALL,
        name="pass_on",
    )(part, theirs, *arrived)


def leave_kernel(
    meta,
    x_ref,
    q_ref,
    dkv_ref,
    theirs_ref,
    first_ref,
    second_ref,
    raw_ref,
    key_gain_ref,
    cos_ref,
    sin_ref,
    q_w_ref,
    key_w_ref,
    value_w_ref,
    key_ref,
    value_ref,
    gain_grad_ref,
    norm_grad_ref,
    *refs,
    arranged,
):
    *outs, arrived_ref = refs

    @pl.when(pl.program_id(0) == 0)
    def _():
        size = first_ref.shape[0]
        for i, ref in enumerate((first_ref, second_ref)):
            arrived_ref[i * size : (i + 1) * size, :] = ref[...]
        gain_grad_ref[...] = jnp.zeros_like(gain_grad_ref)
        norm_grad_ref[...] = jnp.zeros_like(norm_grad_ref)

    rows = dkv_ref.shape[0]
    here = pl.ds(pl.multiple_of(pl.program_id(0) * rows, rows), rows)
    arrived = arrived_ref[here, :]
    dkv = dkv_ref[...] + theirs_ref[...].astype(f32) + arrived.astype(f32)
    for j in range(key_ref.shape[1] // HEAD_WIDTH):
        head = slice(j * HEAD_WIDTH, (j + 1) * HEAD_WIDTH)
        start = 2 * j * HEAD_WIDTH
        grad, gain_grad = head_backward(
            raw_ref[:, head],
            dkv[:, start : start + HEAD_WIDTH] * (1.0 / LOG2E),
            key_gain_ref[...],
            cos_ref[...],
            sin_ref[...],
        )
        key_ref[:, head] = grad
        value_ref[:, head] = dkv[:, start + HEAD_WIDTH : start + 2 * HEAD_WIDTH].astype(bf16)
        gain_grad_ref[...] += gain_grad
    total = dot_nt(q_ref[...], q_w_ref[...])
    total += dot_nt(key_ref[...], key_w_ref[...])
    total += dot_nt(value_ref[...], value_w_ref[...])
    result = total.astype(bf16)
    if arranged:
        block = result.shape[0] // 4
        for i in range(4):
            store_arranged(
                meta[0],
                outs,
                pl.program_id(0),
                i // 2,
                i % 2,
                result[i * block : (i + 1) * block, :],
            )
    else:
        outs[0][...] = result
    x = x_ref[...].astype(f32)
    hat = x * lax.rsqrt(jnp.mean(x * x, axis=-1, keepdims=True) + EPSILON)
    norm_grad_ref[...] += jnp.sum(total * hat, axis=0, keepdims=True)


def leave(tokens, q_grad, dkv, theirs, arrived, key_raw, key_gain, cosine, sine, weights, me, arranged):
    meta = jnp.asarray(me, jnp.int32)[None]
    rows, width = tokens.shape
    kv_width = key_raw.shape[1]
    step = rows // 2

    def per_row(array):
        return pl.BlockSpec((step, array.shape[1]), lambda i, m: (i, 0))

    def full(array):
        return pl.BlockSpec(array.shape, lambda i, m: (0, 0))

    key_gain = key_gain[None, :]
    if arranged:
        shapes = arranged_shapes(rows, width)
        out_specs = [full(v) for v in shapes]
    else:
        shapes = [jax.ShapeDtypeStruct((rows, width), bf16)]
        out_specs = [per_row(shapes[0])]
    return pl.pallas_call(
        functools.partial(leave_kernel, arranged=arranged),
        grid_spec=pltpu.PrefetchScalarGridSpec(
            num_scalar_prefetch=1,
            grid=(2,),
            in_specs=[per_row(v) for v in (tokens, q_grad, dkv, theirs)]
            + [full(v) for v in arrived]
            + [per_row(key_raw), full(key_gain), per_row(cosine), per_row(sine)]
            + [full(v) for v in weights],
            out_specs=[
                per_row(key_raw),
                per_row(key_raw),
                pl.BlockSpec((1, HEAD_WIDTH), lambda i, m: (0, 0)),
                pl.BlockSpec((1, width), lambda i, m: (0, 0)),
            ]
            + out_specs,
            scratch_shapes=[pltpu.VMEM((rows, theirs.shape[1]), bf16)],
        ),
        out_shape=[
            jax.ShapeDtypeStruct((rows, kv_width), bf16),
            jax.ShapeDtypeStruct((rows, kv_width), bf16),
            jax.ShapeDtypeStruct((1, HEAD_WIDTH), f32),
            jax.ShapeDtypeStruct((1, width), f32),
        ]
        + shapes,
        compiler_params=WHOLE_VMEM,
        cost_estimate=SMALL,
        name="leave",
    )(meta, tokens, q_grad, dkv, theirs, *arrived, key_raw, key_gain, cosine, sine, *weights)


def attn_sums_kernel(x_ref, *refs):
    *terms, out_ref = refs
    x = x_ref[...]
    start = 0
    for ref in terms:
        out_ref[:, start : start + ref.shape[1]] = dot_tn(x, ref[...]).astype(bf16)
        start += ref.shape[1]


def attn_sums(x, terms):
    rows, width = x.shape
    step = width // 8
    out_width = sum(term.shape[1] for term in terms)
    return pl.pallas_call(
        attn_sums_kernel,
        grid=(width // step,),
        in_specs=[pl.BlockSpec((rows, step), lambda i: (0, i))]
        + [pl.BlockSpec(term.shape, lambda i: (0, 0)) for term in terms],
        out_specs=pl.BlockSpec((step, out_width), lambda i: (i, 0)),
        out_shape=jax.ShapeDtypeStruct((width, out_width), bf16),
        compiler_params=WHOLE_VMEM,
        cost_estimate=SMALL,
        name="attn_sums",
    )(x, *terms)


def after(values):
    return lax.optimization_barrier(values)


def pick(array, index):
    return lax.dynamic_index_in_dim(array, index, 0, keepdims=False)


def solution(mesh):
    n_seq = mesh.shape["seq"]
    n_head = mesh.shape["head"]
    n_chip = n_seq // 2

    def swap_core(value):
        return lax.ppermute(value, "seq", [(i, i ^ 1) for i in range(n_seq)])

    def to_next(value):
        return lax.ppermute(value, "seq", [(i, i + 2) for i in range(n_seq - 2)])

    def to_previous(value):
        return lax.ppermute(value, "seq", [(i + 2, i) for i in range(n_seq - 2)])

    def across(value, bits):
        return lax.ppermute(value, "head", [(i, i ^ bits) for i in range(n_head)])

    def gather_steps(value):
        me = lax.axis_index("head")
        if n_head != 4:
            every = yield lax.all_gather(value, "head", axis=0)
            return [(every[i], i) for i in range(n_head)]
        half = value.shape[0] // 2
        by_x, by_y = yield across(value, 1), across(value, 2)
        low, high = yield across(by_x[:half], 2), across(by_y[half:], 1)
        far = jnp.concatenate([low, high], axis=0)
        return [(value, me), (by_x, me ^ 1), (by_y, me ^ 2), (far, me ^ 3)]

    def rider_entries(value, count):
        me = lax.axis_index("head")
        half = count // 2
        if n_head != 4:
            every = yield lax.all_gather(value, "head", axis=0)
            entries = [(every[i], k, 2 * i + k) for i in range(n_head) for k in range(2)]
            return entries, [every[i, count:] for i in range(n_head)]
        by_x, by_y = yield across(value, 1), across(value, 2)
        low, high = yield across(by_x[:half], 2), across(by_y[half:], 1)
        owners = ((value, me), (by_x, me ^ 1), (by_y, me ^ 2))
        entries = [(array, k, 2 * owner + k) for array, owner in owners for k in range(2)]
        entries += [(low, 0, 2 * (me ^ 3)), (high, 0, 2 * (me ^ 3) + 1)]
        return entries, [value[count:], by_x[count:], by_y[count:], high[half:]]

    def scatter_steps(value):
        if n_head != 4:
            total = yield lax.psum_scatter(value[0], "head", scatter_dimension=0, tiled=True)
            return (total,)
        along_x, along_y, stays = value
        from_x, from_y = yield across(along_x, 1), across(along_y, 2)
        mine, to_y, to_x = meet(stays, from_x, from_y)
        first, second = yield across(to_y, 2), across(to_x, 1)
        return mine, first, second

    def run_steps(steps, works=()):
        works = list(works)
        made = []
        arrived = next(steps)
        while True:
            if works:
                arrived, done = after((arrived, works.pop(0)()))
                made.append(done)
            try:
                arrived = steps.send(arrived)
            except StopIteration as stop:
                return stop.value, made + [work() for work in works]

    def end_steps(steps, arrived):
        try:
            steps.send(arrived)
        except StopIteration as stop:
            return stop.value

    def exchange_head(value):
        me = lax.axis_index("head")
        if n_head == 4:
            return [(value[0], me)] + [(across(value[i], i), me ^ i) for i in (3, 1, 2)]
        value = jnp.stack(value)
        ordered = jnp.stack([pick(value, i ^ me) for i in range(n_head)])
        got = lax.all_to_all(ordered, "head", 0, 0)
        return [(got[i], i) for i in range(n_head)]

    def body(
        tokens,
        lengths,
        norm1_gain,
        w_query,
        key_matrix,
        value_matrix,
        query_gain,
        key_gain,
        w_output,
        norm2_gain,
        w_gate,
        w_up,
        w_down,
        cotangent,
    ):
        rows = tokens.shape[0]
        share = rows // n_head
        seq_index = lax.axis_index("seq")
        head_index = lax.axis_index("head")
        chip, core = seq_index // 2, seq_index % 2
        cut = n_head == 4

        index = seq_index * rows + jnp.arange(rows, dtype=jnp.int32)
        begin = locate(index, lengths)
        cosine, sine = rotary(index - begin)
        ends = jnp.cumsum(lengths)
        n_lengths = lengths.shape[0]
        bounds = jnp.zeros((8, HEAD_WIDTH), jnp.int32).at[0].set(2**30)
        bounds = bounds.at[0, :n_lengths].set(ends - lengths).at[1, :n_lengths].set(ends)

        def stage_meta(stage):
            source = 2 * (chip - stage)
            return jnp.stack(
                [seq_index * rows, begin[0], (source + core) * rows, (source + 1 - core) * rows]
            ).astype(jnp.int32)

        metas = [stage_meta(stage) for stage in range(n_chip)]

        first_in, key_raw, current = enter(
            tokens, norm1_gain, key_matrix, value_matrix, key_gain, cosine, sine
        )
        sibling = swap_core(current)
        following = to_next(current)

        half_rows = w_output.shape[0] // 2
        w_late, unused = after((w_output, current))
        w_half = lax.dynamic_slice_in_dim(w_late, core * half_rows, half_rows, 0)
        w_mine = lax.all_gather(w_half, "head", axis=0)

        query_raw = dot(first_in, w_query)
        q_wide = query_prep(metas[0], query_raw, query_gain, cosine, sine, bounds)
        following, q_wide = after((following, q_wide))

        blocks = []
        carried = ()
        for stage in range(n_chip):
            blocks.append((current, sibling))
            if stage + 2 < n_chip:
                current = following
                sibling = swap_core(current)
                following = to_next(current)
            if stage == n_chip - 1:
                break
            carried = attend_stage(q_wide, blocks[stage], (0, 1), bounds, metas[stage], carried)
            if stage + 3 < n_chip:
                following, carried = after((following, carried))
            if stage + 2 == n_chip:
                current, carried = after((following, carried))
                sibling = swap_core(current)
        groups = 2 if cut else 1
        w_mine, sibling, carried = after((w_mine, sibling, carried))
        blocks[-1] = (current, sibling)
        w_other = swap_core(w_mine)
        outcome, total = carried
        o_first, q_back, outcome = attend_stage(
            q_wide, blocks[-1], (0, 1), bounds, metas[-1], (outcome, total), (0, groups)
        )
        if cut:
            first_steps = gather_steps(o_first)
            got_first = next(first_steps)
            o_second, q_back, outcome = attend_stage(
                q_back, blocks[-1], (0, 1), bounds, metas[-1], (outcome, total), (1, groups)
            )
            got_first, o_second = after((got_first, o_second))
            second_steps = gather_steps(o_second)
            got_second = next(second_steps)
            got_first = first_steps.send(got_first)
            o_groups = (o_first, o_second)
            dy, unused = after((cotangent, o_second))
            d_mixed = dot_nt(dy, w_down)
            got_second, d_mixed = after((got_second, d_mixed))
            got_second = second_steps.send(got_second)
            got_first, d_mixed = after((got_first, d_mixed))
            first_pieces = end_steps(first_steps, got_first)
            second_pieces = end_steps(second_steps, got_second)
            pieces = [(low[0], high[0], low[1]) for low, high in zip(first_pieces, second_pieces)]
        else:
            o_groups = (o_first,)
            half = o_first.shape[1] // 2
            every = lax.all_gather(o_first, "head", axis=0)
            pieces = [(every[i, :, :half], every[i, :, half:], i) for i in range(n_head)]
            d_mixed = dot_nt(cotangent, w_down)
        my_hidden, second_in = project(
            tokens, pieces, w_mine, w_other, core, head_index, norm2_gain
        )
        def scatter_seq(value, tiled):
            return lax.psum_scatter(value, "seq", scatter_dimension=0, tiled=tiled)

        mixed_low, gate_low, up_low, gate_up_sum = feed(second_in, w_gate, w_up, d_mixed)
        grad_gate_up = scatter_seq(gate_up_sum, True)

        flow = scatter_steps(products((gate_low, up_low), (w_gate, w_up), True, head_index, cut))
        got = next(flow)
        down_part = products((mixed_low,), (w_down,), False, head_index, cut)
        got, down_part = after((got, down_part))
        if cut:
            got = flow.send(got)
        column_sum = down_sums(mixed_low, cotangent, n_seq, w_output.shape[0])
        got, column_sum = after((got, column_sum))
        terms = end_steps(flow, got)
        *do_pieces, hidden_grad, my_branch, grad_norm2 = turn(
            terms, my_hidden, cotangent, norm2_gain, w_mine, w_other, core, head_index
        )
        do_wide = with_delta(exchange_head(do_pieces), outcome)
        down_part, my_branch, do_wide = after((down_part, my_branch, do_wide))

        dq = None
        parts = []
        moving = []
        landed = []
        hops = 0

        def hop_piece():
            if not moving:
                return None
            value = moving.pop(0)
            return lambda: to_previous(value)

        def stage_work(stage, places=(0, 1)):
            chosen = [blocks[stage][place] for place in places]
            return attend_back(
                q_back, do_wide, chosen, places, bounds, metas[stage], dq, stage == 0
            )

        def next_hop():
            nonlocal dq, hops
            if hops < n_chip - 1 and len(parts) > hops and len(landed) == (2 if hops else 0) and hops < n_chip - 1:
                sent, dq = after((pass_on(*parts[hops], landed, 2), dq))
                landed.clear()
                moving.extend(sent)
                hops += 1

        branch_steps = gather_steps(my_branch)
        (dq, dkv_a, dkv_b), got_branch = after(
            (stage_work(n_chip - 1), next(branch_steps))
        )
        theirs, dq = after((swap_core(dkv_b), dq))
        parts.append((dkv_a, theirs))
        next_hop()
        flying = hop_piece()()
        if cut:
            got_branch = branch_steps.send(got_branch)
        (dq, dkv_a, dkv_b), got_branch, flying = after(
            (stage_work(n_chip - 2), got_branch, flying)
        )
        branch_pieces = end_steps(branch_steps, got_branch)
        landed.append(flying)
        parts.append((dkv_a, swap_core(dkv_b)))
        flying = hop_piece()()
        column_sum = output_sums(o_groups, branch_pieces, column_sum)
        dkv_a, theirs = parts[1]
        column_sum, flying, theirs, dq = after((column_sum, flying, theirs, dq))
        parts[1] = (dkv_a, theirs)
        landed.append(flying)
        grad_gate_up, column_sum, dq, landed[:] = after(
            (grad_gate_up, column_sum, dq, list(landed))
        )
        grad_columns = scatter_seq(column_sum, False)
        next_hop()
        down_part, dq = after((down_part, dq))
        mixed_steps = scatter_steps(down_part)
        got_mixed = next(mixed_steps)
        for stage in reversed(range(1, n_chip - 2)):
            hop = hop_piece()
            flying = None if hop is None else hop()
            (dq, dkv_a, dkv_b), got_mixed, flying = after((stage_work(stage), got_mixed, flying))
            if hop is not None:
                landed.append(flying)
            parts.append((dkv_a, swap_core(dkv_b)))
            next_hop()
        if cut:
            got_mixed = mixed_steps.send(got_mixed)
        hop = hop_piece()
        flying = None if hop is None else hop()
        (dq, dkv_b), got_mixed, flying = after((stage_work(0, (1,)), got_mixed, flying))
        if hop is not None:
            landed.append(flying)
        theirs = swap_core(dkv_b)
        next_hop()
        my_mixed = add_rows(my_hidden, end_steps(mixed_steps, got_mixed))
        my_mixed, dq = after((my_mixed, dq))
        mixed_steps = gather_steps(my_mixed)
        got_mixed = next(mixed_steps)
        hop = hop_piece()
        flying = None if hop is None else hop()
        (dq, dkv_a), theirs, flying = after((stage_work(0, (0,)), theirs, flying))
        if hop is not None:
            landed.append(flying)
        parts.append((dkv_a, theirs))
        while hops < n_chip - 1:
            while len(landed) < 2:
                landed.append(hop_piece()())
            next_hop()
        flying = [hop_piece()() for unused in range(2 - len(landed))]
        query_grad, grad_qgain = head_back(query_raw, dq, query_gain, cosine, sine, SCORE_SCALE, 1)
        if cut:
            got_mixed, query_grad = after((got_mixed, query_grad))
            got_mixed = mixed_steps.send(got_mixed)
        flying, got_mixed, query_grad = after((flying, got_mixed, query_grad))
        landed = (*landed, *flying)
        mixed_pieces = end_steps(mixed_steps, got_mixed)
        key_grad, value_grad, grad_kgain, grad_norm1, *first_part = leave(
            tokens,
            query_grad,
            *parts[-1],
            landed,
            key_raw,
            key_gain,
            cosine,
            sine,
            (w_query, key_matrix, value_matrix),
            head_index,
            cut,
        )
        gains = jnp.concatenate([grad_norm1[0], grad_norm2[0], grad_qgain[0], grad_kgain[0]])
        gains = gains.reshape(-1, HEAD_WIDTH)

        def sum_seq(total, bits):
            for bit in bits:
                total = total + lax.ppermute(total, "seq", [(i, i ^ bit) for i in range(n_seq)])
            return total

        bits = [1 << k for k in range(n_seq.bit_length() - 1)]
        steps = scatter_steps(first_part)
        got = next(steps)
        attn_sum = attn_sums(first_in, (query_grad, key_grad, value_grad))
        gains = sum_seq(gains, bits[:1])
        gains, attn_sum = after((gains, attn_sum))
        got, gains, attn_sum = after((got, gains, attn_sum))
        if cut:
            got = steps.send(got)
        grad_columns, attn_sum = after((grad_columns, attn_sum))
        grad_attn = scatter_seq(attn_sum, True)
        grad_query, grad_key, grad_value = cut_columns(
            grad_attn, (query_grad.shape[1], key_grad.shape[1], value_grad.shape[1])
        )
        got, gains = after((got, sum_seq(gains, bits[1:])))
        terms = end_steps(steps, got)

        width = tokens.shape[1]
        n_gains = gains.size
        gain_rows = -(-n_gains // width)
        flat = jnp.pad(gains.reshape(-1), (0, gain_rows * width - n_gains))
        high = lax.reduce_precision(flat, 8, 7)
        middle = lax.reduce_precision(flat - high, 8, 7)
        rider = jnp.concatenate([high, middle, flat - high - middle]).astype(bf16)
        rider = rider.reshape(3 * gain_rows, width)
        rider = jnp.pad(rider, ((0, -rider.shape[0] % 16), (0, 0)))
        my_tokens_grad = last(terms, tokens, hidden_grad, norm1_gain, rider, head_index)
        steps = rider_entries(my_tokens_grad, share)
        got = next(steps)
        mixed = assemble([(piece, 0, owner) for piece, owner in mixed_pieces], share, bf16)
        grad_down, grad_output = cut_rows(grad_columns, (w_gate.shape[1], w_output.shape[0]))
        grad_gate, grad_up = split_gate_up(grad_gate_up)
        got, mixed, grad_down, grad_output, grad_gate, grad_up = after(
            (got, mixed, grad_down, grad_output, grad_gate, grad_up)
        )
        if cut:
            got = steps.send(got)
        entries, gain_pieces = end_steps(steps, got)
        near = len(entries) - 2
        grad_tokens = assemble(entries[:near], share // 2, f32, len(entries))
        grad_tokens = assemble(entries[near:], share // 2, f32, len(entries), grad_tokens)
        gains = sum(part[: 3 * gain_rows].astype(f32) for part in gain_pieces)
        gains = jnp.sum(gains.reshape(3, -1), axis=0)
        grad_norm1, grad_norm2 = gains[:width], gains[width : 2 * width]
        grad_qgain = gains[2 * width : 2 * width + HEAD_WIDTH]
        grad_kgain = gains[2 * width + HEAD_WIDTH : n_gains]
        return (
            mixed,
            grad_tokens,
            grad_norm1,
            grad_query,
            grad_key,
            grad_value,
            grad_qgain,
            grad_kgain,
            grad_output,
            grad_norm2,
            grad_gate,
            grad_up,
            grad_down,
        )

    in_specs = (
        P("seq", None),
        P(),
        P(),
        P(None, "head"),
        P(None, "head"),
        P(None, "head"),
        P(),
        P(),
        P("head", None),
        P(),
        P(None, "head"),
        P(None, "head"),
        P("head", None),
        P("seq", None),
    )
    out_specs = (
        P("seq", None),
        P("seq", None),
        P(),
        P("seq", "head"),
        P("seq", "head"),
        P("seq", "head"),
        P(),
        P(),
        P("head", "seq"),
        P(),
        P("seq", "head"),
        P("seq", "head"),
        P("head", "seq"),
    )
    return jax.shard_map(body, mesh=mesh, in_specs=in_specs, out_specs=out_specs, check_vma=False)
```

```python
import functools
import math

import jax
import jax.numpy as jnp
from jax import lax
from jax.experimental import pallas as pl
from jax.experimental.pallas import tpu as pltpu
from jax.sharding import PartitionSpec as P

HEAD_WIDTH = 128
EPSILON = 1e-06
ROPE_BASE = 1000000.0
LOG2E = math.log2(math.e)
SCORE_SCALE = 1.0 / math.sqrt(HEAD_WIDTH)
SCORE_SCALE_2 = LOG2E / math.sqrt(HEAD_WIDTH)
KEY_CHUNK = 256
HIDDEN_STEP = 256
FAR = 512.0
LOG_LANE = 64
MIB = 2**20
SMALL = pl.CostEstimate(flops=1, bytes_accessed=1, transcendentals=0)
WHOLE_VMEM = pltpu.CompilerParams(vmem_limit_bytes=52 * MIB)

f32 = jnp.float32
bf16 = jnp.bfloat16
NT = (((1,), (1,)), ((), ()))
TN = (((0,), (0,)), ((), ()))


def dot(left, right):
    return jnp.dot(left, right, preferred_element_type=f32)


def dot_nt(left, right):
    return lax.dot_general(left, right, NT, preferred_element_type=f32)


def dot_tn(left, right):
    return lax.dot_general(left, right, TN, preferred_element_type=f32)


def locate(index, lengths):
    ends = jnp.cumsum(lengths)
    starts = ends - lengths
    segment = jnp.sum((index[:, None] >= ends[None, :]).astype(jnp.int32), axis=1)
    chosen = segment[:, None] == jnp.arange(lengths.shape[0], dtype=jnp.int32)[None, :]
    return jnp.sum(jnp.where(chosen, starts[None, :], 0), axis=1)


def rotary(position):
    half = HEAD_WIDTH // 2
    freq = jnp.exp(jnp.arange(half, dtype=f32) * (-2.0 * math.log(ROPE_BASE) / HEAD_WIDTH))
    angle = position.astype(f32)[:, None] * freq[None, :]
    cosine = jnp.cos(angle)
    sine = jnp.sin(angle)
    return (
        jnp.concatenate([cosine, cosine], axis=1),
        jnp.concatenate([-sine, sine], axis=1),
    )


def lane_index(rows):
    return lax.broadcasted_iota(jnp.int32, (rows, HEAD_WIDTH), 1)


def row_index(rows):
    return lax.broadcasted_iota(jnp.int32, (rows, HEAD_WIDTH), 0)


def in_segment(index, bounds_ref):
    return (index >= bounds_ref[0:1, :]) & (index < bounds_ref[1:2, :])


def split_parts(value):
    high = value.astype(bf16)
    rest = value - high.astype(f32)
    middle = rest.astype(bf16)
    return high, middle, (rest - middle.astype(f32)).astype(bf16)


def normed(raw, gain, cosine, sine):
    inverse = lax.rsqrt(jnp.mean(raw * raw, axis=-1, keepdims=True) + EPSILON)
    scaled = raw * inverse * gain
    return scaled * cosine + pltpu.roll(scaled, HEAD_WIDTH // 2, 1) * sine


def enter_kernel(
    x_ref, gain_ref, key_w_ref, value_w_ref, key_gain_ref, cos_ref, sin_ref, in_ref, raw_ref, kv_ref
):
    x = x_ref[...].astype(f32)
    inverse = lax.rsqrt(jnp.mean(x * x, axis=-1, keepdims=True) + EPSILON)
    first_in = (x * inverse * gain_ref[...]).astype(bf16)
    in_ref[...] = first_in
    raw = dot(first_in, key_w_ref[...])
    raw_ref[...] = raw
    value = dot(first_in, value_w_ref[...]).astype(bf16)
    for j in range(raw.shape[1] // HEAD_WIDTH):
        head = slice(j * HEAD_WIDTH, (j + 1) * HEAD_WIDTH)
        key = normed(raw[:, head], key_gain_ref[...], cos_ref[...], sin_ref[...])
        start = 2 * j * HEAD_WIDTH
        kv_ref[:, start : start + HEAD_WIDTH] = key.astype(bf16)
        kv_ref[:, start + HEAD_WIDTH : start + 2 * HEAD_WIDTH] = value[:, head]


def enter(tokens, gain, key_w, value_w, key_gain, cosine, sine):
    rows, width = tokens.shape
    kv_width = key_w.shape[1]
    step = rows // 3 if rows % 768 == 0 else rows
    table = pl.BlockSpec((step, HEAD_WIDTH), lambda i: (i, 0))
    weight = pl.BlockSpec((width, kv_width), lambda i: (0, 0))
    return pl.pallas_call(
        enter_kernel,
        grid=(rows // step,),
        in_specs=[
            pl.BlockSpec((step, width), lambda i: (i, 0)),
            pl.BlockSpec((1, width), lambda i: (0, 0)),
            weight,
            weight,
            pl.BlockSpec((1, HEAD_WIDTH), lambda i: (0, 0)),
            table,
            table,
        ],
        out_specs=[
            pl.BlockSpec((step, width), lambda i: (i, 0)),
            pl.BlockSpec((step, kv_width), lambda i: (i, 0)),
            pl.BlockSpec((step, 2 * kv_width), lambda i: (i, 0)),
        ],
        out_shape=[
            jax.ShapeDtypeStruct((rows, width), bf16),
            jax.ShapeDtypeStruct((rows, kv_width), f32),
            jax.ShapeDtypeStruct((rows, 2 * kv_width), bf16),
        ],
        compiler_params=WHOLE_VMEM,
        cost_estimate=SMALL,
        name="enter",
    )(tokens, gain[None, :], key_w, value_w, key_gain[None, :], cosine, sine)


def query_prep_kernel(meta, raw_ref, gain_ref, cos_ref, sin_ref, bounds_ref, out_ref):
    rows = raw_ref.shape[0]
    query = normed(raw_ref[...], gain_ref[...], cos_ref[...], sin_ref[...])
    out_ref[:, :HEAD_WIDTH] = (query * SCORE_SCALE_2).astype(bf16)
    inside = in_segment(meta[0] + row_index(rows), bounds_ref)
    free = inside | (lane_index(rows) >= LOG_LANE)
    out_ref[:, HEAD_WIDTH:] = jnp.where(free, 0.0, -FAR).astype(bf16)


def query_prep(meta, raw, gain, cosine, sine, bounds):
    rows, width = raw.shape
    table = pl.BlockSpec((rows, HEAD_WIDTH), lambda j, m: (0, 0))
    return pl.pallas_call(
        query_prep_kernel,
        grid_spec=pltpu.PrefetchScalarGridSpec(
            num_scalar_prefetch=1,
            grid=(width // HEAD_WIDTH,),
            in_specs=[
                pl.BlockSpec((rows, HEAD_WIDTH), lambda j, m: (0, j)),
                pl.BlockSpec((1, HEAD_WIDTH), lambda j, m: (0, 0)),
                table,
                table,
                pl.BlockSpec((8, HEAD_WIDTH), lambda j, m: (0, 0)),
            ],
            out_specs=pl.BlockSpec((rows, 2 * HEAD_WIDTH), lambda j, m: (0, j)),
        ),
        out_shape=jax.ShapeDtypeStruct((rows, 2 * width), bf16),
        compiler_params=WHOLE_VMEM,
        cost_estimate=SMALL,
        name="query_prep",
    )(meta, raw, gain[None, :], cosine, sine, bounds)


def head_backward(raw, grad, gain, cosine, sine):
    inverse = lax.rsqrt(jnp.mean(raw * raw, axis=-1, keepdims=True) + EPSILON)
    hat = raw * inverse
    back = grad * cosine - pltpu.roll(grad, HEAD_WIDTH // 2, 1) * sine
    gain_grad = jnp.sum(back * hat, axis=0, keepdims=True)
    back = back * gain
    back = inverse * (back - hat * jnp.mean(back * hat, axis=-1, keepdims=True))
    return back.astype(bf16), gain_grad


def head_back_kernel(raw_ref, grad_ref, gain_ref, cos_ref, sin_ref, out_ref, gain_grad_ref, *, scale):
    @pl.when(pl.program_id(0) == 0)
    def _():
        gain_grad_ref[...] = jnp.zeros_like(gain_grad_ref)

    out_ref[...], gain_grad = head_backward(
        raw_ref[...], grad_ref[...] * scale, gain_ref[...], cos_ref[...], sin_ref[...]
    )
    gain_grad_ref[...] += gain_grad


def head_back(raw, grad, gain, cosine, sine, scale, stride):
    rows, width = raw.shape
    block = pl.BlockSpec((rows, HEAD_WIDTH), lambda j: (0, j))
    spaced = pl.BlockSpec((rows, HEAD_WIDTH), lambda j: (0, j * stride))
    table = pl.BlockSpec((rows, HEAD_WIDTH), lambda j: (0, 0))
    one = pl.BlockSpec((1, HEAD_WIDTH), lambda j: (0, 0))
    return pl.pallas_call(
        functools.partial(head_back_kernel, scale=scale),
        grid=(width // HEAD_WIDTH,),
        in_specs=[block, spaced, one, table, table],
        out_specs=[block, one],
        out_shape=[
            jax.ShapeDtypeStruct((rows, width), bf16),
            jax.ShapeDtypeStruct((1, HEAD_WIDTH), f32),
        ],
        compiler_params=WHOLE_VMEM,
        cost_estimate=SMALL,
        name="head_back",
    )(raw, grad, gain[None, :], cosine, sine)


def key_lanes(meta, key_start, rows, bounds_ref):
    inside = in_segment(key_start + row_index(rows), bounds_ref)
    lanes = lane_index(rows)
    log_lanes = (lanes >= LOG_LANE) & (lanes < LOG_LANE + 3)
    return jnp.where(inside | log_lanes, 1.0, 0.0).astype(bf16)


def block_used(meta, key_start, key_rows, rows):
    return (
        (key_start >= 0) & (key_start <= meta[0] + rows - 1) & (key_start + key_rows - 1 >= meta[1])
    )


def lower_mask(transposed):
    shape = (KEY_CHUNK, KEY_CHUNK)
    first = lax.broadcasted_iota(jnp.int32, shape, 0)
    second = lax.broadcasted_iota(jnp.int32, shape, 1)
    return first <= second if transposed else second <= first


def chunk(i, n=1):
    return slice(i * KEY_CHUNK, (i + n) * KEY_CHUNK)


def attend_kernel(meta, q_ref, *refs, places, first, last):
    kv_refs, bounds_ref, refs = refs[: len(places)], refs[len(places)], refs[len(places) + 1 :]
    rows = q_ref.shape[0]
    if last:
        acc_in, sum_in, o_ref, q_out_ref, acc_ref, sum_ref = refs
    elif first:
        acc_ref, sum_ref = refs
    else:
        acc_in, sum_in, acc_ref, sum_ref = refs
    if first:
        acc_ref[...] = jnp.zeros_like(acc_ref)
        sum_ref[...] = jnp.zeros_like(sum_ref)
    else:
        acc_ref[...] = acc_in[...]
        sum_ref[...] = sum_in[...]
    ones = jnp.ones((KEY_CHUNK, HEAD_WIDTH), bf16)

    def work(kv_ref, lanes, keys, queries, mask):
        key = jnp.concatenate([kv_ref[keys, :HEAD_WIDTH], lanes[keys, :]], axis=1)
        weight = jnp.exp2(dot_nt(q_ref[queries, :], key))
        if mask:
            weight = jnp.where(lower_mask(False), weight, 0.0)
        value = jnp.concatenate([kv_ref[keys, HEAD_WIDTH:], ones], axis=1)
        out = dot(weight.astype(bf16), value)
        acc_ref[queries, :] += out[:, :HEAD_WIDTH]
        sum_ref[queries, :] += out[:, HEAD_WIDTH:]

    for place, kv_ref in zip(places, kv_refs):
        key_start = meta[2 + place]
        key_rows = kv_ref.shape[0]
        diagonal = first and place == 0

        @pl.when(block_used(meta, key_start, key_rows, rows))
        def _():
            lanes = key_lanes(meta, key_start, key_rows, bounds_ref)
            for c in range(key_rows // KEY_CHUNK):
                if diagonal:
                    work(kv_ref, lanes, chunk(c), chunk(c), True)
                    if c + 1 < rows // KEY_CHUNK:
                        work(kv_ref, lanes, chunk(c), slice((c + 1) * KEY_CHUNK, rows), False)
                else:
                    work(kv_ref, lanes, chunk(c), slice(0, rows), False)

    if last:
        total = sum_ref[...]
        outcome = acc_ref[...] / total
        acc_ref[...] = outcome
        o_ref[...] = outcome.astype(bf16)
        lanes = lane_index(rows)
        extra = q_ref[:, HEAD_WIDTH:].astype(f32)
        for i, part in enumerate(split_parts(jnp.log2(total))):
            extra = jnp.where(lanes == LOG_LANE + i, -part.astype(f32), extra)
        q_out_ref[:, :HEAD_WIDTH] = q_ref[:, :HEAD_WIDTH]
        q_out_ref[:, HEAD_WIDTH:] = extra.astype(bf16)


def attend_stage(q, blocks, places, bounds, meta, carried, last=None):
    rows = q.shape[0]
    kv = blocks[0]
    q_heads = q.shape[1] // (2 * HEAD_WIDTH)
    group = q.shape[1] // kv.shape[1]
    width = q_heads * HEAD_WIDTH
    first = not carried
    wide = 2 * HEAD_WIDTH
    count = len(blocks)
    grid = q_heads if last is None else q_heads // last[1]
    start = 0 if last is None else last[0] * grid
    per_q = pl.BlockSpec((rows, wide), lambda j, m: (0, j + start))
    per_kv = pl.BlockSpec((kv.shape[0], wide), lambda j, m: (0, (j + start) // group))
    per_out = pl.BlockSpec((rows, HEAD_WIDTH), lambda j, m: (0, j + start))
    table = pl.BlockSpec((8, HEAD_WIDTH), lambda j, m: (0, 0))
    running = jax.ShapeDtypeStruct((rows, width), f32)
    if last is not None:
        out_specs = [pl.BlockSpec((rows, HEAD_WIDTH), lambda j, m: (0, j)), per_q, per_out]
        out_shape = [
            jax.ShapeDtypeStruct((rows, grid * HEAD_WIDTH), bf16),
            jax.ShapeDtypeStruct(q.shape, bf16),
            running,
        ]
        scratch = [pltpu.VMEM((rows, HEAD_WIDTH), f32)]
        aliases = {1: 1, 3 + count: 2}
    else:
        out_specs = [per_out, per_out]
        out_shape = [running, running]
        scratch = []
        aliases = {} if first else {3 + count: 0, 4 + count: 1}
    return pl.pallas_call(
        functools.partial(attend_kernel, places=places, first=first, last=last is not None),
        grid_spec=pltpu.PrefetchScalarGridSpec(
            num_scalar_prefetch=1,
            grid=(grid,),
            in_specs=[per_q] + [per_kv] * count + [table] + [per_out] * len(carried),
            out_specs=out_specs,
            scratch_shapes=scratch,
        ),
        out_shape=out_shape,
        input_output_aliases=aliases,
        compiler_params=WHOLE_VMEM,
        cost_estimate=SMALL,
        name="attend_stage",
    )(meta, q, *blocks, bounds, *carried)


def delta_kernel(owners, *refs):
    *pieces, outcome_ref, out_ref = refs
    for i, piece in enumerate(pieces):

        @pl.when(pl.program_id(0) == i)
        def _():
            rows, width = piece.shape
            lanes = lane_index(rows)
            for j in range(width // HEAD_WIDTH):
                head = slice(j * HEAD_WIDTH, (j + 1) * HEAD_WIDTH)
                do = piece[:, head]
                delta = jnp.sum(do.astype(f32) * outcome_ref[:, head], axis=-1, keepdims=True)
                extra = jnp.zeros((rows, HEAD_WIDTH), f32)
                for k, part in enumerate(split_parts(delta)):
                    extra = jnp.where(lanes == k, -part.astype(f32), extra)
                start = 2 * j * HEAD_WIDTH
                out_ref[:, start : start + HEAD_WIDTH] = do
                out_ref[:, start + HEAD_WIDTH : start + 2 * HEAD_WIDTH] = extra.astype(bf16)


def with_delta(pieces, outcome):
    owners = jnp.stack([jnp.asarray(owner, jnp.int32) for unused, owner in pieces])
    rows, width = outcome.shape
    share = rows // len(pieces)
    whole = pl.BlockSpec((share, width), lambda i, m: (0, 0))
    return pl.pallas_call(
        delta_kernel,
        grid_spec=pltpu.PrefetchScalarGridSpec(
            num_scalar_prefetch=1,
            grid=(len(pieces),),
            in_specs=[whole] * len(pieces) + [pl.BlockSpec((share, width), lambda i, m: (m[i], 0))],
            out_specs=pl.BlockSpec((share, 2 * width), lambda i, m: (m[i], 0)),
        ),
        out_shape=jax.ShapeDtypeStruct((rows, 2 * width), bf16),
        compiler_params=WHOLE_VMEM,
        cost_estimate=SMALL,
        name="with_delta",
    )(owners, *[piece for piece, unused in pieces], outcome)


def assemble_kernel(places, *refs, count):
    blocks, out_ref = refs[:count], refs[-1]
    for i, block in enumerate(blocks):

        @pl.when(pl.program_id(0) == i)
        def _():
            out_ref[...] = block[...].astype(out_ref.dtype)


def assemble(entries, rows, kind, total=None, base=None):
    places = jnp.stack([jnp.asarray(place, jnp.int32) for unused, also, place in entries])
    width = entries[0][0].shape[1]
    count = len(entries)
    in_specs = [
        pl.BlockSpec((rows, width), lambda i, m, k=block: (k, 0)) for unused, block, also in entries
    ]
    args = [array for array, unused, also in entries]
    if base is not None:
        in_specs.append(pl.BlockSpec(memory_space=pl.ANY))
        args.append(base)
    return pl.pallas_call(
        functools.partial(assemble_kernel, count=count),
        grid_spec=pltpu.PrefetchScalarGridSpec(
            num_scalar_prefetch=1,
            grid=(count,),
            in_specs=in_specs,
            out_specs=pl.BlockSpec((rows, width), lambda i, m: (m[i], 0)),
        ),
        out_shape=jax.ShapeDtypeStruct((rows * (total or count), width), kind),
        input_output_aliases={} if base is None else {1 + count: 0},
        compiler_params=WHOLE_VMEM,
        cost_estimate=SMALL,
        name="assemble",
    )(places, *args)


def cut_kernel(in_ref, *outs, axis):
    start = 0
    for out_ref in outs:
        size = out_ref.shape[axis]
        part = in_ref[start : start + size, :] if axis == 0 else in_ref[:, start : start + size]
        out_ref[...] = part.astype(f32)
        start += size


def cut_up(array, shapes, axis):
    return pl.pallas_call(
        functools.partial(cut_kernel, axis=axis),
        out_shape=[jax.ShapeDtypeStruct(shape, f32) for shape in shapes],
        compiler_params=WHOLE_VMEM,
        cost_estimate=SMALL,
        name="cut_up",
    )(array)


def cut_columns(array, widths):
    return cut_up(array, [(array.shape[0], width) for width in widths], 1)


def cut_rows(array, heights):
    return cut_up(array, [(height, array.shape[1]) for height in heights], 0)


def attend_back_kernel(meta, q_ref, do_ref, *refs, places, first, group, diagonal):
    count = len(places)
    kv_refs, bounds_ref, refs = refs[:count], refs[count], refs[count + 1 :]
    if not first:
        dq_in, *refs = refs
    dq_ref, dkv_refs, dq_turned, sums = refs[0], refs[1 : 1 + count], refs[1 + count], refs[2 + count :]
    rows = q_ref.shape[0]
    step = lax.rem(pl.program_id(0), group)
    dq_turned[...] = jnp.zeros_like(dq_turned)

    @pl.when(step == 0)
    def _():
        for total in sums:
            total[...] = jnp.zeros_like(total)

    def work(kv_ref, total, lanes, ones, keys, queries, mask):
        key = kv_ref[keys, :HEAD_WIDTH]
        q = q_ref[queries, :]
        do = do_ref[queries, :]
        weight = jnp.exp2(dot_nt(jnp.concatenate([key, lanes[keys, :]], axis=1), q))
        if mask:
            weight = jnp.where(lower_mask(True), weight, 0.0)
        value = jnp.concatenate([kv_ref[keys, HEAD_WIDTH:], ones], axis=1)
        d_score = (weight * dot_nt(value, do)).astype(bf16)
        total[keys, HEAD_WIDTH:] += dot(weight.astype(bf16), do[:, :HEAD_WIDTH])
        total[keys, :HEAD_WIDTH] += dot(d_score, q[:, :HEAD_WIDTH])
        dq_turned[:, queries] += dot_tn(key, d_score)

    for place, kv_ref, total in zip(places, kv_refs, sums):
        key_start = meta[2 + place]
        key_rows = kv_ref.shape[0]

        @pl.when(block_used(meta, key_start, key_rows, rows))
        def _():
            lanes = key_lanes(meta, key_start, key_rows, bounds_ref)
            ones = jnp.where(lane_index(KEY_CHUNK) < 3, 1.0, 0.0).astype(bf16)
            for c in range(key_rows // KEY_CHUNK):
                if diagonal and place == 0:
                    work(kv_ref, total, lanes, ones, chunk(c), chunk(c), True)
                    if c + 1 < rows // KEY_CHUNK:
                        later = slice((c + 1) * KEY_CHUNK, rows)
                        work(kv_ref, total, lanes, ones, chunk(c), later, False)
                else:
                    work(kv_ref, total, lanes, ones, chunk(c), slice(0, rows), False)

    turned = dq_turned[...].T
    dq_ref[...] = turned if first else dq_in[...] + turned

    @pl.when(step == group - 1)
    def _():
        for ref, total in zip(dkv_refs, sums):
            ref[...] = total[...].astype(ref.dtype)


def attend_back(q, do, blocks, places, bounds, meta, dq, diagonal):
    rows = q.shape[0]
    kv = blocks[0]
    q_heads = q.shape[1] // (2 * HEAD_WIDTH)
    group = q.shape[1] // kv.shape[1]
    width = q_heads * HEAD_WIDTH
    first = dq is None
    count = len(places)
    wide = 2 * HEAD_WIDTH
    per_q = pl.BlockSpec((rows, wide), lambda j, m: (0, j))
    per_kv = pl.BlockSpec((kv.shape[0], wide), lambda j, m: (0, j // group))
    per_out = pl.BlockSpec((rows, HEAD_WIDTH), lambda j, m: (0, j))
    table = pl.BlockSpec((8, HEAD_WIDTH), lambda j, m: (0, 0))
    return pl.pallas_call(
        functools.partial(
            attend_back_kernel, places=places, first=first, group=group, diagonal=diagonal
        ),
        grid_spec=pltpu.PrefetchScalarGridSpec(
            num_scalar_prefetch=1,
            grid=(q_heads,),
            in_specs=[per_q, per_q] + [per_kv] * count + [table] + ([] if first else [per_out]),
            out_specs=[per_out] + [per_kv] * count,
            scratch_shapes=[pltpu.VMEM((HEAD_WIDTH, rows), f32)]
            + [pltpu.VMEM((kv.shape[0], wide), f32)] * count,
        ),
        out_shape=[jax.ShapeDtypeStruct((rows, width), f32)]
        + [jax.ShapeDtypeStruct(kv.shape, bf16 if place else f32) for place in places],
        input_output_aliases={} if first else {4 + count: 0},
        compiler_params=WHOLE_VMEM,
        cost_estimate=SMALL,
        name="attend_back",
    )(meta, q, do, *blocks, bounds, *(() if first else (dq,)))


def project_kernel(meta, base_ref, *refs, count):
    lows, highs = refs[:count], refs[count : 2 * count]
    mine, other = refs[2 * count : 3 * count], refs[3 * count : 4 * count]
    gain_ref, share_ref, normed_ref = refs[4 * count :]
    first_core = meta[0] == 0
    total = base_ref[...].astype(f32)
    for low_ref, high_ref, mine_ref, other_ref in zip(lows, highs, mine, other):
        low, high = low_ref[...], high_ref[...]
        total += dot(jnp.where(first_core, low, high), mine_ref[0])
        total += dot(jnp.where(first_core, high, low), other_ref[0])
    inverse = lax.rsqrt(jnp.mean(total * total, axis=-1, keepdims=True) + EPSILON)
    normed_ref[...] = (total * inverse * gain_ref[...]).astype(bf16)

    @pl.when(pl.program_id(0) == meta[1])
    def _():
        share_ref[...] = total


def project(base, pieces, w_mine, w_other, core, me, gain):
    meta = jnp.stack(
        [jnp.asarray(v, jnp.int32) for v in [core, me] + [piece[2] for piece in pieces]]
    )
    rows, width = base.shape
    n_head, half, unused = w_mine.shape
    count = len(pieces)
    step = rows // n_head
    per_row = pl.BlockSpec((step, width), lambda i, m: (i, 0))
    per_piece = pl.BlockSpec((step, half), lambda i, m: (i, 0))
    weights = [
        pl.BlockSpec((1, half, width), lambda i, m, k=k: (m[2 + k], 0, 0)) for k in range(count)
    ]
    return pl.pallas_call(
        functools.partial(project_kernel, count=count),
        grid_spec=pltpu.PrefetchScalarGridSpec(
            num_scalar_prefetch=1,
            grid=(n_head,),
            in_specs=[per_row]
            + [per_piece] * (2 * count)
            + weights
            + weights
            + [pl.BlockSpec((1, width), lambda i, m: (0, 0))],
            out_specs=[pl.BlockSpec((step, width), lambda i, m: (0, 0)), per_row],
        ),
        out_shape=[
            jax.ShapeDtypeStruct((step, width), f32),
            jax.ShapeDtypeStruct((rows, width), bf16),
        ],
        compiler_params=WHOLE_VMEM,
        cost_estimate=SMALL,
        name="project",
    )(
        meta,
        base,
        *[piece[0] for piece in pieces],
        *[piece[1] for piece in pieces],
        *[w_mine] * count,
        *[w_other] * count,
        gain[None, :],
    )


def arranged_shapes(rows, width):
    return [
        jax.ShapeDtypeStruct((rows // 4, width), bf16),
        jax.ShapeDtypeStruct((rows // 4, width), bf16),
        jax.ShapeDtypeStruct((rows // 2, width), bf16),
    ]


def store_arranged(me, outs, share_y, share_x, half, value):
    along_x, along_y, stays = outs
    rows = value.shape[0]
    other_x = share_x ^ (me & 1)
    other_y = share_y ^ (me >> 1)

    def store(ref, place):
        ref[pl.ds(pl.multiple_of(place * rows, rows), rows), :] = value

    if half == 0:
        pl.when(other_x == 1)(lambda: store(along_x, other_y))
        pl.when(other_x == 0)(lambda: store(stays, other_y))
    else:
        pl.when(other_y == 1)(lambda: store(along_y, other_x))
        pl.when(other_y == 0)(lambda: store(stays, 2 + other_x))


def store_all_arranged(me, outs, value):
    rows = value.shape[0] // 8
    for i in range(8):
        block = value[i * rows : (i + 1) * rows, :]
        store_arranged(me, outs, i // 4, i // 2 % 2, i % 2, block)


def meet_kernel(stays_ref, x_ref, y_ref, mine_ref, to_y_ref, to_x_ref):
    rows = mine_ref.shape[0] // 2
    for start, got_ref, sent_ref in ((0, x_ref, to_y_ref), (2, y_ref, to_x_ref)):
        total = stays_ref[start * rows : (start + 2) * rows, :].astype(f32) + got_ref[...].astype(f32)
        mine_ref[start // 2 * rows : (start // 2 + 1) * rows, :] = total[:rows]
        sent_ref[...] = total[rows:].astype(bf16)


def meet(stays, from_x, from_y):
    rows, width = stays.shape
    return pl.pallas_call(
        meet_kernel,
        out_shape=[
            jax.ShapeDtypeStruct((rows // 2, width), f32),
            jax.ShapeDtypeStruct((rows // 4, width), bf16),
            jax.ShapeDtypeStruct((rows // 4, width), bf16),
        ],
        compiler_params=WHOLE_VMEM,
        cost_estimate=SMALL,
        name="meet",
    )(stays, from_x, from_y)


def share_sum(terms):
    first, *rest = terms
    total = first[...].astype(f32)
    if len(rest) == 2:
        return total + jnp.concatenate([part[...].astype(f32) for part in rest], axis=0)
    return total


def add_rows_kernel(base_ref, *refs):
    *terms, out_ref = refs
    out_ref[...] = (base_ref[...] + share_sum(terms)).astype(bf16)


def add_rows(base, terms):
    return pl.pallas_call(
        add_rows_kernel,
        out_shape=jax.ShapeDtypeStruct(base.shape, bf16),
        compiler_params=WHOLE_VMEM,
        cost_estimate=SMALL,
        name="add_rows",
    )(base, *terms)


def norm_backward(grad, x, gain):
    inverse = lax.rsqrt(jnp.mean(x * x, axis=-1, keepdims=True) + EPSILON)
    hat = x * inverse
    scaled = grad * gain
    back = inverse * (scaled - hat * jnp.mean(scaled * hat, axis=-1, keepdims=True))
    return back, jnp.sum(grad * hat, axis=0, keepdims=True)


def turn_kernel(meta, *refs, count):
    terms = refs[:count]
    hidden_ref, dy_ref, gain_ref, mine_ref, other_ref = refs[count : count + 5]
    *outs, grad_ref, branch_ref, gain_grad_ref = refs[count + 5 :]

    @pl.when(pl.program_id(0) == 0)
    def _():
        back, gain_grad_ref[...] = norm_backward(
            share_sum(terms), hidden_ref[...], gain_ref[...]
        )
        total = dy_ref[...].astype(f32) + back
        grad_ref[...] = total
        branch_ref[...] = total.astype(bf16)

    half = mine_ref.shape[1]
    branch = branch_ref[...]
    mine = dot_nt(branch, mine_ref[0])
    other = dot_nt(branch, other_ref[0])
    first_core = meta[0] == 0
    low = jnp.where(first_core, mine, other).astype(bf16)
    high = jnp.where(first_core, other, mine).astype(bf16)
    for i, out_ref in enumerate(outs):

        @pl.when(pl.program_id(0) == i)
        def _():
            out_ref[:, :half] = low
            out_ref[:, half:] = high


def turn(terms, hidden, dy, gain, w_mine, w_other, core, me):
    rows, width = hidden.shape
    n_head, half, unused = w_mine.shape
    meta = jnp.stack([jnp.asarray(v, jnp.int32) for v in (core, me)])

    def full(array):
        return pl.BlockSpec(array.shape, lambda i, m: (0, 0))

    weight = pl.BlockSpec((1, half, width), lambda i, m: (i ^ m[1], 0, 0))
    share = pl.BlockSpec((rows, width), lambda i, m: (0, 0))
    return pl.pallas_call(
        functools.partial(turn_kernel, count=len(terms)),
        grid_spec=pltpu.PrefetchScalarGridSpec(
            num_scalar_prefetch=1,
            grid=(n_head,),
            in_specs=[full(term) for term in terms]
            + [
                share,
                pl.BlockSpec((rows, width), lambda i, m: (m[1], 0)),
                pl.BlockSpec((1, width), lambda i, m: (0, 0)),
                weight,
                weight,
            ],
            out_specs=[
                *[pl.BlockSpec((rows, 2 * half), lambda i, m: (0, 0))] * n_head,
                share,
                share,
                pl.BlockSpec((1, width), lambda i, m: (0, 0)),
            ],
        ),
        out_shape=[
            *[jax.ShapeDtypeStruct((rows, 2 * half), bf16)] * n_head,
            jax.ShapeDtypeStruct((rows, width), f32),
            jax.ShapeDtypeStruct((rows, width), bf16),
            jax.ShapeDtypeStruct((1, width), f32),
        ],
        compiler_params=WHOLE_VMEM,
        cost_estimate=SMALL,
        name="turn",
    )(meta, *terms, hidden, dy, gain[None, :], w_mine, w_other)


def last_kernel(meta, *refs, count):
    terms = refs[:count]
    x_ref, grad_ref, gain_ref, rider_ref, out_ref = refs[count:]
    rows = x_ref.shape[0]
    back, unused = norm_backward(share_sum(terms), x_ref[...].astype(f32), gain_ref[...])
    out_ref[:rows, :] = (grad_ref[...] + back).astype(bf16)
    out_ref[rows:, :] = rider_ref[...]


def last(terms, tokens, hidden_grad, gain, rider, me):
    rows, width = hidden_grad.shape
    meta = jnp.asarray(me, jnp.int32)[None]

    def full(array):
        return pl.BlockSpec(array.shape, lambda i, m: (0, 0))

    out_rows = rows + rider.shape[0]
    return pl.pallas_call(
        functools.partial(last_kernel, count=len(terms)),
        grid_spec=pltpu.PrefetchScalarGridSpec(
            num_scalar_prefetch=1,
            grid=(1,),
            in_specs=[full(term) for term in terms]
            + [
                pl.BlockSpec((rows, width), lambda i, m: (m[0], 0)),
                full(hidden_grad),
                pl.BlockSpec((1, width), lambda i, m: (0, 0)),
                full(rider),
            ],
            out_specs=pl.BlockSpec((out_rows, width), lambda i, m: (0, 0)),
        ),
        out_shape=jax.ShapeDtypeStruct((out_rows, width), bf16),
        compiler_params=WHOLE_VMEM,
        cost_estimate=SMALL,
        name="last",
    )(meta, *terms, tokens, hidden_grad, gain[None, :], rider)


def feed_kernel(x_ref, gate_w_ref, up_w_ref, d_mixed_ref, mixed_ref, gate_ref, up_ref, sum_ref):
    x = x_ref[...]
    gate = dot(x, gate_w_ref[...])
    up = dot(x, up_w_ref[...])
    d_mixed = d_mixed_ref[...]
    sigmoid = 0.5 * jnp.tanh(0.5 * gate) + 0.5
    silu = gate * sigmoid
    mixed_ref[...] = (silu * up).astype(bf16)
    gate_low = (d_mixed * up * (sigmoid * (1.0 + gate * (1.0 - sigmoid)))).astype(bf16)
    up_low = (d_mixed * silu).astype(bf16)
    gate_ref[...] = gate_low
    up_ref[...] = up_low
    step = gate_low.shape[1]
    sum_ref[:, :step] = dot_tn(x, gate_low).astype(bf16)
    sum_ref[:, step:] = dot_tn(x, up_low).astype(bf16)


def feed(x, w_gate, w_up, d_mixed):
    rows, width = x.shape
    hidden = w_gate.shape[1]
    whole = pl.BlockSpec((rows, width), lambda i: (0, 0))
    weight = pl.BlockSpec((width, HIDDEN_STEP), lambda i: (0, i))
    act = pl.BlockSpec((rows, HIDDEN_STEP), lambda i: (0, i))
    return pl.pallas_call(
        feed_kernel,
        grid=(hidden // HIDDEN_STEP,),
        in_specs=[whole, weight, weight, act],
        out_specs=[act, act, act, pl.BlockSpec((width, 2 * HIDDEN_STEP), lambda i: (0, i))],
        out_shape=[jax.ShapeDtypeStruct((rows, hidden), bf16)] * 3
        + [jax.ShapeDtypeStruct((width, 2 * hidden), bf16)],
        compiler_params=WHOLE_VMEM,
        cost_estimate=SMALL,
        name="feed",
    )(x, w_gate, w_up, d_mixed)


def split_kernel(sum_ref, gate_ref, up_ref):
    step = gate_ref.shape[1]
    gate_ref[...] = sum_ref[:, :step].astype(f32)
    up_ref[...] = sum_ref[:, step:].astype(f32)


def split_gate_up(sums):
    rows, width = sums.shape
    out = pl.BlockSpec((rows, HIDDEN_STEP), lambda i: (0, i))
    return pl.pallas_call(
        split_kernel,
        grid=(width // (2 * HIDDEN_STEP),),
        in_specs=[pl.BlockSpec((rows, 2 * HIDDEN_STEP), lambda i: (0, i))],
        out_specs=[out, out],
        out_shape=[jax.ShapeDtypeStruct((rows, width // 2), f32)] * 2,
        compiler_params=WHOLE_VMEM,
        cost_estimate=SMALL,
        name="split_gate_up",
    )(sums)


def products_kernel(meta, *refs, count, turned, arranged):
    lefts, rights, outs = refs[:count], refs[count : 2 * count], refs[2 * count :]
    total = 0.0
    for left, right in zip(lefts, rights):
        total += (dot_nt if turned else dot)(left[...], right[...])
    if arranged:
        store_all_arranged(meta[0], outs, total.astype(bf16))
    else:
        outs[0][...] = total.astype(bf16)


def products(lefts, rights, turned, me, arranged):
    meta = jnp.asarray(me, jnp.int32)[None]
    rows, depth = lefts[0].shape
    width = rights[0].shape[0 if turned else 1]
    step = width // 4
    whole = pl.BlockSpec((rows, depth), lambda i, m: (0, 0))
    if turned:
        right = pl.BlockSpec((step, depth), lambda i, m: (i, 0))
    else:
        right = pl.BlockSpec((depth, step), lambda i, m: (0, i))
    shapes = arranged_shapes(rows, width) if arranged else [jax.ShapeDtypeStruct((rows, width), bf16)]
    return pl.pallas_call(
        functools.partial(products_kernel, count=len(lefts), turned=turned, arranged=arranged),
        grid_spec=pltpu.PrefetchScalarGridSpec(
            num_scalar_prefetch=1,
            grid=(width // step,),
            in_specs=[whole] * len(lefts) + [right] * len(lefts),
            out_specs=[pl.BlockSpec((v.shape[0], step), lambda i, m: (0, i)) for v in shapes],
        ),
        out_shape=shapes,
        compiler_params=pltpu.CompilerParams(vmem_limit_bytes=46 * MIB),
        cost_estimate=SMALL,
        name="products",
    )(meta, *lefts, *rights)


def down_sums_kernel(mixed_ref, dy_ref, out_ref):
    count, unused, share = out_ref.shape
    for i in range(count):
        out_ref[i] = dot_tn(mixed_ref[...], dy_ref[:, i * share : (i + 1) * share]).astype(bf16)


def down_sums(mixed, dy, shares, more):
    rows, width = dy.shape
    share = width // shares
    hidden = mixed.shape[1]
    return pl.pallas_call(
        down_sums_kernel,
        grid=(shares // 2,),
        in_specs=[
            pl.BlockSpec(mixed.shape, lambda i: (0, 0)),
            pl.BlockSpec((rows, 2 * share), lambda i: (0, i)),
        ],
        out_specs=pl.BlockSpec((2, hidden, share), lambda i: (i, 0, 0)),
        out_shape=jax.ShapeDtypeStruct((shares, hidden + more, share), bf16),
        compiler_params=WHOLE_VMEM,
        cost_estimate=SMALL,
        name="down_sums",
    )(mixed, dy)


def output_sums_kernel(owners, *refs, groups):
    o_refs, pieces, (out_ref, branch) = refs[:groups], refs[groups:-3], refs[-2:]
    for i, piece in enumerate(pieces):
        rows = piece.shape[0]
        branch[pl.ds(pl.multiple_of(owners[i] * rows, rows), rows), :] = piece[...]
    count, unused, share = out_ref.shape
    start = 0
    for o_ref in o_refs:
        end = start + o_ref.shape[1]
        for i in range(count):
            part = branch[:, i * share : (i + 1) * share]
            out_ref[i, start:end, :] = dot_tn(o_ref[...], part).astype(bf16)
        start = end


def output_sums(o_groups, pieces, base):
    owners = jnp.stack([jnp.asarray(owner, jnp.int32) for unused, owner in pieces])
    shares, all_rows, share = base.shape
    size = sum(o.shape[1] for o in o_groups)
    place = all_rows // size - 1
    return pl.pallas_call(
        functools.partial(output_sums_kernel, groups=len(o_groups)),
        grid_spec=pltpu.PrefetchScalarGridSpec(
            num_scalar_prefetch=1,
            grid=(shares // 2,),
            in_specs=[pl.BlockSpec(o.shape, lambda i, m: (0, 0)) for o in o_groups]
            + [
                pl.BlockSpec((piece.shape[0], 2 * share), lambda i, m: (0, i))
                for piece, unused in pieces
            ]
            + [pl.BlockSpec(memory_space=pl.ANY)],
            out_specs=pl.BlockSpec((2, size, share), lambda i, m: (i, place, 0)),
            scratch_shapes=[pltpu.VMEM((o_groups[0].shape[0], 2 * share), bf16)],
        ),
        out_shape=jax.ShapeDtypeStruct(base.shape, bf16),
        input_output_aliases={1 + len(o_groups) + len(pieces): 0},
        compiler_params=WHOLE_VMEM,
        cost_estimate=SMALL,
        name="output_sums",
    )(owners, *o_groups, *[piece for piece, unused in pieces], base)


def pass_on_kernel(part_ref, theirs_ref, *refs, count):
    arrived, outs = refs[:-count], refs[-count:]
    size = outs[0].shape[0]
    for i, out_ref in enumerate(outs):
        rows = slice(i * size, (i + 1) * size)
        out_ref[...] = (part_ref[rows, :] + theirs_ref[rows, :].astype(f32)).astype(bf16)
    if arrived:
        whole = jnp.concatenate([ref[...] for ref in arrived], axis=0).astype(f32)
        for i, out_ref in enumerate(outs):
            rows = slice(i * size, (i + 1) * size)
            total = part_ref[rows, :] + theirs_ref[rows, :].astype(f32) + whole[rows]
            out_ref[...] = total.astype(bf16)


def pass_on(part, theirs, arrived, count):
    rows, width = part.shape
    return pl.pallas_call(
        functools.partial(pass_on_kernel, count=count),
        out_shape=[jax.ShapeDtypeStruct((rows // count, width), bf16)] * count,
        compiler_params=WHOLE_VMEM,
        cost_estimate=SMALL,
        name="pass_on",
    )(part, theirs, *arrived)


def leave_kernel(
    meta,
    x_ref,
    q_ref,
    dkv_ref,
    theirs_ref,
    first_ref,
    second_ref,
    raw_ref,
    key_gain_ref,
    cos_ref,
    sin_ref,
    q_w_ref,
    key_w_ref,
    value_w_ref,
    key_ref,
    value_ref,
    gain_grad_ref,
    norm_grad_ref,
    *refs,
    arranged,
):
    *outs, arrived_ref = refs

    @pl.when(pl.program_id(0) == 0)
    def _():
        size = first_ref.shape[0]
        for i, ref in enumerate((first_ref, second_ref)):
            arrived_ref[i * size : (i + 1) * size, :] = ref[...]
        gain_grad_ref[...] = jnp.zeros_like(gain_grad_ref)
        norm_grad_ref[...] = jnp.zeros_like(norm_grad_ref)

    rows = dkv_ref.shape[0]
    here = pl.ds(pl.multiple_of(pl.program_id(0) * rows, rows), rows)
    arrived = arrived_ref[here, :]
    dkv = dkv_ref[...] + theirs_ref[...].astype(f32) + arrived.astype(f32)
    for j in range(key_ref.shape[1] // HEAD_WIDTH):
        head = slice(j * HEAD_WIDTH, (j + 1) * HEAD_WIDTH)
        start = 2 * j * HEAD_WIDTH
        grad, gain_grad = head_backward(
            raw_ref[:, head],
            dkv[:, start : start + HEAD_WIDTH] * (1.0 / LOG2E),
            key_gain_ref[...],
            cos_ref[...],
            sin_ref[...],
        )
        key_ref[:, head] = grad
        value_ref[:, head] = dkv[:, start + HEAD_WIDTH : start + 2 * HEAD_WIDTH].astype(bf16)
        gain_grad_ref[...] += gain_grad
    total = dot_nt(q_ref[...], q_w_ref[...])
    total += dot_nt(key_ref[...], key_w_ref[...])
    total += dot_nt(value_ref[...], value_w_ref[...])
    result = total.astype(bf16)
    if arranged:
        block = result.shape[0] // 4
        for i in range(4):
            store_arranged(
                meta[0],
                outs,
                pl.program_id(0),
                i // 2,
                i % 2,
                result[i * block : (i + 1) * block, :],
            )
    else:
        outs[0][...] = result
    x = x_ref[...].astype(f32)
    hat = x * lax.rsqrt(jnp.mean(x * x, axis=-1, keepdims=True) + EPSILON)
    norm_grad_ref[...] += jnp.sum(total * hat, axis=0, keepdims=True)


def leave(tokens, q_grad, dkv, theirs, arrived, key_raw, key_gain, cosine, sine, weights, me, arranged):
    meta = jnp.asarray(me, jnp.int32)[None]
    rows, width = tokens.shape
    kv_width = key_raw.shape[1]
    step = rows // 2

    def per_row(array):
        return pl.BlockSpec((step, array.shape[1]), lambda i, m: (i, 0))

    def full(array):
        return pl.BlockSpec(array.shape, lambda i, m: (0, 0))

    key_gain = key_gain[None, :]
    if arranged:
        shapes = arranged_shapes(rows, width)
        out_specs = [full(v) for v in shapes]
    else:
        shapes = [jax.ShapeDtypeStruct((rows, width), bf16)]
        out_specs = [per_row(shapes[0])]
    return pl.pallas_call(
        functools.partial(leave_kernel, arranged=arranged),
        grid_spec=pltpu.PrefetchScalarGridSpec(
            num_scalar_prefetch=1,
            grid=(2,),
            in_specs=[per_row(v) for v in (tokens, q_grad, dkv, theirs)]
            + [full(v) for v in arrived]
            + [per_row(key_raw), full(key_gain), per_row(cosine), per_row(sine)]
            + [full(v) for v in weights],
            out_specs=[
                per_row(key_raw),
                per_row(key_raw),
                pl.BlockSpec((1, HEAD_WIDTH), lambda i, m: (0, 0)),
                pl.BlockSpec((1, width), lambda i, m: (0, 0)),
            ]
            + out_specs,
            scratch_shapes=[pltpu.VMEM((rows, theirs.shape[1]), bf16)],
        ),
        out_shape=[
            jax.ShapeDtypeStruct((rows, kv_width), bf16),
            jax.ShapeDtypeStruct((rows, kv_width), bf16),
            jax.ShapeDtypeStruct((1, HEAD_WIDTH), f32),
            jax.ShapeDtypeStruct((1, width), f32),
        ]
        + shapes,
        compiler_params=WHOLE_VMEM,
        cost_estimate=SMALL,
        name="leave",
    )(meta, tokens, q_grad, dkv, theirs, *arrived, key_raw, key_gain, cosine, sine, *weights)


def attn_sums_kernel(x_ref, *refs):
    *terms, out_ref = refs
    x = x_ref[...]
    start = 0
    for ref in terms:
        out_ref[:, start : start + ref.shape[1]] = dot_tn(x, ref[...]).astype(bf16)
        start += ref.shape[1]


def attn_sums(x, terms):
    rows, width = x.shape
    step = width // 8
    out_width = sum(term.shape[1] for term in terms)
    return pl.pallas_call(
        attn_sums_kernel,
        grid=(width // step,),
        in_specs=[pl.BlockSpec((rows, step), lambda i: (0, i))]
        + [pl.BlockSpec(term.shape, lambda i: (0, 0)) for term in terms],
        out_specs=pl.BlockSpec((step, out_width), lambda i: (i, 0)),
        out_shape=jax.ShapeDtypeStruct((width, out_width), bf16),
        compiler_params=WHOLE_VMEM,
        cost_estimate=SMALL,
        name="attn_sums",
    )(x, *terms)


def after(values):
    return lax.optimization_barrier(values)


def pick(array, index):
    return lax.dynamic_index_in_dim(array, index, 0, keepdims=False)


def solution(mesh):
    n_seq = mesh.shape["seq"]
    n_head = mesh.shape["head"]
    n_chip = n_seq // 2

    def swap_core(value):
        return lax.ppermute(value, "seq", [(i, i ^ 1) for i in range(n_seq)])

    def to_next(value):
        return lax.ppermute(value, "seq", [(i, i + 2) for i in range(n_seq - 2)])

    def to_previous(value):
        return lax.ppermute(value, "seq", [(i + 2, i) for i in range(n_seq - 2)])

    def across(value, bits):
        return lax.ppermute(value, "head", [(i, i ^ bits) for i in range(n_head)])

    def gather_steps(value):
        me = lax.axis_index("head")
        if n_head != 4:
            every = yield lax.all_gather(value, "head", axis=0)
            return [(every[i], i) for i in range(n_head)]
        half = value.shape[0] // 2
        by_x, by_y = yield across(value, 1), across(value, 2)
        low, high = yield across(by_x[:half], 2), across(by_y[half:], 1)
        far = jnp.concatenate([low, high], axis=0)
        return [(value, me), (by_x, me ^ 1), (by_y, me ^ 2), (far, me ^ 3)]

    def rider_entries(value, count):
        me = lax.axis_index("head")
        half = count // 2
        if n_head != 4:
            every = yield lax.all_gather(value, "head", axis=0)
            entries = [(every[i], k, 2 * i + k) for i in range(n_head) for k in range(2)]
            return entries, [every[i, count:] for i in range(n_head)]
        by_x, by_y = yield across(value, 1), across(value, 2)
        low, high = yield across(by_x[:half], 2), across(by_y[half:], 1)
        owners = ((value, me), (by_x, me ^ 1), (by_y, me ^ 2))
        entries = [(array, k, 2 * owner + k) for array, owner in owners for k in range(2)]
        entries += [(low, 0, 2 * (me ^ 3)), (high, 0, 2 * (me ^ 3) + 1)]
        return entries, [value[count:], by_x[count:], by_y[count:], high[half:]]

    def scatter_steps(value):
        if n_head != 4:
            total = yield lax.psum_scatter(value[0], "head", scatter_dimension=0, tiled=True)
            return (total,)
        along_x, along_y, stays = value
        from_x, from_y = yield across(along_x, 1), across(along_y, 2)
        mine, to_y, to_x = meet(stays, from_x, from_y)
        first, second = yield across(to_y, 2), across(to_x, 1)
        return mine, first, second

    def run_steps(steps, works=()):
        works = list(works)
        made = []
        arrived = next(steps)
        while True:
            if works:
                arrived, done = after((arrived, works.pop(0)()))
                made.append(done)
            try:
                arrived = steps.send(arrived)
            except StopIteration as stop:
                return stop.value, made + [work() for work in works]

    def end_steps(steps, arrived):
        try:
            steps.send(arrived)
        except StopIteration as stop:
            return stop.value

    def exchange_head(value):
        me = lax.axis_index("head")
        if n_head == 4:
            return [(value[0], me)] + [(across(value[i], i), me ^ i) for i in (3, 1, 2)]
        value = jnp.stack(value)
        ordered = jnp.stack([pick(value, i ^ me) for i in range(n_head)])
        got = lax.all_to_all(ordered, "head", 0, 0)
        return [(got[i], i) for i in range(n_head)]

    def body(
        tokens,
        lengths,
        norm1_gain,
        w_query,
        key_matrix,
        value_matrix,
        query_gain,
        key_gain,
        w_output,
        norm2_gain,
        w_gate,
        w_up,
        w_down,
        cotangent,
    ):
        rows = tokens.shape[0]
        share = rows // n_head
        seq_index = lax.axis_index("seq")
        head_index = lax.axis_index("head")
        chip, core = seq_index // 2, seq_index % 2
        cut = n_head == 4

        index = seq_index * rows + jnp.arange(rows, dtype=jnp.int32)
        begin = locate(index, lengths)
        cosine, sine = rotary(index - begin)
        ends = jnp.cumsum(lengths)
        n_lengths = lengths.shape[0]
        bounds = jnp.zeros((8, HEAD_WIDTH), jnp.int32).at[0].set(2**30)
        bounds = bounds.at[0, :n_lengths].set(ends - lengths).at[1, :n_lengths].set(ends)

        def stage_meta(stage):
            source = 2 * (chip - stage)
            return jnp.stack(
                [seq_index * rows, begin[0], (source + core) * rows, (source + 1 - core) * rows]
            ).astype(jnp.int32)

        metas = [stage_meta(stage) for stage in range(n_chip)]

        first_in, key_raw, current = enter(
            tokens, norm1_gain, key_matrix, value_matrix, key_gain, cosine, sine
        )
        sibling = swap_core(current)
        following = to_next(current)

        half_rows = w_output.shape[0] // 2
        w_late, unused = after((w_output, current))
        w_half = lax.dynamic_slice_in_dim(w_late, core * half_rows, half_rows, 0)
        w_mine = lax.all_gather(w_half, "head", axis=0)

        query_raw = dot(first_in, w_query)
        q_wide = query_prep(metas[0], query_raw, query_gain, cosine, sine, bounds)
        following, q_wide = after((following, q_wide))

        blocks = []
        carried = ()
        for stage in range(n_chip):
            blocks.append((current, sibling))
            if stage + 2 < n_chip:
                current = following
                sibling = swap_core(current)
                following = to_next(current)
            if stage == n_chip - 1:
                break
            carried = attend_stage(q_wide, blocks[stage], (0, 1), bounds, metas[stage], carried)
            if stage + 3 < n_chip:
                following, carried = after((following, carried))
            if stage + 2 == n_chip:
                current, carried = after((following, carried))
                sibling = swap_core(current)
        groups = 2 if cut else 1
        w_mine, sibling, carried = after((w_mine, sibling, carried))
        blocks[-1] = (current, sibling)
        w_other = swap_core(w_mine)
        outcome, total = carried
        o_first, q_back, outcome = attend_stage(
            q_wide, blocks[-1], (0, 1), bounds, metas[-1], (outcome, total), (0, groups)
        )
        if cut:
            first_steps = gather_steps(o_first)
            got_first = next(first_steps)
            o_second, q_back, outcome = attend_stage(
                q_back, blocks[-1], (0, 1), bounds, metas[-1], (outcome, total), (1, groups)
            )
            got_first, o_second = after((got_first, o_second))
            second_steps = gather_steps(o_second)
            got_second = next(second_steps)
            got_first = first_steps.send(got_first)
            o_groups = (o_first, o_second)
            dy, unused = after((cotangent, o_second))
            d_mixed = dot_nt(dy, w_down)
            got_second, d_mixed = after((got_second, d_mixed))
            got_second = second_steps.send(got_second)
            got_first, d_mixed = after((got_first, d_mixed))
            first_pieces = end_steps(first_steps, got_first)
            second_pieces = end_steps(second_steps, got_second)
            pieces = [(low[0], high[0], low[1]) for low, high in zip(first_pieces, second_pieces)]
        else:
            o_groups = (o_first,)
            half = o_first.shape[1] // 2
            every = lax.all_gather(o_first, "head", axis=0)
            pieces = [(every[i, :, :half], every[i, :, half:], i) for i in range(n_head)]
            d_mixed = dot_nt(cotangent, w_down)
        my_hidden, second_in = project(
            tokens, pieces, w_mine, w_other, core, head_index, norm2_gain
        )
        def scatter_seq(value, tiled):
            return lax.psum_scatter(value, "seq", scatter_dimension=0, tiled=tiled)

        mixed_low, gate_low, up_low, gate_up_sum = feed(second_in, w_gate, w_up, d_mixed)
        grad_gate_up = scatter_seq(gate_up_sum, True)

        flow = scatter_steps(products((gate_low, up_low), (w_gate, w_up), True, head_index, cut))
        got = next(flow)
        down_part = products((mixed_low,), (w_down,), False, head_index, cut)
        got, down_part = after((got, down_part))
        if cut:
            got = flow.send(got)
        column_sum = down_sums(mixed_low, cotangent, n_seq, w_output.shape[0])
        got, column_sum = after((got, column_sum))
        terms = end_steps(flow, got)
        *do_pieces, hidden_grad, my_branch, grad_norm2 = turn(
            terms, my_hidden, cotangent, norm2_gain, w_mine, w_other, core, head_index
        )
        do_wide = with_delta(exchange_head(do_pieces), outcome)
        down_part, my_branch, do_wide = after((down_part, my_branch, do_wide))

        dq = None
        parts = []
        moving = []
        landed = []
        hops = 0

        def hop_piece():
            if not moving:
                return None
            value = moving.pop(0)
            return lambda: to_previous(value)

        def stage_work(stage, places=(0, 1)):
            chosen = [blocks[stage][place] for place in places]
            return attend_back(
                q_back, do_wide, chosen, places, bounds, metas[stage], dq, stage == 0
            )

        def next_hop():
            nonlocal dq, hops
            if hops < n_chip - 1 and len(parts) > hops and len(landed) == (2 if hops else 0) and hops < n_chip - 1:
                sent, dq = after((pass_on(*parts[hops], landed, 2), dq))
                landed.clear()
                moving.extend(sent)
                hops += 1

        branch_steps = gather_steps(my_branch)
        (dq, dkv_a, dkv_b), got_branch = after(
            (stage_work(n_chip - 1), next(branch_steps))
        )
        theirs, dq = after((swap_core(dkv_b), dq))
        parts.append((dkv_a, theirs))
        next_hop()
        flying = hop_piece()()
        if cut:
            got_branch = branch_steps.send(got_branch)
        (dq, dkv_a, dkv_b), got_branch, flying = after(
            (stage_work(n_chip - 2), got_branch, flying)
        )
        branch_pieces = end_steps(branch_steps, got_branch)
        landed.append(flying)
        parts.append((dkv_a, swap_core(dkv_b)))
        flying = hop_piece()()
        column_sum = output_sums(o_groups, branch_pieces, column_sum)
        dkv_a, theirs = parts[1]
        column_sum, flying, theirs, dq = after((column_sum, flying, theirs, dq))
        parts[1] = (dkv_a, theirs)
        landed.append(flying)
        grad_gate_up, column_sum, dq, landed[:] = after(
            (grad_gate_up, column_sum, dq, list(landed))
        )
        grad_columns = scatter_seq(column_sum, False)
        next_hop()
        down_part, dq = after((down_part, dq))
        mixed_steps = scatter_steps(down_part)
        got_mixed = next(mixed_steps)
        for stage in reversed(range(1, n_chip - 2)):
            hop = hop_piece()
            flying = None if hop is None else hop()
            (dq, dkv_a, dkv_b), got_mixed, flying = after((stage_work(stage), got_mixed, flying))
            if hop is not None:
                landed.append(flying)
            parts.append((dkv_a, swap_core(dkv_b)))
            next_hop()
        if cut:
            got_mixed = mixed_steps.send(got_mixed)
        hop = hop_piece()
        flying = None if hop is None else hop()
        (dq, dkv_b), got_mixed, flying = after((stage_work(0, (1,)), got_mixed, flying))
        if hop is not None:
            landed.append(flying)
        theirs = swap_core(dkv_b)
        next_hop()
        my_mixed = add_rows(my_hidden, end_steps(mixed_steps, got_mixed))
        my_mixed, dq = after((my_mixed, dq))
        mixed_steps = gather_steps(my_mixed)
        got_mixed = next(mixed_steps)
        hop = hop_piece()
        flying = None if hop is None else hop()
        (dq, dkv_a), theirs, flying = after((stage_work(0, (0,)), theirs, flying))
        if hop is not None:
            landed.append(flying)
        parts.append((dkv_a, theirs))
        while hops < n_chip - 1:
            while len(landed) < 2:
                landed.append(hop_piece()())
            next_hop()
        flying = [hop_piece()() for unused in range(2 - len(landed))]
        query_grad, grad_qgain = head_back(query_raw, dq, query_gain, cosine, sine, SCORE_SCALE, 1)
        if cut:
            got_mixed, query_grad = after((got_mixed, query_grad))
            got_mixed = mixed_steps.send(got_mixed)
        flying, got_mixed, query_grad = after((flying, got_mixed, query_grad))
        landed = (*landed, *flying)
        mixed_pieces = end_steps(mixed_steps, got_mixed)
        key_grad, value_grad, grad_kgain, grad_norm1, *first_part = leave(
            tokens,
            query_grad,
            *parts[-1],
            landed,
            key_raw,
            key_gain,
            cosine,
            sine,
            (w_query, key_matrix, value_matrix),
            head_index,
            cut,
        )
        gains = jnp.concatenate([grad_norm1[0], grad_norm2[0], grad_qgain[0], grad_kgain[0]])
        gains = gains.reshape(-1, HEAD_WIDTH)

        def sum_seq(total, bits):
            for bit in bits:
                total = total + lax.ppermute(total, "seq", [(i, i ^ bit) for i in range(n_seq)])
            return total

        bits = [1 << k for k in range(n_seq.bit_length() - 1)]
        steps = scatter_steps(first_part)
        got = next(steps)
        attn_sum = attn_sums(first_in, (query_grad, key_grad, value_grad))
        gains = sum_seq(gains, bits[:1])
        gains, attn_sum = after((gains, attn_sum))
        got, gains, attn_sum = after((got, gains, attn_sum))
        if cut:
            got = steps.send(got)
        grad_columns, attn_sum = after((grad_columns, attn_sum))
        grad_attn = scatter_seq(attn_sum, True)
        grad_query, grad_key, grad_value = cut_columns(
            grad_attn, (query_grad.shape[1], key_grad.shape[1], value_grad.shape[1])
        )
        got, gains = after((got, sum_seq(gains, bits[1:])))
        terms = end_steps(steps, got)

        width = tokens.shape[1]
        n_gains = gains.size
        gain_rows = -(-n_gains // width)
        flat = jnp.pad(gains.reshape(-1), (0, gain_rows * width - n_gains))
        high = lax.reduce_precision(flat, 8, 7)
        middle = lax.reduce_precision(flat - high, 8, 7)
        rider = jnp.concatenate([high, middle, flat - high - middle]).astype(bf16)
        rider = rider.reshape(3 * gain_rows, width)
        rider = jnp.pad(rider, ((0, -rider.shape[0] % 16), (0, 0)))
        my_tokens_grad = last(terms, tokens, hidden_grad, norm1_gain, rider, head_index)
        steps = rider_entries(my_tokens_grad, share)
        got = next(steps)
        mixed = assemble([(piece, 0, owner) for piece, owner in mixed_pieces], share, bf16)
        grad_down, grad_output = cut_rows(grad_columns, (w_gate.shape[1], w_output.shape[0]))
        grad_gate, grad_up = split_gate_up(grad_gate_up)
        got, mixed, grad_down, grad_output, grad_gate, grad_up = after(
            (got, mixed, grad_down, grad_output, grad_gate, grad_up)
        )
        if cut:
            got = steps.send(got)
        entries, gain_pieces = end_steps(steps, got)
        near = len(entries) - 2
        grad_tokens = assemble(entries[:near], share // 2, f32, len(entries))
        grad_tokens = assemble(entries[near:], share // 2, f32, len(entries), grad_tokens)
        gains = sum(part[: 3 * gain_rows].astype(f32) for part in gain_pieces)
        gains = jnp.sum(gains.reshape(3, -1), axis=0)
        grad_norm1, grad_norm2 = gains[:width], gains[width : 2 * width]
        grad_qgain = gains[2 * width : 2 * width + HEAD_WIDTH]
        grad_kgain = gains[2 * width + HEAD_WIDTH : n_gains]
        return (
            mixed,
            grad_tokens,
            grad_norm1,
            grad_query,
            grad_key,
            grad_value,
            grad_qgain,
            grad_kgain,
            grad_output,
            grad_norm2,
            grad_gate,
            grad_up,
            grad_down,
        )

    in_specs = (
        P("seq", None),
        P(),
        P(),
        P(None, "head"),
        P(None, "head"),
        P(None, "head"),
        P(),
        P(),
        P("head", None),
        P(),
        P(None, "head"),
        P(None, "head"),
        P("head", None),
        P("seq", None),
    )
    out_specs = (
        P("seq", None),
        P("seq", None),
        P(),
        P("seq", "head"),
        P("seq", "head"),
        P("seq", "head"),
        P(),
        P(),
        P("head", "seq"),
        P(),
        P("seq", "head"),
        P("seq", "head"),
        P("head", "seq"),
    )
    return jax.shard_map(body, mesh=mesh, in_specs=in_specs, out_specs=out_specs, check_vma=False)
```

```python
import functools
import math

import jax
import jax.numpy as jnp
from jax import lax
from jax.experimental import pallas as pl
from jax.experimental.pallas import tpu as pltpu
from jax.sharding import PartitionSpec as P

HEAD_WIDTH = 128
EPSILON = 1e-06
ROPE_BASE = 1000000.0
LOG2E = math.log2(math.e)
SCORE_SCALE = 1.0 / math.sqrt(HEAD_WIDTH)
SCORE_SCALE_2 = LOG2E / math.sqrt(HEAD_WIDTH)
KEY_CHUNK = 256
HIDDEN_STEP = 256
FAR = 512.0
LOG_LANE = 64
MIB = 2**20
SMALL = pl.CostEstimate(flops=1, bytes_accessed=1, transcendentals=0)
WHOLE_VMEM = pltpu.CompilerParams(vmem_limit_bytes=52 * MIB)

f32 = jnp.float32
bf16 = jnp.bfloat16
NT = (((1,), (1,)), ((), ()))
TN = (((0,), (0,)), ((), ()))


def dot(left, right):
    return jnp.dot(left, right, preferred_element_type=f32)


def dot_nt(left, right):
    return lax.dot_general(left, right, NT, preferred_element_type=f32)


def dot_tn(left, right):
    return lax.dot_general(left, right, TN, preferred_element_type=f32)


def locate(index, lengths):
    ends = jnp.cumsum(lengths)
    starts = ends - lengths
    segment = jnp.sum((index[:, None] >= ends[None, :]).astype(jnp.int32), axis=1)
    chosen = segment[:, None] == jnp.arange(lengths.shape[0], dtype=jnp.int32)[None, :]
    return jnp.sum(jnp.where(chosen, starts[None, :], 0), axis=1)


def rotary(position):
    half = HEAD_WIDTH // 2
    freq = jnp.exp(jnp.arange(half, dtype=f32) * (-2.0 * math.log(ROPE_BASE) / HEAD_WIDTH))
    angle = position.astype(f32)[:, None] * freq[None, :]
    cosine = jnp.cos(angle)
    sine = jnp.sin(angle)
    return (
        jnp.concatenate([cosine, cosine], axis=1),
        jnp.concatenate([-sine, sine], axis=1),
    )


def lane_index(rows):
    return lax.broadcasted_iota(jnp.int32, (rows, HEAD_WIDTH), 1)


def row_index(rows):
    return lax.broadcasted_iota(jnp.int32, (rows, HEAD_WIDTH), 0)


def in_segment(index, bounds_ref):
    return (index >= bounds_ref[0:1, :]) & (index < bounds_ref[1:2, :])


def split_parts(value):
    high = value.astype(bf16)
    rest = value - high.astype(f32)
    middle = rest.astype(bf16)
    return high, middle, (rest - middle.astype(f32)).astype(bf16)


def normed(raw, gain, cosine, sine):
    inverse = lax.rsqrt(jnp.mean(raw * raw, axis=-1, keepdims=True) + EPSILON)
    scaled = raw * inverse * gain
    return scaled * cosine + pltpu.roll(scaled, HEAD_WIDTH // 2, 1) * sine


def enter_kernel(
    x_ref, gain_ref, key_w_ref, value_w_ref, key_gain_ref, cos_ref, sin_ref, in_ref, raw_ref, kv_ref
):
    x = x_ref[...].astype(f32)
    inverse = lax.rsqrt(jnp.mean(x * x, axis=-1, keepdims=True) + EPSILON)
    first_in = (x * inverse * gain_ref[...]).astype(bf16)
    in_ref[...] = first_in
    raw = dot(first_in, key_w_ref[...])
    raw_ref[...] = raw
    value = dot(first_in, value_w_ref[...]).astype(bf16)
    for j in range(raw.shape[1] // HEAD_WIDTH):
        head = slice(j * HEAD_WIDTH, (j + 1) * HEAD_WIDTH)
        key = normed(raw[:, head], key_gain_ref[...], cos_ref[...], sin_ref[...])
        start = 2 * j * HEAD_WIDTH
        kv_ref[:, start : start + HEAD_WIDTH] = key.astype(bf16)
        kv_ref[:, start + HEAD_WIDTH : start + 2 * HEAD_WIDTH] = value[:, head]


def enter(tokens, gain, key_w, value_w, key_gain, cosine, sine):
    rows, width = tokens.shape
    kv_width = key_w.shape[1]
    step = rows // 3 if rows % 768 == 0 else rows
    table = pl.BlockSpec((step, HEAD_WIDTH), lambda i: (i, 0))
    weight = pl.BlockSpec((width, kv_width), lambda i: (0, 0))
    return pl.pallas_call(
        enter_kernel,
        grid=(rows // step,),
        in_specs=[
            pl.BlockSpec((step, width), lambda i: (i, 0)),
            pl.BlockSpec((1, width), lambda i: (0, 0)),
            weight,
            weight,
            pl.BlockSpec((1, HEAD_WIDTH), lambda i: (0, 0)),
            table,
            table,
        ],
        out_specs=[
            pl.BlockSpec((step, width), lambda i: (i, 0)),
            pl.BlockSpec((step, kv_width), lambda i: (i, 0)),
            pl.BlockSpec((step, 2 * kv_width), lambda i: (i, 0)),
        ],
        out_shape=[
            jax.ShapeDtypeStruct((rows, width), bf16),
            jax.ShapeDtypeStruct((rows, kv_width), f32),
            jax.ShapeDtypeStruct((rows, 2 * kv_width), bf16),
        ],
        compiler_params=WHOLE_VMEM,
        cost_estimate=SMALL,
        name="enter",
    )(tokens, gain[None, :], key_w, value_w, key_gain[None, :], cosine, sine)


def query_prep_kernel(meta, raw_ref, gain_ref, cos_ref, sin_ref, bounds_ref, out_ref):
    rows = raw_ref.shape[0]
    query = normed(raw_ref[...], gain_ref[...], cos_ref[...], sin_ref[...])
    out_ref[:, :HEAD_WIDTH] = (query * SCORE_SCALE_2).astype(bf16)
    inside = in_segment(meta[0] + row_index(rows), bounds_ref)
    free = inside | (lane_index(rows) >= LOG_LANE)
    out_ref[:, HEAD_WIDTH:] = jnp.where(free, 0.0, -FAR).astype(bf16)


def query_prep(meta, raw, gain, cosine, sine, bounds):
    rows, width = raw.shape
    table = pl.BlockSpec((rows, HEAD_WIDTH), lambda j, m: (0, 0))
    return pl.pallas_call(
        query_prep_kernel,
        grid_spec=pltpu.PrefetchScalarGridSpec(
            num_scalar_prefetch=1,
            grid=(width // HEAD_WIDTH,),
            in_specs=[
                pl.BlockSpec((rows, HEAD_WIDTH), lambda j, m: (0, j)),
                pl.BlockSpec((1, HEAD_WIDTH), lambda j, m: (0, 0)),
                table,
                table,
                pl.BlockSpec((8, HEAD_WIDTH), lambda j, m: (0, 0)),
            ],
            out_specs=pl.BlockSpec((rows, 2 * HEAD_WIDTH), lambda j, m: (0, j)),
        ),
        out_shape=jax.ShapeDtypeStruct((rows, 2 * width), bf16),
        compiler_params=WHOLE_VMEM,
        cost_estimate=SMALL,
        name="query_prep",
    )(meta, raw, gain[None, :], cosine, sine, bounds)


def head_backward(raw, grad, gain, cosine, sine):
    inverse = lax.rsqrt(jnp.mean(raw * raw, axis=-1, keepdims=True) + EPSILON)
    hat = raw * inverse
    back = grad * cosine - pltpu.roll(grad, HEAD_WIDTH // 2, 1) * sine
    gain_grad = jnp.sum(back * hat, axis=0, keepdims=True)
    back = back * gain
    back = inverse * (back - hat * jnp.mean(back * hat, axis=-1, keepdims=True))
    return back.astype(bf16), gain_grad


def head_back_kernel(raw_ref, grad_ref, gain_ref, cos_ref, sin_ref, out_ref, gain_grad_ref, *, scale):
    @pl.when(pl.program_id(0) == 0)
    def _():
        gain_grad_ref[...] = jnp.zeros_like(gain_grad_ref)

    out_ref[...], gain_grad = head_backward(
        raw_ref[...], grad_ref[...] * scale, gain_ref[...], cos_ref[...], sin_ref[...]
    )
    gain_grad_ref[...] += gain_grad


def head_back(raw, grad, gain, cosine, sine, scale, stride):
    rows, width = raw.shape
    block = pl.BlockSpec((rows, HEAD_WIDTH), lambda j: (0, j))
    spaced = pl.BlockSpec((rows, HEAD_WIDTH), lambda j: (0, j * stride))
    table = pl.BlockSpec((rows, HEAD_WIDTH), lambda j: (0, 0))
    one = pl.BlockSpec((1, HEAD_WIDTH), lambda j: (0, 0))
    return pl.pallas_call(
        functools.partial(head_back_kernel, scale=scale),
        grid=(width // HEAD_WIDTH,),
        in_specs=[block, spaced, one, table, table],
        out_specs=[block, one],
        out_shape=[
            jax.ShapeDtypeStruct((rows, width), bf16),
            jax.ShapeDtypeStruct((1, HEAD_WIDTH), f32),
        ],
        compiler_params=WHOLE_VMEM,
        cost_estimate=SMALL,
        name="head_back",
    )(raw, grad, gain[None, :], cosine, sine)


def key_lanes(meta, key_start, rows, bounds_ref):
    inside = in_segment(key_start + row_index(rows), bounds_ref)
    lanes = lane_index(rows)
    log_lanes = (lanes >= LOG_LANE) & (lanes < LOG_LANE + 3)
    return jnp.where(inside | log_lanes, 1.0, 0.0).astype(bf16)


def block_used(meta, key_start, key_rows, rows):
    return (
        (key_start >= 0) & (key_start <= meta[0] + rows - 1) & (key_start + key_rows - 1 >= meta[1])
    )


def lower_mask(transposed):
    shape = (KEY_CHUNK, KEY_CHUNK)
    first = lax.broadcasted_iota(jnp.int32, shape, 0)
    second = lax.broadcasted_iota(jnp.int32, shape, 1)
    return first <= second if transposed else second <= first


def chunk(i, n=1):
    return slice(i * KEY_CHUNK, (i + n) * KEY_CHUNK)


def attend_kernel(meta, q_ref, *refs, places, first, last):
    kv_refs, bounds_ref, refs = refs[: len(places)], refs[len(places)], refs[len(places) + 1 :]
    rows = q_ref.shape[0]
    if last:
        acc_in, sum_in, o_ref, q_out_ref, acc_ref, sum_ref = refs
    elif first:
        acc_ref, sum_ref = refs
    else:
        acc_in, sum_in, acc_ref, sum_ref = refs
    if first:
        acc_ref[...] = jnp.zeros_like(acc_ref)
        sum_ref[...] = jnp.zeros_like(sum_ref)
    else:
        acc_ref[...] = acc_in[...]
        sum_ref[...] = sum_in[...]
    ones = jnp.ones((KEY_CHUNK, HEAD_WIDTH), bf16)

    def work(kv_ref, lanes, keys, queries, mask):
        key = jnp.concatenate([kv_ref[keys, :HEAD_WIDTH], lanes[keys, :]], axis=1)
        weight = jnp.exp2(dot_nt(q_ref[queries, :], key))
        if mask:
            weight = jnp.where(lower_mask(False), weight, 0.0)
        value = jnp.concatenate([kv_ref[keys, HEAD_WIDTH:], ones], axis=1)
        out = dot(weight.astype(bf16), value)
        acc_ref[queries, :] += out[:, :HEAD_WIDTH]
        sum_ref[queries, :] += out[:, HEAD_WIDTH:]

    for place, kv_ref in zip(places, kv_refs):
        key_start = meta[2 + place]
        key_rows = kv_ref.shape[0]
        diagonal = first and place == 0

        @pl.when(block_used(meta, key_start, key_rows, rows))
        def _():
            lanes = key_lanes(meta, key_start, key_rows, bounds_ref)
            for c in range(key_rows // KEY_CHUNK):
                if diagonal:
                    work(kv_ref, lanes, chunk(c), chunk(c), True)
                    if c + 1 < rows // KEY_CHUNK:
                        work(kv_ref, lanes, chunk(c), slice((c + 1) * KEY_CHUNK, rows), False)
                else:
                    work(kv_ref, lanes, chunk(c), slice(0, rows), False)

    if last:
        total = sum_ref[...]
        outcome = acc_ref[...] / total
        acc_ref[...] = outcome
        o_ref[...] = outcome.astype(bf16)
        lanes = lane_index(rows)
        extra = q_ref[:, HEAD_WIDTH:].astype(f32)
        for i, part in enumerate(split_parts(jnp.log2(total))):
            extra = jnp.where(lanes == LOG_LANE + i, -part.astype(f32), extra)
        q_out_ref[:, :HEAD_WIDTH] = q_ref[:, :HEAD_WIDTH]
        q_out_ref[:, HEAD_WIDTH:] = extra.astype(bf16)


def attend_stage(q, blocks, places, bounds, meta, carried, last=None):
    rows = q.shape[0]
    kv = blocks[0]
    q_heads = q.shape[1] // (2 * HEAD_WIDTH)
    group = q.shape[1] // kv.shape[1]
    width = q_heads * HEAD_WIDTH
    first = not carried
    wide = 2 * HEAD_WIDTH
    count = len(blocks)
    grid = q_heads if last is None else q_heads // last[1]
    start = 0 if last is None else last[0] * grid
    per_q = pl.BlockSpec((rows, wide), lambda j, m: (0, j + start))
    per_kv = pl.BlockSpec((kv.shape[0], wide), lambda j, m: (0, (j + start) // group))
    per_out = pl.BlockSpec((rows, HEAD_WIDTH), lambda j, m: (0, j + start))
    table = pl.BlockSpec((8, HEAD_WIDTH), lambda j, m: (0, 0))
    running = jax.ShapeDtypeStruct((rows, width), f32)
    if last is not None:
        out_specs = [pl.BlockSpec((rows, HEAD_WIDTH), lambda j, m: (0, j)), per_q, per_out]
        out_shape = [
            jax.ShapeDtypeStruct((rows, grid * HEAD_WIDTH), bf16),
            jax.ShapeDtypeStruct(q.shape, bf16),
            running,
        ]
        scratch = [pltpu.VMEM((rows, HEAD_WIDTH), f32)]
        aliases = {1: 1, 3 + count: 2}
    else:
        out_specs = [per_out, per_out]
        out_shape = [running, running]
        scratch = []
        aliases = {} if first else {3 + count: 0, 4 + count: 1}
    return pl.pallas_call(
        functools.partial(attend_kernel, places=places, first=first, last=last is not None),
        grid_spec=pltpu.PrefetchScalarGridSpec(
            num_scalar_prefetch=1,
            grid=(grid,),
            in_specs=[per_q] + [per_kv] * count + [table] + [per_out] * len(carried),
            out_specs=out_specs,
            scratch_shapes=scratch,
        ),
        out_shape=out_shape,
        input_output_aliases=aliases,
        compiler_params=WHOLE_VMEM,
        cost_estimate=SMALL,
        name="attend_stage",
    )(meta, q, *blocks, bounds, *carried)


def delta_kernel(owners, *refs):
    *pieces, outcome_ref, out_ref = refs
    for i, piece in enumerate(pieces):

        @pl.when(pl.program_id(0) == i)
        def _():
            rows, width = piece.shape
            lanes = lane_index(rows)
            for j in range(width // HEAD_WIDTH):
                head = slice(j * HEAD_WIDTH, (j + 1) * HEAD_WIDTH)
                do = piece[:, head]
                delta = jnp.sum(do.astype(f32) * outcome_ref[:, head], axis=-1, keepdims=True)
                extra = jnp.zeros((rows, HEAD_WIDTH), f32)
                for k, part in enumerate(split_parts(delta)):
                    extra = jnp.where(lanes == k, -part.astype(f32), extra)
                start = 2 * j * HEAD_WIDTH
                out_ref[:, start : start + HEAD_WIDTH] = do
                out_ref[:, start + HEAD_WIDTH : start + 2 * HEAD_WIDTH] = extra.astype(bf16)


def with_delta(pieces, outcome):
    owners = jnp.stack([jnp.asarray(owner, jnp.int32) for unused, owner in pieces])
    rows, width = outcome.shape
    share = rows // len(pieces)
    whole = pl.BlockSpec((share, width), lambda i, m: (0, 0))
    return pl.pallas_call(
        delta_kernel,
        grid_spec=pltpu.PrefetchScalarGridSpec(
            num_scalar_prefetch=1,
            grid=(len(pieces),),
            in_specs=[whole] * len(pieces) + [pl.BlockSpec((share, width), lambda i, m: (m[i], 0))],
            out_specs=pl.BlockSpec((share, 2 * width), lambda i, m: (m[i], 0)),
        ),
        out_shape=jax.ShapeDtypeStruct((rows, 2 * width), bf16),
        compiler_params=WHOLE_VMEM,
        cost_estimate=SMALL,
        name="with_delta",
    )(owners, *[piece for piece, unused in pieces], outcome)


def assemble_kernel(places, *refs, count):
    blocks, out_ref = refs[:count], refs[-1]
    for i, block in enumerate(blocks):

        @pl.when(pl.program_id(0) == i)
        def _():
            out_ref[...] = block[...].astype(out_ref.dtype)


def assemble(entries, rows, kind, total=None, base=None):
    places = jnp.stack([jnp.asarray(place, jnp.int32) for unused, also, place in entries])
    width = entries[0][0].shape[1]
    count = len(entries)
    in_specs = [
        pl.BlockSpec((rows, width), lambda i, m, k=block: (k, 0)) for unused, block, also in entries
    ]
    args = [array for array, unused, also in entries]
    if base is not None:
        in_specs.append(pl.BlockSpec(memory_space=pl.ANY))
        args.append(base)
    return pl.pallas_call(
        functools.partial(assemble_kernel, count=count),
        grid_spec=pltpu.PrefetchScalarGridSpec(
            num_scalar_prefetch=1,
            grid=(count,),
            in_specs=in_specs,
            out_specs=pl.BlockSpec((rows, width), lambda i, m: (m[i], 0)),
        ),
        out_shape=jax.ShapeDtypeStruct((rows * (total or count), width), kind),
        input_output_aliases={} if base is None else {1 + count: 0},
        compiler_params=WHOLE_VMEM,
        cost_estimate=SMALL,
        name="assemble",
    )(places, *args)


def cut_kernel(in_ref, *outs, axis):
    start = 0
    for out_ref in outs:
        size = out_ref.shape[axis]
        part = in_ref[start : start + size, :] if axis == 0 else in_ref[:, start : start + size]
        out_ref[...] = part.astype(f32)
        start += size


def cut_up(array, shapes, axis):
    return pl.pallas_call(
        functools.partial(cut_kernel, axis=axis),
        out_shape=[jax.ShapeDtypeStruct(shape, f32) for shape in shapes],
        compiler_params=WHOLE_VMEM,
        cost_estimate=SMALL,
        name="cut_up",
    )(array)


def cut_columns(array, widths):
    return cut_up(array, [(array.shape[0], width) for width in widths], 1)


def cut_rows(array, heights):
    return cut_up(array, [(height, array.shape[1]) for height in heights], 0)


def attend_back_kernel(meta, q_ref, do_ref, *refs, places, first, group, diagonal):
    count = len(places)
    kv_refs, bounds_ref, refs = refs[:count], refs[count], refs[count + 1 :]
    if not first:
        dq_in, *refs = refs
    dq_ref, dkv_refs, dq_turned, sums = refs[0], refs[1 : 1 + count], refs[1 + count], refs[2 + count :]
    rows = q_ref.shape[0]
    step = lax.rem(pl.program_id(0), group)
    dq_turned[...] = jnp.zeros_like(dq_turned)

    @pl.when(step == 0)
    def _():
        for total in sums:
            total[...] = jnp.zeros_like(total)

    def work(kv_ref, total, lanes, ones, keys, queries, mask):
        key = kv_ref[keys, :HEAD_WIDTH]
        q = q_ref[queries, :]
        do = do_ref[queries, :]
        weight = jnp.exp2(dot_nt(jnp.concatenate([key, lanes[keys, :]], axis=1), q))
        if mask:
            weight = jnp.where(lower_mask(True), weight, 0.0)
        value = jnp.concatenate([kv_ref[keys, HEAD_WIDTH:], ones], axis=1)
        d_score = (weight * dot_nt(value, do)).astype(bf16)
        total[keys, HEAD_WIDTH:] += dot(weight.astype(bf16), do[:, :HEAD_WIDTH])
        total[keys, :HEAD_WIDTH] += dot(d_score, q[:, :HEAD_WIDTH])
        dq_turned[:, queries] += dot_tn(key, d_score)

    for place, kv_ref, total in zip(places, kv_refs, sums):
        key_start = meta[2 + place]
        key_rows = kv_ref.shape[0]

        @pl.when(block_used(meta, key_start, key_rows, rows))
        def _():
            lanes = key_lanes(meta, key_start, key_rows, bounds_ref)
            ones = jnp.where(lane_index(KEY_CHUNK) < 3, 1.0, 0.0).astype(bf16)
            for c in range(key_rows // KEY_CHUNK):
                if diagonal and place == 0:
                    work(kv_ref, total, lanes, ones, chunk(c), chunk(c), True)
                    if c + 1 < rows // KEY_CHUNK:
                        later = slice((c + 1) * KEY_CHUNK, rows)
                        work(kv_ref, total, lanes, ones, chunk(c), later, False)
                else:
                    work(kv_ref, total, lanes, ones, chunk(c), slice(0, rows), False)

    turned = dq_turned[...].T
    dq_ref[...] = turned if first else dq_in[...] + turned

    @pl.when(step == group - 1)
    def _():
        for ref, total in zip(dkv_refs, sums):
            ref[...] = total[...].astype(ref.dtype)


def attend_back(q, do, blocks, places, bounds, meta, dq, diagonal):
    rows = q.shape[0]
    kv = blocks[0]
    q_heads = q.shape[1] // (2 * HEAD_WIDTH)
    group = q.shape[1] // kv.shape[1]
    width = q_heads * HEAD_WIDTH
    first = dq is None
    count = len(places)
    wide = 2 * HEAD_WIDTH
    per_q = pl.BlockSpec((rows, wide), lambda j, m: (0, j))
    per_kv = pl.BlockSpec((kv.shape[0], wide), lambda j, m: (0, j // group))
    per_out = pl.BlockSpec((rows, HEAD_WIDTH), lambda j, m: (0, j))
    table = pl.BlockSpec((8, HEAD_WIDTH), lambda j, m: (0, 0))
    return pl.pallas_call(
        functools.partial(
            attend_back_kernel, places=places, first=first, group=group, diagonal=diagonal
        ),
        grid_spec=pltpu.PrefetchScalarGridSpec(
            num_scalar_prefetch=1,
            grid=(q_heads,),
            in_specs=[per_q, per_q] + [per_kv] * count + [table] + ([] if first else [per_out]),
            out_specs=[per_out] + [per_kv] * count,
            scratch_shapes=[pltpu.VMEM((HEAD_WIDTH, rows), f32)]
            + [pltpu.VMEM((kv.shape[0], wide), f32)] * count,
        ),
        out_shape=[jax.ShapeDtypeStruct((rows, width), f32)]
        + [jax.ShapeDtypeStruct(kv.shape, bf16 if place else f32) for place in places],
        input_output_aliases={} if first else {4 + count: 0},
        compiler_params=WHOLE_VMEM,
        cost_estimate=SMALL,
        name="attend_back",
    )(meta, q, do, *blocks, bounds, *(() if first else (dq,)))


def project_kernel(meta, base_ref, *refs, count):
    lows, highs = refs[:count], refs[count : 2 * count]
    mine, other = refs[2 * count : 3 * count], refs[3 * count : 4 * count]
    gain_ref, share_ref, normed_ref = refs[4 * count :]
    first_core = meta[0] == 0
    total = base_ref[...].astype(f32)
    for low_ref, high_ref, mine_ref, other_ref in zip(lows, highs, mine, other):
        low, high = low_ref[...], high_ref[...]
        total += dot(jnp.where(first_core, low, high), mine_ref[0])
        total += dot(jnp.where(first_core, high, low), other_ref[0])
    inverse = lax.rsqrt(jnp.mean(total * total, axis=-1, keepdims=True) + EPSILON)
    normed_ref[...] = (total * inverse * gain_ref[...]).astype(bf16)

    @pl.when(pl.program_id(0) == meta[1])
    def _():
        share_ref[...] = total


def project(base, pieces, w_mine, w_other, core, me, gain):
    meta = jnp.stack(
        [jnp.asarray(v, jnp.int32) for v in [core, me] + [piece[2] for piece in pieces]]
    )
    rows, width = base.shape
    n_head, half, unused = w_mine.shape
    count = len(pieces)
    step = rows // n_head
    per_row = pl.BlockSpec((step, width), lambda i, m: (i, 0))
    per_piece = pl.BlockSpec((step, half), lambda i, m: (i, 0))
    weights = [
        pl.BlockSpec((1, half, width), lambda i, m, k=k: (m[2 + k], 0, 0)) for k in range(count)
    ]
    return pl.pallas_call(
        functools.partial(project_kernel, count=count),
        grid_spec=pltpu.PrefetchScalarGridSpec(
            num_scalar_prefetch=1,
            grid=(n_head,),
            in_specs=[per_row]
            + [per_piece] * (2 * count)
            + weights
            + weights
            + [pl.BlockSpec((1, width), lambda i, m: (0, 0))],
            out_specs=[pl.BlockSpec((step, width), lambda i, m: (0, 0)), per_row],
        ),
        out_shape=[
            jax.ShapeDtypeStruct((step, width), f32),
            jax.ShapeDtypeStruct((rows, width), bf16),
        ],
        compiler_params=WHOLE_VMEM,
        cost_estimate=SMALL,
        name="project",
    )(
        meta,
        base,
        *[piece[0] for piece in pieces],
        *[piece[1] for piece in pieces],
        *[w_mine] * count,
        *[w_other] * count,
        gain[None, :],
    )


def arranged_shapes(rows, width):
    return [
        jax.ShapeDtypeStruct((rows // 4, width), bf16),
        jax.ShapeDtypeStruct((rows // 4, width), bf16),
        jax.ShapeDtypeStruct((rows // 2, width), bf16),
    ]


def store_arranged(me, outs, share_y, share_x, half, value):
    along_x, along_y, stays = outs
    rows = value.shape[0]
    other_x = share_x ^ (me & 1)
    other_y = share_y ^ (me >> 1)

    def store(ref, place):
        ref[pl.ds(pl.multiple_of(place * rows, rows), rows), :] = value

    if half == 0:
        pl.when(other_x == 1)(lambda: store(along_x, other_y))
        pl.when(other_x == 0)(lambda: store(stays, other_y))
    else:
        pl.when(other_y == 1)(lambda: store(along_y, other_x))
        pl.when(other_y == 0)(lambda: store(stays, 2 + other_x))


def store_all_arranged(me, outs, value):
    rows = value.shape[0] // 8
    for i in range(8):
        block = value[i * rows : (i + 1) * rows, :]
        store_arranged(me, outs, i // 4, i // 2 % 2, i % 2, block)


def meet_kernel(stays_ref, x_ref, y_ref, mine_ref, to_y_ref, to_x_ref):
    rows = mine_ref.shape[0] // 2
    for start, got_ref, sent_ref in ((0, x_ref, to_y_ref), (2, y_ref, to_x_ref)):
        total = stays_ref[start * rows : (start + 2) * rows, :].astype(f32) + got_ref[...].astype(f32)
        mine_ref[start // 2 * rows : (start // 2 + 1) * rows, :] = total[:rows]
        sent_ref[...] = total[rows:].astype(bf16)


def meet(stays, from_x, from_y):
    rows, width = stays.shape
    return pl.pallas_call(
        meet_kernel,
        out_shape=[
            jax.ShapeDtypeStruct((rows // 2, width), f32),
            jax.ShapeDtypeStruct((rows // 4, width), bf16),
            jax.ShapeDtypeStruct((rows // 4, width), bf16),
        ],
        compiler_params=WHOLE_VMEM,
        cost_estimate=SMALL,
        name="meet",
    )(stays, from_x, from_y)


def share_sum(terms):
    first, *rest = terms
    total = first[...].astype(f32)
    if len(rest) == 2:
        return total + jnp.concatenate([part[...].astype(f32) for part in rest], axis=0)
    return total


def add_rows_kernel(base_ref, *refs):
    *terms, out_ref = refs
    out_ref[...] = (base_ref[...] + share_sum(terms)).astype(bf16)


def add_rows(base, terms):
    return pl.pallas_call(
        add_rows_kernel,
        out_shape=jax.ShapeDtypeStruct(base.shape, bf16),
        compiler_params=WHOLE_VMEM,
        cost_estimate=SMALL,
        name="add_rows",
    )(base, *terms)


def norm_backward(grad, x, gain):
    inverse = lax.rsqrt(jnp.mean(x * x, axis=-1, keepdims=True) + EPSILON)
    hat = x * inverse
    scaled = grad * gain
    back = inverse * (scaled - hat * jnp.mean(scaled * hat, axis=-1, keepdims=True))
    return back, jnp.sum(grad * hat, axis=0, keepdims=True)


def turn_kernel(meta, *refs, count):
    terms = refs[:count]
    hidden_ref, dy_ref, gain_ref, mine_ref, other_ref = refs[count : count + 5]
    *outs, grad_ref, branch_ref, gain_grad_ref = refs[count + 5 :]

    @pl.when(pl.program_id(0) == 0)
    def _():
        back, gain_grad_ref[...] = norm_backward(
            share_sum(terms), hidden_ref[...], gain_ref[...]
        )
        total = dy_ref[...].astype(f32) + back
        grad_ref[...] = total
        branch_ref[...] = total.astype(bf16)

    half = mine_ref.shape[1]
    branch = branch_ref[...]
    mine = dot_nt(branch, mine_ref[0])
    other = dot_nt(branch, other_ref[0])
    first_core = meta[0] == 0
    low = jnp.where(first_core, mine, other).astype(bf16)
    high = jnp.where(first_core, other, mine).astype(bf16)
    for i, out_ref in enumerate(outs):

        @pl.when(pl.program_id(0) == i)
        def _():
            out_ref[:, :half] = low
            out_ref[:, half:] = high


def turn(terms, hidden, dy, gain, w_mine, w_other, core, me):
    rows, width = hidden.shape
    n_head, half, unused = w_mine.shape
    meta = jnp.stack([jnp.asarray(v, jnp.int32) for v in (core, me)])

    def full(array):
        return pl.BlockSpec(array.shape, lambda i, m: (0, 0))

    weight = pl.BlockSpec((1, half, width), lambda i, m: (i ^ m[1], 0, 0))
    share = pl.BlockSpec((rows, width), lambda i, m: (0, 0))
    return pl.pallas_call(
        functools.partial(turn_kernel, count=len(terms)),
        grid_spec=pltpu.PrefetchScalarGridSpec(
            num_scalar_prefetch=1,
            grid=(n_head,),
            in_specs=[full(term) for term in terms]
            + [
                share,
                pl.BlockSpec((rows, width), lambda i, m: (m[1], 0)),
                pl.BlockSpec((1, width), lambda i, m: (0, 0)),
                weight,
                weight,
            ],
            out_specs=[
                *[pl.BlockSpec((rows, 2 * half), lambda i, m: (0, 0))] * n_head,
                share,
                share,
                pl.BlockSpec((1, width), lambda i, m: (0, 0)),
            ],
        ),
        out_shape=[
            *[jax.ShapeDtypeStruct((rows, 2 * half), bf16)] * n_head,
            jax.ShapeDtypeStruct((rows, width), f32),
            jax.ShapeDtypeStruct((rows, width), bf16),
            jax.ShapeDtypeStruct((1, width), f32),
        ],
        compiler_params=WHOLE_VMEM,
        cost_estimate=SMALL,
        name="turn",
    )(meta, *terms, hidden, dy, gain[None, :], w_mine, w_other)


def last_kernel(meta, *refs, count):
    terms = refs[:count]
    x_ref, grad_ref, gain_ref, rider_ref, out_ref = refs[count:]
    rows = x_ref.shape[0]
    back, unused = norm_backward(share_sum(terms), x_ref[...].astype(f32), gain_ref[...])
    out_ref[:rows, :] = (grad_ref[...] + back).astype(bf16)
    out_ref[rows:, :] = rider_ref[...]


def last(terms, tokens, hidden_grad, gain, rider, me):
    rows, width = hidden_grad.shape
    meta = jnp.asarray(me, jnp.int32)[None]

    def full(array):
        return pl.BlockSpec(array.shape, lambda i, m: (0, 0))

    out_rows = rows + rider.shape[0]
    return pl.pallas_call(
        functools.partial(last_kernel, count=len(terms)),
        grid_spec=pltpu.PrefetchScalarGridSpec(
            num_scalar_prefetch=1,
            grid=(1,),
            in_specs=[full(term) for term in terms]
            + [
                pl.BlockSpec((rows, width), lambda i, m: (m[0], 0)),
                full(hidden_grad),
                pl.BlockSpec((1, width), lambda i, m: (0, 0)),
                full(rider),
            ],
            out_specs=pl.BlockSpec((out_rows, width), lambda i, m: (0, 0)),
        ),
        out_shape=jax.ShapeDtypeStruct((out_rows, width), bf16),
        compiler_params=WHOLE_VMEM,
        cost_estimate=SMALL,
        name="last",
    )(meta, *terms, tokens, hidden_grad, gain[None, :], rider)


def feed_kernel(x_ref, gate_w_ref, up_w_ref, d_mixed_ref, mixed_ref, gate_ref, up_ref, sum_ref):
    x = x_ref[...]
    gate = dot(x, gate_w_ref[...])
    up = dot(x, up_w_ref[...])
    d_mixed = d_mixed_ref[...]
    sigmoid = 0.5 * jnp.tanh(0.5 * gate) + 0.5
    silu = gate * sigmoid
    mixed_ref[...] = (silu * up).astype(bf16)
    gate_low = (d_mixed * up * (sigmoid * (1.0 + gate * (1.0 - sigmoid)))).astype(bf16)
    up_low = (d_mixed * silu).astype(bf16)
    gate_ref[...] = gate_low
    up_ref[...] = up_low
    step = gate_low.shape[1]
    sum_ref[:, :step] = dot_tn(x, gate_low).astype(bf16)
    sum_ref[:, step:] = dot_tn(x, up_low).astype(bf16)


def feed(x, w_gate, w_up, d_mixed):
    rows, width = x.shape
    hidden = w_gate.shape[1]
    whole = pl.BlockSpec((rows, width), lambda i: (0, 0))
    weight = pl.BlockSpec((width, HIDDEN_STEP), lambda i: (0, i))
    act = pl.BlockSpec((rows, HIDDEN_STEP), lambda i: (0, i))
    return pl.pallas_call(
        feed_kernel,
        grid=(hidden // HIDDEN_STEP,),
        in_specs=[whole, weight, weight, act],
        out_specs=[act, act, act, pl.BlockSpec((width, 2 * HIDDEN_STEP), lambda i: (0, i))],
        out_shape=[jax.ShapeDtypeStruct((rows, hidden), bf16)] * 3
        + [jax.ShapeDtypeStruct((width, 2 * hidden), bf16)],
        compiler_params=WHOLE_VMEM,
        cost_estimate=SMALL,
        name="feed",
    )(x, w_gate, w_up, d_mixed)


def split_kernel(sum_ref, gate_ref, up_ref):
    step = gate_ref.shape[1]
    gate_ref[...] = sum_ref[:, :step].astype(f32)
    up_ref[...] = sum_ref[:, step:].astype(f32)


def split_gate_up(sums):
    rows, width = sums.shape
    out = pl.BlockSpec((rows, HIDDEN_STEP), lambda i: (0, i))
    return pl.pallas_call(
        split_kernel,
        grid=(width // (2 * HIDDEN_STEP),),
        in_specs=[pl.BlockSpec((rows, 2 * HIDDEN_STEP), lambda i: (0, i))],
        out_specs=[out, out],
        out_shape=[jax.ShapeDtypeStruct((rows, width // 2), f32)] * 2,
        compiler_params=WHOLE_VMEM,
        cost_estimate=SMALL,
        name="split_gate_up",
    )(sums)


def products_kernel(meta, *refs, count, turned, arranged):
    lefts, rights, outs = refs[:count], refs[count : 2 * count], refs[2 * count :]
    total = 0.0
    for left, right in zip(lefts, rights):
        total += (dot_nt if turned else dot)(left[...], right[...])
    if arranged:
        store_all_arranged(meta[0], outs, total.astype(bf16))
    else:
        outs[0][...] = total.astype(bf16)


def products(lefts, rights, turned, me, arranged):
    meta = jnp.asarray(me, jnp.int32)[None]
    rows, depth = lefts[0].shape
    width = rights[0].shape[0 if turned else 1]
    step = width // 4
    whole = pl.BlockSpec((rows, depth), lambda i, m: (0, 0))
    if turned:
        right = pl.BlockSpec((step, depth), lambda i, m: (i, 0))
    else:
        right = pl.BlockSpec((depth, step), lambda i, m: (0, i))
    shapes = arranged_shapes(rows, width) if arranged else [jax.ShapeDtypeStruct((rows, width), bf16)]
    return pl.pallas_call(
        functools.partial(products_kernel, count=len(lefts), turned=turned, arranged=arranged),
        grid_spec=pltpu.PrefetchScalarGridSpec(
            num_scalar_prefetch=1,
            grid=(width // step,),
            in_specs=[whole] * len(lefts) + [right] * len(lefts),
            out_specs=[pl.BlockSpec((v.shape[0], step), lambda i, m: (0, i)) for v in shapes],
        ),
        out_shape=shapes,
        compiler_params=pltpu.CompilerParams(vmem_limit_bytes=46 * MIB),
        cost_estimate=SMALL,
        name="products",
    )(meta, *lefts, *rights)


def down_sums_kernel(mixed_ref, dy_ref, out_ref):
    count, unused, share = out_ref.shape
    for i in range(count):
        out_ref[i] = dot_tn(mixed_ref[...], dy_ref[:, i * share : (i + 1) * share]).astype(bf16)


def down_sums(mixed, dy, shares, more):
    rows, width = dy.shape
    share = width // shares
    hidden = mixed.shape[1]
    return pl.pallas_call(
        down_sums_kernel,
        grid=(shares // 2,),
        in_specs=[
            pl.BlockSpec(mixed.shape, lambda i: (0, 0)),
            pl.BlockSpec((rows, 2 * share), lambda i: (0, i)),
        ],
        out_specs=pl.BlockSpec((2, hidden, share), lambda i: (i, 0, 0)),
        out_shape=jax.ShapeDtypeStruct((shares, hidden + more, share), bf16),
        compiler_params=WHOLE_VMEM,
        cost_estimate=SMALL,
        name="down_sums",
    )(mixed, dy)


def output_sums_kernel(owners, *refs, groups):
    o_refs, pieces, (out_ref, branch) = refs[:groups], refs[groups:-3], refs[-2:]
    for i, piece in enumerate(pieces):
        rows = piece.shape[0]
        branch[pl.ds(pl.multiple_of(owners[i] * rows, rows), rows), :] = piece[...]
    count, unused, share = out_ref.shape
    start = 0
    for o_ref in o_refs:
        end = start + o_ref.shape[1]
        for i in range(count):
            part = branch[:, i * share : (i + 1) * share]
            out_ref[i, start:end, :] = dot_tn(o_ref[...], part).astype(bf16)
        start = end


def output_sums(o_groups, pieces, base):
    owners = jnp.stack([jnp.asarray(owner, jnp.int32) for unused, owner in pieces])
    shares, all_rows, share = base.shape
    size = sum(o.shape[1] for o in o_groups)
    place = all_rows // size - 1
    return pl.pallas_call(
        functools.partial(output_sums_kernel, groups=len(o_groups)),
        grid_spec=pltpu.PrefetchScalarGridSpec(
            num_scalar_prefetch=1,
            grid=(shares // 2,),
            in_specs=[pl.BlockSpec(o.shape, lambda i, m: (0, 0)) for o in o_groups]
            + [
                pl.BlockSpec((piece.shape[0], 2 * share), lambda i, m: (0, i))
                for piece, unused in pieces
            ]
            + [pl.BlockSpec(memory_space=pl.ANY)],
            out_specs=pl.BlockSpec((2, size, share), lambda i, m: (i, place, 0)),
            scratch_shapes=[pltpu.VMEM((o_groups[0].shape[0], 2 * share), bf16)],
        ),
        out_shape=jax.ShapeDtypeStruct(base.shape, bf16),
        input_output_aliases={1 + len(o_groups) + len(pieces): 0},
        compiler_params=WHOLE_VMEM,
        cost_estimate=SMALL,
        name="output_sums",
    )(owners, *o_groups, *[piece for piece, unused in pieces], base)


def pass_on_kernel(part_ref, theirs_ref, *refs, count):
    arrived, outs = refs[:-count], refs[-count:]
    size = outs[0].shape[0]
    for i, out_ref in enumerate(outs):
        rows = slice(i * size, (i + 1) * size)
        out_ref[...] = (part_ref[rows, :] + theirs_ref[rows, :].astype(f32)).astype(bf16)
    if arrived:
        whole = jnp.concatenate([ref[...] for ref in arrived], axis=0).astype(f32)
        for i, out_ref in enumerate(outs):
            rows = slice(i * size, (i + 1) * size)
            total = part_ref[rows, :] + theirs_ref[rows, :].astype(f32) + whole[rows]
            out_ref[...] = total.astype(bf16)


def pass_on(part, theirs, arrived, count):
    rows, width = part.shape
    return pl.pallas_call(
        functools.partial(pass_on_kernel, count=count),
        out_shape=[jax.ShapeDtypeStruct((rows // count, width), bf16)] * count,
        compiler_params=WHOLE_VMEM,
        cost_estimate=SMALL,
        name="pass_on",
    )(part, theirs, *arrived)


def leave_kernel(
    meta,
    x_ref,
    q_ref,
    dkv_ref,
    theirs_ref,
    first_ref,
    second_ref,
    raw_ref,
    key_gain_ref,
    cos_ref,
    sin_ref,
    q_w_ref,
    key_w_ref,
    value_w_ref,
    key_ref,
    value_ref,
    gain_grad_ref,
    norm_grad_ref,
    *refs,
    arranged,
):
    *outs, arrived_ref = refs

    @pl.when(pl.program_id(0) == 0)
    def _():
        size = first_ref.shape[0]
        for i, ref in enumerate((first_ref, second_ref)):
            arrived_ref[i * size : (i + 1) * size, :] = ref[...]
        gain_grad_ref[...] = jnp.zeros_like(gain_grad_ref)
        norm_grad_ref[...] = jnp.zeros_like(norm_grad_ref)

    rows = dkv_ref.shape[0]
    here = pl.ds(pl.multiple_of(pl.program_id(0) * rows, rows), rows)
    arrived = arrived_ref[here, :]
    dkv = dkv_ref[...] + theirs_ref[...].astype(f32) + arrived.astype(f32)
    for j in range(key_ref.shape[1] // HEAD_WIDTH):
        head = slice(j * HEAD_WIDTH, (j + 1) * HEAD_WIDTH)
        start = 2 * j * HEAD_WIDTH
        grad, gain_grad = head_backward(
            raw_ref[:, head],
            dkv[:, start : start + HEAD_WIDTH] * (1.0 / LOG2E),
            key_gain_ref[...],
            cos_ref[...],
            sin_ref[...],
        )
        key_ref[:, head] = grad
        value_ref[:, head] = dkv[:, start + HEAD_WIDTH : start + 2 * HEAD_WIDTH].astype(bf16)
        gain_grad_ref[...] += gain_grad
    total = dot_nt(q_ref[...], q_w_ref[...])
    total += dot_nt(key_ref[...], key_w_ref[...])
    total += dot_nt(value_ref[...], value_w_ref[...])
    result = total.astype(bf16)
    if arranged:
        block = result.shape[0] // 4
        for i in range(4):
            store_arranged(
                meta[0],
                outs,
                pl.program_id(0),
                i // 2,
                i % 2,
                result[i * block : (i + 1) * block, :],
            )
    else:
        outs[0][...] = result
    x = x_ref[...].astype(f32)
    hat = x * lax.rsqrt(jnp.mean(x * x, axis=-1, keepdims=True) + EPSILON)
    norm_grad_ref[...] += jnp.sum(total * hat, axis=0, keepdims=True)


def leave(tokens, q_grad, dkv, theirs, arrived, key_raw, key_gain, cosine, sine, weights, me, arranged):
    meta = jnp.asarray(me, jnp.int32)[None]
    rows, width = tokens.shape
    kv_width = key_raw.shape[1]
    step = rows // 2

    def per_row(array):
        return pl.BlockSpec((step, array.shape[1]), lambda i, m: (i, 0))

    def full(array):
        return pl.BlockSpec(array.shape, lambda i, m: (0, 0))

    key_gain = key_gain[None, :]
    if arranged:
        shapes = arranged_shapes(rows, width)
        out_specs = [full(v) for v in shapes]
    else:
        shapes = [jax.ShapeDtypeStruct((rows, width), bf16)]
        out_specs = [per_row(shapes[0])]
    return pl.pallas_call(
        functools.partial(leave_kernel, arranged=arranged),
        grid_spec=pltpu.PrefetchScalarGridSpec(
            num_scalar_prefetch=1,
            grid=(2,),
            in_specs=[per_row(v) for v in (tokens, q_grad, dkv, theirs)]
            + [full(v) for v in arrived]
            + [per_row(key_raw), full(key_gain), per_row(cosine), per_row(sine)]
            + [full(v) for v in weights],
            out_specs=[
                per_row(key_raw),
                per_row(key_raw),
                pl.BlockSpec((1, HEAD_WIDTH), lambda i, m: (0, 0)),
                pl.BlockSpec((1, width), lambda i, m: (0, 0)),
            ]
            + out_specs,
            scratch_shapes=[pltpu.VMEM((rows, theirs.shape[1]), bf16)],
        ),
        out_shape=[
            jax.ShapeDtypeStruct((rows, kv_width), bf16),
            jax.ShapeDtypeStruct((rows, kv_width), bf16),
            jax.ShapeDtypeStruct((1, HEAD_WIDTH), f32),
            jax.ShapeDtypeStruct((1, width), f32),
        ]
        + shapes,
        compiler_params=WHOLE_VMEM,
        cost_estimate=SMALL,
        name="leave",
    )(meta, tokens, q_grad, dkv, theirs, *arrived, key_raw, key_gain, cosine, sine, *weights)


def attn_sums_kernel(x_ref, *refs):
    *terms, out_ref = refs
    x = x_ref[...]
    start = 0
    for ref in terms:
        out_ref[:, start : start + ref.shape[1]] = dot_tn(x, ref[...]).astype(bf16)
        start += ref.shape[1]


def attn_sums(x, terms):
    rows, width = x.shape
    step = width // 8
    out_width = sum(term.shape[1] for term in terms)
    return pl.pallas_call(
        attn_sums_kernel,
        grid=(width // step,),
        in_specs=[pl.BlockSpec((rows, step), lambda i: (0, i))]
        + [pl.BlockSpec(term.shape, lambda i: (0, 0)) for term in terms],
        out_specs=pl.BlockSpec((step, out_width), lambda i: (i, 0)),
        out_shape=jax.ShapeDtypeStruct((width, out_width), bf16),
        compiler_params=WHOLE_VMEM,
        cost_estimate=SMALL,
        name="attn_sums",
    )(x, *terms)


def after(values):
    return lax.optimization_barrier(values)


def pick(array, index):
    return lax.dynamic_index_in_dim(array, index, 0, keepdims=False)


def solution(mesh):
    n_seq = mesh.shape["seq"]
    n_head = mesh.shape["head"]
    n_chip = n_seq // 2

    def swap_core(value):
        return lax.ppermute(value, "seq", [(i, i ^ 1) for i in range(n_seq)])

    def to_next(value):
        return lax.ppermute(value, "seq", [(i, i + 2) for i in range(n_seq - 2)])

    def to_previous(value):
        return lax.ppermute(value, "seq", [(i + 2, i) for i in range(n_seq - 2)])

    def across(value, bits):
        return lax.ppermute(value, "head", [(i, i ^ bits) for i in range(n_head)])

    def gather_steps(value):
        me = lax.axis_index("head")
        if n_head != 4:
            every = yield lax.all_gather(value, "head", axis=0)
            return [(every[i], i) for i in range(n_head)]
        half = value.shape[0] // 2
        by_x, by_y = yield across(value, 1), across(value, 2)
        low, high = yield across(by_x[:half], 2), across(by_y[half:], 1)
        far = jnp.concatenate([low, high], axis=0)
        return [(value, me), (by_x, me ^ 1), (by_y, me ^ 2), (far, me ^ 3)]

    def rider_entries(value, count):
        me = lax.axis_index("head")
        half = count // 2
        if n_head != 4:
            every = yield lax.all_gather(value, "head", axis=0)
            entries = [(every[i], k, 2 * i + k) for i in range(n_head) for k in range(2)]
            return entries, [every[i, count:] for i in range(n_head)]
        by_x, by_y = yield across(value, 1), across(value, 2)
        low, high = yield across(by_x[:half], 2), across(by_y[half:], 1)
        owners = ((value, me), (by_x, me ^ 1), (by_y, me ^ 2))
        entries = [(array, k, 2 * owner + k) for array, owner in owners for k in range(2)]
        entries += [(low, 0, 2 * (me ^ 3)), (high, 0, 2 * (me ^ 3) + 1)]
        return entries, [value[count:], by_x[count:], by_y[count:], high[half:]]

    def scatter_steps(value):
        if n_head != 4:
            total = yield lax.psum_scatter(value[0], "head", scatter_dimension=0, tiled=True)
            return (total,)
        along_x, along_y, stays = value
        from_x, from_y = yield across(along_x, 1), across(along_y, 2)
        mine, to_y, to_x = meet(stays, from_x, from_y)
        first, second = yield across(to_y, 2), across(to_x, 1)
        return mine, first, second

    def run_steps(steps, works=()):
        works = list(works)
        made = []
        arrived = next(steps)
        while True:
            if works:
                arrived, done = after((arrived, works.pop(0)()))
                made.append(done)
            try:
                arrived = steps.send(arrived)
            except StopIteration as stop:
                return stop.value, made + [work() for work in works]

    def end_steps(steps, arrived):
        try:
            steps.send(arrived)
        except StopIteration as stop:
            return stop.value

    def exchange_head(value):
        me = lax.axis_index("head")
        if n_head == 4:
            return [(value[0], me)] + [(across(value[i], i), me ^ i) for i in (3, 1, 2)]
        value = jnp.stack(value)
        ordered = jnp.stack([pick(value, i ^ me) for i in range(n_head)])
        got = lax.all_to_all(ordered, "head", 0, 0)
        return [(got[i], i) for i in range(n_head)]

    def body(
        tokens,
        lengths,
        norm1_gain,
        w_query,
        key_matrix,
        value_matrix,
        query_gain,
        key_gain,
        w_output,
        norm2_gain,
        w_gate,
        w_up,
        w_down,
        cotangent,
    ):
        rows = tokens.shape[0]
        share = rows // n_head
        seq_index = lax.axis_index("seq")
        head_index = lax.axis_index("head")
        chip, core = seq_index // 2, seq_index % 2
        cut = n_head == 4

        index = seq_index * rows + jnp.arange(rows, dtype=jnp.int32)
        begin = locate(index, lengths)
        cosine, sine = rotary(index - begin)
        ends = jnp.cumsum(lengths)
        n_lengths = lengths.shape[0]
        bounds = jnp.zeros((8, HEAD_WIDTH), jnp.int32).at[0].set(2**30)
        bounds = bounds.at[0, :n_lengths].set(ends - lengths).at[1, :n_lengths].set(ends)

        def stage_meta(stage):
            source = 2 * (chip - stage)
            return jnp.stack(
                [seq_index * rows, begin[0], (source + core) * rows, (source + 1 - core) * rows]
            ).astype(jnp.int32)

        metas = [stage_meta(stage) for stage in range(n_chip)]

        first_in, key_raw, current = enter(
            tokens, norm1_gain, key_matrix, value_matrix, key_gain, cosine, sine
        )
        sibling = swap_core(current)
        following = to_next(current)

        half_rows = w_output.shape[0] // 2
        w_late, unused = after((w_output, current))
        w_half = lax.dynamic_slice_in_dim(w_late, core * half_rows, half_rows, 0)
        w_mine = lax.all_gather(w_half, "head", axis=0)

        query_raw = dot(first_in, w_query)
        q_wide = query_prep(metas[0], query_raw, query_gain, cosine, sine, bounds)
        following, q_wide = after((following, q_wide))

        blocks = []
        carried = ()
        for stage in range(n_chip):
            blocks.append((current, sibling))
            if stage + 2 < n_chip:
                current = following
                sibling = swap_core(current)
                following = to_next(current)
            if stage == n_chip - 1:
                break
            carried = attend_stage(q_wide, blocks[stage], (0, 1), bounds, metas[stage], carried)
            if stage + 3 < n_chip:
                following, carried = after((following, carried))
            if stage + 2 == n_chip:
                current, carried = after((following, carried))
                sibling = swap_core(current)
        groups = 2 if cut else 1
        w_mine, sibling, carried = after((w_mine, sibling, carried))
        blocks[-1] = (current, sibling)
        w_other = swap_core(w_mine)
        outcome, total = carried
        o_first, q_back, outcome = attend_stage(
            q_wide, blocks[-1], (0, 1), bounds, metas[-1], (outcome, total), (0, groups)
        )
        if cut:
            first_steps = gather_steps(o_first)
            got_first = next(first_steps)
            o_second, q_back, outcome = attend_stage(
                q_back, blocks[-1], (0, 1), bounds, metas[-1], (outcome, total), (1, groups)
            )
            got_first, unused = after((got_first, o_second))
            second_steps = gather_steps(o_second)
            got_second = next(second_steps)
            got_first = first_steps.send(got_first)
            o_groups = (o_first, o_second)
            dy, unused = after((cotangent, o_second))
            d_mixed = dot_nt(dy, w_down)
            got_second, d_mixed = after((got_second, d_mixed))
            got_second = second_steps.send(got_second)
            got_first, d_mixed = after((got_first, d_mixed))
            first_pieces = end_steps(first_steps, got_first)
            second_pieces = end_steps(second_steps, got_second)
            pieces = [(low[0], high[0], low[1]) for low, high in zip(first_pieces, second_pieces)]
        else:
            o_groups = (o_first,)
            half = o_first.shape[1] // 2
            every = lax.all_gather(o_first, "head", axis=0)
            pieces = [(every[i, :, :half], every[i, :, half:], i) for i in range(n_head)]
            d_mixed = dot_nt(cotangent, w_down)
        my_hidden, second_in = project(
            tokens, pieces, w_mine, w_other, core, head_index, norm2_gain
        )
        def scatter_seq(value, tiled):
            return lax.psum_scatter(value, "seq", scatter_dimension=0, tiled=tiled)

        mixed_low, gate_low, up_low, gate_up_sum = feed(second_in, w_gate, w_up, d_mixed)
        grad_gate_up = scatter_seq(gate_up_sum, True)

        flow = scatter_steps(products((gate_low, up_low), (w_gate, w_up), True, head_index, cut))
        got = next(flow)
        down_part = products((mixed_low,), (w_down,), False, head_index, cut)
        got, down_part = after((got, down_part))
        if cut:
            got = flow.send(got)
        column_sum = down_sums(mixed_low, cotangent, n_seq, w_output.shape[0])
        got, column_sum = after((got, column_sum))
        terms = end_steps(flow, got)
        *do_pieces, hidden_grad, my_branch, grad_norm2 = turn(
            terms, my_hidden, cotangent, norm2_gain, w_mine, w_other, core, head_index
        )
        do_wide = with_delta(exchange_head(do_pieces), outcome)
        down_part, my_branch, do_wide = after((down_part, my_branch, do_wide))

        dq = None
        parts = []
        moving = []
        landed = []
        hops = 0

        def hop_piece():
            if not moving:
                return None
            value = moving.pop(0)
            return lambda: to_previous(value)

        def stage_work(stage, places=(0, 1)):
            chosen = [blocks[stage][place] for place in places]
            return attend_back(
                q_back, do_wide, chosen, places, bounds, metas[stage], dq, stage == 0
            )

        def next_hop():
            nonlocal dq, hops
            if hops < n_chip - 1 and len(parts) > hops and len(landed) == (2 if hops else 0) and hops < n_chip - 1:
                sent, dq = after((pass_on(*parts[hops], landed, 2), dq))
                landed.clear()
                moving.extend(sent)
                hops += 1

        branch_steps = gather_steps(my_branch)
        (dq, dkv_a, dkv_b), got_branch = after(
            (stage_work(n_chip - 1), next(branch_steps))
        )
        theirs, dq = after((swap_core(dkv_b), dq))
        parts.append((dkv_a, theirs))
        next_hop()
        flying = hop_piece()()
        if cut:
            got_branch = branch_steps.send(got_branch)
        (dq, dkv_a, dkv_b), got_branch, flying = after(
            (stage_work(n_chip - 2), got_branch, flying)
        )
        branch_pieces = end_steps(branch_steps, got_branch)
        landed.append(flying)
        parts.append((dkv_a, swap_core(dkv_b)))
        flying = hop_piece()()
        column_sum = output_sums(o_groups, branch_pieces, column_sum)
        dkv_a, theirs = parts[1]
        column_sum, flying, theirs, dq = after((column_sum, flying, theirs, dq))
        parts[1] = (dkv_a, theirs)
        landed.append(flying)
        grad_gate_up, column_sum, dq, landed[:] = after(
            (grad_gate_up, column_sum, dq, list(landed))
        )
        grad_columns = scatter_seq(column_sum, False)
        next_hop()
        down_part, dq = after((down_part, dq))
        mixed_steps = scatter_steps(down_part)
        got_mixed = next(mixed_steps)
        for stage in reversed(range(1, n_chip - 2)):
            hop = hop_piece()
            flying = None if hop is None else hop()
            (dq, dkv_a, dkv_b), got_mixed, flying = after((stage_work(stage), got_mixed, flying))
            if hop is not None:
                landed.append(flying)
            parts.append((dkv_a, swap_core(dkv_b)))
            next_hop()
        if cut:
            got_mixed = mixed_steps.send(got_mixed)
        hop = hop_piece()
        flying = None if hop is None else hop()
        (dq, dkv_b), got_mixed, flying = after((stage_work(0, (1,)), got_mixed, flying))
        if hop is not None:
            landed.append(flying)
        theirs = swap_core(dkv_b)
        next_hop()
        my_mixed = add_rows(my_hidden, end_steps(mixed_steps, got_mixed))
        my_mixed, dq = after((my_mixed, dq))
        mixed_steps = gather_steps(my_mixed)
        got_mixed = next(mixed_steps)
        hop = hop_piece()
        flying = None if hop is None else hop()
        (dq, dkv_a), theirs, flying = after((stage_work(0, (0,)), theirs, flying))
        if hop is not None:
            landed.append(flying)
        parts.append((dkv_a, theirs))
        while hops < n_chip - 1:
            while len(landed) < 2:
                landed.append(hop_piece()())
            next_hop()
        flying = [hop_piece()() for unused in range(2 - len(landed))]
        query_grad, grad_qgain = head_back(query_raw, dq, query_gain, cosine, sine, SCORE_SCALE, 1)
        if cut:
            got_mixed, query_grad = after((got_mixed, query_grad))
            got_mixed = mixed_steps.send(got_mixed)
        flying, got_mixed, query_grad = after((flying, got_mixed, query_grad))
        landed = (*landed, *flying)
        mixed_pieces = end_steps(mixed_steps, got_mixed)
        key_grad, value_grad, grad_kgain, grad_norm1, *first_part = leave(
            tokens,
            query_grad,
            *parts[-1],
            landed,
            key_raw,
            key_gain,
            cosine,
            sine,
            (w_query, key_matrix, value_matrix),
            head_index,
            cut,
        )
        gains = jnp.concatenate([grad_norm1[0], grad_norm2[0], grad_qgain[0], grad_kgain[0]])
        gains = gains.reshape(-1, HEAD_WIDTH)

        def sum_seq(total, bits):
            for bit in bits:
                total = total + lax.ppermute(total, "seq", [(i, i ^ bit) for i in range(n_seq)])
            return total

        bits = [1 << k for k in range(n_seq.bit_length() - 1)]
        steps = scatter_steps(first_part)
        got = next(steps)
        attn_sum = attn_sums(first_in, (query_grad, key_grad, value_grad))
        gains = sum_seq(gains, bits[:1])
        gains, attn_sum = after((gains, attn_sum))
        got, gains, attn_sum = after((got, gains, attn_sum))
        if cut:
            got = steps.send(got)
        grad_columns, attn_sum = after((grad_columns, attn_sum))
        grad_attn = scatter_seq(attn_sum, True)
        grad_query, grad_key, grad_value = cut_columns(
            grad_attn, (query_grad.shape[1], key_grad.shape[1], value_grad.shape[1])
        )
        got, gains = after((got, sum_seq(gains, bits[1:])))
        terms = end_steps(steps, got)

        width = tokens.shape[1]
        n_gains = gains.size
        gain_rows = -(-n_gains // width)
        flat = jnp.pad(gains.reshape(-1), (0, gain_rows * width - n_gains))
        high = lax.reduce_precision(flat, 8, 7)
        middle = lax.reduce_precision(flat - high, 8, 7)
        rider = jnp.concatenate([high, middle, flat - high - middle]).astype(bf16)
        rider = rider.reshape(3 * gain_rows, width)
        rider = jnp.pad(rider, ((0, -rider.shape[0] % 16), (0, 0)))
        my_tokens_grad = last(terms, tokens, hidden_grad, norm1_gain, rider, head_index)
        steps = rider_entries(my_tokens_grad, share)
        got = next(steps)
        mixed = assemble([(piece, 0, owner) for piece, owner in mixed_pieces], share, bf16)
        grad_down, grad_output = cut_rows(grad_columns, (w_gate.shape[1], w_output.shape[0]))
        grad_gate, grad_up = split_gate_up(grad_gate_up)
        got, mixed, grad_down, grad_output, grad_gate, grad_up = after(
            (got, mixed, grad_down, grad_output, grad_gate, grad_up)
        )
        if cut:
            got = steps.send(got)
        entries, gain_pieces = end_steps(steps, got)
        near = len(entries) - 2
        grad_tokens = assemble(entries[:near], share // 2, f32, len(entries))
        grad_tokens = assemble(entries[near:], share // 2, f32, len(entries), grad_tokens)
        gains = sum(part[: 3 * gain_rows].astype(f32) for part in gain_pieces)
        gains = jnp.sum(gains.reshape(3, -1), axis=0)
        grad_norm1, grad_norm2 = gains[:width], gains[width : 2 * width]
        grad_qgain = gains[2 * width : 2 * width + HEAD_WIDTH]
        grad_kgain = gains[2 * width + HEAD_WIDTH : n_gains]
        return (
            mixed,
            grad_tokens,
            grad_norm1,
            grad_query,
            grad_key,
            grad_value,
            grad_qgain,
            grad_kgain,
            grad_output,
            grad_norm2,
            grad_gate,
            grad_up,
            grad_down,
        )

    in_specs = (
        P("seq", None),
        P(),
        P(),
        P(None, "head"),
        P(None, "head"),
        P(None, "head"),
        P(),
        P(),
        P("head", None),
        P(),
        P(None, "head"),
        P(None, "head"),
        P("head", None),
        P("seq", None),
    )
    out_specs = (
        P("seq", None),
        P("seq", None),
        P(),
        P("seq", "head"),
        P("seq", "head"),
        P("seq", "head"),
        P(),
        P(),
        P("head", "seq"),
        P(),
        P("seq", "head"),
        P("seq", "head"),
        P("head", "seq"),
    )
    return jax.shard_map(body, mesh=mesh, in_specs=in_specs, out_specs=out_specs, check_vma=False)
```
